32 devices in a mesh: section: 2 (over core), seq: 4 (over y, x), dp: 4 (over z).
Axes of the slice: x: 2, y: 2, z: 4, core: 2. Of those that a mesh axis runs over, the one named last changes fastest.
Arguments:
- hidden_in: bfloat16 [8, 1024, 768], P('dp', 'seq'), may hold values from -6 to 6
- cotangent: bfloat16 [8, 1024, 768], P('dp', 'seq'), may hold values from -6 to 6
- norm_gain: float32 [2, 768], P('section'), may hold values from 0.5 to 1.5
- in_weight: bfloat16 [2, 768, 3352], P('section', 'seq'), may hold values from -0.21875 to 0.21875
- conv_weight: float32 [2, 4, 1792], P('section'), may hold values from -3 to 3
- conv_bias: float32 [2, 1792], P('section'), may hold values from -2 to 2
- dt_bias: float32 [2, 24], P('section'), may hold values from -9 to -4.5
- a_log: float32 [2, 24], P('section'), may hold values from 0 to 2.8
- skip: float32 [2, 24], P('section'), may hold values from 0.5 to 1.5
- gate_gain: float32 [2, 1536], P('section'), may hold values from 0.5 to 1.5
- out_weight: bfloat16 [2, 1536, 768], P('section', 'seq'), may hold values from -0.15625 to 0.15625
Outputs:
- hidden_out: bfloat16 [8, 1024, 768], P('dp', 'seq', 'section')
- grad_in: bfloat16 [8, 1024, 768], P('dp', 'seq', 'section')
- grad_norm_gain: float32 [2, 768], P('section')
- grad_in_weight: float32 [2, 768, 3352], P('section', 'seq')
- grad_conv_weight: float32 [2, 4, 1792], P('section')
- grad_conv_bias: float32 [2, 1792], P('section')
- grad_dt_bias: float32 [2, 24], P('section')
- grad_a_log: float32 [2, 24], P('section')
- grad_skip: float32 [2, 24], P('section')
- grad_gate_gain: float32 [2, 1536], P('section')
- grad_out_weight: float32 [2, 1536, 768], P('section', 'seq')
The draws below stay inside these ranges and needn't reach their ends.
All inputs are finite; a program needn't handle non-finite values.
Results may differ from the reference program's by a relative error of at most 0.018.
Values may be sent and summed in bfloat16 or wider, within the bound.
No kernel may reach another device: no remote copies, remote signals or barrier semaphores. Data moves between devices by JAX's collectives and lax.ppermute only.
A program may use at most 192 MiB of HBM per device.

```python
import jax
import jax.numpy as jnp
from jax import lax

D = 768
HEADS = 24
HDIM = 64
STATE = 128
KERNEL = 4
BLOCK = 256
INNER = 1536
CONV = 1792
PROJ = 3352
SEQS = 8
LEN = 1024


def level_of(key, shape, cuts, low, high):
    loudness, own = 1.0, jax.random.fold_in(key, 6)
    for axis_at, blocks in cuts:
        heights = jnp.exp(jax.random.uniform(jax.random.fold_in(own, axis_at), (blocks,), jnp.float32, low / len(cuts), high / len(cuts)))
        loudness = loudness * jnp.repeat(heights, shape[axis_at] // blocks).reshape([-1 if axis == axis_at else 1 for axis in range(len(shape))])
    return loudness


def bell_draw(key, extent, width, reach, split=(), dtype=jnp.bfloat16):
    array = width * jax.random.normal(key, extent, jnp.float32)
    if split:
        array = array * level_of(key, extent, split, -0.22, 0.18)
    return jnp.clip(array, -reach, reach).astype(dtype)


def setup_inputs(seed: int = 0) -> dict:
    key_of = jax.random.split(jax.random.key(seed), 12)
    return {
        "hidden_in": bell_draw(key_of[0], (SEQS, LEN, D), 1.0, 6.0, ((0, 4), (1, 4))),
        "cotangent": bell_draw(key_of[1], (SEQS, LEN, D), 1.0, 6.0, ((0, 4), (1, 4))),
        "norm_gain": jnp.clip(1.0 + 0.1 * jax.random.normal(key_of[2], (2, D), jnp.float32), 0.5, 1.5),
        "in_weight": bell_draw(key_of[3], (2, D, PROJ), D ** -0.5, 0.21875, ((0, 2), (1, 4))),
        "conv_weight": bell_draw(key_of[4], (2, KERNEL, CONV), KERNEL ** -0.5, 3.0, ((0, 2),), jnp.float32),
        "conv_bias": bell_draw(key_of[5], (2, CONV), 0.3, 2.0, ((0, 2),), jnp.float32),
        "dt_bias": jnp.clip(-9.0 + 4.5 * jax.random.uniform(key_of[6], (2, HEADS), jnp.float32) ** level_of(key_of[6], (2, HEADS), ((0, 2),), -0.2, 0.2), -9.0, -4.5),
        "a_log": jnp.clip(2.8 * jax.random.uniform(key_of[7], (2, HEADS), jnp.float32) ** level_of(key_of[7], (2, HEADS), ((0, 2),), -0.2, 0.2), 0.0, 2.8),
        "skip": jnp.clip(0.5 + 1.0 * jax.random.uniform(key_of[8], (2, HEADS), jnp.float32) ** level_of(key_of[8], (2, HEADS), ((0, 2),), -0.2, 0.2), 0.5, 1.5),
        "gate_gain": jnp.clip(1.0 + 0.1 * jax.random.normal(key_of[9], (2, INNER), jnp.float32), 0.5, 1.5),
        "out_weight": bell_draw(key_of[10], (2, INNER, D), INNER ** -0.5, 0.15625, ((0, 2), (1, 4))),
    }


EPSILON = 1e-05

@jax.custom_vjp
def low(v):
    return lax.optimization_barrier(v.astype(jnp.bfloat16)).astype(jnp.float32)

@jax.custom_vjp
def low_back(v):
    return v

def low_keep(v):
    return (low(v), None)

def low_pass(kept, grad):
    return (grad,)

def back_keep(v):
    return (v, None)

def back_low(kept, grad):
    return (low(grad),)
low.defvjp(low_keep, low_pass)
low_back.defvjp(back_keep, back_low)

def product(pattern, first_in, second_in):
    return jnp.einsum(pattern, first_in, second_in, precision=lax.Precision.HIGHEST)

def matmul(first_in, second_in):
    return jnp.dot(first_in, second_in, precision=lax.Precision.HIGHEST)

def rms_scale(values, scale_gain):
    return values * lax.rsqrt(lax.optimization_barrier(jnp.mean(values * values, axis=-1, keepdims=True)) + EPSILON) * scale_gain

def front_part(conv_in, before, dt_raw, conv_kernel, conv_shift, dt_offset, log_rate):
    length = conv_in.shape[0]
    extended = jnp.concatenate([before, conv_in], axis=0)
    conv_sum = conv_shift + jnp.zeros_like(conv_in)
    for offset in range(conv_kernel.shape[0]):
        conv_sum = conv_sum + extended[offset:offset + length] * conv_kernel[offset]
    active = jax.nn.silu(conv_sum)
    inputs = active[:, :INNER].reshape(length, HEADS, HDIM)
    b_low = low(active[:, INNER:INNER + STATE])
    c_low = low(active[:, INNER + STATE:])
    step_size = jax.nn.softplus(dt_raw + dt_offset)
    running = jnp.cumsum(-jnp.exp(log_rate) * step_size, axis=0)
    scaled = low(inputs * step_size[:, :, None])
    to_end = jnp.exp(running[-1][None, :] - running)
    decayed = low(scaled * to_end[:, :, None])
    local_state = low_back(product('lhp,ln->hpn', decayed, b_low))
    return (inputs, b_low, c_low, scaled, running, local_state, jnp.exp(running[-1]))

def back_part(inputs, b_low, c_low, scaled, running, carried, gate_in, skip_gain, gate_gain):
    length = inputs.shape[0]
    scores = low_back(product('ln,sn->ls', c_low, b_low))
    across = running.T
    log_gap = across[:, :, None] - across[:, None, :]
    causal = (jnp.arange(length)[:, None] >= jnp.arange(length)[None, :])[None]
    decay_mask = jnp.where(causal, jnp.exp(jnp.where(causal, log_gap, 0.0)), 0.0)
    weights = low(scores[None] * decay_mask)
    within = low_back(product('hls,shp->lhp', weights, scaled))
    from_state = low_back(product('ln,hpn->lhp', c_low, low(carried)))
    output = within + jnp.exp(running)[:, :, None] * from_state + skip_gain[None, :, None] * inputs
    output = output.reshape(length, INNER)
    gated_out = output * jax.nn.silu(gate_in)
    return rms_scale(gated_out, gate_gain)

def layer(hidden, params):
    norm_gain, in_matrix, conv_kernel, conv_shift, dt_offset, log_rate, skip_gain, gate_gain, out_matrix = params
    length = hidden.shape[0]
    blocks = length // BLOCK
    normed = low(rms_scale(hidden, norm_gain))
    projected = low_back(matmul(normed, in_matrix))
    gate_in = projected[:, :INNER]
    conv_in = projected[:, INNER:INNER + CONV]
    dt_raw = projected[:, INNER + CONV:]
    padded = jnp.concatenate([jnp.zeros((KERNEL - 1, CONV), jnp.float32), conv_in], axis=0)
    before = padded[:length].reshape(blocks, BLOCK, CONV)[:, :KERNEL - 1]

    def front_block(pieces):
        return front_part(pieces[0], pieces[1], pieces[2], conv_kernel, conv_shift, dt_offset, log_rate)
    fronts = lax.map(jax.checkpoint(front_block), (conv_in.reshape(blocks, BLOCK, CONV), before, dt_raw.reshape(blocks, BLOCK, HEADS)))
    inputs, b_low, c_low, scaled, running, local_state, decays = fronts

    def advance(state_now, pieces):
        return (pieces[0][:, None, None] * state_now + pieces[1], state_now)
    _, carried = lax.scan(advance, jnp.zeros((HEADS, HDIM, STATE), jnp.float32), (decays, local_state))

    def back_block(pieces):
        return back_part(pieces[0], pieces[1], pieces[2], pieces[3], pieces[4], pieces[5], pieces[6], skip_gain, gate_gain)
    normed_out = lax.map(jax.checkpoint(back_block), (inputs, b_low, c_low, scaled, running, carried, gate_in.reshape(blocks, BLOCK, INNER)))
    branch = low_back(matmul(low(normed_out.reshape(length, INNER)), out_matrix))
    return hidden + branch

def model(hidden, params):
    section_zero = tuple((p[0] for p in params))
    section_one = tuple((p[1] for p in params))
    middle = low_back(low(layer(hidden, section_zero)))
    return layer(middle, section_one)

def reference(hidden_in, cotangent, norm_gain, in_weight, conv_weight, conv_bias, dt_bias, a_log, skip, gate_gain, out_weight):
    params = tuple((p.astype(jnp.float32) for p in (norm_gain, in_weight, conv_weight, conv_bias, dt_bias, a_log, skip, gate_gain, out_weight)))

    def one_sequence(totals, pieces):
        final_out, pull_back = jax.vjp(model, pieces[0].astype(jnp.float32), params)
        grad_hidden, grad_list = pull_back(pieces[1].astype(jnp.float32))
        totals = jax.tree.map(lambda a, b: a + b, totals, grad_list)
        return (totals, (final_out.astype(jnp.bfloat16), grad_hidden.astype(jnp.bfloat16)))
    zero_grads = jax.tree.map(jnp.zeros_like, params)
    totals, outputs = lax.scan(one_sequence, zero_grads, (hidden_in, cotangent))
    return (outputs[0], outputs[1], totals[0], totals[1], totals[2], totals[3], totals[4], totals[5], totals[6], totals[7], totals[8])
```

```python
import jax
import jax.numpy as jnp
from jax import lax
from jax.experimental import pallas as pl
from jax.experimental.pallas import tpu as pltpu
from jax.sharding import PartitionSpec as P

HDIM = 64
STATE = 128
INNER = 1536
CONV = 1792
EPS = 1e-05
f32, bf16 = jnp.float32, jnp.bfloat16

WIDTH = 768
OWN = 768
HEADS = 12
XC = OWN + 2 * STATE
XD = XC + 128
R = 64
BLOCK = 256


def nn(a, b):
    return lax.dot_general(a, b, (((1,), (0,)), ((), ())), preferred_element_type=f32)


def nt(a, b):
    return lax.dot_general(a, b, (((1,), (1,)), ((), ())), preferred_element_type=f32)


def tn(a, b):
    return lax.dot_general(a, b, (((0,), (0,)), ((), ())), preferred_element_type=f32)


def loop(count, body):
    def step(k, carry):
        body(k)
        return carry

    lax.fori_loop(0, count, step, 0)


def at(k, size):
    return pl.ds(pl.multiple_of(k * size, size), size)


def iotas(shape):
    return lax.broadcasted_iota(jnp.int32, shape, 0), lax.broadcasted_iota(jnp.int32, shape, 1)


def spread_matrix(width, per):
    r, c = iotas((128, width))
    return jnp.where(((r & 15) == c // per) & (r < 48), 1.0, 0.0).astype(bf16)


def collect_matrix():
    r, c = iotas((OWN, 128))
    return jnp.where(((c & 15) == r // HDIM) & (c < 48), 1.0, 0.0).astype(bf16)


def thirds(v):
    high = v.astype(bf16).astype(f32)
    rest = v - high
    mid = rest.astype(bf16).astype(f32)
    lane = iotas(v.shape)[1]
    out = jnp.where(lane < 16, high, jnp.where(lane < 32, mid, rest - mid))
    return jnp.where(lane < 48, out, 0.0).astype(bf16)


def halves(v):
    high = v.astype(bf16)
    return high, (v - high.astype(f32)).astype(bf16)


def running_sum(v, backward=False):
    r, c = iotas((BLOCK, BLOCK))
    tri = jnp.where((c >= r) if backward else (r >= c), 1.0, 0.0).astype(bf16)
    high = v.astype(bf16)
    rest = v - high.astype(f32)
    mid = rest.astype(bf16)
    last = (rest - mid.astype(f32)).astype(bf16)
    return nn(tri, high) + nn(tri, mid) + nn(tri, last)


def sig(v):
    return 0.5 * jnp.tanh(0.5 * v) + 0.5


def softplus(v):
    e = jnp.exp(-jnp.abs(v))
    u = 1.0 + e
    small = u == 1.0
    return jnp.maximum(v, 0.0) + jnp.where(small, e, jnp.log(u) * e / jnp.where(small, 1.0, u - 1.0))


def fold(v):
    return jnp.sum(v.reshape(v.shape[0] // 8, 8, v.shape[1]), axis=0)


def run(kernel, name, outs, *ins, scratch=(), flops=0):
    vmem = pl.BlockSpec(memory_space=pltpu.VMEM)
    shapes = [jax.ShapeDtypeStruct(s, d) for s, d in outs]
    size = sum(a.size * a.dtype.itemsize for a in (*ins, *shapes))
    return pl.pallas_call(
        kernel,
        name=name,
        out_shape=shapes,
        in_specs=[vmem] * len(ins),
        out_specs=[vmem] * len(outs),
        scratch_shapes=[pltpu.VMEM(s, d) for s, d in scratch],
        compiler_params=pltpu.CompilerParams(vmem_limit_bytes=50 * 2**20),
        cost_estimate=pl.CostEstimate(flops=flops, bytes_accessed=size, transcendentals=0),
    )(*ins)


def norm_project(t, normed_ref, w_ref, xb_ref):
    xb_ref[0:8, :] = jnp.zeros((8, XD), f32)

    def cols(c):
        xb_ref[8 : 8 + t, at(c, 384)] = nn(normed_ref[...], w_ref[:, at(c, 384)])

    loop(XD // 384, cols)


def k_in(h_ref, gain_ref, w_ref, normed_ref, xb_ref):
    t = h_ref.shape[0]

    def rows(r):
        h = h_ref[at(r, R), :].astype(f32)
        scale = lax.rsqrt(jnp.mean(h * h, axis=1, keepdims=True) + EPS)
        normed_ref[at(r, R), :] = (h * scale * gain_ref[...]).astype(bf16)

    loop(t // R, rows)
    norm_project(t, normed_ref, w_ref, xb_ref)


def k_mid(h_ref, po_ref, pr_ref, so_ref, sr_ref, gain_ref, w_ref, h1_ref, pt_ref, rs_ref, normed_ref, xb_ref):
    t = h_ref.shape[0]

    def rows(r):
        s = at(r, R)
        rs = lax.rsqrt((so_ref[s, :] + sr_ref[s, :]) * (1.0 / INNER) + EPS)
        rs_ref[s, :] = rs
        p = po_ref[s, :] + pr_ref[s, :].astype(f32)
        pt_ref[s, :] = p
        h1 = (h_ref[s, :].astype(f32) + rs[:, 0:1] * p).astype(bf16)
        h1_ref[s, :] = h1
        h = h1.astype(f32)
        scale = lax.rsqrt(jnp.mean(h * h, axis=1, keepdims=True) + EPS)
        normed_ref[s, :] = (h * scale * gain_ref[...]).astype(bf16)

    loop(t // R, rows)
    norm_project(t, normed_ref, w_ref, xb_ref)


def k_z(normed_ref, w_ref, z_ref):
    def cols(c):
        z_ref[:, at(c, 384)] = nn(normed_ref[...], w_ref[:, at(c, 384)])

    loop(OWN // 384, cols)


def k_front(xb_ref, cw_ref, hv_ref, act_ref, bc_ref, xdt_ref, dt_ref, cum_ref, s_ref, dec_ref, tot_ref, wide):
    t = act_ref.shape[0]

    def conv(c):
        cols = at(c, 128)
        w = cw_ref[:, cols]
        total = w[4:5] + w[0:1] * xb_ref[pl.ds(5, t), cols]
        for k in range(1, 4):
            total = total + w[k : k + 1] * xb_ref[pl.ds(5 + k, t), cols]
        act_ref[:, cols] = total * sig(total)

    loop(XC // 128, conv)
    bc_ref[...] = act_ref[:, OWN:].astype(bf16)
    dt = softplus(xb_ref[8 : 8 + t, XC:] + hv_ref[0:1, :])
    dt_ref[...] = dt
    rate = -jnp.exp(hv_ref[1:2, :])
    spread = spread_matrix(OWN, HDIM)
    wide[...] = nn(thirds(dt), spread)

    def rows(r):
        s = at(r, R)
        xdt_ref[s, :] = (act_ref[s, :OWN] * wide[s, :]).astype(bf16)

    loop(t // R, rows)
    for b in range(t // BLOCK):
        s = pl.ds(b * BLOCK, BLOCK)
        cum = running_sum(rate * dt[b * BLOCK : (b + 1) * BLOCK])
        cum_ref[s, :] = cum
        end = cum[BLOCK - 1 : BLOCK, :]
        dec_ref[8 * b : 8 * b + 8, :] = nn(thirds(jnp.exp(jnp.broadcast_to(end, (8, 128)))), spread)
        wide[s, :] = nn(thirds(jnp.exp(end - cum)), spread)
        bl = bc_ref[s, 0:STATE]

        def cols(c):
            decayed = (xdt_ref[s, at(c, 256)].astype(f32) * wide[s, at(c, 256)]).astype(bf16)
            s_ref[pl.ds(b * STATE, STATE), at(c, 256)] = tn(bl, decayed)

        loop(OWN // 256, cols)
    tot_ref[...] = (s_ref[STATE:, :] + dec_ref[8:9, :] * s_ref[:STATE, :]).astype(bf16)


def decay_tables(cum_ref, tall, flat):
    t = cum_ref.shape[0]
    parts = thirds(cum_ref[...])
    tall[...] = nn(parts, spread_matrix(HEADS * 128, 128))
    r, c = iotas((HEADS * 8, 128))
    pick = jnp.where(((c & 15) == r // 8) & (c < 48), 1.0, 0.0).astype(bf16)
    for b in range(t // 128):
        flat[b] = nt(pick, parts[b * 128 : (b + 1) * 128])


def k_within(cum_ref, bc_ref, xdt_ref, y_ref, tall, flat, scores):
    t = cum_ref.shape[0]
    decay_tables(cum_ref, tall, flat)
    blocks = t // BLOCK
    for b in range(blocks):
        s = pl.ds(b * BLOCK, BLOCK)
        scores[s, :] = nt(bc_ref[s, STATE:], bc_ref[s, 0:STATE])
    r, c = iotas((128, 128))
    causal = r >= c
    lane = iotas((BLOCK, 128))[1]

    def pair(p):
        cols = at(p, 128)
        for b in range(blocks):
            o = b * BLOCK
            u = xdt_ref[pl.ds(o, BLOCK), cols]
            top = jnp.zeros((128, 128), f32)
            low = jnp.zeros((128, 128), f32)
            for a in range(2):
                head = 2 * p + a
                own = jnp.where((lane >= 64) == (a == 1), u, jnp.zeros_like(u))
                hc = at(head, 128)
                hr = pl.ds(pl.multiple_of(head * 8, 8), 8)
                t0, t1 = tall[pl.ds(o, 128), hc], tall[pl.ds(o + 128, 128), hc]
                u0, u1 = flat[2 * b, hr, :][0:1], flat[2 * b + 1, hr, :][0:1]
                sc = scores
                w00 = jnp.where(causal, sc[pl.ds(o, 128), 0:128] * jnp.exp(jnp.where(causal, t0 - u0, 0.0)), 0.0)
                w10 = sc[pl.ds(o + 128, 128), 0:128] * jnp.exp(t1 - u0)
                w11 = jnp.where(causal, sc[pl.ds(o + 128, 128), 128:] * jnp.exp(jnp.where(causal, t1 - u1, 0.0)), 0.0)
                top = top + nn(w00.astype(bf16), own[:128])
                low = low + nn(w10.astype(bf16), own[:128]) + nn(w11.astype(bf16), own[128:])
            y_ref[pl.ds(o, 128), cols] = top
            y_ref[pl.ds(o + 128, 128), cols] = low

    loop(OWN // 128, pair)


def k_out(yw_ref, act_ref, bc_ref, cum_ref, cin_ref, s_ref, dec_ref, z_ref, vec_ref, w_ref, g_ref,
          y_ref, p_ref, pb_ref, st_ref, c_ref, wide, u_ref):
    t = yw_ref.shape[0]
    c_ref[0:STATE, :] = cin_ref[...].astype(f32)
    c_ref[STATE:, :] = s_ref[:STATE, :] + dec_ref[0:1, :] * c_ref[0:STATE, :]
    spread = spread_matrix(OWN, HDIM)
    wide[...] = nn(thirds(jnp.exp(cum_ref[...])), spread)
    for b in range(t // BLOCK):
        s = pl.ds(b * BLOCK, BLOCK)

        def cols(c):
            from_state = nn(bc_ref[s, STATE:], c_ref[pl.ds(b * STATE, STATE), at(c, 256)].astype(bf16))
            wide[s, at(c, 256)] = wide[s, at(c, 256)] * from_state

        loop(OWN // 256, cols)

    def rows(r):
        s = at(r, R)
        y = yw_ref[s, :] + wide[s, :] + vec_ref[1:2, :] * act_ref[s, :OWN]
        y_ref[s, :] = y
        z = z_ref[s, :]
        gated = y * z * sig(z)
        u_ref[s, :] = (gated * vec_ref[0:1, :]).astype(bf16)
        st_ref[s, 0:128] = jnp.broadcast_to(jnp.sum(gated * gated, axis=1, keepdims=True), (R, 128))

    loop(t // R, rows)

    def out(c):
        p = nn(u_ref[...], w_ref[:, at(c, 256)])
        p_ref[:, at(c, 256)] = p
        pb_ref[:, at(c, 256)] = p.astype(bf16)

    loop(WIDTH // 256, out)
    if g_ref is not None:

        def dots(r):
            s = at(r, R)
            d = jnp.sum(p_ref[s, :] * g_ref[s, :].astype(f32), axis=1, keepdims=True)
            st_ref[s, 128:256] = jnp.broadcast_to(d, (R, 128))

        loop(t // R, dots)


def k_out_first(*refs):
    k_out(*refs[:10], None, *refs[10:])


def kb_gate(g_ref, w_ref, y_ref, yw_ref, z_ref, act_ref, bc_ref, cum_ref, rs_ref, rd_ref, vec_ref, dec_ref,
            qz_ref, dy_ref, df_ref, dca_ref, dwo_ref, d_ref, e_ref, small_ref, dgn, wide, gn):
    t = g_ref.shape[0]

    def back(c):
        dgn[:, at(c, 256)] = nt(g_ref[...], w_ref[at(c, 256), :])

    loop(OWN // 256, back)
    wide[...] = nn(thirds(jnp.exp(cum_ref[...])), spread_matrix(OWN, HDIM))
    small_ref[...] = jnp.zeros(small_ref.shape, f32)
    collect = collect_matrix()

    def rows(r):
        s = at(r, R)
        z, y, d, x = z_ref[s, :], y_ref[s, :], dgn[s, :], act_ref[s, :OWN]
        gg = vec_ref[0:1, :]
        rs, rd = rs_ref[s, 0:1], rd_ref[s, 0:1]
        sg = sig(z)
        sz = z * sg
        gated = y * sz
        scaled = gated * rs
        small_ref[0:8, :] += fold(d * scaled)
        gn[s, :] = (scaled * gg).astype(bf16)
        dgated = rs * (gg * d) - gated * (rs * rs * rs * rd * (1.0 / INNER))
        dy = dgated * sz
        dy_ref[s, :] = dy
        qz_ref[s, :] = (dgated * y * (sg * (1.0 + z - sz))).astype(bf16)
        small_ref[8:16, :] += fold(dy * x)
        df_ref[s, :] = (wide[s, :] * dy).astype(bf16)
        yw = yw_ref[s, :]
        high, low = halves(dy.astype(bf16).astype(f32) * yw + dy * (y - yw - vec_ref[1:2, :] * x))
        dca_ref[s, :] = nn(high, collect) + nn(low, collect)

    loop(t // R, rows)
    for b in range(t // BLOCK):
        s = pl.ds(b * BLOCK, BLOCK)
        cl = bc_ref[s, STATE:]

        def cols(c):
            d_ref[pl.ds(b * STATE, STATE), at(c, 256)] = tn(cl, df_ref[s, at(c, 256)])

        loop(OWN // 256, cols)
    e_ref[...] = (d_ref[:STATE, :] + dec_ref[0:1, :] * d_ref[STATE:, :]).astype(bf16)

    def weight(c):
        dwo_ref[at(c, 256), :] = tn(gn[:, at(c, 256)], g_ref[...]).astype(bf16)

    loop(OWN // 256, weight)


def kb_within(dy_ref, xdt_ref, cum_ref, bc_ref, df_ref, c_ref, dx_ref, dbc_ref, tall, flat, scores, ds):
    t = cum_ref.shape[0]
    decay_tables(cum_ref, tall, flat)
    blocks = t // BLOCK
    for b in range(blocks):
        s = pl.ds(b * BLOCK, BLOCK)
        scores[s, :] = nt(bc_ref[s, STATE:], bc_ref[s, 0:STATE])
    ds[...] = jnp.zeros(ds.shape, f32)
    r, c = iotas((128, 128))
    causal = r >= c
    lane = iotas((BLOCK, 128))[1]

    def pair(p):
        cols = at(p, 128)
        for b in range(blocks):
            o = b * BLOCK
            u = xdt_ref[pl.ds(o, BLOCK), cols]
            g = dy_ref[pl.ds(o, BLOCK), cols].astype(bf16)
            top = jnp.zeros((128, 128), f32)
            low = jnp.zeros((128, 128), f32)
            for a in range(2):
                head = 2 * p + a
                own = jnp.where((lane >= 64) == (a == 1), g, jnp.zeros_like(g))
                hc = at(head, 128)
                hr = pl.ds(pl.multiple_of(head * 8, 8), 8)
                t0, t1 = tall[pl.ds(o, 128), hc], tall[pl.ds(o + 128, 128), hc]
                u0, u1 = flat[2 * b, hr, :][0:1], flat[2 * b + 1, hr, :][0:1]
                e00 = jnp.where(causal, jnp.exp(jnp.where(causal, t0 - u0, 0.0)), 0.0)
                e10 = jnp.exp(t1 - u0)
                e11 = jnp.where(causal, jnp.exp(jnp.where(causal, t1 - u1, 0.0)), 0.0)
                q0, q1 = pl.ds(o, 128), pl.ds(o + 128, 128)
                w00 = (scores[q0, 0:128] * e00).astype(bf16)
                w10 = (scores[q1, 0:128] * e10).astype(bf16)
                w11 = (scores[q1, 128:] * e11).astype(bf16)
                top = top + tn(w00, own[:128]) + tn(w10, own[128:])
                low = low + tn(w11, own[128:])
                ds[q0, 0:128] += nt(own[:128], u[:128]) * e00
                ds[q1, 0:128] += nt(own[128:], u[:128]) * e10
                ds[q1, 128:] += nt(own[128:], u[128:]) * e11
            dx_ref[pl.ds(o, 128), cols] = top
            dx_ref[pl.ds(o + 128, 128), cols] = low

    loop(OWN // 128, pair)
    for b in range(blocks):
        s = pl.ds(b * BLOCK, BLOCK)
        d = ds[s, :].astype(bf16)
        carried = c_ref[pl.ds(b * STATE, STATE), :].astype(bf16)
        dbc_ref[s, 0:STATE] = tn(d, bc_ref[s, STATE:])
        dbc_ref[s, STATE:] = nn(d, bc_ref[s, 0:STATE]) + nt(df_ref[s, :], carried)


def kb_front(gin_ref, d_ref, c_ref, dec_ref, bc_ref, xdt_ref, act_ref, xb_ref, dt_ref, cum_ref, dxw_ref, dbc_ref,
             dy_ref, dca_ref, cw_ref, hv_ref, vec_ref,
             dxb_ref, qdt_ref, small_ref, head_ref, gs, dd, te, dtw, dact, red, red2, ends, pad):
    t = act_ref.shape[0]
    blocks = t // BLOCK
    spread, collect = spread_matrix(OWN, HDIM), collect_matrix()
    gs[STATE:, :] = gin_ref[...].astype(f32)
    gs[:STATE, :] = d_ref[STATE:, :] + dec_ref[8:9, :] * gs[STATE:, :]
    dact[:, OWN:] = dbc_ref[...]
    dtw[...] = nn(thirds(dt_ref[...]), spread)
    for b in range(blocks):
        s = pl.ds(b * BLOCK, BLOCK)
        ss = pl.ds(b * STATE, STATE)
        end = cum_ref[pl.ds((b + 1) * BLOCK - 8, 8), :][7:8]
        te[s, :] = nn(thirds(jnp.exp(end - cum_ref[s, :])), spread)
        bl = bc_ref[s, 0:STATE]
        ends[8 * b : 8 * b + 8, :] = fold(gs[ss, :] * c_ref[ss, :]) * dec_ref[8 * b : 8 * b + 8, :]

        def cols(c):
            q = at(c, 256)
            low = gs[ss, q].astype(bf16)
            dd[s, q] = nn(bl, low)
            decayed = (xdt_ref[s, q].astype(f32) * te[s, q]).astype(bf16)
            dact[s, OWN : OWN + STATE] += nt(decayed, low)

        loop(OWN // 256, cols)

        def rows(r):
            q = pl.ds(pl.multiple_of(b * BLOCK + r * R, R), R)
            w = dd[q, :] * te[q, :]
            ends[8 * b : 8 * b + 8, :] += fold(w * xdt_ref[q, :].astype(f32))
            dxdt = dxw_ref[q, :] + w
            dact[q, :OWN] = dxdt * dtw[q, :] + vec_ref[1:2, :] * dy_ref[q, :]
            high, low = halves(dxdt * act_ref[q, :OWN])
            red[q, :] = nn(high, collect) + nn(low, collect)
            high, low = halves(dxdt * xdt_ref[q, :].astype(f32))
            red2[q, :] = nn(high, collect) + nn(low, collect)

        loop(BLOCK // R, rows)
    high, low = halves(ends[...])
    at_end = nn(high, collect) + nn(low, collect)
    rate = -jnp.exp(hv_ref[1:2, :])
    head_ref[...] = jnp.zeros(head_ref.shape, f32)
    for b in range(blocks):
        s = pl.ds(b * BLOCK, BLOCK)
        dt = dt_ref[s, :]
        total = running_sum(dca_ref[s, :] - red2[s, :], True)
        total = total + jnp.sum(at_end[8 * b : 8 * b + 8], axis=0, keepdims=True)
        ddt = red[s, :] + rate * total
        raw = xb_ref[pl.ds(8 + b * BLOCK, BLOCK), XC:] + hv_ref[0:1, :]
        draw = ddt * jax.nn.sigmoid(raw)
        head_ref[0:8, :] += fold(draw)
        head_ref[8:16, :] += fold(rate * dt * total)
        lane = iotas(draw.shape)[1]
        qdt_ref[s, :] = jnp.where(lane < HEADS, draw, 0.0).astype(bf16)
    pad[0:8, :] = jnp.zeros((8, 128), f32)
    pad[8 + t :, :] = jnp.zeros((8, 128), f32)

    def conv(c):
        cols = at(c, 128)
        w = cw_ref[:, cols]
        taps = [xb_ref[pl.ds(5 + k, t), cols] for k in range(4)]
        total = w[4:5] + w[0:1] * taps[0]
        for k in range(1, 4):
            total = total + w[k : k + 1] * taps[k]
        sg = sig(total)
        d = dact[:, cols] * (sg * (1.0 + total * (1.0 - sg)))
        pad[8 : 8 + t, :] = d
        for k in range(4):
            small_ref[8 * k : 8 * k + 8, cols] = fold(d * xb_ref[pl.ds(5 + k, t), cols])
        small_ref[32:40, cols] = fold(d)
        out = w[3:4] * pad[0 : 8 + t, :]
        for k in range(3):
            out = out + w[k : k + 1] * pad[3 - k : 11 - k + t, :]
        dxb_ref[:, cols] = out

    loop(XC // 128, conv)


def kb_z(normed_ref, qz_ref, w_ref, dw_ref, dn_ref):
    def weight(c):
        dw_ref[at(c, 256), :] = tn(normed_ref[:, at(c, 256)], qz_ref[...]).astype(bf16)

    loop(WIDTH // 256, weight)

    def back(c):
        dn_ref[:, at(c, 256)] = nt(qz_ref[...], w_ref[at(c, 256), :])

    loop(WIDTH // 256, back)


def kb_x(normed_ref, dxb_ref, ret_ref, qdt_ref, dnz_ref, w_ref, dw_ref, dn_ref, dnb_ref, q):
    t = normed_ref.shape[0]

    def rows(r):
        q[at(r, R), :XC] = dxb_ref[pl.ds(pl.multiple_of(r * R, R) + 8, R), :].astype(bf16)

    loop(t // R, rows)
    q[t - 16 :, :XC] = (
        dxb_ref[t - 8 : t + 8, :] + jnp.concatenate([jnp.zeros((8, XC), f32), ret_ref[...]], axis=0)
    ).astype(bf16)
    q[:, XC:] = qdt_ref[...]

    def back(c):
        cols = at(c, 256)
        d = dnz_ref[:, cols] + nt(q[...], w_ref[cols, :])
        dn_ref[:, cols] = d
        dnb_ref[:, cols] = d.astype(bf16)

    loop(WIDTH // 256, back)

    def weight(c):
        dw_ref[at(c, 256), :] = tn(normed_ref[:, at(c, 256)], q[...]).astype(bf16)

    loop(WIDTH // 256, weight)


def kb_norm(h_ref, dn_ref, dr_ref, g_ref, gain_ref, pt_ref, gh_ref, small_ref, rd_ref):
    t = h_ref.shape[0]
    small_ref[...] = jnp.zeros(small_ref.shape, f32)

    def rows(r):
        s = at(r, R)
        h = h_ref[s, :].astype(f32)
        d = dn_ref[s, :] + dr_ref[s, :].astype(f32)
        scale = lax.rsqrt(jnp.mean(h * h, axis=1, keepdims=True) + EPS)
        hs = h * scale
        small_ref[...] += fold(d * hs)
        gd = gain_ref[...] * d
        back = scale * (gd - hs * jnp.mean(hs * gd, axis=1, keepdims=True))
        gh = (g_ref[s, :].astype(f32) + back).astype(bf16)
        gh_ref[s, :] = gh
        if rd_ref is not None:
            dot = jnp.sum(gh.astype(f32) * pt_ref[s, :], axis=1, keepdims=True)
            rd_ref[s, :] = jnp.broadcast_to(dot, (R, 128))

    loop(t // R, rows)


def kb_norm_last(h_ref, dn_ref, dr_ref, g_ref, gain_ref, gh_ref, small_ref):
    kb_norm(h_ref, dn_ref, dr_ref, g_ref, gain_ref, None, gh_ref, small_ref, None)


def across(x):
    return lax.ppermute(x, "section", [(0, 1), (1, 0)])


def flip(x, axis, bits):
    return lax.ppermute(x, axis, [(k, k ^ bits) for k in range(lax.axis_size(axis))])


def chain_step(x, steps, backward):
    n = lax.axis_size("seq")
    hop = -2 * steps if backward else 2 * steps
    return lax.ppermute(x, "seq", [(k, k + hop) for k in range(n) if 0 <= k + hop < n])


def chain(value, decay, backward):
    entered = chain_step(value, 1, backward)
    count = lax.axis_size("seq") // 2
    if count > 2:
        rate = chain_step(decay, 1, backward)
        total = entered.astype(f32)
        steps = 1
        while steps < count - 1:
            total = total + rate[0:1] * chain_step(total.astype(bf16), steps, backward).astype(f32)
            rate = rate * chain_step(rate, steps, backward)
            steps *= 2
        entered = total.astype(bf16)
    return entered


def gather_rows(x):
    n = lax.axis_size("seq")
    if n != 4:
        return lax.all_gather(x, "seq", axis=0, tiled=True)
    parts = [x] + [flip(x, "seq", k) for k in range(1, 4)]
    rows = x.shape[0]

    def kernel(p0, p1, p2, p3, out):
        me = lax.axis_index("seq")
        step = 48
        for k, part in enumerate((p0, p1, p2, p3)):
            start = (me ^ k) * rows

            def move(r, part=part, start=start):
                place = pl.ds(pl.multiple_of(start + r * step, 16), step)
                out[place, :] = part[at(r, step), :]

            loop(rows // step, move)

    return run(kernel, "gather_rows", [((n * rows, x.shape[1]), x.dtype)], *parts)[0]


def scatter_rows(x):
    n = lax.axis_size("seq")
    if n != 4:
        return lax.psum_scatter(x, "seq", scatter_dimension=0, tiled=True)
    me = lax.axis_index("seq")
    rows = x.shape[0] // n

    def block(k):
        return lax.dynamic_slice_in_dim(x, (me ^ k) * rows, rows, 0)

    total = block(0).astype(f32)
    for k in range(1, 4):
        total = total + flip(block(k), "seq", k).astype(f32)
    return total.astype(bf16)


def sum_dp(x):
    n = lax.axis_size("dp")
    if n == 1:
        return x.astype(f32)
    if n & (n - 1):
        return lax.psum(x, "dp").astype(f32)
    me = lax.axis_index("dp")
    half = x.shape[0] // 2
    odd = (me & 1) == 1
    low, high = x[:half], x[half:]
    keep, give = jnp.where(odd, high, low), jnp.where(odd, low, high)
    keep = keep.astype(f32) + flip(give, "dp", 1).astype(f32)
    bit = 2
    while bit < n:
        sent = keep.astype(bf16)
        keep = sent.astype(f32) + flip(sent, "dp", bit).astype(f32)
        bit *= 2
    mine = keep.astype(bf16)
    other = flip(mine, "dp", 1)
    return jnp.concatenate([jnp.where(odd, other, mine), jnp.where(odd, mine, other)], axis=0).astype(f32)


def sum_small(x):
    for axis in ("seq", "dp"):
        n = lax.axis_size(axis)
        if n & (n - 1):
            x = lax.psum(x, axis)
            continue
        bit = 1
        while bit < n:
            x = x + flip(x, axis, bit)
            bit *= 2
    return x


def on_device(hidden_in, cotangent, norm_gain, in_weight, conv_weight, conv_bias, dt_bias, a_log, skip, gate_gain, out_weight):
    section = lax.axis_index("section")
    first = section == 0
    seq = lax.axis_index("seq")
    even = seq % 2 == 0
    length = hidden_in.shape[1]
    t = 2 * length
    heads = 2 * HEADS

    def own_sequence(x):
        mine, theirs = jnp.where(even, x[0], x[1]), jnp.where(even, x[1], x[0])
        got = flip(theirs, "seq", 1)
        return jnp.concatenate([jnp.where(even, mine, got), jnp.where(even, got, mine)], axis=0)

    def both_sequences(x):
        mine, theirs = jnp.where(even, x[:length], x[length:]), jnp.where(even, x[length:], x[:length])
        got = flip(theirs, "seq", 1)
        return jnp.stack([jnp.where(even, mine, got), jnp.where(even, got, mine)])

    def routed(own_layer_own, own_layer_other):
        got = across(own_layer_other)
        return jnp.where(first, own_layer_own, got), jnp.where(first, got, own_layer_own)

    w = in_weight[0]

    def lanes(x):
        rows = x.shape[0]
        one = jnp.concatenate([x, jnp.zeros((rows, 4), x.dtype)], axis=1)
        return jnp.concatenate([one, one, one, jnp.zeros((rows, 80), x.dtype)], axis=1)

    shared = w[:, 2 * INNER : 2 * INNER + 2 * STATE]
    packs_x = [
        jnp.concatenate(
            [
                w[:, INNER + c * OWN : INNER + (c + 1) * OWN],
                shared,
                lanes(w[:, INNER + CONV + c * HEADS : INNER + CONV + (c + 1) * HEADS]),
            ],
            axis=1,
        )
        for c in range(2)
    ]
    packs_z = [w[:, c * OWN : (c + 1) * OWN] for c in range(2)]
    packs_o = [out_weight[0][:, c * (WIDTH // 2) : (c + 1) * (WIDTH // 2)] for c in range(2)]

    def chosen(pair):
        return jnp.where(first, pair[0], pair[1]), jnp.where(first, pair[1], pair[0])

    wx = routed(*chosen(packs_x))
    wz = routed(*chosen(packs_z))
    wo = routed(*chosen(packs_o))

    def own_rows(half):
        mine, theirs = chosen((half[:OWN], half[OWN:]))
        got = across(theirs)
        return jnp.concatenate([jnp.where(first, mine, got), jnp.where(first, got, mine)], axis=1)

    def layer_params(x):
        got = across(x)
        return jnp.where(first, x, got), jnp.where(first, got, x)

    tiny = jnp.concatenate(
        [conv_weight[0].reshape(-1), conv_bias[0], norm_gain[0], gate_gain[0], dt_bias[0], a_log[0], skip[0]]
    )
    tiny = jnp.pad(tiny, (0, -tiny.shape[0] % 1024)).reshape(-1, 128)
    tinies = layer_params(tiny)

    def unpacked(v):
        v = v.reshape(-1)
        sizes = [4 * CONV, CONV, WIDTH, INNER, heads, heads, heads]
        out, start = [], 0
        for size in sizes:
            out.append(v[start : start + size])
            start += size
        cw, cb, ng, gg, db, al, sk = out
        taps = jnp.concatenate([cw.reshape(4, CONV), cb[None], jnp.zeros((3, CONV), f32)], axis=0)
        taps = jnp.concatenate(
            [jnp.where(first, taps[:, :OWN], taps[:, OWN : 2 * OWN]), taps[:, 2 * OWN :]], axis=1
        )

        def pick(x):
            n = x.shape[0] // 2
            return jnp.where(first, x[:n], x[n:])

        hv = lanes(jnp.stack([pick(db), pick(al)] + [jnp.zeros((HEADS,), f32)] * 6))
        vec = jnp.concatenate([pick(gg)[None], jnp.repeat(pick(sk), HDIM)[None], jnp.zeros((6, OWN), f32)], axis=0)
        return taps, hv, vec, ng[None]

    params = [unpacked(v) for v in tinies]

    h0 = own_sequence(hidden_in)
    full_x0 = gather_rows(wx[0])
    full_z0 = gather_rows(wz[0])
    full_o0 = own_rows(gather_rows(wo[0]))
    wx1, wz1, wo1, cotangent, _ = lax.optimization_barrier((wx[1], wz[1], wo[1], cotangent, full_x0))
    full_x = [full_x0, gather_rows(wx1)]
    full_z = [full_z0, gather_rows(wz1)]
    full_o = [full_o0, own_rows(gather_rows(wo1))]
    g1 = own_sequence(cotangent)

    saved = []

    def scan_part(layer, normed, xb, g):
        taps, hv, vec, _ = params[layer]
        before = chain_step(xb[t:, :XC], 1, False)
        z = run(k_z, "gate_in", [((t, OWN), f32)], normed, full_z[layer])[0]
        xb = lax.dynamic_update_slice(xb, before, (0, 0))
        act, bc, xdt, dt, cum, s, dec, tot = run(
            k_front, "front",
            [((t, XC), f32), ((t, 2 * STATE), bf16), ((t, OWN), bf16), ((t, 128), f32), ((t, 128), f32),
             ((2 * STATE, OWN), f32), ((16, OWN), f32), ((STATE, OWN), bf16)],
            xb, taps, hv, scratch=[((t, OWN), f32)],
        )
        decay = dec[:8] * dec[8:]
        entered = chain(tot, decay, False)
        yw = run(
            k_within, "within", [((t, OWN), f32)], cum, bc, xdt,
            scratch=[((t, HEADS * 128), f32), ((t // 128, HEADS * 8, 128), f32), ((t, BLOCK), f32)],
        )[0]
        ins = [yw, act, bc, cum, entered, s, dec, z, vec, full_o[layer]]
        y, p, pb, st, c = run(
            k_out if g is not None else k_out_first, "out",
            [((t, OWN), f32), ((t, WIDTH), f32), ((t, WIDTH), bf16), ((t, 256 if g is not None else 128), f32),
             ((2 * STATE, OWN), f32)],
            *ins, *([g] if g is not None else []), scratch=[((t, OWN), f32), ((t, OWN), bf16)],
        )
        saved.append(dict(yw=yw, normed=normed, xb=xb, z=z, act=act, bc=bc, xdt=xdt, dt=dt, cum=cum, dec=dec, decay=decay, y=y, c=c))
        return p, pb, st

    normed, xb = run(k_in, "project", [((t, WIDTH), bf16), ((t + 8, XD), f32)], h0, params[0][3], full_x[0])
    p, pb, st = scan_part(0, normed, xb, None)
    pr, sr = across(pb), across(st)
    h1, pt, rs0, normed, xb = run(
        k_mid, "middle",
        [((t, WIDTH), bf16), ((t, WIDTH), f32), ((t, 128), f32), ((t, WIDTH), bf16), ((t + 8, XD), f32)],
        h0, p, pr, st, sr, params[1][3], full_x[1],
    )
    p, pb, st = scan_part(1, normed, xb, g1)
    st = st + across(st)
    rs1 = lax.rsqrt(st[:, :128] * (1.0 / INNER) + EPS)
    rd1 = st[:, 128:]
    half = WIDTH // 2
    mine, _ = chosen((p[:, :half], p[:, half:]))
    _, theirs = chosen((pb[:, :half], pb[:, half:]))
    mine = mine + across(theirs).astype(f32)
    final = chosen((h1[:, :half], h1[:, half:]))[0].astype(f32) + rs1[:, 0:1] * mine
    hidden_out = both_sequences(final.astype(bf16))

    def backward(layer, g, h, rs, rd, point):
        v = saved[layer]
        taps, hv, vec, gain = params[layer]
        qz, dy, df, dca, dwo, d, e, small_a = run(
            kb_gate, "back_gate",
            [((t, OWN), bf16), ((t, OWN), f32), ((t, OWN), bf16), ((t, 128), f32), ((OWN, WIDTH), bf16),
             ((2 * STATE, OWN), f32), ((STATE, OWN), bf16), ((16, OWN), f32)],
            g, full_o[layer], v["y"], v["yw"], v["z"], v["act"], v["bc"], v["cum"], rs, rd, vec, v["dec"],
            scratch=[((t, OWN), f32), ((t, OWN), f32), ((t, OWN), bf16)],
        )
        entered = chain(e, v["decay"], True)
        dxw, dbc = run(
            kb_within, "back_within", [((t, OWN), f32), ((t, 2 * STATE), f32)],
            dy, v["xdt"], v["cum"], v["bc"], df, v["c"],
            scratch=[((t, HEADS * 128), f32), ((t // 128, HEADS * 8, 128), f32), ((t, BLOCK), f32), ((t, BLOCK), f32)],
        )
        dxb, qdt, small_b, small_c = run(
            kb_front, "back_front",
            [((t + 8, XC), f32), ((t, 128), bf16), ((40, XC), f32), ((16, 128), f32)],
            entered, d, v["c"], v["dec"], v["bc"], v["xdt"], v["act"], v["xb"], v["dt"], v["cum"], dxw, dbc, dy, dca,
            taps, hv, vec,
            scratch=[((2 * STATE, OWN), f32), ((t, OWN), f32), ((t, OWN), f32), ((t, OWN), f32), ((t, XC), f32),
                     ((t, 128), f32), ((t, 128), f32), ((16, OWN), f32), ((t + 16, 128), f32)],
        )
        returned = chain_step(dxb[:8], 1, True)
        dwz, dnz = run(kb_z, "back_z", [((WIDTH, OWN), bf16), ((t, WIDTH), f32)], v["normed"], qz, full_z[layer])
        dwx, dn, dnb = run(
            kb_x, "back_x", [((WIDTH, XD), bf16), ((t, WIDTH), f32), ((t, WIDTH), bf16)],
            v["normed"], dxb, returned, qdt, dnz, full_x[layer], scratch=[((t, XD), bf16)],
        )
        dr = across(dnb)
        if point is None:
            gh, small_d = run(kb_norm_last, "back_norm", [((t, WIDTH), bf16), ((8, WIDTH), f32)], h, dn, dr, g, gain)
            rd = None
        else:
            gh, small_d, rd = run(
                kb_norm, "back_norm", [((t, WIDTH), bf16), ((8, WIDTH), f32), ((t, 128), f32)], h, dn, dr, g, gain, point
            )
        small = jnp.concatenate(
            [
                small_b.reshape(5, 8, XC).sum(1).reshape(-1),
                small_d.sum(0),
                small_a.reshape(2, 8, OWN).sum(1).reshape(-1),
                small_c.reshape(2, 8, 128).sum(1).reshape(-1),
            ]
        )
        return gh, rd, dwo, dwz, dwx, small

    def reduced(dwo, dwz, dwx):
        half = WIDTH // 2
        mine, theirs = chosen((dwo[:, :half], dwo[:, half:]))
        got = across(theirs)
        rows = jnp.concatenate([jnp.where(first, mine, got), jnp.where(first, got, mine)], axis=0)
        return [sum_dp(scatter_rows(x)) for x in (rows, dwz, dwx)]

    g0, rd0, *dw1, small1 = backward(1, g1, h1, rs1, rd1, pt)
    sums1 = reduced(*dw1)
    gh, _, *dw0, small0 = backward(0, g0, h0, rs0, rd0, None)
    sums0 = reduced(*dw0)
    outs = both_sequences(chosen((gh[:, :half], gh[:, half:]))[0])
    smalls = jnp.concatenate([small0, small1])
    count = small0.shape[0]
    smalls = sum_small(jnp.pad(smalls, (0, -2 * count % 1024)).reshape(-1, 128)).reshape(-1)[: 2 * count]

    def home(zero, one):
        mine = jnp.where(first, zero, one)
        return mine, across(jnp.where(first, one, zero).astype(zero.dtype))

    def by_core(mine, got):
        return jnp.where(first, mine, got), jnp.where(first, got, mine)

    o = by_core(*home(sums0[0].astype(bf16), sums1[0].astype(bf16)))
    z = by_core(*home(sums0[1].astype(bf16), sums1[1].astype(bf16)))
    x = by_core(*home(sums0[2].astype(bf16), sums1[2].astype(bf16)))
    grad_out_weight = jnp.concatenate(o, axis=1).astype(f32)
    grad_in_weight = jnp.concatenate(
        [
            z[0], z[1], x[0][:, :OWN], x[1][:, :OWN],
            (x[0][:, OWN:XC].astype(f32) + x[1][:, OWN:XC].astype(f32)).astype(f32),
            x[0][:, XC : XC + HEADS], x[1][:, XC : XC + HEADS],
        ],
        axis=1,
    ).astype(f32)
    s = by_core(*home(smalls[:count], smalls[count:]))

    def parts(v):
        taps = v[: 5 * XC].reshape(5, XC)
        v = v[5 * XC :]
        return taps, v[:WIDTH], v[WIDTH : WIDTH + OWN], v[WIDTH + OWN : WIDTH + 2 * OWN], v[WIDTH + 2 * OWN :]

    a, b = parts(s[0]), parts(s[1])
    taps = jnp.concatenate([a[0][:, :OWN], b[0][:, :OWN], a[0][:, OWN:] + b[0][:, OWN:]], axis=1)
    gate = jnp.concatenate([a[2], b[2]])
    skips = jnp.concatenate([a[3], b[3]]).reshape(heads, HDIM).sum(1)
    dtb = jnp.concatenate([a[4][:HEADS], b[4][:HEADS]])
    rates = jnp.concatenate([a[4][128 : 128 + HEADS], b[4][128 : 128 + HEADS]])
    return (
        hidden_out,
        outs,
        a[1][None],
        grad_in_weight[None],
        taps[None, :4],
        taps[None, 4],
        dtb[None],
        rates[None],
        skips[None],
        gate[None],
        grad_out_weight[None],
    )


def solution(mesh):
    by_section = P("section", None)
    rows = P("section", "seq", None)
    tokens = P("dp", "seq", None)
    taps = P("section", None, None)
    out = P("dp", "seq", "section")
    small = (by_section,) * 4
    return jax.shard_map(
        on_device,
        mesh=mesh,
        in_specs=(tokens, tokens, by_section, rows, taps, by_section, *small, rows),
        out_specs=(out, out, by_section, rows, taps, by_section, *small, rows),
        check_vma=False,
    )
```

```python
import functools

import jax
import jax.numpy as jnp
from jax import lax
from jax.experimental import pallas as pl
from jax.experimental.pallas import tpu as pltpu
from jax.sharding import PartitionSpec as P

HDIM = 64
STATE = 128
INNER = 1536
CONV = 1792
EPS = 1e-05
f32, bf16 = jnp.float32, jnp.bfloat16

WIDTH = 768
OWN = 768
HEADS = 12
XC = OWN + 2 * STATE
XD = XC + 128
R = 64
BLOCK = 256


def nn(a, b):
    return lax.dot_general(a, b, (((1,), (0,)), ((), ())), preferred_element_type=f32)


def nt(a, b):
    return lax.dot_general(a, b, (((1,), (1,)), ((), ())), preferred_element_type=f32)


def tn(a, b):
    return lax.dot_general(a, b, (((0,), (0,)), ((), ())), preferred_element_type=f32)


def loop(count, body):
    def step(k, carry):
        body(k)
        return carry

    lax.fori_loop(0, count, step, 0)


def at(k, size):
    return pl.ds(pl.multiple_of(k * size, size), size)


def iotas(shape):
    return lax.broadcasted_iota(jnp.int32, shape, 0), lax.broadcasted_iota(jnp.int32, shape, 1)


def spread_matrix(width, per):
    r, c = iotas((128, width))
    return jnp.where(((r & 15) == c // per) & (r < 48), 1.0, 0.0).astype(bf16)


def collect_matrix():
    r, c = iotas((OWN, 128))
    return jnp.where(((c & 15) == r // HDIM) & (c < 48), 1.0, 0.0).astype(bf16)


def thirds(v):
    high = v.astype(bf16).astype(f32)
    rest = v - high
    mid = rest.astype(bf16).astype(f32)
    lane = iotas(v.shape)[1]
    out = jnp.where(lane < 16, high, jnp.where(lane < 32, mid, rest - mid))
    return jnp.where(lane < 48, out, 0.0).astype(bf16)


def halves(v):
    high = v.astype(bf16)
    return high, (v - high.astype(f32)).astype(bf16)


def running_sum(v, backward=False):
    r, c = iotas((BLOCK, BLOCK))
    tri = jnp.where((c >= r) if backward else (r >= c), 1.0, 0.0).astype(bf16)
    high = v.astype(bf16)
    rest = v - high.astype(f32)
    mid = rest.astype(bf16)
    last = (rest - mid.astype(f32)).astype(bf16)
    return nn(tri, high) + nn(tri, mid) + nn(tri, last)


def sig(v):
    return 0.5 * jnp.tanh(0.5 * v) + 0.5


def softplus(v):
    e = jnp.exp(-jnp.abs(v))
    u = 1.0 + e
    small = u == 1.0
    return jnp.maximum(v, 0.0) + jnp.where(small, e, jnp.log(u) * e / jnp.where(small, 1.0, u - 1.0))


def fold(v):
    return jnp.sum(v.reshape(v.shape[0] // 8, 8, v.shape[1]), axis=0)


def copy_rows(dst, start, src, cols=None):
    rows = src.shape[0]
    step = next(k for k in (48, 32, 16, 8, rows) if rows % k == 0)

    def move(r):
        place = pl.ds(pl.multiple_of(start + r * step, 16), step)
        if cols is None:
            dst[place, :] = src[at(r, step), :]
        else:
            dst[place, :] = src[at(r, step), cols]

    loop(rows // step, move)


def place_rows(dst, parts, cols=None):
    if len(parts) == 1:
        return copy_rows(dst, 0, parts[0], cols)
    me = lax.axis_index("seq")
    rows = parts[0].shape[0]
    for k in range(min(len(parts), 4)):
        copy_rows(dst, (me ^ k) * rows, parts[k], cols)
    if len(parts) > 4:
        copy_rows(dst, (me ^ 3) * rows + rows // 2, parts[4], cols)


def on_core(body):
    me = lax.axis_index("section")
    for core in range(2):
        pl.when(me == core)(lambda core=core: body(core))


def exact(a, b):
    return lax.dot_general(
        a, b, (((1,), (0,)), ((), ())), preferred_element_type=f32, precision=lax.Precision.HIGHEST
    )


def stats_out(a, b):
    lane = iotas(a.shape)[1]
    v = jnp.where(lane < 64, a, b)
    high = v.astype(bf16).astype(f32)
    rest = v - high
    mid = rest.astype(bf16).astype(f32)
    l = lane & 63
    out = jnp.where(l < 16, high, jnp.where(l < 32, mid, rest - mid))
    return jnp.where(l < 48, out, 0.0).astype(bf16)


def stats_in(v):
    v = v.astype(f32)
    lane = iotas(v.shape)[1]
    a = jnp.sum(jnp.where(lane < 64, v, 0.0), axis=1, keepdims=True)
    b = jnp.sum(jnp.where(lane < 64, 0.0, v), axis=1, keepdims=True)
    return a * (1.0 / 16), b * (1.0 / 16)


class Copies:

    def __init__(self, pairs_in, pairs_ahead, pairs_out, sems_in, sems_out):
        self.waiting, self.ready, self.started, self.ahead = {}, {}, [], []
        for k, (far, near, whole) in enumerate(pairs_in):
            copy = pltpu.make_async_copy(far, near, sems_in.at[k])
            copy.start()
            self.waiting.setdefault(id(whole), []).append(copy)
        for k, (far, near) in enumerate(pairs_ahead):
            copy = pltpu.make_async_copy(far, near, sems_in.at[len(pairs_in) + k])
            copy.start()
            self.ahead.append(copy)
        for k, (far, near, whole) in enumerate(pairs_out):
            self.ready.setdefault(id(whole), []).append(pltpu.make_async_copy(near, far, sems_out.at[k]))

    def need(self, refs):
        for key in [id(r) for r in refs] if refs else list(self.waiting):
            for copy in self.waiting.pop(key, ()):
                copy.wait()

    def done(self, refs):
        for key in [id(r) for r in refs] if refs else list(self.ready):
            for copy in self.ready.pop(key, ()):
                copy.start()
                self.started.append(copy)


COPIES = []


def need(*refs):
    COPIES[-1].need(refs)


def done(*refs):
    COPIES[-1].done(refs)


FAR = []
NEAR = []


def near(*arrays):
    NEAR.extend(arrays)
    return arrays if len(arrays) > 1 else arrays[0]


def far_away(array):
    FAR.append(array)
    return array


def run(kernel, name, outs, *ins, scratch=(), ahead=()):
    far, close = pl.BlockSpec(memory_space=pltpu.HBM), pl.BlockSpec(memory_space=pltpu.VMEM)
    loose = pl.BlockSpec(memory_space=pl.ANY)
    modes = [o[2] if len(o) > 2 else "h" for o in outs]
    units = [m for mode in modes for m in mode] + ["v"] * len(ahead)
    shapes, specs = [], []
    for (shape, dtype, *_), mode in zip(outs, modes):
        for m in mode:
            if m == "p":
                shapes += [jax.ShapeDtypeStruct((shape[0] // 2, *shape[1:]), dtype)] * 2
                specs += [loose] * 2
            else:
                space = dict(v=pltpu.VMEM, h=pltpu.HBM, a=jax.ShapeDtypeStruct)[m]
                shapes.append(space(shape, dtype))
                specs.append(dict(v=close, h=far, a=loose)[m])
    for a in ahead:
        shapes.append(pltpu.VMEM(a.shape, a.dtype))
        specs.append(close)
    groups = [a if isinstance(a, (tuple, list)) else (a,) for a in (*ins, *ahead)]
    flat = [a for group in groups for a in group]
    held = [any(a is k for k in NEAR) for a in flat]
    kept = [any(a is k for k in FAR) for a in flat]
    flat = [
        pltpu.with_memory_space_constraint(a, pltpu.VMEM if h else pltpu.HBM) if h or k else a
        for a, h, k in zip(flat, held, kept)
    ]
    n_in, n_out, n_own = len(flat), len(shapes), sum(len(group) for group in groups[: len(ins)])
    buffers = [
        pltpu.VMEM((sum(a.shape[0] for a in group), *group[0].shape[1:]), group[0].dtype)
        for group in groups[: len(ins)]
        if not any(group[0] is k for k in NEAR)
    ]
    buffers += [pltpu.VMEM(shape, dtype) for (shape, dtype, *_), mode in zip(outs, modes) if "v" not in mode]

    def body(*refs):
        given, made, rest = list(refs[:n_in]), list(refs[n_in : n_in + n_out]), list(refs[n_in + n_out :])
        pairs_in, pairs_out, vin, vout = [], [], [], []
        pairs_ahead = list(zip(given[n_own:], made[n_out - len(ahead) :])) if ahead else []
        at_ref = 0
        for group in groups[: len(ins)]:
            if held[at_ref]:
                vin.append(given[at_ref])
            else:
                vin.append(rest.pop(0))
                start = 0
                for k, part in enumerate(group):
                    rows = part.shape[0]
                    place = vin[-1] if len(group) == 1 else vin[-1].at[pl.ds(start, rows)]
                    pairs_in.append((given[at_ref + k], place, vin[-1]))
                    start += rows
            at_ref += len(group)
        for mode in modes:
            vout.append(made.pop(0) if "v" in mode else rest.pop(0))
            if mode == "p":
                rows = vout[-1].shape[0] // 2
                for k in range(2):
                    pairs_out.append((made.pop(0), vout[-1].at[pl.ds(k * rows, rows)], vout[-1]))
            elif mode != "v":
                pairs_out.append((made.pop(0), vout[-1], vout[-1]))
        *extra, sems_in, sems_out = rest
        copies = Copies(pairs_in, pairs_ahead, pairs_out, sems_in, sems_out)
        COPIES.append(copies)
        kernel(*vin, *vout, *extra)
        need()
        done()
        for copy in [*copies.ahead, *copies.started]:
            copy.wait()
        COPIES.pop()

    results = list(
        pl.pallas_call(
            body,
            name=name,
            out_shape=shapes,
            in_specs=[close if h else far if k else loose for h, k in zip(held, kept)],
            out_specs=specs,
            scratch_shapes=[
                *buffers,
                *[pltpu.VMEM(s, d) for s, d in scratch],
                pltpu.SemaphoreType.DMA((max(n_in, 1),)),
                pltpu.SemaphoreType.DMA((max(n_out, 1),)),
            ],
            compiler_params=pltpu.CompilerParams(vmem_limit_bytes=MIB * 2**20),
            cost_estimate=pl.CostEstimate(flops=1, bytes_accessed=1, transcendentals=0),
        )(*flat)
    )
    grouped = []
    for unit in units:
        if unit == "p":
            grouped.append((results.pop(0), results.pop(0)))
            continue
        grouped.append(results.pop(0))
        if unit != "a":
            (NEAR if unit == "v" else FAR).append(grouped[-1])
    return grouped


MIB = 24


TAPS, BIAS, NORM, GATE, SKIP, STEP, RATE = 0, 4, 5, 6, 7, 8, 9
PARAMS = 16


def k_prep(w_ref, o_ref, ng_ref, cw_ref, cb_ref, db_ref, al_ref, sk_ref, gg_ref, mine_w, give_w, mine_p, give_p):
    need()
    rows = w_ref.shape[0]
    half = WIDTH // 2
    r24, c24 = iotas((2 * HEADS, 128))
    rk, ck = iotas((2 * HEADS, OWN))

    def pack(core, out, par):
        own = core * OWN
        out[:, 0:OWN] = w_ref[:, INNER + own : INNER + own + OWN]
        out[:, OWN:XC] = w_ref[:, 2 * INNER : 2 * INNER + 2 * STATE]
        pick = ((c24 & 15) == r24 - core * HEADS) & (c24 < 48)
        steps = w_ref[:, INNER + CONV : INNER + CONV + 2 * HEADS]
        out[:, XC:XD] = nn(steps, jnp.where(pick, 1.0, 0.0).astype(bf16)).astype(bf16)
        out[:, XD : XD + OWN] = w_ref[:, own : own + OWN]
        for t in range(2):
            at_lane = XD + OWN + t * half
            out[:, at_lane : at_lane + half] = o_ref[t * rows : (t + 1) * rows, core * half : (core + 1) * half]
        par[...] = jnp.zeros(par.shape, f32)
        par[TAPS : TAPS + 4, :OWN] = cw_ref[:, own : own + OWN]
        par[TAPS : TAPS + 4, OWN:] = cw_ref[:, INNER:]
        par[BIAS : BIAS + 1, :OWN] = cb_ref[:, own : own + OWN]
        par[BIAS : BIAS + 1, OWN:] = cb_ref[:, INNER:]
        par[NORM : NORM + 1, :WIDTH] = ng_ref[...]
        par[GATE : GATE + 1, :OWN] = gg_ref[:, own : own + OWN]
        spread = jnp.where(rk - core * HEADS == ck // HDIM, 1.0, 0.0)
        par[SKIP : SKIP + 1, :OWN] = exact(jnp.broadcast_to(sk_ref[...], (8, 2 * HEADS)), spread)[0:1]
        lanes = jnp.where(pick, 1.0, 0.0)
        par[STEP : STEP + 1, 0:128] = exact(jnp.broadcast_to(db_ref[...], (8, 2 * HEADS)), lanes)[0:1]
        par[RATE : RATE + 1, 0:128] = exact(jnp.broadcast_to(al_ref[...], (8, 2 * HEADS)), lanes)[0:1]

    def body(core):
        pack(core, mine_w, mine_p)
        pack(1 - core, give_w, give_p)

    on_core(body)


def k_pick(mine_w, got_w, mine_p, got_p, x0, zo0, x1, zo1, p0, p1):
    need()

    def body(core):
        pairs = ((mine_w, mine_p), (got_w, got_p))
        for layer, (x, zo, p) in enumerate(((x0, zo0, p0), (x1, zo1, p1))):
            w, par = pairs[layer ^ core]
            x[...] = w[:, 0:XD]
            zo[...] = w[:, XD:]
            p[...] = par[...]

    on_core(body)


def norm_rows(h, gain):
    scale = lax.rsqrt(jnp.mean(h * h, axis=1, keepdims=True) + EPS)
    return (h * scale * gain).astype(bf16)


def project(t, normed_ref, wx_ref, xb_ref, tail_ref):
    xb_ref[0:8, :] = jnp.zeros((8, XD), f32)

    def cols(c):
        xb_ref[8 : 8 + t, at(c, 384)] = nn(normed_ref[...], wx_ref[:, at(c, 384)])

    loop(XD // 384, cols)
    tail_ref[...] = xb_ref[t:, :XC]


def k_in(hid_ref, ga_ref, gb_ref, par_ref, *rest):
    *parts, h_ref, normed_ref, xb_ref, wx_ref, tail_ref = rest
    need(hid_ref, ga_ref, gb_ref, par_ref)
    t = h_ref.shape[0]
    half = t // 2
    odd = lax.rem(lax.axis_index("seq"), 2)
    core = lax.axis_index("section")
    copy_rows(h_ref, odd * half, hid_ref.at[odd])
    copy_rows(h_ref, (1 - odd) * half + core * (half // 2), ga_ref)
    copy_rows(h_ref, (1 - odd) * half + (1 - core) * (half // 2), gb_ref)

    def rows(r):
        normed_ref[at(r, R), :] = norm_rows(h_ref[at(r, R), :].astype(f32), par_ref[NORM : NORM + 1, :WIDTH])

    loop(t // R, rows)
    done(h_ref, normed_ref)
    need(*parts)
    place_rows(wx_ref, parts)
    done(wx_ref)
    project(t, normed_ref, wx_ref, xb_ref, tail_ref)


def k_mid(h_ref, p_ref, st_ref, msg_ref, par_ref, *rest):
    *parts, h1_ref, pt_ref, rs_ref, normed_ref, xb_ref, wx_ref, tail_ref = rest
    need(h_ref, p_ref, st_ref, msg_ref, par_ref)
    t = h_ref.shape[0]

    def rows(r):
        s = at(r, R)
        other = stats_in(msg_ref[s, WIDTH:])[0]
        rs = lax.rsqrt((st_ref[s, 0:128] + other) * (1.0 / INNER) + EPS)
        rs_ref[s, :] = rs
        p = p_ref[s, :] + msg_ref[s, :WIDTH].astype(f32)
        pt_ref[s, :] = p
        h1 = (h_ref[s, :].astype(f32) + rs[:, 0:1] * p).astype(bf16)
        h1_ref[s, :] = h1
        normed_ref[s, :] = norm_rows(h1.astype(f32), par_ref[NORM : NORM + 1, :WIDTH])

    loop(t // R, rows)
    done(h1_ref, pt_ref, rs_ref, normed_ref)
    need(*parts)
    place_rows(wx_ref, parts)
    done(wx_ref)
    project(t, normed_ref, wx_ref, xb_ref, tail_ref)


def k_z(normed_ref, *rest):
    *parts, z_ref, wz_ref, keep_ref, give_ref, o = rest
    need(*parts)
    place_rows(wz_ref, parts, slice(0, OWN))
    done(wz_ref)
    place_rows(o, parts, slice(OWN, 2 * OWN))

    def split(core):
        rows = keep_ref.shape[0]
        keep_ref[...] = o[core * rows : (core + 1) * rows, :]
        give_ref[...] = o[(1 - core) * rows : (2 - core) * rows, :]

    on_core(split)
    done(keep_ref, give_ref)
    need(normed_ref)

    def cols(c):
        z_ref[:, at(c, 384)] = nn(normed_ref[...], wz_ref[:, at(c, 384)])

    loop(OWN // 384, cols)


def k_front(xb_ref, before_ref, par_ref, act_ref, bc_ref, xdt_ref, dt_ref, cum_ref, s_ref, dec_ref, tot_ref, wide, edge):
    t = act_ref.shape[0]
    need()
    edge[0:8, :] = before_ref[...]
    edge[8:16, :] = jnp.zeros((8, XC), f32)

    def conv(c):
        cols = at(c, 128)
        w = par_ref[0:8, cols]
        total = w[4:5] + w[0:1] * xb_ref[pl.ds(5, t), cols]
        for k in range(1, 4):
            total = total + w[k : k + 1] * xb_ref[pl.ds(5 + k, t), cols]
        act_ref[:, cols] = total * sig(total)
        first = total[0:8]
        for k in range(4):
            first = first + w[k : k + 1] * edge[5 + k : 13 + k, cols]
        act_ref[0:8, cols] = first * sig(first)

    loop(XC // 128, conv)
    bc_ref[...] = act_ref[:, OWN:].astype(bf16)
    done(act_ref, bc_ref)
    dt = softplus(xb_ref[8 : 8 + t, XC:] + par_ref[STEP : STEP + 1, 0:128])
    dt_ref[...] = dt
    done(dt_ref)
    rate = -jnp.exp(par_ref[RATE : RATE + 1, 0:128])
    spread = spread_matrix(OWN, HDIM)
    wide[...] = nn(thirds(dt), spread)

    def rows(r):
        s = at(r, R)
        xdt_ref[s, :] = (act_ref[s, :OWN] * wide[s, :]).astype(bf16)

    loop(t // R, rows)
    done(xdt_ref)
    for b in range(t // BLOCK):
        s = pl.ds(b * BLOCK, BLOCK)
        cum = running_sum(rate * dt[b * BLOCK : (b + 1) * BLOCK])
        cum_ref[s, :] = cum
        end = cum[BLOCK - 1 : BLOCK, :]
        dec_ref[8 * b : 8 * b + 8, :] = nn(thirds(jnp.exp(jnp.broadcast_to(end, (8, 128)))), spread)
        wide[s, :] = nn(thirds(jnp.exp(end - cum)), spread)
        bl = bc_ref[s, 0:STATE]

        def cols(c):
            decayed = (xdt_ref[s, at(c, 256)].astype(f32) * wide[s, at(c, 256)]).astype(bf16)
            s_ref[pl.ds(b * STATE, STATE), at(c, 256)] = tn(bl, decayed)

        loop(OWN // 256, cols)
    tot_ref[...] = (s_ref[STATE:, :] + dec_ref[8:9, :] * s_ref[:STATE, :]).astype(bf16)


def decay_tables(cum_ref, tall, flat):
    t = cum_ref.shape[0]
    parts = thirds(cum_ref[...])
    tall[...] = nn(parts, spread_matrix(HEADS * 128, 128))
    r, c = iotas((HEADS * 8, 128))
    pick = jnp.where(((c & 15) == r // 8) & (c < 48), 1.0, 0.0).astype(bf16)
    for b in range(t // 128):
        flat[b] = nt(pick, parts[b * 128 : (b + 1) * 128])


def k_within(cum_ref, bc_ref, xdt_ref, y_ref, tall, flat, scores):
    t = cum_ref.shape[0]
    need(cum_ref)
    decay_tables(cum_ref, tall, flat)
    blocks = t // BLOCK
    need(bc_ref, xdt_ref)
    for b in range(blocks):
        s = pl.ds(b * BLOCK, BLOCK)
        scores[s, :] = nt(bc_ref[s, STATE:], bc_ref[s, 0:STATE])
    r, c = iotas((128, 128))
    causal = r >= c
    lane = iotas((BLOCK, 128))[1]

    def pair(p):
        cols = at(p, 128)
        for b in range(blocks):
            o = b * BLOCK
            u = xdt_ref[pl.ds(o, BLOCK), cols]
            top = jnp.zeros((128, 128), f32)
            low = jnp.zeros((128, 128), f32)
            for a in range(2):
                head = 2 * p + a
                own = jnp.where((lane >= 64) == (a == 1), u, jnp.zeros_like(u))
                hc = at(head, 128)
                hr = pl.ds(pl.multiple_of(head * 8, 8), 8)
                t0, t1 = tall[pl.ds(o, 128), hc], tall[pl.ds(o + 128, 128), hc]
                u0, u1 = flat[2 * b, hr, :][0:1], flat[2 * b + 1, hr, :][0:1]
                sc = scores
                w00 = jnp.where(causal, sc[pl.ds(o, 128), 0:128] * jnp.exp(jnp.where(causal, t0 - u0, 0.0)), 0.0)
                w10 = sc[pl.ds(o + 128, 128), 0:128] * jnp.exp(t1 - u0)
                w11 = jnp.where(causal, sc[pl.ds(o + 128, 128), 128:] * jnp.exp(jnp.where(causal, t1 - u1, 0.0)), 0.0)
                top = top + nn(w00.astype(bf16), own[:128])
                low = low + nn(w10.astype(bf16), own[:128]) + nn(w11.astype(bf16), own[128:])
            y_ref[pl.ds(o, 128), cols] = top
            y_ref[pl.ds(o + 128, 128), cols] = low

    loop(OWN // 128, pair)


def k_out(first_layer, yw_ref, act_ref, bc_ref, cum_ref, cin_ref, s_ref, dec_ref, z_ref, par_ref, keep_ref, got_ref, *rest):
    if first_layer:
        y_ref, p_ref, msg_ref, st_ref, c_ref, wo_ref, wide, u_ref = rest
    else:
        cot_ref, ca_ref, cb_ref, y_ref, p_ref, msg_ref, st_ref, c_ref, wo_ref, g_ref, wide, u_ref = rest
    t = yw_ref.shape[0]
    half = WIDTH // 2
    shard = o_rows(keep_ref)

    def weights(core):
        for r in range(keep_ref.shape[0] // shard):
            for k in range(2):
                for src, side in ((keep_ref, core), (got_ref, 1 - core)):
                    wo_ref[(2 * r + k) * shard : (2 * r + k + 1) * shard, side * half : (side + 1) * half] = src[
                        r * shard : (r + 1) * shard, k * half : (k + 1) * half
                    ]

    need(keep_ref, got_ref)
    on_core(weights)
    done(wo_ref)
    need(bc_ref, cum_ref, cin_ref, s_ref, dec_ref)
    c_ref[0:STATE, :] = cin_ref[...].astype(f32)
    c_ref[STATE:, :] = s_ref[:STATE, :] + dec_ref[0:1, :] * c_ref[0:STATE, :]
    wide[...] = nn(thirds(jnp.exp(cum_ref[...])), spread_matrix(OWN, HDIM))
    for b in range(t // BLOCK):
        s = pl.ds(b * BLOCK, BLOCK)

        def cols(c):
            from_state = nn(bc_ref[s, STATE:], c_ref[pl.ds(b * STATE, STATE), at(c, 256)].astype(bf16))
            wide[s, at(c, 256)] = wide[s, at(c, 256)] * from_state

        loop(OWN // 256, cols)

    done(c_ref)
    need(yw_ref, act_ref, z_ref, par_ref)

    def rows(r):
        s = at(r, R)
        y = yw_ref[s, :] + wide[s, :] + par_ref[SKIP : SKIP + 1, :OWN] * act_ref[s, :OWN]
        y_ref[s, :] = y
        z = z_ref[s, :]
        gated = y * z * sig(z)
        u_ref[s, :] = (gated * par_ref[GATE : GATE + 1, :OWN]).astype(bf16)
        st_ref[s, 0:128] = jnp.broadcast_to(jnp.sum(gated * gated, axis=1, keepdims=True), (R, 128))

    loop(t // R, rows)
    done(y_ref)

    def project_out(c):
        p_ref[:, at(c, 256)] = nn(u_ref[...], wo_ref[:, at(c, 256)])

    loop(WIDTH // 256, project_out)
    done(p_ref)
    if first_layer:

        def send(r):
            s = at(r, R)
            msg_ref[s, :WIDTH] = p_ref[s, :].astype(bf16)
            v = st_ref[s, 0:128]
            msg_ref[s, WIDTH:] = stats_out(v, v)

        loop(t // R, send)
    else:
        odd = lax.rem(lax.axis_index("seq"), 2)
        need(cot_ref, ca_ref, cb_ref)
        copy_rows(g_ref, odd * (t // 2), cot_ref.at[odd])
        core = lax.axis_index("section")
        copy_rows(g_ref, (1 - odd) * (t // 2) + core * (t // 4), ca_ref)
        copy_rows(g_ref, (1 - odd) * (t // 2) + (1 - core) * (t // 4), cb_ref)
        done(g_ref)

        def dots(r):
            s = at(r, R)
            d = jnp.sum(p_ref[s, :] * g_ref[s, :].astype(f32), axis=1, keepdims=True)
            d = jnp.broadcast_to(d, (R, 128))
            st_ref[s, 128:256] = d
            msg_ref[s, half:] = stats_out(st_ref[s, 0:128], d)

        loop(t // R, dots)

        def send(core):
            msg_ref[:, :half] = p_ref[:, (1 - core) * half : (2 - core) * half].astype(bf16)

        on_core(send)


def o_rows(keep_ref):
    return keep_ref.shape[0] // (lax.axis_size("seq") // 2)


def k_final(h_ref, p_ref, st_ref, msg_ref, keep_ref, give_ref):
    need()
    half = WIDTH // 2
    rows_each = keep_ref.shape[0]
    odd = lax.rem(lax.axis_index("seq"), 2)

    def body(core):
        cols = slice(core * half, (core + 1) * half)

        def half_out(dst, start):
            def rows(r):
                s = pl.ds(pl.multiple_of(start + r * R, R), R)
                other = stats_in(msg_ref[s, half:])[0]
                rs = lax.rsqrt((st_ref[s, 0:1] + other) * (1.0 / INNER) + EPS)
                p = p_ref[s, cols] + msg_ref[s, :half].astype(f32)
                dst[at(r, R), :] = (h_ref[s, cols].astype(f32) + rs * p).astype(bf16)

            loop(rows_each // R, rows)

        half_out(keep_ref, odd * rows_each)
        half_out(give_ref, (1 - odd) * rows_each)

    on_core(body)


def kb_gate(g_ref, w_ref, y_ref, yw_ref, z_ref, act_ref, bc_ref, cum_ref, rs_ref, rd_ref, par_ref, dec_ref,
            qz_ref, dy_ref, df_ref, dca_ref, keep_ref, give_ref, d_ref, e_ref, small_ref, dgn, wide, gn):
    t = g_ref.shape[0]
    need(g_ref, w_ref)

    def back(c):
        dgn[:, at(c, 256)] = nt(g_ref[...], w_ref[at(c, 256), :])

    loop(OWN // 256, back)
    need(cum_ref)
    wide[...] = nn(thirds(jnp.exp(cum_ref[...])), spread_matrix(OWN, HDIM))
    small_ref[...] = jnp.zeros(small_ref.shape, f32)
    collect = collect_matrix()
    need()

    def rows(r):
        s = at(r, R)
        z, y, d, x = z_ref[s, :], y_ref[s, :], dgn[s, :], act_ref[s, :OWN]
        gg = par_ref[GATE : GATE + 1, :OWN]
        if rs_ref.shape[1] == 128:
            rs, rd = rs_ref[s, 0:1], rd_ref[s, 0:1]
        else:
            squares, dots = stats_in(rd_ref[s, WIDTH // 2 :])
            rs = lax.rsqrt((rs_ref[s, 0:1] + squares) * (1.0 / INNER) + EPS)
            rd = rs_ref[s, 128:129] + dots
        sg = sig(z)
        sz = z * sg
        gated = y * sz
        scaled = gated * rs
        small_ref[0:8, :] += fold(d * scaled)
        gn[s, :] = (scaled * gg).astype(bf16)
        dgated = rs * (gg * d) - gated * (rs * rs * rs * rd * (1.0 / INNER))
        dy = dgated * sz
        dy_ref[s, :] = dy
        qz_ref[s, :] = (dgated * y * (sg * (1.0 + z - sz))).astype(bf16)
        small_ref[8:16, :] += fold(dy * x)
        df_ref[s, :] = (wide[s, :] * dy).astype(bf16)
        yw = yw_ref[s, :]
        high, low = halves(dy.astype(bf16).astype(f32) * yw + dy * (y - yw - par_ref[SKIP : SKIP + 1, :OWN] * x))
        dca_ref[s, :] = nn(high, collect) + nn(low, collect)

    loop(t // R, rows)
    done(dy_ref, qz_ref, df_ref, dca_ref, small_ref)
    for b in range(t // BLOCK):
        s = pl.ds(b * BLOCK, BLOCK)
        cl = bc_ref[s, STATE:]

        def cols(c):
            d_ref[pl.ds(b * STATE, STATE), at(c, 256)] = tn(cl, df_ref[s, at(c, 256)])

        loop(OWN // 256, cols)
    e_ref[...] = (d_ref[:STATE, :] + dec_ref[0:1, :] * d_ref[STATE:, :]).astype(bf16)

    done(d_ref, e_ref)
    half = WIDTH // 2

    def halves_of(core):
        def weight(c):
            dw = tn(gn[:, at(c, 256)], g_ref[...]).astype(bf16)
            keep_ref[at(c, 256), :] = dw[:, core * half : (core + 1) * half]
            give_ref[at(c, 256), :] = dw[:, (1 - core) * half : (2 - core) * half]

        loop(OWN // 256, weight)

    on_core(halves_of)


def kb_within(dy_ref, xdt_ref, cum_ref, bc_ref, df_ref, c_ref, dx_ref, dbc_ref, tall, flat, scores, ds):
    t = cum_ref.shape[0]
    need(cum_ref)
    decay_tables(cum_ref, tall, flat)
    blocks = t // BLOCK
    need(bc_ref, xdt_ref, dy_ref)
    for b in range(blocks):
        s = pl.ds(b * BLOCK, BLOCK)
        scores[s, :] = nt(bc_ref[s, STATE:], bc_ref[s, 0:STATE])
    ds[...] = jnp.zeros(ds.shape, f32)
    r, c = iotas((128, 128))
    causal = r >= c
    lane = iotas((BLOCK, 128))[1]

    def pair(p):
        cols = at(p, 128)
        for b in range(blocks):
            o = b * BLOCK
            u = xdt_ref[pl.ds(o, BLOCK), cols]
            g = dy_ref[pl.ds(o, BLOCK), cols].astype(bf16)
            top = jnp.zeros((128, 128), f32)
            low = jnp.zeros((128, 128), f32)
            for a in range(2):
                head = 2 * p + a
                own = jnp.where((lane >= 64) == (a == 1), g, jnp.zeros_like(g))
                hc = at(head, 128)
                hr = pl.ds(pl.multiple_of(head * 8, 8), 8)
                t0, t1 = tall[pl.ds(o, 128), hc], tall[pl.ds(o + 128, 128), hc]
                u0, u1 = flat[2 * b, hr, :][0:1], flat[2 * b + 1, hr, :][0:1]
                e00 = jnp.where(causal, jnp.exp(jnp.where(causal, t0 - u0, 0.0)), 0.0)
                e10 = jnp.exp(t1 - u0)
                e11 = jnp.where(causal, jnp.exp(jnp.where(causal, t1 - u1, 0.0)), 0.0)
                q0, q1 = pl.ds(o, 128), pl.ds(o + 128, 128)
                w00 = (scores[q0, 0:128] * e00).astype(bf16)
                w10 = (scores[q1, 0:128] * e10).astype(bf16)
                w11 = (scores[q1, 128:] * e11).astype(bf16)
                top = top + tn(w00, own[:128]) + tn(w10, own[128:])
                low = low + tn(w11, own[128:])
                ds[q0, 0:128] += nt(own[:128], u[:128]) * e00
                ds[q1, 0:128] += nt(own[128:], u[:128]) * e10
                ds[q1, 128:] += nt(own[128:], u[128:]) * e11
            dx_ref[pl.ds(o, 128), cols] = top
            dx_ref[pl.ds(o + 128, 128), cols] = low

    loop(OWN // 128, pair)
    done(dx_ref)
    need(df_ref, c_ref)
    for b in range(blocks):
        s = pl.ds(b * BLOCK, BLOCK)
        d = ds[s, :].astype(bf16)
        carried = c_ref[pl.ds(b * STATE, STATE), :].astype(bf16)
        dbc_ref[s, 0:STATE] = tn(d, bc_ref[s, STATE:])
        dbc_ref[s, STATE:] = nn(d, bc_ref[s, 0:STATE]) + nt(df_ref[s, :], carried)


def kb_front(gin_ref, d_ref, c_ref, dec_ref, bc_ref, xdt_ref, act_ref, xb_ref, before_ref, dt_ref, cum_ref, dxw_ref, dbc_ref,
             dy_ref, dca_ref, par_ref,
             dxb_ref, halo_ref, qdt_ref, small_ref, head_ref, gs, dd, te, dtw, dact, red, red2, ends, pad, edge):
    t = act_ref.shape[0]
    blocks = t // BLOCK
    spread, collect = spread_matrix(OWN, HDIM), collect_matrix()
    need(gin_ref, d_ref, dec_ref)
    gs[STATE:, :] = gin_ref[...].astype(f32)
    gs[:STATE, :] = d_ref[STATE:, :] + dec_ref[8:9, :] * gs[STATE:, :]
    need(dbc_ref, dt_ref, c_ref, cum_ref, bc_ref, xdt_ref)
    dact[:, OWN:] = dbc_ref[...]
    dtw[...] = nn(thirds(dt_ref[...]), spread)
    for b in range(blocks):
        s = pl.ds(b * BLOCK, BLOCK)
        ss = pl.ds(b * STATE, STATE)
        end = cum_ref[pl.ds((b + 1) * BLOCK - 8, 8), :][7:8]
        te[s, :] = nn(thirds(jnp.exp(end - cum_ref[s, :])), spread)
        bl = bc_ref[s, 0:STATE]
        ends[8 * b : 8 * b + 8, :] = fold(gs[ss, :] * c_ref[ss, :]) * dec_ref[8 * b : 8 * b + 8, :]

        def cols(c):
            q = at(c, 256)
            low = gs[ss, q].astype(bf16)
            dd[s, q] = nn(bl, low)
            decayed = (xdt_ref[s, q].astype(f32) * te[s, q]).astype(bf16)
            dact[s, OWN : OWN + STATE] += nt(decayed, low)

        loop(OWN // 256, cols)
        if b == 0:
            need(dxw_ref, dy_ref, act_ref, par_ref)

        def rows(r):
            q = pl.ds(pl.multiple_of(b * BLOCK + r * R, R), R)
            w = dd[q, :] * te[q, :]
            ends[8 * b : 8 * b + 8, :] += fold(w * xdt_ref[q, :].astype(f32))
            dxdt = dxw_ref[q, :] + w
            dact[q, :OWN] = dxdt * dtw[q, :] + par_ref[SKIP : SKIP + 1, :OWN] * dy_ref[q, :]
            high, low = halves(dxdt * act_ref[q, :OWN])
            red[q, :] = nn(high, collect) + nn(low, collect)
            high, low = halves(dxdt * xdt_ref[q, :].astype(f32))
            red2[q, :] = nn(high, collect) + nn(low, collect)

        loop(BLOCK // R, rows)
    need()
    high, low = halves(ends[...])
    at_end = nn(high, collect) + nn(low, collect)
    rate = -jnp.exp(par_ref[RATE : RATE + 1, 0:128])
    head_ref[...] = jnp.zeros(head_ref.shape, f32)
    for b in range(blocks):
        s = pl.ds(b * BLOCK, BLOCK)
        dt = dt_ref[s, :]
        total = running_sum(dca_ref[s, :] - red2[s, :], True)
        total = total + jnp.sum(at_end[8 * b : 8 * b + 8], axis=0, keepdims=True)
        ddt = red[s, :] + rate * total
        raw = xb_ref[pl.ds(8 + b * BLOCK, BLOCK), XC:] + par_ref[STEP : STEP + 1, 0:128]
        draw = ddt * jax.nn.sigmoid(raw)
        head_ref[0:8, :] += fold(draw)
        head_ref[8:16, :] += fold(rate * dt * total)
        lane = iotas(draw.shape)[1]
        qdt_ref[s, :] = jnp.where(lane < HEADS, draw, 0.0).astype(bf16)
    done(qdt_ref, head_ref)
    pad[0:8, :] = jnp.zeros((8, 128), f32)
    pad[8 + t :, :] = jnp.zeros((8, 128), f32)
    edge[0:8, :] = before_ref[...]
    edge[8:16, :] = jnp.zeros((8, XC), f32)

    def conv(c):
        cols = at(c, 128)
        w = par_ref[0:8, cols]
        taps = [xb_ref[pl.ds(5 + k, t), cols] for k in range(4)]
        total = w[4:5] + w[0:1] * taps[0]
        for k in range(1, 4):
            total = total + w[k : k + 1] * taps[k]
        sg = sig(total)
        pad[8 : 8 + t, :] = dact[:, cols] * (sg * (1.0 + total * (1.0 - sg)))
        first = total[0:8]
        for k in range(4):
            first = first + w[k : k + 1] * edge[5 + k : 13 + k, cols]
        sg = sig(first)
        top = dact[0:8, cols] * (sg * (1.0 + first * (1.0 - sg)))
        pad[8:16, :] = top
        d = pad[8 : 8 + t, :]
        for k in range(4):
            small_ref[8 * k : 8 * k + 8, cols] = (
                fold(d * xb_ref[pl.ds(5 + k, t), cols]) + top * edge[5 + k : 13 + k, cols]
            )
        small_ref[32:40, cols] = fold(d)
        out = w[3:4] * pad[0 : 8 + t, :]
        for k in range(3):
            out = out + w[k : k + 1] * pad[3 - k : 11 - k + t, :]
        dxb_ref[:, cols] = out
        halo_ref[:, cols] = out[0:8]

    loop(XC // 128, conv)


def z_weight(dw_ref, first, normed_ref, qz_ref, okeep_ref, ogot_ref):
    def weight(c):
        dw_ref[at(c, 256), first : first + OWN] = tn(normed_ref[:, at(c, 256)], qz_ref[...]).astype(bf16)

    loop(WIDTH // 256, weight)
    n = lax.axis_size("seq")
    shard, half = WIDTH // n, WIDTH // 2
    need()

    def out(core):
        for j in range(n):
            src = okeep_ref if j // (n // 2) == core else ogot_ref
            for k in range(2):
                row, col = (2 * (j % (n // 2)) + k) * shard, first + OWN + k * half
                dw_ref[j * shard : (j + 1) * shard, col : col + half] = src[row : row + shard, :]

    on_core(out)


def kb_z_weight(normed_ref, qz_ref, okeep_ref, ogot_ref, *rest):
    *blocks, dw_ref = rest
    need(normed_ref, qz_ref)
    z_weight(dw_ref, 0, normed_ref, qz_ref, okeep_ref, ogot_ref)
    to_blocks(blocks, dw_ref)


def kb_x_weight(normed_ref, q_ref, *rest):
    *blocks, dw_ref = rest
    need()
    x_weight(normed_ref, q_ref, dw_ref)
    to_blocks(blocks, dw_ref)


def to_blocks(blocks, dw):
    if len(blocks) == 1:
        return copy_rows(blocks[0], 0, dw)
    me = lax.axis_index("seq")
    rows = blocks[0].shape[0]
    for k in reversed(range(len(blocks))):
        block, start = blocks[k], (me ^ k) * rows

        def move(r, block=block, start=start):
            block[at(r, 48), :] = dw[pl.ds(pl.multiple_of(start + r * 48, 16), 48), :]

        loop(rows // 48, move)
        done(block)


def kb_z_normed(qz_ref, w_ref, dn_ref):
    need()

    def back(c):
        dn_ref[:, at(c, 256)] = nt(qz_ref[...], w_ref[at(c, 256), :])

    loop(WIDTH // 256, back)


def make_q(dxb_ref, ret_ref, qdt_ref, q):
    t = q.shape[0]

    def rows(r):
        q[at(r, R), :XC] = dxb_ref[pl.ds(pl.multiple_of(r * R, R) + 8, R), :].astype(bf16)

    loop(t // R, rows)
    q[t - 16 :, :XC] = (
        dxb_ref[t - 8 : t + 8, :] + jnp.concatenate([jnp.zeros((8, XC), f32), ret_ref[...]], axis=0)
    ).astype(bf16)
    q[:, XC:] = qdt_ref[...]


def x_normed(q_ref, dnz_ref, w_ref, dn_ref, dnb_ref):
    def back(c):
        cols = at(c, 256)
        d = dnz_ref[:, cols] + nt(q_ref[...], w_ref[cols, :])
        dn_ref[:, cols] = d
        dnb_ref[:, cols] = d.astype(bf16)

    loop(WIDTH // 256, back)


def x_weight(normed_ref, q_ref, dw_ref):
    def weight(c):
        dw_ref[at(c, 256), :] = tn(normed_ref[:, at(c, 256)], q_ref[...]).astype(bf16)

    loop(WIDTH // 256, weight)


def kb_x_normed(dxb_ref, ret_ref, qdt_ref, dnz_ref, w_ref, q_ref, dn_ref, dnb_ref):
    need(dxb_ref, ret_ref, qdt_ref)
    make_q(dxb_ref, ret_ref, qdt_ref, q_ref)
    done(q_ref)
    need()
    x_normed(q_ref, dnz_ref, w_ref, dn_ref, dnb_ref)


def kb_x_weight_first(normed_ref, dxb_ref, ret_ref, qdt_ref, q_ref, *rest):
    *blocks, dw = rest
    need()
    make_q(dxb_ref, ret_ref, qdt_ref, q_ref)
    done(q_ref)
    x_weight(normed_ref, q_ref, dw)
    to_blocks(blocks, dw)


def kb_x_normed_last(q_ref, dnz_ref, w_ref, dn_ref, dnb_ref):
    need()
    x_normed(q_ref, dnz_ref, w_ref, dn_ref, dnb_ref)


def kb_norm(h_ref, dn_ref, dr_ref, g_ref, par_ref, pt_ref, gh_ref, small_ref, rd_ref):
    t = h_ref.shape[0]
    need()
    small_ref[...] = jnp.zeros(small_ref.shape, f32)

    def rows(r):
        s = at(r, R)
        h = h_ref[s, :].astype(f32)
        d = dn_ref[s, :] + dr_ref[s, :].astype(f32)
        scale = lax.rsqrt(jnp.mean(h * h, axis=1, keepdims=True) + EPS)
        hs = h * scale
        small_ref[...] += fold(d * hs)
        gd = par_ref[NORM : NORM + 1, :WIDTH] * d
        back = scale * (gd - hs * jnp.mean(hs * gd, axis=1, keepdims=True))
        gh = (g_ref[s, :].astype(f32) + back).astype(bf16)
        gh_ref[s, :] = gh
        if rd_ref is not None:
            dot = jnp.sum(gh.astype(f32) * pt_ref[s, :], axis=1, keepdims=True)
            rd_ref[s, :] = jnp.broadcast_to(dot, (R, 128))

    loop(t // R, rows)


def kb_norm_last(h_ref, dn_ref, dr_ref, g_ref, par_ref, keep_ref, give_ref, small_ref, gh):
    kb_norm(h_ref, dn_ref, dr_ref, g_ref, par_ref, None, gh, small_ref, None)
    half = WIDTH // 2
    each = keep_ref.shape[0]
    odd = lax.rem(lax.axis_index("seq"), 2)

    def body(core):
        def rows(r):
            for dst, start in ((keep_ref, odd * each), (give_ref, (1 - odd) * each)):
                s = pl.ds(pl.multiple_of(start + r * R, R), R)
                dst[at(r, R), :] = gh[s, core * half : (core + 1) * half]

        loop(each // R, rows)

    on_core(body)


SMALL = 12


def k_small(*refs):
    *ins, out = refs
    need()
    out[...] = jnp.zeros(out.shape, f32)

    def total(x):
        return jnp.sum(x, axis=0, keepdims=True)

    for layer in range(2):
        a, b, c, d = ins[4 * layer : 4 * layer + 4]
        base = SMALL * layer
        for k in range(5):
            out[base + k : base + k + 1, :] = total(b[8 * k : 8 * k + 8, :])
        out[base + NORM : base + NORM + 1, :WIDTH] = total(d[...])
        out[base + GATE : base + GATE + 1, :OWN] = total(a[0:8, :])
        out[base + SKIP : base + SKIP + 1, :OWN] = total(a[8:16, :])
        out[base + STEP : base + STEP + 1, 0:128] = total(c[0:8, :])
        out[base + RATE : base + RATE + 1, 0:128] = total(c[8:16, :])


def k_small_out(mine_ref, got_ref, ng_ref, cw_ref, cb_ref, db_ref, al_ref, sk_ref, gg_ref):
    need()

    def body(core):
        base = SMALL * core
        cores = (mine_ref, got_ref) if core == 0 else (got_ref, mine_ref)
        ng_ref[...] = mine_ref[base + NORM : base + NORM + 1, :WIDTH]
        for c, src in enumerate(cores):
            cw_ref[:, c * OWN : (c + 1) * OWN] = src[base : base + 4, :OWN]
            cb_ref[:, c * OWN : (c + 1) * OWN] = src[base + BIAS : base + BIAS + 1, :OWN]
            gg_ref[:, c * OWN : (c + 1) * OWN] = src[base + GATE : base + GATE + 1, :OWN]
        a, b = cores
        cw_ref[:, INNER:] = a[base : base + 4, OWN:] + b[base : base + 4, OWN:]
        cb_ref[:, INNER:] = a[base + BIAS : base + BIAS + 1, OWN:] + b[base + BIAS : base + BIAS + 1, OWN:]
        r, c = iotas((128, 2 * HEADS))
        r2, c2 = iotas((OWN, 2 * HEADS))
        wide = lambda v: jnp.broadcast_to(v, (8, v.shape[1]))
        for ref, row in ((db_ref, STEP), (al_ref, RATE)):
            acc = jnp.zeros((8, 2 * HEADS), f32)
            for k, src in enumerate(cores):
                pick = jnp.where((r == c - k * HEADS) & (r < HEADS), 1.0, 0.0)
                acc = acc + exact(wide(src[base + row : base + row + 1, 0:128]), pick)
            ref[...] = acc[0:1]
        acc = jnp.zeros((8, 2 * HEADS), f32)
        for k, src in enumerate(cores):
            pick = jnp.where(r2 // HDIM == c2 - k * HEADS, 1.0, 0.0)
            acc = acc + exact(wide(src[base + SKIP : base + SKIP + 1, :OWN]), pick)
        sk_ref[...] = acc[0:1]

    on_core(body)


def in_place(refs, full):
    odd = lax.rem(lax.axis_index("dp"), 2)
    half = refs[0].shape[0]
    copy_rows(full, odd * half, refs[0])
    copy_rows(full, (1 - odd) * half, refs[1])


def k_home(m1_ref, o1_ref, mz_ref, oz_ref, mx_ref, ox_ref, give_ref, zo, x):
    need()

    def body(core):
        if core == 0:
            in_place((m1_ref, o1_ref), give_ref)
        else:
            in_place((mz_ref, oz_ref), zo)
            in_place((mx_ref, ox_ref), x)
            give_ref[:, :XD] = x[...]
            give_ref[:, XD:] = zo[...]

    on_core(body)


def k_grads(m1_ref, o1_ref, mz_ref, oz_ref, mx_ref, ox_ref, got_ref, gw_ref, go_ref, dw1, zo0, x0):
    need()
    rows, half = got_ref.shape[0], WIDTH // 2
    in_place((m1_ref, o1_ref), dw1)
    in_place((mz_ref, oz_ref), zo0)
    in_place((mx_ref, ox_ref), x0)

    def body(core):
        mine = (x0, zo0, 0) if core == 0 else (dw1, dw1, XD)
        other = (got_ref, got_ref, XD)
        cores = (mine, other) if core == 0 else (other, mine)
        for c, (x, zo, first) in enumerate(cores):
            gw_ref[:, c * OWN : (c + 1) * OWN] = zo[:, first : first + OWN].astype(f32)
            gw_ref[:, INNER + c * OWN : INNER + (c + 1) * OWN] = x[:, :OWN].astype(f32)
            for k in range(2):
                col = first + OWN + k * half
                go_ref[k * rows : (k + 1) * rows, c * half : (c + 1) * half] = zo[:, col : col + half].astype(f32)
        a, b = cores[0][0], cores[1][0]
        gw_ref[:, 2 * INNER : 2 * INNER + 2 * STATE] = a[:, OWN:XC].astype(f32) + b[:, OWN:XC].astype(f32)
        r, c = iotas((128, 2 * HEADS))
        acc = 0.0
        for k, x in enumerate((a, b)):
            pick = jnp.where((r == c - k * HEADS) & (r < HEADS), 1.0, 0.0).astype(bf16)
            acc = acc + nn(x[:, XC:XD], pick)
        gw_ref[:, INNER + CONV :] = acc

    on_core(body)


def across(x):
    return jax.tree.map(lambda a: lax.ppermute(a, "section", [(0, 1), (1, 0)]), x)


def flip(x, axis, bits):
    return lax.ppermute(x, axis, [(k, k ^ bits) for k in range(lax.axis_size(axis))])


def chain_step(x, steps, backward):
    n = lax.axis_size("seq")
    hop = -2 * steps if backward else 2 * steps
    return lax.ppermute(x, "seq", [(k, k + hop) for k in range(n) if 0 <= k + hop < n])


def chain(value, decay, backward):
    entered = chain_step(value, 1, backward)
    count = lax.axis_size("seq") // 2
    if count > 2:
        rate = chain_step(decay, 1, backward)
        total = entered.astype(f32)
        steps = 1
        while steps < count - 1:
            total = total + rate[0:1] * chain_step(total.astype(bf16), steps, backward).astype(f32)
            rate = rate * chain_step(rate, steps, backward)
            steps *= 2
        entered = total.astype(bf16)
    return entered


def gather_rows(x):
    n = lax.axis_size("seq")
    if n != 4:
        return [lax.all_gather(x, "seq", axis=0, tiled=True)]
    return [x, *[flip(x, "seq", k) for k in (1, 2, 3)]]


def gather_near(x):
    if lax.axis_size("seq") != 4:
        return gather_rows(x)
    return [x, flip(x, "seq", 1), flip(x, "seq", 2)]


def gather_across(parts, *release):
    if len(parts) == 1:
        return parts
    x, gx, gy = parts
    gx, gy, *_ = lax.optimization_barrier((gx, gy, *release))
    half = x.shape[0] // 2
    return [x, gx, gy, flip(gx[:half], "seq", 2), flip(gy[half:], "seq", 1)]


def k_sum(count, *refs):
    *blocks, keep_ref, give_ref = refs
    need()
    odd = lax.rem(lax.axis_index("dp"), 2)
    half = keep_ref.shape[0]
    for dst, start in ((give_ref, (1 - odd) * half), (keep_ref, odd * half)):

        def rows(r, dst=dst, start=start):
            s = pl.ds(pl.multiple_of(start + r * 16, 16), 16)
            first = 0
            for k in range(count):
                total = 0.0
                for ref in blocks[k * len(blocks) // count : (k + 1) * len(blocks) // count]:
                    total = total + ref[s, :].astype(f32)
                dst[at(r, 16), first : first + total.shape[1]] = total.astype(dst.dtype)
                first += total.shape[1]

        loop(half // 16, rows)
        done(dst)


def k_add(a_ref, b_ref, out_ref):
    need()

    def rows(r):
        s = at(r, 16)
        out_ref[s, :] = (a_ref[s, :].astype(f32) + b_ref[s, :].astype(f32)).astype(bf16)

    loop(out_ref.shape[0] // 16, rows)


def send_blocks(blocks):
    if len(blocks) > 1:
        return [blocks[0]] + [flip(blocks[k], "seq", k) for k in (3, 2, 1)]
    return [lax.psum_scatter(blocks[0], "seq", scatter_dimension=0, tiled=True)]


def halved(groups, *pins):
    got = [b for group in groups for b in group]
    rows, width = got[0].shape[0], sum(group[0].shape[1] for group in groups)
    shape = (rows // 2, width)
    return run(
        functools.partial(k_sum, len(groups)), "sum", [(shape, f32, "a"), (shape, bf16, "a")],
        after(got[0], *pins), *got[1:],
    )


def paired(mine, got, *pins):
    return run(k_add, "add", [(got.shape, bf16, "a")], after(mine, *pins), got)[0]


def over_dp(keep, got, *pins):
    mine = paired(keep, got, *pins)
    bit = 2
    while bit < lax.axis_size("dp"):
        mine = paired(mine, flip(mine, "dp", bit))
        bit *= 2
    return mine, flip(mine, "dp", 1)


def simple_dp():
    n = lax.axis_size("dp")
    return n == 1 or n & (n - 1) != 0


def summed_dp(keep, give, *pins):
    if not simple_dp():
        return over_dp(keep, flip(give, "dp", 1), *pins)
    odd = lax.axis_index("dp") % 2 == 1
    keep = keep.astype(bf16)
    low, high = jnp.where(odd, give, keep), jnp.where(odd, keep, give)
    low, high = lax.psum((low, high), "dp")
    return jnp.where(odd, high, low), jnp.where(odd, low, high)


def sum_small(x):
    for axis in ("seq", "dp"):
        n = lax.axis_size(axis)
        if n == 4:
            a, b, c = [flip(x, axis, k) for k in (1, 2, 3)]
            x = (x + a) + (b + c)
        elif n & (n - 1):
            x = lax.psum(x, axis)
        else:
            bit = 1
            while bit < n:
                x = x + flip(x, axis, bit)
                bit *= 2
    return x


def after(x, *others):
    return lax.optimization_barrier((x, *others))[0]


AHEAD = ["xdt", "cum", "bc", "c"], ["act", "xb"], ["wz", "wx"]
AHEAD_NORM = ["wo", "y", "yw", "z", "act"]


def on_device(hidden_in, cotangent, norm_gain, in_weight, conv_weight, conv_bias, dt_bias, a_log, skip, gate_gain, out_weight):
    core = lax.axis_index("section")
    first = core == 0
    odd = lax.axis_index("seq") % 2
    even = odd == 0
    length = hidden_in.shape[1]
    t = 2 * length
    n = lax.axis_size("seq")
    shard = in_weight.shape[1]
    half = WIDTH // 2
    packed = XD + 2 * OWN

    def given(x):
        return lax.dynamic_index_in_dim(x, 1 - odd, 0, keepdims=False)

    def both_sequences(mine, give):
        got = flip(give, "seq", 1)
        return jnp.stack([jnp.where(even, mine, got), jnp.where(even, got, mine)])

    mine_w, give_w, mine_p, give_p = run(
        k_prep, "prep",
        [((shard, packed), bf16, "v"), ((shard, packed), bf16, "a"), ((PARAMS, XC), f32, "v"), ((PARAMS, XC), f32, "a")],
        *[
            far_away(a)
            for a in (in_weight[0], out_weight[0], norm_gain, conv_weight[0], conv_bias, dt_bias, a_log, skip, gate_gain)
        ],
    )
    x0, zo0, x1, zo1, par0, par1 = run(
        k_pick, "pick",
        [((shard, XD), bf16, "a"), ((shard, 2 * OWN), bf16, "a"), ((shard, XD), bf16, "a"),
         ((shard, 2 * OWN), bf16, "a"), ((PARAMS, XC), f32), ((PARAMS, XC), f32)],
        mine_w, across(give_w), mine_p, across(give_p),
    )
    params = [par0, par1]

    def half_given(x):
        return lax.dynamic_slice_in_dim(given(x), core * (length // 2), length // 2, 0)

    def both_halves(mine):
        got = flip(mine, "seq", 1)
        return got, across(got)

    ga, gb = both_halves(half_given(hidden_in))
    give_cot = half_given(cotangent)
    parts_x0 = gather_rows(after(x0, ga, give_cot))
    near_zo0 = gather_near(after(zo0, *parts_x0))

    saved = [{}, {}]

    def keeping(layer, soon):
        return "vh" if soon else "h"

    def named(layer, names, results, modes):
        soon, at_result = {}, 0
        for name, mode in zip(names, modes):
            for m in mode:
                value = results[at_result]
                at_result += 1
                if m != "h":
                    soon[name] = value
                if m == mode[-1]:
                    saved[layer][name] = value
        return soon

    def scan_part(layer, x, tail, zo_parts, before_front):
        par = params[layer]
        soon, last = keeping(layer, True), keeping(layer, False)
        before = chain_step(tail, 1, False)
        saved[layer]["before"] = before
        modes = [soon, soon, soon, last, soon, "v", soon, "a"]
        shapes = [((t, XC), f32), ((t, 2 * STATE), bf16), ((t, OWN), bf16), ((t, 128), f32), ((t, 128), f32),
                  ((2 * STATE, OWN), f32), ((16, OWN), f32), ((STATE, OWN), bf16)]
        x |= named(
            layer, ["act", "bc", "xdt", "dt", "cum", "s", "dec", "tot"],
            run(
                k_front, "front", [(*shape, m) for shape, m in zip(shapes, modes)],
                x["xb"], after(before, *before_front), par, scratch=[((t, OWN), f32), ((16, XC), f32)],
            ),
            modes,
        )
        dec = saved[layer]["dec"]
        saved[layer]["decay"] = dec[:8] * dec[8:] if n > 4 else None
        entered = chain(x["tot"], saved[layer]["decay"], False)
        x |= named(
            layer, ["yw"],
            run(
                k_within, "within", [((t, OWN), f32, soon)], x["cum"], x["bc"], x["xdt"],
                scratch=[((t, HEADS * 128), f32), ((t // 128, HEADS * 8, 128), f32), ((t, BLOCK), f32)],
            ),
            [soon],
        )
        parts_zo, next_near = zo_parts(entered)
        modes = ["vh", "h", "v", "p"]
        x |= named(
            layer, ["z", "wz", "keep", "give"],
            run(
                k_z, "gate_in",
                [((t, OWN), f32, modes[0]), ((WIDTH, OWN), bf16, modes[1]), ((WIDTH // 2, OWN), bf16, "v"),
                 ((WIDTH // 2, OWN), bf16, "p")],
                near(after(x["normed"], x["yw"], entered)), *parts_zo, scratch=[((WIDTH, OWN), bf16)],
            ),
            modes,
        )
        ogot = across(x["give"])
        cot_halves = [ca, cb] if layer else []
        ins = [x["yw"], x["act"], x["bc"], x["cum"], entered, x["s"], x["dec"], x["z"], par, x["keep"], ogot]
        modes = [last, "h" if layer else "v", "p", "vh" if layer else "v", last, last] + ["vh"] * layer
        shapes = [((t, OWN), f32), ((t, WIDTH), f32), ((t, half + 128 if layer else WIDTH + 128), bf16),
                  ((t, 256 if layer else 128), f32), ((2 * STATE, OWN), f32), ((OWN, WIDTH), bf16)]
        shapes += [((t, WIDTH), bf16)] * layer
        results = run(
            functools.partial(k_out, layer == 0), "out", [(*shape, m) for shape, m in zip(shapes, modes)],
            *ins, *([cotangent, *cot_halves] if layer else []), scratch=[((t, OWN), f32), ((t, OWN), bf16)],
            ahead=[] if layer else [saved[0]["h"]],
        )
        x |= named(layer, ["y", "p", "msg", "st", "c", "wo", "g"][: len(modes)], results, modes)
        if layer == 0:
            x["h"] = results[-1]
        return x

    outs_in = [((t, WIDTH), bf16), ((t + 8, XD), f32), ((WIDTH, XD), bf16), ((8, XC), f32)]
    names_in = ["normed", "xb", "wx", "tail"]
    modes = ["h", "vh", "vh", "h", "a"]
    shapes = [((t, WIDTH), bf16), *outs_in]
    x = named(
        0, ["h", *names_in],
        run(k_in, "project", [(*shape, m) for shape, m in zip(shapes, modes)], hidden_in, ga, gb, par0, *parts_x0),
        modes,
    )
    next_x = []

    def zo_parts_0(entered):
        next_x.extend(gather_near(after(x1, entered)))
        return gather_across(near_zo0, tail0), next_x[1:]

    tail0 = x["tail"]
    x = scan_part(0, x, tail0, zo_parts_0, [])
    parts_x1 = gather_across(next_x)
    near_zo1 = gather_near(after(zo1, *parts_x1))
    modes = ["h", "h", "h", "vh", "vh", "h", "a"]
    shapes = [((t, WIDTH), bf16), ((t, WIDTH), f32), ((t, 128), f32), *outs_in]
    x = named(
        1, ["h", "pt", "rs", *names_in],
        run(
            k_mid, "middle", [(*shape, m) for shape, m in zip(shapes, modes)],
            x["h"], x["p"], x["st"], across(x["msg"]), par1, *parts_x1,
        ),
        modes,
    )
    h1_far, pt, rs0 = saved[1]["h"], saved[1]["pt"], saved[1]["rs"]
    tail1 = x["tail"]
    ca, cb = both_halves(after(give_cot, tail1))
    x = scan_part(1, x, x["tail"], lambda entered: (gather_across(near_zo1, tail1), []), near_zo1[1:])
    p1, st1, st1_far = saved[1]["p"], x["st"], saved[1]["st"]
    msg = across(x["msg"])
    count = 4 if n == 4 else 1

    ahead_zw, ahead_within, ahead_front = AHEAD

    def backward(layer, v, g, rs, rd, before_within=(), beside=None):
        par = params[layer]
        v = dict(v)
        far = dict(v)

        def fetched(names, results):
            if names:
                v.update(zip(names, results[-len(names) :]))

        qz, dy, df, dca, okeep, ogive, d, e, small_a = run(
            kb_gate, "back_gate",
            [((t, OWN), bf16, "v"), ((t, OWN), f32, "v"), ((t, OWN), bf16, "v"), ((t, 128), f32, "v"),
             ((OWN, half), bf16, "v"), ((OWN, half), bf16, "p"), ((2 * STATE, OWN), f32, "v"),
             ((STATE, OWN), bf16, "a"), ((16, OWN), f32)],
            g, v["wo"], v["y"], v["yw"], v["z"], v["act"], v["bc"], v["cum"], rs, rd, par, v["dec"],
            scratch=[((t, OWN), f32), ((t, OWN), f32), ((t, OWN), bf16)],
        )
        entered = chain(e, v["decay"], True)
        ogot = across(ogive)
        results = run(
            kb_z_weight, "back_zw", [((WIDTH // count, 2 * OWN), bf16, "a")] * count, v["normed"], qz, okeep,
            ogot,
            scratch=[((WIDTH, 2 * OWN), bf16)], ahead=[v[k] for k in ahead_zw],
        )
        zo = list(results[:count])
        beside_zw = [*zo]
        zo = [after(b, entered) for b in zo]
        fetched(ahead_zw, results)
        v["act"] = far["act"]
        dy = near(after(dy, *beside_zw, *before_within))
        results = run(
            kb_within, "back_within", [((t, OWN), f32, "v"), ((t, 2 * STATE), f32, "v")],
            dy, v["xdt"], v["cum"], v["bc"], df, v["c"],
            scratch=[((t, HEADS * 128), f32), ((t // 128, HEADS * 8, 128), f32), ((t, BLOCK), f32), ((t, BLOCK), f32)],
            ahead=[v[k] for k in ahead_within],
        )
        dxw, dbc = results[:2]
        fetched(ahead_within, results)
        results = run(
            kb_front, "back_front",
            [((t + 8, XC), f32, "v"), ((8, XC), f32, "a"), ((t, 128), bf16, "v"), ((40, XC), f32), ((16, 128), f32)],
            entered, d, far["c"], far["dec"], far["bc"], far["xdt"], v["act"], v["xb"], after(v["before"], *(beside() if beside else [])), far["dt"], far["cum"],
            dxw, dbc, dy, dca, par,
            scratch=[((2 * STATE, OWN), f32), ((t, OWN), f32), ((t, OWN), f32), ((t, OWN), f32), ((t, XC), f32),
                     ((t, 128), f32), ((t, 128), f32), ((16, OWN), f32), ((t + 16, 128), f32), ((16, XC), f32)],
            ahead=[v[k] for k in ahead_front],
        )
        dxb, halo, qdt, small_b, small_c = results[:5]
        fetched(ahead_front, results)
        ret = chain_step(halo, 1, True)
        dnz = run(kb_z_normed, "back_z", [((t, WIDTH), f32, "v")], near(after(qz, halo)), v["wz"])[0]
        return dxb, ret, qdt, dnz, zo, (small_a, small_b, small_c), v, (e, dbc, halo)

    shape_q, shape_n = ((t, XD), bf16, "v"), [((t, WIDTH), f32, "v"), ((t, WIDTH), bf16, "p")]
    x_blocks = [((WIDTH // count, XD), bf16, "a")] * count
    x_scratch = [((WIDTH, XD), bf16)]
    dxb, ret, qdt, dnz, zo1, small1, v1, _ = backward(1, saved[1], x["g"], st1, msg)
    got_zo1 = send_blocks(zo1)
    v0 = saved[0]
    early = []
    q, dn, dnb1, *fetched = run(
        kb_x_normed, "back_x", [shape_q, *shape_n], dxb, ret, qdt, dnz, v1["wx"], ahead=[v0[k] for k in early]
    )
    v0.update(zip(early, fetched))
    dr = across(dnb1)
    x1 = run(kb_x_weight, "back_xw", x_blocks, v1["normed"], near(after(q, *dnb1)), scratch=x_scratch)
    got_x1 = send_blocks(x1)
    halves1 = halved([got_x1, got_zo1])
    early = AHEAD_NORM
    g0, g0_far, small_d1, rd0, *fetched = run(
        kb_norm, "back_norm", [((t, WIDTH), bf16, "vh"), ((8, WIDTH), f32), ((t, 128), f32, "v")],
        h1_far, dn, after(dr, *x1, *got_zo1), saved[1]["g"], par1, pt, ahead=[v0[k] for k in early],
    )
    v0.update(zip(early, fetched))
    dxb, ret, qdt, dnz, zo0, small0, v0, (e0, dbc0, halo0) = backward(
        0, v0, g0, rs0, rd0, got_x1[1:], lambda: halves1
    )
    got_zo0 = send_blocks(zo0)
    over1 = [] if simple_dp() else [flip(halves1[1], "dp", 1)]
    q, *x0 = run(kb_x_weight_first, "back_xw", [shape_q] + x_blocks, v0["normed"], dxb, after(ret, *over1, *got_zo0), qdt, scratch=x_scratch)
    got_x0 = send_blocks(x0)
    dn, dnb0 = run(kb_x_normed_last, "back_x", shape_n, near(after(q, *x0)), dnz, v0["wx"])
    dr = across(dnb0)
    sum1 = over_dp(halves1[0], over1[0], x0[0]) if over1 else summed_dp(*halves1)
    sum_zo0 = summed_dp(*halved([got_zo0], x0[0]))
    sum_x0 = summed_dp(*halved([got_x0]))
    sums = [*sum1, *sum_zo0, *sum_x0]
    final = run(
        k_final, "final", [((length, half), bf16, "a"), ((length, half), bf16, "a")],
        h1_far, p1, st1_far, after(msg, *dnb0),
    )
    hidden_out = both_sequences(*final)
    keep, give, small_d0 = run(
        kb_norm_last, "back_norm", [((length, half), bf16, "a"), ((length, half), bf16, "a"), ((8, WIDTH), f32)],
        saved[0]["h"], dn, dr, g0_far, par0, scratch=[((t, WIDTH), bf16)],
    )
    grad_in = both_sequences(keep, give)
    small = run(k_small, "small", [((2 * SMALL, XC), f32, "a")], *small0, small_d0, *small1, small_d1)[0]
    small = sum_small(small)
    heads = 2 * HEADS
    smalls = run(
        k_small_out, "small_out",
        [((1, WIDTH), f32, "a"), ((4, CONV), f32, "a"), ((1, CONV), f32, "a"), ((1, heads), f32, "a"), ((1, heads), f32, "a"), ((1, heads), f32, "a"),
         ((1, INNER), f32, "a")],
        small, across(small),
    )
    give = run(k_home, "home", [((shard, packed), bf16, "a")], *sums, scratch=[((shard, 2 * OWN), bf16), ((shard, XD), bf16)])[0]
    grad_w, grad_o = run(
        k_grads, "grads", [((shard, INNER + CONV + heads), f32, "a"), ((2 * shard, WIDTH), f32, "a")],
        *sums, across(give),
        scratch=[((shard, packed), bf16), ((shard, 2 * OWN), bf16), ((shard, XD), bf16)],
    )
    norm, taps, bias, dtb, rates, skips, gates = smalls
    return (hidden_out, grad_in, norm, grad_w[None], taps[None], bias, dtb, rates, skips, gates, grad_o[None])


def solution(mesh):
    by_section = P("section", None)
    rows = P("section", "seq", None)
    tokens = P("dp", "seq", None)
    taps = P("section", None, None)
    out = P("dp", "seq", "section")
    small = (by_section,) * 4
    return jax.shard_map(
        on_device,
        mesh=mesh,
        in_specs=(tokens, tokens, by_section, rows, taps, by_section, *small, rows),
        out_specs=(out, out, by_section, rows, taps, by_section, *small, rows),
        check_vma=False,
    )
```

```python
import functools

import jax
import jax.numpy as jnp
from jax import lax
from jax.experimental import pallas as pl
from jax.experimental.pallas import tpu as pltpu
from jax.sharding import PartitionSpec as P

HDIM = 64
STATE = 128
INNER = 1536
CONV = 1792
EPS = 1e-05
f32, bf16 = jnp.float32, jnp.bfloat16

WIDTH = 768
OWN = 768
HEADS = 12
XC = OWN + 2 * STATE
XD = XC + 128
R = 64
BLOCK = 256


def nn(a, b):
    return lax.dot_general(a, b, (((1,), (0,)), ((), ())), preferred_element_type=f32)


def nt(a, b):
    return lax.dot_general(a, b, (((1,), (1,)), ((), ())), preferred_element_type=f32)


def tn(a, b):
    return lax.dot_general(a, b, (((0,), (0,)), ((), ())), preferred_element_type=f32)


def loop(count, body):
    def step(k, carry):
        body(k)
        return carry

    lax.fori_loop(0, count, step, 0)


def at(k, size):
    return pl.ds(pl.multiple_of(k * size, size), size)


def iotas(shape):
    return lax.broadcasted_iota(jnp.int32, shape, 0), lax.broadcasted_iota(jnp.int32, shape, 1)


def spread_matrix(width, per):
    r, c = iotas((128, width))
    return jnp.where(((r & 15) == c // per) & (r < 48), 1.0, 0.0).astype(bf16)


def collect_matrix():
    r, c = iotas((OWN, 128))
    return jnp.where(((c & 15) == r // HDIM) & (c < 48), 1.0, 0.0).astype(bf16)


def thirds(v):
    high = v.astype(bf16).astype(f32)
    rest = v - high
    mid = rest.astype(bf16).astype(f32)
    lane = iotas(v.shape)[1]
    out = jnp.where(lane < 16, high, jnp.where(lane < 32, mid, rest - mid))
    return jnp.where(lane < 48, out, 0.0).astype(bf16)


def halves(v):
    high = v.astype(bf16)
    return high, (v - high.astype(f32)).astype(bf16)


def running_sum(v, backward=False):
    r, c = iotas((BLOCK, BLOCK))
    tri = jnp.where((c >= r) if backward else (r >= c), 1.0, 0.0).astype(bf16)
    high = v.astype(bf16)
    rest = v - high.astype(f32)
    mid = rest.astype(bf16)
    last = (rest - mid.astype(f32)).astype(bf16)
    return nn(tri, high) + nn(tri, mid) + nn(tri, last)


def sig(v):
    return 0.5 * jnp.tanh(0.5 * v) + 0.5


def softplus(v):
    e = jnp.exp(-jnp.abs(v))
    u = 1.0 + e
    small = u == 1.0
    return jnp.maximum(v, 0.0) + jnp.where(small, e, jnp.log(u) * e / jnp.where(small, 1.0, u - 1.0))


def fold(v):
    return jnp.sum(v.reshape(v.shape[0] // 8, 8, v.shape[1]), axis=0)


def copy_rows(dst, start, src, cols=None):
    rows = src.shape[0]
    step = next(k for k in (48, 32, 16, 8, rows) if rows % k == 0)

    def move(r):
        place = pl.ds(pl.multiple_of(start + r * step, 16), step)
        if cols is None:
            dst[place, :] = src[at(r, step), :]
        else:
            dst[place, :] = src[at(r, step), cols]

    loop(rows // step, move)


def place_rows(dst, parts, cols=None):
    if len(parts) == 1:
        return copy_rows(dst, 0, parts[0], cols)
    me = lax.axis_index("seq")
    rows = parts[0].shape[0]
    for k in range(min(len(parts), 4)):
        copy_rows(dst, (me ^ k) * rows, parts[k], cols)
    if len(parts) > 4:
        copy_rows(dst, (me ^ 3) * rows + rows // 2, parts[4], cols)


def on_core(body):
    me = lax.axis_index("section")
    for core in range(2):
        pl.when(me == core)(lambda core=core: body(core))


def exact(a, b):
    return lax.dot_general(
        a, b, (((1,), (0,)), ((), ())), preferred_element_type=f32, precision=lax.Precision.HIGHEST
    )


def stats_out(a, b):
    lane = iotas(a.shape)[1]
    v = jnp.where(lane < 64, a, b)
    high = v.astype(bf16).astype(f32)
    rest = v - high
    mid = rest.astype(bf16).astype(f32)
    l = lane & 63
    out = jnp.where(l < 16, high, jnp.where(l < 32, mid, rest - mid))
    return jnp.where(l < 48, out, 0.0).astype(bf16)


def stats_in(v):
    v = v.astype(f32)
    lane = iotas(v.shape)[1]
    a = jnp.sum(jnp.where(lane < 64, v, 0.0), axis=1, keepdims=True)
    b = jnp.sum(jnp.where(lane < 64, 0.0, v), axis=1, keepdims=True)
    return a * (1.0 / 16), b * (1.0 / 16)


class Copies:

    def __init__(self, pairs_in, pairs_ahead, pairs_out, sems_in, sems_out):
        self.waiting, self.ready, self.started, self.ahead = {}, {}, [], []
        for k, (far, near, whole) in enumerate(pairs_in):
            copy = pltpu.make_async_copy(far, near, sems_in.at[k])
            copy.start()
            self.waiting.setdefault(id(whole), []).append(copy)
        for k, (far, near) in enumerate(pairs_ahead):
            copy = pltpu.make_async_copy(far, near, sems_in.at[len(pairs_in) + k])
            copy.start()
            self.ahead.append(copy)
        for k, (far, near, whole) in enumerate(pairs_out):
            self.ready.setdefault(id(whole), []).append(pltpu.make_async_copy(near, far, sems_out.at[k]))

    def need(self, refs):
        for key in [id(r) for r in refs] if refs else list(self.waiting):
            for copy in self.waiting.pop(key, ()):
                copy.wait()

    def done(self, refs):
        for key in [id(r) for r in refs] if refs else list(self.ready):
            for copy in self.ready.pop(key, ()):
                copy.start()
                self.started.append(copy)


COPIES = []


def need(*refs):
    COPIES[-1].need(refs)


def done(*refs):
    COPIES[-1].done(refs)


FAR = []
NEAR = []


def near(*arrays):
    NEAR.extend(arrays)
    return arrays if len(arrays) > 1 else arrays[0]


def far_away(array):
    FAR.append(array)
    return array


def run(kernel, name, outs, *ins, scratch=(), ahead=()):
    far, close = pl.BlockSpec(memory_space=pltpu.HBM), pl.BlockSpec(memory_space=pltpu.VMEM)
    loose = pl.BlockSpec(memory_space=pl.ANY)
    modes = [o[2] if len(o) > 2 else "h" for o in outs]
    units = [m for mode in modes for m in mode] + ["v"] * len(ahead)
    shapes, specs = [], []
    for (shape, dtype, *_), mode in zip(outs, modes):
        for m in mode:
            if m == "p":
                shapes += [jax.ShapeDtypeStruct((shape[0] // 2, *shape[1:]), dtype)] * 2
                specs += [loose] * 2
            else:
                space = dict(v=pltpu.VMEM, h=pltpu.HBM, a=jax.ShapeDtypeStruct)[m]
                shapes.append(space(shape, dtype))
                specs.append(dict(v=close, h=far, a=loose)[m])
    for a in ahead:
        shapes.append(pltpu.VMEM(a.shape, a.dtype))
        specs.append(close)
    groups = [a if isinstance(a, (tuple, list)) else (a,) for a in (*ins, *ahead)]
    flat = [a for group in groups for a in group]
    held = [any(a is k for k in NEAR) for a in flat]
    kept = [any(a is k for k in FAR) for a in flat]
    flat = [
        pltpu.with_memory_space_constraint(a, pltpu.VMEM if h else pltpu.HBM) if h or k else a
        for a, h, k in zip(flat, held, kept)
    ]
    n_in, n_out, n_own = len(flat), len(shapes), sum(len(group) for group in groups[: len(ins)])
    buffers = [
        pltpu.VMEM((sum(a.shape[0] for a in group), *group[0].shape[1:]), group[0].dtype)
        for group in groups[: len(ins)]
        if not any(group[0] is k for k in NEAR)
    ]
    buffers += [pltpu.VMEM(shape, dtype) for (shape, dtype, *_), mode in zip(outs, modes) if "v" not in mode]

    def body(*refs):
        given, made, rest = list(refs[:n_in]), list(refs[n_in : n_in + n_out]), list(refs[n_in + n_out :])
        pairs_in, pairs_out, vin, vout = [], [], [], []
        pairs_ahead = list(zip(given[n_own:], made[n_out - len(ahead) :])) if ahead else []
        at_ref = 0
        for group in groups[: len(ins)]:
            if held[at_ref]:
                vin.append(given[at_ref])
            else:
                vin.append(rest.pop(0))
                start = 0
                for k, part in enumerate(group):
                    rows = part.shape[0]
                    place = vin[-1] if len(group) == 1 else vin[-1].at[pl.ds(start, rows)]
                    pairs_in.append((given[at_ref + k], place, vin[-1]))
                    start += rows
            at_ref += len(group)
        for mode in modes:
            vout.append(made.pop(0) if "v" in mode else rest.pop(0))
            if mode == "p":
                rows = vout[-1].shape[0] // 2
                for k in range(2):
                    pairs_out.append((made.pop(0), vout[-1].at[pl.ds(k * rows, rows)], vout[-1]))
            elif mode != "v":
                pairs_out.append((made.pop(0), vout[-1], vout[-1]))
        *extra, sems_in, sems_out = rest
        copies = Copies(pairs_in, pairs_ahead, pairs_out, sems_in, sems_out)
        COPIES.append(copies)
        kernel(*vin, *vout, *extra)
        need()
        done()
        for copy in [*copies.ahead, *copies.started]:
            copy.wait()
        COPIES.pop()

    results = list(
        pl.pallas_call(
            body,
            name=name,
            out_shape=shapes,
            in_specs=[close if h else far if k else loose for h, k in zip(held, kept)],
            out_specs=specs,
            scratch_shapes=[
                *buffers,
                *[pltpu.VMEM(s, d) for s, d in scratch],
                pltpu.SemaphoreType.DMA((max(n_in, 1),)),
                pltpu.SemaphoreType.DMA((max(n_out, 1),)),
            ],
            compiler_params=pltpu.CompilerParams(vmem_limit_bytes=MIB * 2**20),
            cost_estimate=pl.CostEstimate(flops=1, bytes_accessed=1, transcendentals=0),
        )(*flat)
    )
    grouped = []
    for unit in units:
        if unit == "p":
            grouped.append((results.pop(0), results.pop(0)))
            continue
        grouped.append(results.pop(0))
        if unit != "a":
            (NEAR if unit == "v" else FAR).append(grouped[-1])
    return grouped


MIB = 24


TAPS, BIAS, NORM, GATE, SKIP, STEP, RATE = 0, 4, 5, 6, 7, 8, 9
PARAMS = 16


def k_prep(w_ref, o_ref, ng_ref, cw_ref, cb_ref, db_ref, al_ref, sk_ref, gg_ref, mine_w, give_w, mine_p, give_p):
    need()
    rows = w_ref.shape[0]
    half = WIDTH // 2
    r24, c24 = iotas((2 * HEADS, 128))
    rk, ck = iotas((2 * HEADS, OWN))

    def pack(core, out, par):
        own = core * OWN
        out[:, 0:OWN] = w_ref[:, INNER + own : INNER + own + OWN]
        out[:, OWN:XC] = w_ref[:, 2 * INNER : 2 * INNER + 2 * STATE]
        pick = ((c24 & 15) == r24 - core * HEADS) & (c24 < 48)
        steps = w_ref[:, INNER + CONV : INNER + CONV + 2 * HEADS]
        out[:, XC:XD] = nn(steps, jnp.where(pick, 1.0, 0.0).astype(bf16)).astype(bf16)
        out[:, XD : XD + OWN] = w_ref[:, own : own + OWN]
        for t in range(2):
            at_lane = XD + OWN + t * half
            out[:, at_lane : at_lane + half] = o_ref[t * rows : (t + 1) * rows, core * half : (core + 1) * half]
        par[...] = jnp.zeros(par.shape, f32)
        par[TAPS : TAPS + 4, :OWN] = cw_ref[:, own : own + OWN]
        par[TAPS : TAPS + 4, OWN:] = cw_ref[:, INNER:]
        par[BIAS : BIAS + 1, :OWN] = cb_ref[:, own : own + OWN]
        par[BIAS : BIAS + 1, OWN:] = cb_ref[:, INNER:]
        par[NORM : NORM + 1, :WIDTH] = ng_ref[...]
        par[GATE : GATE + 1, :OWN] = gg_ref[:, own : own + OWN]
        spread = jnp.where(rk - core * HEADS == ck // HDIM, 1.0, 0.0)
        par[SKIP : SKIP + 1, :OWN] = exact(jnp.broadcast_to(sk_ref[...], (8, 2 * HEADS)), spread)[0:1]
        lanes = jnp.where(pick, 1.0, 0.0)
        par[STEP : STEP + 1, 0:128] = exact(jnp.broadcast_to(db_ref[...], (8, 2 * HEADS)), lanes)[0:1]
        par[RATE : RATE + 1, 0:128] = exact(jnp.broadcast_to(al_ref[...], (8, 2 * HEADS)), lanes)[0:1]

    def body(core):
        pack(core, mine_w, mine_p)
        pack(1 - core, give_w, give_p)

    on_core(body)


def k_pick(mine_w, got_w, mine_p, got_p, x0, zo0, x1, zo1, p0, p1):
    need()

    def body(core):
        pairs = ((mine_w, mine_p), (got_w, got_p))
        for layer, (x, zo, p) in enumerate(((x0, zo0, p0), (x1, zo1, p1))):
            w, par = pairs[layer ^ core]
            x[...] = w[:, 0:XD]
            zo[...] = w[:, XD:]
            p[...] = par[...]

    on_core(body)


def norm_rows(h, gain):
    scale = lax.rsqrt(jnp.mean(h * h, axis=1, keepdims=True) + EPS)
    return (h * scale * gain).astype(bf16)


def project(t, normed_ref, wx_ref, xb_ref, tail_ref):
    xb_ref[0:8, :] = jnp.zeros((8, XD), f32)

    def cols(c):
        xb_ref[8 : 8 + t, at(c, 384)] = nn(normed_ref[...], wx_ref[:, at(c, 384)])

    loop(XD // 384, cols)
    tail_ref[...] = xb_ref[t:, :XC]


def k_in(hid_ref, ga_ref, gb_ref, par_ref, *rest):
    *parts, h_ref, normed_ref, xb_ref, wx_ref, tail_ref = rest
    need(hid_ref, ga_ref, gb_ref, par_ref)
    t = h_ref.shape[0]
    half = t // 2
    odd = lax.rem(lax.axis_index("seq"), 2)
    core = lax.axis_index("section")
    copy_rows(h_ref, odd * half, hid_ref.at[odd])
    copy_rows(h_ref, (1 - odd) * half + core * (half // 2), ga_ref)
    copy_rows(h_ref, (1 - odd) * half + (1 - core) * (half // 2), gb_ref)

    def rows(r):
        normed_ref[at(r, R), :] = norm_rows(h_ref[at(r, R), :].astype(f32), par_ref[NORM : NORM + 1, :WIDTH])

    loop(t // R, rows)
    done(h_ref, normed_ref)
    need(*parts)
    place_rows(wx_ref, parts)
    done(wx_ref)
    project(t, normed_ref, wx_ref, xb_ref, tail_ref)


def k_mid(h_ref, p_ref, st_ref, msg_ref, par_ref, *rest):
    *parts, h1_ref, pt_ref, rs_ref, normed_ref, xb_ref, wx_ref, tail_ref = rest
    need(h_ref, p_ref, st_ref, msg_ref, par_ref)
    t = h_ref.shape[0]

    def rows(r):
        s = at(r, R)
        other = stats_in(msg_ref[s, WIDTH:])[0]
        rs = lax.rsqrt((st_ref[s, 0:128] + other) * (1.0 / INNER) + EPS)
        rs_ref[s, :] = rs
        p = p_ref[s, :] + msg_ref[s, :WIDTH].astype(f32)
        pt_ref[s, :] = p
        h1 = (h_ref[s, :].astype(f32) + rs[:, 0:1] * p).astype(bf16)
        h1_ref[s, :] = h1
        normed_ref[s, :] = norm_rows(h1.astype(f32), par_ref[NORM : NORM + 1, :WIDTH])

    loop(t // R, rows)
    done(h1_ref, pt_ref, rs_ref, normed_ref)
    need(*parts)
    place_rows(wx_ref, parts)
    done(wx_ref)
    project(t, normed_ref, wx_ref, xb_ref, tail_ref)


def k_z(normed_ref, *rest):
    *parts, z_ref, wz_ref, keep_ref, give_ref, o = rest
    need(*parts)
    place_rows(wz_ref, parts, slice(0, OWN))
    done(wz_ref)
    place_rows(o, parts, slice(OWN, 2 * OWN))

    def split(core):
        rows = keep_ref.shape[0]
        keep_ref[...] = o[core * rows : (core + 1) * rows, :]
        give_ref[...] = o[(1 - core) * rows : (2 - core) * rows, :]

    on_core(split)
    done(keep_ref, give_ref)
    need(normed_ref)

    def cols(c):
        z_ref[:, at(c, 384)] = nn(normed_ref[...], wz_ref[:, at(c, 384)])

    loop(OWN // 384, cols)


def k_front(xb_ref, before_ref, par_ref, act_ref, slope_ref, bc_ref, xdt_ref, dt_ref, cum_ref, s_ref, dec_ref, tot_ref, wide, edge):
    t = act_ref.shape[0]
    need()
    edge[0:8, :] = before_ref[...]
    edge[8:16, :] = jnp.zeros((8, XC), f32)

    def conv(c):
        cols = at(c, 128)
        w = par_ref[0:8, cols]
        total = w[4:5] + w[0:1] * xb_ref[pl.ds(5, t), cols]
        for k in range(1, 4):
            total = total + w[k : k + 1] * xb_ref[pl.ds(5 + k, t), cols]
        first = total[0:8]
        for k in range(4):
            first = first + w[k : k + 1] * edge[5 + k : 13 + k, cols]
        total = jnp.concatenate([first, total[8:]], axis=0)
        sg = sig(total)
        act = total * sg
        act_ref[:, cols] = act
        slope_ref[:, cols] = (sg + act * (1.0 - sg)).astype(bf16)

    loop(XC // 128, conv)
    bc_ref[...] = act_ref[:, OWN:].astype(bf16)
    done(act_ref, slope_ref, bc_ref)
    dt = softplus(xb_ref[8 : 8 + t, XC:] + par_ref[STEP : STEP + 1, 0:128])
    dt_ref[...] = dt
    done(dt_ref)
    rate = -jnp.exp(par_ref[RATE : RATE + 1, 0:128])
    spread = spread_matrix(OWN, HDIM)
    wide[...] = nn(thirds(dt), spread)

    def rows(r):
        s = at(r, R)
        xdt_ref[s, :] = (act_ref[s, :OWN] * wide[s, :]).astype(bf16)

    loop(t // R, rows)
    done(xdt_ref)
    for b in range(t // BLOCK):
        s = pl.ds(b * BLOCK, BLOCK)
        cum = running_sum(rate * dt[b * BLOCK : (b + 1) * BLOCK])
        cum_ref[s, :] = cum
        end = cum[BLOCK - 1 : BLOCK, :]
        dec_ref[8 * b : 8 * b + 8, :] = nn(thirds(jnp.exp(jnp.broadcast_to(end, (8, 128)))), spread)
        wide[s, :] = nn(thirds(jnp.exp(end - cum)), spread)
        bl = bc_ref[s, 0:STATE]

        def cols(c):
            decayed = (xdt_ref[s, at(c, 256)].astype(f32) * wide[s, at(c, 256)]).astype(bf16)
            s_ref[pl.ds(b * STATE, STATE), at(c, 256)] = tn(bl, decayed)

        loop(OWN // 256, cols)
    tot_ref[...] = (s_ref[STATE:, :] + dec_ref[8:9, :] * s_ref[:STATE, :]).astype(bf16)


def decay_tables(cum_ref, tall, flat):
    t = cum_ref.shape[0]
    parts = thirds(cum_ref[...])
    tall[...] = nn(parts, spread_matrix(HEADS * 128, 128))
    r, c = iotas((HEADS * 8, 128))
    pick = jnp.where(((c & 15) == r // 8) & (c < 48), 1.0, 0.0).astype(bf16)
    for b in range(t // 128):
        flat[b] = nt(pick, parts[b * 128 : (b + 1) * 128])


def k_within(cum_ref, bc_ref, xdt_ref, y_ref, tall, flat, scores):
    t = cum_ref.shape[0]
    need(cum_ref)
    decay_tables(cum_ref, tall, flat)
    blocks = t // BLOCK
    need(bc_ref, xdt_ref)
    for b in range(blocks):
        s = pl.ds(b * BLOCK, BLOCK)
        scores[s, :] = nt(bc_ref[s, STATE:], bc_ref[s, 0:STATE])
    r, c = iotas((128, 128))
    causal = r >= c
    lane = iotas((BLOCK, 128))[1]

    def pair(p):
        cols = at(p, 128)
        for b in range(blocks):
            o = b * BLOCK
            u = xdt_ref[pl.ds(o, BLOCK), cols]
            top = jnp.zeros((128, 128), f32)
            low = jnp.zeros((128, 128), f32)
            for a in range(2):
                head = 2 * p + a
                own = jnp.where((lane >= 64) == (a == 1), u, jnp.zeros_like(u))
                hc = at(head, 128)
                hr = pl.ds(pl.multiple_of(head * 8, 8), 8)
                t0, t1 = tall[pl.ds(o, 128), hc], tall[pl.ds(o + 128, 128), hc]
                u0, u1 = flat[2 * b, hr, :][0:1], flat[2 * b + 1, hr, :][0:1]
                sc = scores
                w00 = jnp.where(causal, sc[pl.ds(o, 128), 0:128] * jnp.exp(jnp.where(causal, t0 - u0, 0.0)), 0.0)
                w10 = sc[pl.ds(o + 128, 128), 0:128] * jnp.exp(t1 - u0)
                w11 = jnp.where(causal, sc[pl.ds(o + 128, 128), 128:] * jnp.exp(jnp.where(causal, t1 - u1, 0.0)), 0.0)
                top = top + nn(w00.astype(bf16), own[:128])
                low = low + nn(w10.astype(bf16), own[:128]) + nn(w11.astype(bf16), own[128:])
            y_ref[pl.ds(o, 128), cols] = top
            y_ref[pl.ds(o + 128, 128), cols] = low

    loop(OWN // 128, pair)


def k_out(first_layer, yw_ref, act_ref, bc_ref, cum_ref, cin_ref, s_ref, dec_ref, z_ref, par_ref, keep_ref, got_ref, *rest):
    if first_layer:
        y_ref, p_ref, msg_ref, st_ref, c_ref, wo_ref, wide, u_ref = rest
    else:
        cot_ref, ca_ref, cb_ref, y_ref, p_ref, msg_ref, st_ref, c_ref, wo_ref, g_ref, wide, u_ref = rest
    t = yw_ref.shape[0]
    half = WIDTH // 2
    shard = o_rows(keep_ref)

    def weights(core):
        for r in range(keep_ref.shape[0] // shard):
            for k in range(2):
                for src, side in ((keep_ref, core), (got_ref, 1 - core)):
                    wo_ref[(2 * r + k) * shard : (2 * r + k + 1) * shard, side * half : (side + 1) * half] = src[
                        r * shard : (r + 1) * shard, k * half : (k + 1) * half
                    ]

    need(keep_ref, got_ref)
    on_core(weights)
    done(wo_ref)
    need(bc_ref, cum_ref, cin_ref, s_ref, dec_ref)
    c_ref[0:STATE, :] = cin_ref[...].astype(f32)
    c_ref[STATE:, :] = s_ref[:STATE, :] + dec_ref[0:1, :] * c_ref[0:STATE, :]
    wide[...] = nn(thirds(jnp.exp(cum_ref[...])), spread_matrix(OWN, HDIM))
    for b in range(t // BLOCK):
        s = pl.ds(b * BLOCK, BLOCK)

        def cols(c):
            from_state = nn(bc_ref[s, STATE:], c_ref[pl.ds(b * STATE, STATE), at(c, 256)].astype(bf16))
            wide[s, at(c, 256)] = wide[s, at(c, 256)] * from_state

        loop(OWN // 256, cols)

    done(c_ref)
    need(yw_ref, act_ref, z_ref, par_ref)

    def rows(r):
        s = at(r, R)
        y = yw_ref[s, :] + wide[s, :] + par_ref[SKIP : SKIP + 1, :OWN] * act_ref[s, :OWN]
        y_ref[s, :] = y
        z = z_ref[s, :]
        gated = y * z * sig(z)
        u_ref[s, :] = (gated * par_ref[GATE : GATE + 1, :OWN]).astype(bf16)
        st_ref[s, 0:128] = jnp.broadcast_to(jnp.sum(gated * gated, axis=1, keepdims=True), (R, 128))

    loop(t // R, rows)
    done(y_ref)

    def project_out(c):
        p_ref[:, at(c, 256)] = nn(u_ref[...], wo_ref[:, at(c, 256)])

    loop(WIDTH // 256, project_out)
    done(p_ref)
    if first_layer:

        def send(r):
            s = at(r, R)
            msg_ref[s, :WIDTH] = p_ref[s, :].astype(bf16)
            v = st_ref[s, 0:128]
            msg_ref[s, WIDTH:] = stats_out(v, v)

        loop(t // R, send)
    else:
        odd = lax.rem(lax.axis_index("seq"), 2)
        need(cot_ref, ca_ref, cb_ref)
        copy_rows(g_ref, odd * (t // 2), cot_ref.at[odd])
        core = lax.axis_index("section")
        copy_rows(g_ref, (1 - odd) * (t // 2) + core * (t // 4), ca_ref)
        copy_rows(g_ref, (1 - odd) * (t // 2) + (1 - core) * (t // 4), cb_ref)
        done(g_ref)

        def dots(r):
            s = at(r, R)
            d = jnp.sum(p_ref[s, :] * g_ref[s, :].astype(f32), axis=1, keepdims=True)
            d = jnp.broadcast_to(d, (R, 128))
            st_ref[s, 128:256] = d
            msg_ref[s, half:] = stats_out(st_ref[s, 0:128], d)

        loop(t // R, dots)

        def send(core):
            msg_ref[:, :half] = p_ref[:, (1 - core) * half : (2 - core) * half].astype(bf16)

        on_core(send)


def o_rows(keep_ref):
    return keep_ref.shape[0] // (lax.axis_size("seq") // 2)


def k_final(h_ref, p_ref, st_ref, msg_ref, keep_ref, give_ref):
    need()
    half = WIDTH // 2
    rows_each = keep_ref.shape[0]
    odd = lax.rem(lax.axis_index("seq"), 2)

    def body(core):
        cols = slice(core * half, (core + 1) * half)

        def half_out(dst, start):
            def rows(r):
                s = pl.ds(pl.multiple_of(start + r * R, R), R)
                other = stats_in(msg_ref[s, half:])[0]
                rs = lax.rsqrt((st_ref[s, 0:1] + other) * (1.0 / INNER) + EPS)
                p = p_ref[s, cols] + msg_ref[s, :half].astype(f32)
                dst[at(r, R), :] = (h_ref[s, cols].astype(f32) + rs * p).astype(bf16)

            loop(rows_each // R, rows)

        half_out(keep_ref, odd * rows_each)
        half_out(give_ref, (1 - odd) * rows_each)

    on_core(body)


def kb_gate(g_ref, w_ref, y_ref, yw_ref, z_ref, act_ref, bc_ref, cum_ref, rs_ref, rd_ref, par_ref, dec_ref,
            qz_ref, dy_ref, df_ref, dca_ref, keep_ref, give_ref, d_ref, e_ref, small_ref, dgn, wide, gn):
    t = g_ref.shape[0]
    need(g_ref, w_ref)

    def back(c):
        dgn[:, at(c, 256)] = nt(g_ref[...], w_ref[at(c, 256), :])

    loop(OWN // 256, back)
    need(cum_ref)
    wide[...] = nn(thirds(jnp.exp(cum_ref[...])), spread_matrix(OWN, HDIM))
    small_ref[...] = jnp.zeros(small_ref.shape, f32)
    collect = collect_matrix()
    need()

    def rows(r):
        s = at(r, R)
        z, y, d, x = z_ref[s, :], y_ref[s, :], dgn[s, :], act_ref[s, :OWN]
        gg = par_ref[GATE : GATE + 1, :OWN]
        if rs_ref.shape[1] == 128:
            rs, rd = rs_ref[s, 0:1], rd_ref[s, 0:1]
        else:
            squares, dots = stats_in(rd_ref[s, WIDTH // 2 :])
            rs = lax.rsqrt((rs_ref[s, 0:1] + squares) * (1.0 / INNER) + EPS)
            rd = rs_ref[s, 128:129] + dots
        sg = sig(z)
        sz = z * sg
        gated = y * sz
        scaled = gated * rs
        small_ref[0:8, :] += fold(d * scaled)
        gn[s, :] = (scaled * gg).astype(bf16)
        dgated = rs * (gg * d) - gated * (rs * rs * rs * rd * (1.0 / INNER))
        dy = dgated * sz
        dy_ref[s, :] = dy
        qz_ref[s, :] = (dgated * y * (sg * (1.0 + z - sz))).astype(bf16)
        small_ref[8:16, :] += fold(dy * x)
        df_ref[s, :] = (wide[s, :] * dy).astype(bf16)
        yw = yw_ref[s, :]
        high, low = halves(dy.astype(bf16).astype(f32) * yw + dy * (y - yw - par_ref[SKIP : SKIP + 1, :OWN] * x))
        sums = nn(jnp.concatenate([high, low], axis=0), collect)
        dca_ref[s, :] = sums[:R] + sums[R:]

    loop(t // R, rows)
    done(dy_ref, qz_ref, df_ref, dca_ref, small_ref)
    for b in range(t // BLOCK):
        s = pl.ds(b * BLOCK, BLOCK)
        cl = bc_ref[s, STATE:]

        def cols(c):
            d_ref[pl.ds(b * STATE, STATE), at(c, 256)] = tn(cl, df_ref[s, at(c, 256)])

        loop(OWN // 256, cols)
    e_ref[...] = (d_ref[:STATE, :] + dec_ref[0:1, :] * d_ref[STATE:, :]).astype(bf16)

    done(d_ref, e_ref)
    half = WIDTH // 2

    def halves_of(core):
        def weight(c):
            dw = tn(gn[:, at(c, 256)], g_ref[...]).astype(bf16)
            keep_ref[at(c, 256), :] = dw[:, core * half : (core + 1) * half]
            give_ref[at(c, 256), :] = dw[:, (1 - core) * half : (2 - core) * half]

        loop(OWN // 256, weight)

    on_core(halves_of)


def kb_within(dy_ref, xdt_ref, cum_ref, bc_ref, df_ref, c_ref, dx_ref, dbc_ref, tall, flat, scores, ds):
    t = cum_ref.shape[0]
    need(cum_ref)
    decay_tables(cum_ref, tall, flat)
    blocks = t // BLOCK
    need(bc_ref, xdt_ref, dy_ref)
    for b in range(blocks):
        s = pl.ds(b * BLOCK, BLOCK)
        scores[s, :] = nt(bc_ref[s, STATE:], bc_ref[s, 0:STATE])
    ds[...] = jnp.zeros(ds.shape, f32)
    r, c = iotas((128, 128))
    causal = r >= c
    lane = iotas((BLOCK, 128))[1]

    def pair(p):
        cols = at(p, 128)
        for b in range(blocks):
            o = b * BLOCK
            u = xdt_ref[pl.ds(o, BLOCK), cols]
            g = dy_ref[pl.ds(o, BLOCK), cols].astype(bf16)
            top = jnp.zeros((128, 128), f32)
            low = jnp.zeros((128, 128), f32)
            for a in range(2):
                head = 2 * p + a
                own = jnp.where((lane >= 64) == (a == 1), g, jnp.zeros_like(g))
                hc = at(head, 128)
                hr = pl.ds(pl.multiple_of(head * 8, 8), 8)
                t0, t1 = tall[pl.ds(o, 128), hc], tall[pl.ds(o + 128, 128), hc]
                u0, u1 = flat[2 * b, hr, :][0:1], flat[2 * b + 1, hr, :][0:1]
                e00 = jnp.where(causal, jnp.exp(jnp.where(causal, t0 - u0, 0.0)), 0.0)
                e10 = jnp.exp(t1 - u0)
                e11 = jnp.where(causal, jnp.exp(jnp.where(causal, t1 - u1, 0.0)), 0.0)
                q0, q1 = pl.ds(o, 128), pl.ds(o + 128, 128)
                w00 = (scores[q0, 0:128] * e00).astype(bf16)
                w10 = (scores[q1, 0:128] * e10).astype(bf16)
                w11 = (scores[q1, 128:] * e11).astype(bf16)
                top = top + tn(w00, own[:128]) + tn(w10, own[128:])
                low = low + tn(w11, own[128:])
                ds[q0, 0:128] += nt(own[:128], u[:128]) * e00
                ds[q1, 0:128] += nt(own[128:], u[:128]) * e10
                ds[q1, 128:] += nt(own[128:], u[128:]) * e11
            dx_ref[pl.ds(o, 128), cols] = top
            dx_ref[pl.ds(o + 128, 128), cols] = low

    loop(OWN // 128, pair)
    done(dx_ref)
    need(df_ref, c_ref)
    for b in range(blocks):
        s = pl.ds(b * BLOCK, BLOCK)
        d = ds[s, :].astype(bf16)
        carried = c_ref[pl.ds(b * STATE, STATE), :].astype(bf16)
        dbc_ref[s, 0:STATE] = tn(d, bc_ref[s, STATE:])
        dbc_ref[s, STATE:] = nn(d, bc_ref[s, 0:STATE]) + nt(df_ref[s, :], carried)


def kb_front(gin_ref, d_ref, c_ref, dec_ref, bc_ref, xdt_ref, act_ref, xb_ref, slope_ref, before_ref, dt_ref, cum_ref, dxw_ref, dbc_ref,
             dy_ref, dca_ref, par_ref,
             dxb_ref, halo_ref, qdt_ref, small_ref, head_ref, gs, dd, te, dtw, dact, red, red2, ends, pad):
    t = act_ref.shape[0]
    blocks = t // BLOCK
    spread, collect = spread_matrix(OWN, HDIM), collect_matrix()
    need(gin_ref, d_ref, dec_ref)
    gs[STATE:, :] = gin_ref[...].astype(f32)
    gs[:STATE, :] = d_ref[STATE:, :] + dec_ref[8:9, :] * gs[STATE:, :]
    need(dbc_ref, dt_ref, c_ref, cum_ref, bc_ref, xdt_ref)
    dact[:, OWN:] = dbc_ref[...]
    dtw[...] = nn(thirds(dt_ref[...]), spread)
    for b in range(blocks):
        s = pl.ds(b * BLOCK, BLOCK)
        ss = pl.ds(b * STATE, STATE)
        end = cum_ref[pl.ds((b + 1) * BLOCK - 8, 8), :][7:8]
        te[s, :] = nn(thirds(jnp.exp(end - cum_ref[s, :])), spread)
        bl = bc_ref[s, 0:STATE]
        ends[8 * b : 8 * b + 8, :] = fold(gs[ss, :] * c_ref[ss, :]) * dec_ref[8 * b : 8 * b + 8, :]

        def cols(c):
            q = at(c, 256)
            low = gs[ss, q].astype(bf16)
            dd[s, q] = nn(bl, low)
            decayed = (xdt_ref[s, q].astype(f32) * te[s, q]).astype(bf16)
            dact[s, OWN : OWN + STATE] += nt(decayed, low)

        loop(OWN // 256, cols)
        if b == 0:
            need(dxw_ref, dy_ref, act_ref, par_ref)

        def rows(r):
            q = pl.ds(pl.multiple_of(b * BLOCK + r * R, R), R)
            w = dd[q, :] * te[q, :]
            ends[8 * b : 8 * b + 8, :] += fold(w * xdt_ref[q, :].astype(f32))
            dxdt = dxw_ref[q, :] + w
            dact[q, :OWN] = dxdt * dtw[q, :] + par_ref[SKIP : SKIP + 1, :OWN] * dy_ref[q, :]
            parts = [(dxdt * act_ref[q, :OWN]).astype(bf16), *halves(dxdt * xdt_ref[q, :].astype(f32))]
            sums = nn(jnp.concatenate(parts, axis=0), collect)
            red[q, :] = sums[:R]
            red2[q, :] = sums[R : 2 * R] + sums[2 * R :]

        loop(BLOCK // R, rows)
    need()
    high, low = halves(ends[...])
    at_end = nn(high, collect) + nn(low, collect)
    rate = -jnp.exp(par_ref[RATE : RATE + 1, 0:128])
    head_ref[...] = jnp.zeros(head_ref.shape, f32)
    for b in range(blocks):
        s = pl.ds(b * BLOCK, BLOCK)
        dt = dt_ref[s, :]
        total = running_sum(dca_ref[s, :] - red2[s, :], True)
        total = total + jnp.sum(at_end[8 * b : 8 * b + 8], axis=0, keepdims=True)
        ddt = red[s, :] + rate * total
        raw = xb_ref[pl.ds(8 + b * BLOCK, BLOCK), XC:] + par_ref[STEP : STEP + 1, 0:128]
        draw = ddt * jax.nn.sigmoid(raw)
        head_ref[0:8, :] += fold(draw)
        head_ref[8:16, :] += fold(rate * dt * total)
        lane = iotas(draw.shape)[1]
        qdt_ref[s, :] = jnp.where(lane < HEADS, draw, 0.0).astype(bf16)
    done(qdt_ref, head_ref)
    pad[0:8, :] = jnp.zeros((8, 128), f32)
    pad[8 + t :, :] = jnp.zeros((8, 128), f32)

    def conv(c):
        cols = at(c, 128)
        w = par_ref[0:8, cols]
        d = dact[:, cols] * slope_ref[:, cols].astype(f32)
        pad[8 : 8 + t, :] = d
        small_ref[32:40, cols] = fold(d)
        xb, before = xb_ref[:, cols], before_ref[:, cols]
        out = 0.0
        for k in range(4):
            later = pad[3 - k : 11 - k + t, :]
            out = out + w[k : k + 1] * later
            small_ref[8 * k : 8 * k + 8, cols] = fold(later * xb) + later[0:8] * before
        dxb_ref[:, cols] = out
        halo_ref[:, cols] = out[0:8]

    loop(XC // 128, conv)


def z_weight(dw_ref, first, normed_ref, qz_ref, okeep_ref, ogot_ref):
    def weight(c):
        dw_ref[at(c, 256), first : first + OWN] = tn(normed_ref[:, at(c, 256)], qz_ref[...]).astype(bf16)

    loop(WIDTH // 256, weight)
    n = lax.axis_size("seq")
    shard, half = WIDTH // n, WIDTH // 2
    need()

    def out(core):
        for j in range(n):
            src = okeep_ref if j // (n // 2) == core else ogot_ref
            for k in range(2):
                row, col = (2 * (j % (n // 2)) + k) * shard, first + OWN + k * half
                dw_ref[j * shard : (j + 1) * shard, col : col + half] = src[row : row + shard, :]

    on_core(out)


def kb_z_weight(normed_ref, qz_ref, okeep_ref, ogot_ref, *rest):
    *blocks, dw_ref = rest
    need(normed_ref, qz_ref)
    z_weight(dw_ref, 0, normed_ref, qz_ref, okeep_ref, ogot_ref)
    to_blocks(blocks, dw_ref)


CUT = 640


def kb_x_weight(normed_ref, q_ref, *rest):
    *parts, dw_ref = rest
    need()
    x_weight(normed_ref, q_ref, dw_ref)
    if len(parts) == 1:
        return copy_rows(parts[0], 0, dw_ref)
    me = lax.axis_index("seq")
    rows = WIDTH // 4
    first, last = slice(0, CUT), slice(CUT, XD)
    for ref, cols, ranks in zip(parts, (first, last, first, last), ((1, 3), (2, 3), (0, 2), (0, 1))):
        for k, bits in enumerate(ranks):
            start = (me ^ bits) * rows

            def move(r, ref=ref, cols=cols, k=k, start=start):
                ref[pl.ds(pl.multiple_of(k * rows + r * 48, 16), 48), :] = dw_ref[
                    pl.ds(pl.multiple_of(start + r * 48, 16), 48), cols
                ]

            loop(rows // 48, move)
        done(ref)


def k_phase(keep_a, keep_b, got_a, got_b, own_a, own_b, give_a, give_b):
    need()
    rows = own_a.shape[0]
    for keep, got, own, give in ((keep_a, got_a, own_a, give_a), (keep_b, got_b, own_b, give_b)):
        for dst, start in ((give, rows), (own, 0)):

            def move(r, keep=keep, got=got, dst=dst, start=start):
                s = pl.ds(pl.multiple_of(start + r * 48, 16), 48)
                dst[at(r, 48), :] = (keep[s, :].astype(f32) + got[s, :].astype(f32)).astype(bf16)

            loop(rows // 48, move)
            done(dst)


def to_blocks(blocks, dw):
    if len(blocks) == 1:
        return copy_rows(blocks[0], 0, dw)
    me = lax.axis_index("seq")
    rows = blocks[0].shape[0]
    for k in reversed(range(len(blocks))):
        block, start = blocks[k], (me ^ k) * rows

        def move(r, block=block, start=start):
            block[at(r, 48), :] = dw[pl.ds(pl.multiple_of(start + r * 48, 16), 48), :]

        loop(rows // 48, move)
        done(block)


def kb_z_normed(qz_ref, w_ref, dn_ref):
    need()

    def back(c):
        dn_ref[:, at(c, 256)] = nt(qz_ref[...], w_ref[at(c, 256), :])

    loop(WIDTH // 256, back)


def make_q(dxb_ref, ret_ref, qdt_ref, q):
    t = q.shape[0]

    def rows(r):
        q[at(r, R), :XC] = dxb_ref[pl.ds(pl.multiple_of(r * R, R) + 8, R), :].astype(bf16)

    loop(t // R, rows)
    q[t - 16 :, :XC] = (
        dxb_ref[t - 8 : t + 8, :] + jnp.concatenate([jnp.zeros((8, XC), f32), ret_ref[...]], axis=0)
    ).astype(bf16)
    q[:, XC:] = qdt_ref[...]


def x_normed(q_ref, dnz_ref, w_ref, dn_ref, dnb_ref):
    def back(c):
        cols = at(c, 256)
        d = dnz_ref[:, cols] + nt(q_ref[...], w_ref[cols, :])
        dn_ref[:, cols] = d
        dnb_ref[:, cols] = d.astype(bf16)

    loop(WIDTH // 256, back)


def x_weight(normed_ref, q_ref, dw_ref):
    def weight(c):
        dw_ref[at(c, 256), :] = tn(normed_ref[:, at(c, 256)], q_ref[...]).astype(bf16)

    loop(WIDTH // 256, weight)


def kb_x_normed(dxb_ref, ret_ref, qdt_ref, dnz_ref, w_ref, q_ref, dn_ref, dnb_ref):
    need(dxb_ref, ret_ref, qdt_ref)
    make_q(dxb_ref, ret_ref, qdt_ref, q_ref)
    done(q_ref)
    need()
    x_normed(q_ref, dnz_ref, w_ref, dn_ref, dnb_ref)


def kb_x_weight_first(normed_ref, dxb_ref, ret_ref, qdt_ref, q_ref, *rest):
    *blocks, dw = rest
    need()
    make_q(dxb_ref, ret_ref, qdt_ref, q_ref)
    done(q_ref)
    x_weight(normed_ref, q_ref, dw)
    to_blocks(blocks, dw)


def kb_x_normed_last(q_ref, dnz_ref, w_ref, dn_ref, dnb_ref):
    need()
    x_normed(q_ref, dnz_ref, w_ref, dn_ref, dnb_ref)


def kb_norm(h_ref, dn_ref, dr_ref, g_ref, par_ref, pt_ref, gh_ref, small_ref, rd_ref):
    t = h_ref.shape[0]
    need()
    small_ref[...] = jnp.zeros(small_ref.shape, f32)

    def rows(r):
        s = at(r, R)
        h = h_ref[s, :].astype(f32)
        d = dn_ref[s, :] + dr_ref[s, :].astype(f32)
        scale = lax.rsqrt(jnp.mean(h * h, axis=1, keepdims=True) + EPS)
        hs = h * scale
        small_ref[...] += fold(d * hs)
        gd = par_ref[NORM : NORM + 1, :WIDTH] * d
        back = scale * (gd - hs * jnp.mean(hs * gd, axis=1, keepdims=True))
        gh = (g_ref[s, :].astype(f32) + back).astype(bf16)
        gh_ref[s, :] = gh
        if rd_ref is not None:
            dot = jnp.sum(gh.astype(f32) * pt_ref[s, :], axis=1, keepdims=True)
            rd_ref[s, :] = jnp.broadcast_to(dot, (R, 128))

    loop(t // R, rows)


def kb_norm_last(h_ref, dn_ref, dr_ref, g_ref, par_ref, keep_ref, give_ref, small_ref, gh):
    kb_norm(h_ref, dn_ref, dr_ref, g_ref, par_ref, None, gh, small_ref, None)
    half = WIDTH // 2
    each = keep_ref.shape[0]
    odd = lax.rem(lax.axis_index("seq"), 2)

    def body(core):
        def rows(r):
            for dst, start in ((keep_ref, odd * each), (give_ref, (1 - odd) * each)):
                s = pl.ds(pl.multiple_of(start + r * R, R), R)
                dst[at(r, R), :] = gh[s, core * half : (core + 1) * half]

        loop(each // R, rows)

    on_core(body)


SMALL = 12


def k_small(*refs):
    *ins, out = refs
    need()
    out[...] = jnp.zeros(out.shape, f32)

    def total(x):
        return jnp.sum(x, axis=0, keepdims=True)

    for layer in range(2):
        a, b, c, d = ins[4 * layer : 4 * layer + 4]
        base = SMALL * layer
        for k in range(5):
            out[base + k : base + k + 1, :] = total(b[8 * k : 8 * k + 8, :])
        out[base + NORM : base + NORM + 1, :WIDTH] = total(d[...])
        out[base + GATE : base + GATE + 1, :OWN] = total(a[0:8, :])
        out[base + SKIP : base + SKIP + 1, :OWN] = total(a[8:16, :])
        out[base + STEP : base + STEP + 1, 0:128] = total(c[0:8, :])
        out[base + RATE : base + RATE + 1, 0:128] = total(c[8:16, :])


def k_small_out(mine_ref, got_ref, ng_ref, cw_ref, cb_ref, db_ref, al_ref, sk_ref, gg_ref):
    need()

    def body(core):
        base = SMALL * core
        cores = (mine_ref, got_ref) if core == 0 else (got_ref, mine_ref)
        ng_ref[...] = mine_ref[base + NORM : base + NORM + 1, :WIDTH]
        for c, src in enumerate(cores):
            cw_ref[:, c * OWN : (c + 1) * OWN] = src[base : base + 4, :OWN]
            cb_ref[:, c * OWN : (c + 1) * OWN] = src[base + BIAS : base + BIAS + 1, :OWN]
            gg_ref[:, c * OWN : (c + 1) * OWN] = src[base + GATE : base + GATE + 1, :OWN]
        a, b = cores
        cw_ref[:, INNER:] = a[base : base + 4, OWN:] + b[base : base + 4, OWN:]
        cb_ref[:, INNER:] = a[base + BIAS : base + BIAS + 1, OWN:] + b[base + BIAS : base + BIAS + 1, OWN:]
        r, c = iotas((128, 2 * HEADS))
        r2, c2 = iotas((OWN, 2 * HEADS))
        wide = lambda v: jnp.broadcast_to(v, (8, v.shape[1]))
        for ref, row in ((db_ref, STEP), (al_ref, RATE)):
            acc = jnp.zeros((8, 2 * HEADS), f32)
            for k, src in enumerate(cores):
                pick = jnp.where((r == c - k * HEADS) & (r < HEADS), 1.0, 0.0)
                acc = acc + exact(wide(src[base + row : base + row + 1, 0:128]), pick)
            ref[...] = acc[0:1]
        acc = jnp.zeros((8, 2 * HEADS), f32)
        for k, src in enumerate(cores):
            pick = jnp.where(r2 // HDIM == c2 - k * HEADS, 1.0, 0.0)
            acc = acc + exact(wide(src[base + SKIP : base + SKIP + 1, :OWN]), pick)
        sk_ref[...] = acc[0:1]

    on_core(body)


def in_place(refs, full):
    odd = lax.rem(lax.axis_index("dp"), 2)
    half = refs[0].shape[0]
    copy_rows(full, odd * half, refs[0])
    copy_rows(full, (1 - odd) * half, refs[1])


def k_home(m1_ref, o1_ref, mz_ref, oz_ref, mx_ref, ox_ref, give_ref, zo, x):
    need()

    def body(core):
        if core == 0:
            in_place((m1_ref, o1_ref), give_ref)
        else:
            in_place((mz_ref, oz_ref), zo)
            in_place((mx_ref, ox_ref), x)
            give_ref[:, :XD] = x[...]
            give_ref[:, XD:] = zo[...]

    on_core(body)


def k_grads(m1_ref, o1_ref, mz_ref, oz_ref, mx_ref, ox_ref, got_ref, gw_ref, go_ref, dw1, zo0, x0):
    need()
    rows, half = got_ref.shape[0], WIDTH // 2
    in_place((m1_ref, o1_ref), dw1)
    in_place((mz_ref, oz_ref), zo0)
    in_place((mx_ref, ox_ref), x0)

    def body(core):
        mine = (x0, zo0, 0) if core == 0 else (dw1, dw1, XD)
        other = (got_ref, got_ref, XD)
        cores = (mine, other) if core == 0 else (other, mine)
        for c, (x, zo, first) in enumerate(cores):
            gw_ref[:, c * OWN : (c + 1) * OWN] = zo[:, first : first + OWN].astype(f32)
            gw_ref[:, INNER + c * OWN : INNER + (c + 1) * OWN] = x[:, :OWN].astype(f32)
            for k in range(2):
                col = first + OWN + k * half
                go_ref[k * rows : (k + 1) * rows, c * half : (c + 1) * half] = zo[:, col : col + half].astype(f32)
        a, b = cores[0][0], cores[1][0]
        gw_ref[:, 2 * INNER : 2 * INNER + 2 * STATE] = a[:, OWN:XC].astype(f32) + b[:, OWN:XC].astype(f32)
        r, c = iotas((128, 2 * HEADS))
        acc = 0.0
        for k, x in enumerate((a, b)):
            pick = jnp.where((r == c - k * HEADS) & (r < HEADS), 1.0, 0.0).astype(bf16)
            acc = acc + nn(x[:, XC:XD], pick)
        gw_ref[:, INNER + CONV :] = acc

    on_core(body)


def across(x):
    return jax.tree.map(lambda a: lax.ppermute(a, "section", [(0, 1), (1, 0)]), x)


def flip(x, axis, bits):
    return lax.ppermute(x, axis, [(k, k ^ bits) for k in range(lax.axis_size(axis))])


def chain_step(x, steps, backward):
    n = lax.axis_size("seq")
    hop = -2 * steps if backward else 2 * steps
    return lax.ppermute(x, "seq", [(k, k + hop) for k in range(n) if 0 <= k + hop < n])


def chain(value, decay, backward):
    entered = chain_step(value, 1, backward)
    count = lax.axis_size("seq") // 2
    if count > 2:
        rate = chain_step(decay, 1, backward)
        total = entered.astype(f32)
        steps = 1
        while steps < count - 1:
            total = total + rate[0:1] * chain_step(total.astype(bf16), steps, backward).astype(f32)
            rate = rate * chain_step(rate, steps, backward)
            steps *= 2
        entered = total.astype(bf16)
    return entered


def gather_rows(x):
    n = lax.axis_size("seq")
    if n != 4:
        return [lax.all_gather(x, "seq", axis=0, tiled=True)]
    return [x, *[flip(x, "seq", k) for k in (1, 2, 3)]]


def gather_near(x):
    if lax.axis_size("seq") != 4:
        return gather_rows(x)
    return [x, flip(x, "seq", 1), flip(x, "seq", 2)]


def gather_across(parts, *release):
    if len(parts) == 1:
        return parts
    x, gx, gy = parts
    gx, gy, *_ = lax.optimization_barrier((gx, gy, *release))
    half = x.shape[0] // 2
    return [x, gx, gy, flip(gx[:half], "seq", 2), flip(gy[half:], "seq", 1)]


def k_sum(counts, *refs):
    *blocks, keep_ref, give_ref = refs
    starts = [sum(counts[:k]) for k in range(len(counts))]
    need()
    odd = lax.rem(lax.axis_index("dp"), 2)
    half = keep_ref.shape[0]
    for dst, start in ((give_ref, (1 - odd) * half), (keep_ref, odd * half)):

        def rows(r, dst=dst, start=start):
            s = pl.ds(pl.multiple_of(start + r * 16, 16), 16)
            first = 0
            for begin, count in zip(starts, counts):
                total = 0.0
                for ref in blocks[begin : begin + count]:
                    total = total + ref[s, :].astype(f32)
                dst[at(r, 16), first : first + total.shape[1]] = total.astype(dst.dtype)
                first += total.shape[1]

        loop(half // 16, rows)
        done(dst)


def k_add(a_ref, b_ref, out_ref):
    need()

    def rows(r):
        s = at(r, 16)
        out_ref[s, :] = (a_ref[s, :].astype(f32) + b_ref[s, :].astype(f32)).astype(bf16)

    loop(out_ref.shape[0] // 16, rows)


def send_blocks(blocks):
    if len(blocks) > 1:
        return [blocks[0]] + [flip(blocks[k], "seq", k) for k in (3, 2, 1)]
    return [lax.psum_scatter(blocks[0], "seq", scatter_dimension=0, tiled=True)]


def halved(groups, *pins):
    got = [b for group in groups for b in group]
    rows, width = got[0].shape[0], sum(group[0].shape[1] for group in groups)
    shape = (rows // 2, width)
    return run(
        functools.partial(k_sum, [len(group) for group in groups]), "sum", [(shape, f32, "a"), (shape, bf16, "a")],
        after(got[0], *pins), *got[1:],
    )


def paired(mine, got, *pins):
    return run(k_add, "add", [(got.shape, bf16, "a")], after(mine, *pins), got)[0]


def over_dp(keep, got, *pins, later=()):
    mine = paired(keep, got, *pins)
    bit = 2
    while bit < lax.axis_size("dp"):
        mine = paired(mine, flip(mine, "dp", bit), *later)
        bit *= 2
    return mine, flip(mine, "dp", 1)


def simple_dp():
    n = lax.axis_size("dp")
    return n == 1 or n & (n - 1) != 0


def summed_dp(keep, give, *pins, later=()):
    if not simple_dp():
        return over_dp(keep, flip(give, "dp", 1), *pins, later=later)
    odd = lax.axis_index("dp") % 2 == 1
    keep = keep.astype(bf16)
    low, high = jnp.where(odd, give, keep), jnp.where(odd, keep, give)
    low, high = lax.psum((low, high), "dp")
    return jnp.where(odd, high, low), jnp.where(odd, low, high)


def k_add_small(*refs):
    *ins, out_ref = refs
    need()
    if len(ins) == 2:
        out_ref[...] = ins[0][...] + ins[1][...]
    else:
        out_ref[...] = (ins[0][...] + ins[1][...]) + (ins[2][...] + ins[3][...])


def sum_small(x, axes):
    for axis in axes:
        n = lax.axis_size(axis)
        if n == 4:
            x = run(k_add_small, "add_small", [(x.shape, f32, "a")], x, *[flip(x, axis, k) for k in (1, 2, 3)])[0]
        elif n & (n - 1):
            x = lax.psum(x, axis)
        else:
            bit = 1
            while bit < n:
                x = run(k_add_small, "add_small", [(x.shape, f32, "a")], x, flip(x, axis, bit))[0]
                bit *= 2
    return x


def sum_small_dp(x):
    n = lax.axis_size("dp")
    if n & (n - 1):
        return lax.psum(x, "dp"), x
    half_way, bit = x, 1
    while bit < n:
        x = run(k_add_small, "add_small", [(x.shape, f32, "a")], x, flip(x, "dp", bit))[0]
        half_way = x if bit == 1 else half_way
        bit *= 2
    return x, half_way


def after(x, *others):
    return lax.optimization_barrier((x, *others))[0]


AHEAD = ["xdt", "cum", "bc", "c"], ["act", "xb"], ["wz", "wx"]
AHEAD_NORM = ["wo", "y", "yw", "z", "act"]


def on_device(hidden_in, cotangent, norm_gain, in_weight, conv_weight, conv_bias, dt_bias, a_log, skip, gate_gain, out_weight):
    core = lax.axis_index("section")
    first = core == 0
    odd = lax.axis_index("seq") % 2
    even = odd == 0
    length = hidden_in.shape[1]
    t = 2 * length
    n = lax.axis_size("seq")
    shard = in_weight.shape[1]
    half = WIDTH // 2
    packed = XD + 2 * OWN

    def given(x):
        return lax.dynamic_index_in_dim(x, 1 - odd, 0, keepdims=False)

    def both_sequences(mine, give):
        got = flip(give, "seq", 1)
        return jnp.stack([jnp.where(even, mine, got), jnp.where(even, got, mine)])

    mine_w, give_w, mine_p, give_p = run(
        k_prep, "prep",
        [((shard, packed), bf16, "v"), ((shard, packed), bf16, "a"), ((PARAMS, XC), f32, "v"), ((PARAMS, XC), f32, "a")],
        *[
            far_away(a)
            for a in (in_weight[0], out_weight[0], norm_gain, conv_weight[0], conv_bias, dt_bias, a_log, skip, gate_gain)
        ],
    )
    x0, zo0, x1, zo1, par0, par1 = run(
        k_pick, "pick",
        [((shard, XD), bf16, "a"), ((shard, 2 * OWN), bf16, "a"), ((shard, XD), bf16, "a"),
         ((shard, 2 * OWN), bf16, "a"), ((PARAMS, XC), f32), ((PARAMS, XC), f32)],
        mine_w, across(give_w), mine_p, across(give_p),
    )
    params = [par0, par1]

    def half_given(x):
        return lax.dynamic_slice_in_dim(given(x), core * (length // 2), length // 2, 0)

    def both_halves(mine):
        got = flip(mine, "seq", 1)
        return got, across(got)

    ga, gb = both_halves(half_given(hidden_in))
    give_cot = half_given(cotangent)
    parts_x0 = gather_rows(after(x0, ga, give_cot))
    near_zo0 = gather_near(after(zo0, *parts_x0))

    saved = [{}, {}]

    def keeping(layer, soon):
        return "vh" if soon else "h"

    def named(layer, names, results, modes):
        soon, at_result = {}, 0
        for name, mode in zip(names, modes):
            for m in mode:
                value = results[at_result]
                at_result += 1
                if m != "h":
                    soon[name] = value
                if m == mode[-1]:
                    saved[layer][name] = value
        return soon

    def scan_part(layer, x, tail, near_zo, before_front):
        par = params[layer]
        soon, last = keeping(layer, True), keeping(layer, False)
        before = chain_step(tail, 1, False)
        saved[layer]["before"] = before
        modes = [soon, last, soon, soon, last, soon, "v", soon, "a"]
        shapes = [((t, XC), f32), ((t, XC), bf16), ((t, 2 * STATE), bf16), ((t, OWN), bf16), ((t, 128), f32), ((t, 128), f32),
                  ((2 * STATE, OWN), f32), ((16, OWN), f32), ((STATE, OWN), bf16)]
        x |= named(
            layer, ["act", "slope", "bc", "xdt", "dt", "cum", "s", "dec", "tot"],
            run(
                k_front, "front", [(*shape, m) for shape, m in zip(shapes, modes)],
                x["xb"], after(before, *before_front), par, scratch=[((t, OWN), f32), ((16, XC), f32)],
            ),
            modes,
        )
        dec = saved[layer]["dec"]
        saved[layer]["decay"] = dec[:8] * dec[8:] if n > 4 else None
        entered = chain(x["tot"], saved[layer]["decay"], False)
        x |= named(
            layer, ["yw"],
            run(
                k_within, "within", [((t, OWN), f32, soon)], x["cum"], x["bc"], x["xdt"],
                scratch=[((t, HEADS * 128), f32), ((t // 128, HEADS * 8, 128), f32), ((t, BLOCK), f32)],
            ),
            [soon],
        )
        parts_zo = gather_across(near_zo, before)
        x["parts_zo"] = parts_zo
        modes = ["vh", "h", "v", "p"]
        x |= named(
            layer, ["z", "wz", "keep", "give"],
            run(
                k_z, "gate_in",
                [((t, OWN), f32, modes[0]), ((WIDTH, OWN), bf16, modes[1]), ((WIDTH // 2, OWN), bf16, "v"),
                 ((WIDTH // 2, OWN), bf16, "p")],
                near(after(x["normed"], x["yw"], entered)), *parts_zo, scratch=[((WIDTH, OWN), bf16)],
            ),
            modes,
        )
        ogot = across(x["give"])
        x["entered"] = entered
        cot_halves = [ca, cb] if layer else []
        ins = [x["yw"], x["act"], x["bc"], x["cum"], entered, x["s"], x["dec"], x["z"], par, x["keep"], ogot]
        kept = "v" if layer else "h"
        modes = [kept, "h" if layer else "v", "p", "vh" if layer else "v", last, kept] + ["vh"] * layer
        shapes = [((t, OWN), f32), ((t, WIDTH), f32), ((t, half + 128 if layer else WIDTH + 128), bf16),
                  ((t, 256 if layer else 128), f32), ((2 * STATE, OWN), f32), ((OWN, WIDTH), bf16)]
        shapes += [((t, WIDTH), bf16)] * layer
        results = run(
            functools.partial(k_out, layer == 0), "out", [(*shape, m) for shape, m in zip(shapes, modes)],
            *ins, *([cotangent, *cot_halves] if layer else []), scratch=[((t, OWN), f32), ((t, OWN), bf16)],
            ahead=[] if layer else [saved[0]["h"]],
        )
        x |= named(layer, ["y", "p", "msg", "st", "c", "wo", "g"][: len(modes)], results, modes)
        if layer == 0:
            x["h"] = results[-1]
        return x

    outs_in = [((t, WIDTH), bf16), ((t + 8, XD), f32), ((WIDTH, XD), bf16), ((8, XC), f32)]
    names_in = ["normed", "xb", "wx", "tail"]
    modes = ["h", "vh", "vh", "h", "a"]
    shapes = [((t, WIDTH), bf16), *outs_in]
    x = named(
        0, ["h", *names_in],
        run(k_in, "project", [(*shape, m) for shape, m in zip(shapes, modes)], hidden_in, ga, gb, par0, *parts_x0),
        modes,
    )
    tail0 = x["tail"]
    x = scan_part(0, x, tail0, near_zo0, [])
    parts_x1 = gather_across(gather_near(after(x1, x["entered"], x["yw"], *x["parts_zo"][3:])), x["msg"])
    msg = across(x["msg"])
    near_zo1 = gather_near(after(zo1, *parts_x1, *msg))
    modes = ["h", "h", "h", "vh", "vh", "h", "a"]
    shapes = [((t, WIDTH), bf16), ((t, WIDTH), f32), ((t, 128), f32), *outs_in]
    x = named(
        1, ["h", "pt", "rs", *names_in],
        run(
            k_mid, "middle", [(*shape, m) for shape, m in zip(shapes, modes)],
            x["h"], x["p"], x["st"], msg, par1, *parts_x1,
        ),
        modes,
    )
    h1_far, pt, rs0 = saved[1]["h"], saved[1]["pt"], saved[1]["rs"]
    tail1 = x["tail"]
    ca, cb = both_halves(after(give_cot, tail1))
    x = scan_part(1, x, x["tail"], near_zo1, near_zo1[1:])
    p1, st1, st1_far = saved[1]["p"], x["st"], saved[1]["st"]
    msg = across(x["msg"])
    count = 4 if n == 4 else 1

    ahead_zw, ahead_within, ahead_front = AHEAD

    def backward(layer, v, g, rs, rd, close=None, before_zw=(), before_zo=()):
        par = params[layer]
        v = dict(v)
        far = dict(v)

        def fetched(names, results):
            if names:
                v.update(zip(names, results[-len(names) :]))

        qz, dy, df, dca, okeep, ogive, d, e, small_a = run(
            kb_gate, "back_gate",
            [((t, OWN), bf16, "v"), ((t, OWN), f32, "v"), ((t, OWN), bf16, "v"), ((t, 128), f32, "v"),
             ((OWN, half), bf16, "v"), ((OWN, half), bf16, "p"), ((2 * STATE, OWN), f32, "v"),
             ((STATE, OWN), bf16, "a"), ((16, OWN), f32)],
            g, *[(close or v)[k] for k in ("wo", "y", "yw", "z", "act", "bc", "cum")], rs, rd, par, (close or v)["dec"],
            scratch=[((t, OWN), f32), ((t, OWN), f32), ((t, OWN), bf16)],
        )
        entered = chain(e, v["decay"], True)
        ogot = across(ogive)
        results = run(
            kb_z_weight, "back_zw", [((WIDTH // count, 2 * OWN), bf16, "a")] * count, v["normed"], qz, okeep,
            after(ogot, *before_zw),
            scratch=[((WIDTH, 2 * OWN), bf16)], ahead=[v[k] for k in ahead_zw],
        )
        zo = list(results[:count])
        beside_zw = [*zo]
        if layer:
            zo = [after(b, entered) for b in zo]
        fetched(ahead_zw, results)
        v["act"] = far["act"]
        dy = near(after(dy, *beside_zw))
        results = run(
            kb_within, "back_within", [((t, OWN), f32, "v"), ((t, 2 * STATE), f32, "v")],
            dy, v["xdt"], v["cum"], v["bc"], df, v["c"],
            scratch=[((t, HEADS * 128), f32), ((t // 128, HEADS * 8, 128), f32), ((t, BLOCK), f32), ((t, BLOCK), f32)],
            ahead=[v[k] for k in ahead_within],
        )
        dxw, dbc = results[:2]
        if layer == 0:
            dxw, dbc = near(*lax.optimization_barrier((dxw, dbc)))
            zo = [after(b, entered, dxw, *before_zo) for b in zo]
        fetched(ahead_within, results)
        results = run(
            kb_front, "back_front",
            [((t + 8, XC), f32, "v"), ((8, XC), f32, "a"), ((t, 128), bf16, "v"), ((40, XC), f32), ((16, 128), f32)],
            entered, d, far["c"], far["dec"], far["bc"], far["xdt"], v["act"], v["xb"], v["slope"], v["before"], far["dt"], far["cum"],
            dxw, dbc, dy, dca, par,
            scratch=[((2 * STATE, OWN), f32), ((t, OWN), f32), ((t, OWN), f32), ((t, OWN), f32), ((t, XC), f32),
                     ((t, 128), f32), ((t, 128), f32), ((16, OWN), f32), ((t + 16, 128), f32)],
            ahead=[v[k] for k in ahead_front],
        )
        dxb, halo, qdt, small_b, small_c = results[:5]
        fetched(ahead_front, results)
        ret = chain_step(halo, 1, True)
        dnz = run(kb_z_normed, "back_z", [((t, WIDTH), f32, "v")], near(after(qz, halo)), v["wz"])[0]
        return dxb, ret, qdt, dnz, zo, (small_a, small_b, small_c), v, (e, dbc, halo)

    shape_q, shape_n = ((t, XD), bf16, "v"), [((t, WIDTH), f32, "v"), ((t, WIDTH), bf16, "p")]
    x_blocks = [((WIDTH // count, XD), bf16, "a")] * count
    x_scratch = [((WIDTH, XD), bf16)]
    dxb, ret, qdt, dnz, zo1, small1, v1, _ = backward(1, saved[1], x["g"], st1, msg, x)
    got_zo1 = send_blocks(zo1)
    v0 = saved[0]
    early = []
    q, dn, dnb1, *fetched = run(
        kb_x_normed, "back_x", [shape_q, *shape_n], dxb, ret, qdt, dnz, v1["wx"], ahead=[v0[k] for k in early]
    )
    v0.update(zip(early, fetched))
    dr = across(dnb1)
    shapes_x = [((2 * shard, CUT), bf16, "a"), ((2 * shard, XD - CUT), bf16, "a")] * 2
    x1 = run(
        kb_x_weight, "back_xw", shapes_x if count > 1 else [((WIDTH, XD), bf16, "a")], v1["normed"],
        near(after(q, *dnb1, *got_zo1)), scratch=x_scratch,
    )
    got_x1 = [flip(x1[0], "seq", 1), flip(x1[1], "seq", 2)] if count > 1 else []

    def second_phase(*pins):
        if count == 1:
            return [[lax.psum_scatter(x1[0], "seq", scatter_dimension=0, tiled=True)]]
        own_a, own_b, give_a, give_b = run(
            k_phase, "phase", [((shard, CUT), bf16, "a"), ((shard, XD - CUT), bf16, "a")] * 2,
            after(x1[2], *pins), x1[3], *got_x1,
        )
        return [[own_a, flip(give_a, "seq", 2)], [own_b, flip(give_b, "seq", 1)]]

    phase = second_phase()
    early = AHEAD_NORM
    g0, g0_far, small_d1, rd0, *fetched = run(
        kb_norm, "back_norm", [((t, WIDTH), bf16, "vh"), ((8, WIDTH), f32), ((t, 128), f32, "v")],
        h1_far, dn, after(dr, *x1), saved[1]["g"], par1, pt, ahead=[v0[k] for k in early],
    )
    v0.update(zip(early, fetched))
    dxb, ret, qdt, dnz, zo0, small0, v0, (e0, dbc0, halo0) = backward(
        0, v0, g0, rs0, rd0, before_zw=phase[0][:1], before_zo=[p[-1] for p in phase]
    )
    got_zo0 = send_blocks(zo0)
    halves1 = halved([*phase, got_zo1], dbc0)
    over1 = [] if simple_dp() else [flip(halves1[1], "dp", 1)]
    q, *x0 = run(kb_x_weight_first, "back_xw", [shape_q] + x_blocks, v0["normed"], dxb, after(ret, *over1, *got_zo0), qdt, scratch=x_scratch)
    got_x0 = send_blocks(x0)
    dn, dnb0 = run(kb_x_normed_last, "back_x", [shape_n[0], ((t, WIDTH), bf16, "a")], near(after(q, *x0)), dnz, v0["wx"])
    dr = across(dnb0)
    sum1 = over_dp(halves1[0], *over1, x0[0]) if over1 else summed_dp(*halves1)
    sum_zo0 = summed_dp(*halved([got_zo0], x0[0]))
    final = run(
        k_final, "final", [((length, half), bf16, "a"), ((length, half), bf16, "a")],
        h1_far, p1, st1_far, after(msg, dnb0),
    )
    hidden_out = both_sequences(*final)
    keep, give, small_d0 = run(
        kb_norm_last, "back_norm", [((length, half), bf16, "a"), ((length, half), bf16, "a"), ((8, WIDTH), f32)],
        saved[0]["h"], dn, dr, g0_far, par0, scratch=[((t, WIDTH), bf16)],
    )
    halves0 = halved([got_x0], final[0], keep)
    grad_in = both_sequences(keep, give)
    small = run(k_small, "small", [((2 * SMALL, XC), f32, "a")], *small0, small_d0, *small1, small_d1)[0]
    small = sum_small(small, ["seq"])
    first_small = small
    small, half_way = sum_small_dp(small)
    sum_x0 = summed_dp(*halves0, first_small, later=[half_way])
    sums = [*sum1, *sum_zo0, after(sum_x0[0], small), sum_x0[1]]
    heads = 2 * HEADS
    smalls = run(
        k_small_out, "small_out",
        [((1, WIDTH), f32, "a"), ((4, CONV), f32, "a"), ((1, CONV), f32, "a"), ((1, heads), f32, "a"), ((1, heads), f32, "a"), ((1, heads), f32, "a"),
         ((1, INNER), f32, "a")],
        small, across(small),
    )
    give = run(k_home, "home", [((shard, packed), bf16, "p")], *sums, scratch=[((shard, 2 * OWN), bf16), ((shard, XD), bf16)])[0]
    grad_w, grad_o = run(
        k_grads, "grads", [((shard, INNER + CONV + heads), f32, "a"), ((2 * shard, WIDTH), f32, "a")],
        *sums, across(give),
        scratch=[((shard, packed), bf16), ((shard, 2 * OWN), bf16), ((shard, XD), bf16)],
    )
    norm, taps, bias, dtb, rates, skips, gates = smalls
    return (hidden_out, grad_in, norm, grad_w[None], taps[None], bias, dtb, rates, skips, gates, grad_o[None])


def solution(mesh):
    by_section = P("section", None)
    rows = P("section", "seq", None)
    tokens = P("dp", "seq", None)
    taps = P("section", None, None)
    out = P("dp", "seq", "section")
    small = (by_section,) * 4
    return jax.shard_map(
        on_device,
        mesh=mesh,
        in_specs=(tokens, tokens, by_section, rows, taps, by_section, *small, rows),
        out_specs=(out, out, by_section, rows, taps, by_section, *small, rows),
        check_vma=False,
    )
```

```python
import functools

import jax
import jax.numpy as jnp
from jax import lax
from jax.experimental import pallas as pl
from jax.experimental.pallas import tpu as pltpu
from jax.sharding import PartitionSpec as P

HDIM = 64
STATE = 128
INNER = 1536
CONV = 1792
EPS = 1e-05
f32, bf16 = jnp.float32, jnp.bfloat16

WIDTH = 768
OWN = 768
HEADS = 12
XC = OWN + 2 * STATE
XD = XC + 128
R = 64
BLOCK = 256


def nn(a, b):
    return lax.dot_general(a, b, (((1,), (0,)), ((), ())), preferred_element_type=f32)


def nt(a, b):
    return lax.dot_general(a, b, (((1,), (1,)), ((), ())), preferred_element_type=f32)


def tn(a, b):
    return lax.dot_general(a, b, (((0,), (0,)), ((), ())), preferred_element_type=f32)


def loop(count, body):
    def step(k, carry):
        body(k)
        return carry

    lax.fori_loop(0, count, step, 0)


def at(k, size):
    return pl.ds(pl.multiple_of(k * size, size), size)


def iotas(shape):
    return lax.broadcasted_iota(jnp.int32, shape, 0), lax.broadcasted_iota(jnp.int32, shape, 1)


def spread_matrix(width, per):
    r, c = iotas((128, width))
    return jnp.where(((r & 15) == c // per) & (r < 48), 1.0, 0.0).astype(bf16)


def collect_matrix():
    r, c = iotas((OWN, 128))
    return jnp.where(((c & 15) == r // HDIM) & (c < 48), 1.0, 0.0).astype(bf16)


def thirds(v):
    high = v.astype(bf16).astype(f32)
    rest = v - high
    mid = rest.astype(bf16).astype(f32)
    lane = iotas(v.shape)[1]
    out = jnp.where(lane < 16, high, jnp.where(lane < 32, mid, rest - mid))
    return jnp.where(lane < 48, out, 0.0).astype(bf16)


def halves(v):
    high = v.astype(bf16)
    return high, (v - high.astype(f32)).astype(bf16)


def running_sum(v, backward=False):
    r, c = iotas((BLOCK, BLOCK))
    tri = jnp.where((c >= r) if backward else (r >= c), 1.0, 0.0).astype(bf16)
    high = v.astype(bf16)
    rest = v - high.astype(f32)
    mid = rest.astype(bf16)
    last = (rest - mid.astype(f32)).astype(bf16)
    return nn(tri, high) + nn(tri, mid) + nn(tri, last)


def sig(v):
    return 0.5 * jnp.tanh(0.5 * v) + 0.5


def softplus(v):
    e = jnp.exp(-jnp.abs(v))
    u = 1.0 + e
    small = u == 1.0
    return jnp.maximum(v, 0.0) + jnp.where(small, e, jnp.log(u) * e / jnp.where(small, 1.0, u - 1.0))


def fold(v):
    return jnp.sum(v.reshape(v.shape[0] // 8, 8, v.shape[1]), axis=0)


def copy_rows(dst, start, src, cols=None):
    rows = src.shape[0]
    step = next(k for k in (48, 32, 16, 8, rows) if rows % k == 0)

    def move(r):
        place = pl.ds(pl.multiple_of(start + r * step, 16), step)
        if cols is None:
            dst[place, :] = src[at(r, step), :]
        else:
            dst[place, :] = src[at(r, step), cols]

    loop(rows // step, move)


def place_rows(dst, parts, cols=None):
    if len(parts) == 1:
        return copy_rows(dst, 0, parts[0], cols)
    me = lax.axis_index("seq")
    rows = parts[0].shape[0]
    for k in range(min(len(parts), 4)):
        copy_rows(dst, (me ^ k) * rows, parts[k], cols)
    if len(parts) > 4:
        copy_rows(dst, (me ^ 3) * rows + rows // 2, parts[4], cols)


def on_core(body):
    me = lax.axis_index("section")
    for core in range(2):
        pl.when(me == core)(lambda core=core: body(core))


def exact(a, b):
    return lax.dot_general(
        a, b, (((1,), (0,)), ((), ())), preferred_element_type=f32, precision=lax.Precision.HIGHEST
    )


def stats_out(a, b):
    lane = iotas(a.shape)[1]
    v = jnp.where(lane < 64, a, b)
    high = v.astype(bf16).astype(f32)
    rest = v - high
    mid = rest.astype(bf16).astype(f32)
    l = lane & 63
    out = jnp.where(l < 16, high, jnp.where(l < 32, mid, rest - mid))
    return jnp.where(l < 48, out, 0.0).astype(bf16)


def stats_in(v):
    v = v.astype(f32)
    lane = iotas(v.shape)[1]
    a = jnp.sum(jnp.where(lane < 64, v, 0.0), axis=1, keepdims=True)
    b = jnp.sum(jnp.where(lane < 64, 0.0, v), axis=1, keepdims=True)
    return a * (1.0 / 16), b * (1.0 / 16)


class Copies:

    def __init__(self, pairs_in, pairs_ahead, pairs_out, sems_in, sems_out):
        self.waiting, self.ready, self.started, self.ahead = {}, {}, [], []
        for k, (far, near, whole) in enumerate(pairs_in):
            copy = pltpu.make_async_copy(far, near, sems_in.at[k])
            copy.start()
            self.waiting.setdefault(id(whole), []).append(copy)
        for k, (far, near) in enumerate(pairs_ahead):
            copy = pltpu.make_async_copy(far, near, sems_in.at[len(pairs_in) + k])
            copy.start()
            self.ahead.append(copy)
        for k, (far, near, whole) in enumerate(pairs_out):
            self.ready.setdefault(id(whole), []).append(pltpu.make_async_copy(near, far, sems_out.at[k]))

    def need(self, refs):
        for key in [id(r) for r in refs] if refs else list(self.waiting):
            for copy in self.waiting.pop(key, ()):
                copy.wait()

    def done(self, refs):
        for key in [id(r) for r in refs] if refs else list(self.ready):
            for copy in self.ready.pop(key, ()):
                copy.start()
                self.started.append(copy)


COPIES = []


def need(*refs):
    COPIES[-1].need(refs)


def done(*refs):
    COPIES[-1].done(refs)


FAR = []
NEAR = []


def near(*arrays):
    NEAR.extend(arrays)
    return arrays if len(arrays) > 1 else arrays[0]


def far_away(array):
    FAR.append(array)
    return array


def run(kernel, name, outs, *ins, scratch=(), ahead=(), stay=()):
    far, close = pl.BlockSpec(memory_space=pltpu.HBM), pl.BlockSpec(memory_space=pltpu.VMEM)
    loose = pl.BlockSpec(memory_space=pl.ANY)
    modes = [o[2] if len(o) > 2 else "h" for o in outs]
    units = [m for mode in modes for m in mode] + ["v"] * len(ahead) + ["h"] * len(stay)
    shapes, specs = [], []
    for (shape, dtype, *_), mode in zip(outs, modes):
        for m in mode:
            if m == "p":
                shapes += [jax.ShapeDtypeStruct((shape[0] // 2, *shape[1:]), dtype)] * 2
                specs += [loose] * 2
            else:
                space = dict(v=pltpu.VMEM, h=pltpu.HBM, a=jax.ShapeDtypeStruct)[m]
                shapes.append(space(shape, dtype))
                specs.append(dict(v=close, h=far, a=loose)[m])
    for a in ahead:
        shapes.append(pltpu.VMEM(a.shape, a.dtype))
        specs.append(close)
    for a in stay:
        shapes.append(pltpu.HBM(a.shape, a.dtype))
        specs.append(far)
    groups = [a if isinstance(a, (tuple, list)) else (a,) for a in (*ins, *ahead, *stay)]
    flat = [a for group in groups for a in group]
    held = [any(a is k for k in NEAR) for a in flat]
    kept = [any(a is k for k in FAR) for a in flat]
    flat = [
        pltpu.with_memory_space_constraint(a, pltpu.VMEM if h else pltpu.HBM) if h or k else a
        for a, h, k in zip(flat, held, kept)
    ]
    n_in, n_out, n_own = len(flat), len(shapes), sum(len(group) for group in groups[: len(ins)])
    buffers = [
        pltpu.VMEM((sum(a.shape[0] for a in group), *group[0].shape[1:]), group[0].dtype)
        for group in groups[: len(ins)]
        if not any(group[0] is k for k in NEAR)
    ]
    buffers += [pltpu.VMEM(shape, dtype) for (shape, dtype, *_), mode in zip(outs, modes) if "v" not in mode]

    def body(*refs):
        given, made, rest = list(refs[:n_in]), list(refs[n_in : n_in + n_out]), list(refs[n_in + n_out :])
        pairs_in, pairs_out, vin, vout = [], [], [], []
        pairs_ahead = list(zip(given[n_own:], made[n_out - len(ahead) - len(stay) :]))
        at_ref = 0
        for group in groups[: len(ins)]:
            if held[at_ref]:
                vin.append(given[at_ref])
            else:
                vin.append(rest.pop(0))
                start = 0
                for k, part in enumerate(group):
                    rows = part.shape[0]
                    place = vin[-1] if len(group) == 1 else vin[-1].at[pl.ds(start, rows)]
                    pairs_in.append((given[at_ref + k], place, vin[-1]))
                    start += rows
            at_ref += len(group)
        for mode in modes:
            vout.append(made.pop(0) if "v" in mode else rest.pop(0))
            if mode == "p":
                rows = vout[-1].shape[0] // 2
                for k in range(2):
                    pairs_out.append((made.pop(0), vout[-1].at[pl.ds(k * rows, rows)], vout[-1]))
            elif mode != "v":
                pairs_out.append((made.pop(0), vout[-1], vout[-1]))
        *extra, sems_in, sems_out = rest
        copies = Copies(pairs_in, pairs_ahead, pairs_out, sems_in, sems_out)
        COPIES.append(copies)
        kernel(*vin, *vout, *extra)
        need()
        done()
        for copy in [*copies.ahead, *copies.started]:
            copy.wait()
        COPIES.pop()

    results = list(
        pl.pallas_call(
            body,
            name=name,
            out_shape=shapes,
            in_specs=[close if h else far if k else loose for h, k in zip(held, kept)],
            out_specs=specs,
            scratch_shapes=[
                *buffers,
                *[pltpu.VMEM(s, d) for s, d in scratch],
                pltpu.SemaphoreType.DMA((max(n_in, 1),)),
                pltpu.SemaphoreType.DMA((max(n_out, 1),)),
            ],
            compiler_params=pltpu.CompilerParams(vmem_limit_bytes=MIB * 2**20),
            cost_estimate=pl.CostEstimate(flops=1, bytes_accessed=1, transcendentals=0),
        )(*flat)
    )
    grouped = []
    for unit in units:
        if unit == "p":
            grouped.append((results.pop(0), results.pop(0)))
            continue
        grouped.append(results.pop(0))
        if unit != "a":
            (NEAR if unit == "v" else FAR).append(grouped[-1])
    return grouped


MIB = 24


TAPS, BIAS, NORM, GATE, SKIP, STEP, RATE = 0, 4, 5, 6, 7, 8, 9
PARAMS = 16


def k_prep(hid_ref, cot_ref, w_ref, o_ref, ng_ref, cw_ref, cb_ref, db_ref, al_ref, sk_ref, gg_ref, hid_half, cot_half, mine_x, give_x, mine_zo, give_zo, mine_p, give_p):
    need()
    rows = w_ref.shape[0]
    half = WIDTH // 2
    r24, c24 = iotas((2 * HEADS, 128))
    rk, ck = iotas((2 * HEADS, OWN))

    def pack(core, out):
        own = core * OWN
        out[:, 0:OWN] = w_ref[:, INNER + own : INNER + own + OWN]
        out[:, OWN:XC] = w_ref[:, 2 * INNER : 2 * INNER + 2 * STATE]
        pick = ((c24 & 15) == r24 - core * HEADS) & (c24 < 48)
        steps = w_ref[:, INNER + CONV : INNER + CONV + 2 * HEADS]
        out[:, XC:XD] = nn(steps, jnp.where(pick, 1.0, 0.0).astype(bf16)).astype(bf16)

    def pack_rest(core, out, par):
        own = core * OWN
        pick = ((c24 & 15) == r24 - core * HEADS) & (c24 < 48)
        out[:, 0:OWN] = w_ref[:, own : own + OWN]
        for t in range(2):
            at_lane = OWN + t * half
            out[:, at_lane : at_lane + half] = o_ref[t * rows : (t + 1) * rows, core * half : (core + 1) * half]
        par[...] = jnp.zeros(par.shape, f32)
        par[TAPS : TAPS + 4, :OWN] = cw_ref[:, own : own + OWN]
        par[TAPS : TAPS + 4, OWN:] = cw_ref[:, INNER:]
        par[BIAS : BIAS + 1, :OWN] = cb_ref[:, own : own + OWN]
        par[BIAS : BIAS + 1, OWN:] = cb_ref[:, INNER:]
        par[NORM : NORM + 1, :WIDTH] = ng_ref[...]
        par[GATE : GATE + 1, :OWN] = gg_ref[:, own : own + OWN]
        spread = jnp.where(rk - core * HEADS == ck // HDIM, 1.0, 0.0)
        par[SKIP : SKIP + 1, :OWN] = exact(jnp.broadcast_to(sk_ref[...], (8, 2 * HEADS)), spread)[0:1]
        lanes = jnp.where(pick, 1.0, 0.0)
        par[STEP : STEP + 1, 0:128] = exact(jnp.broadcast_to(db_ref[...], (8, 2 * HEADS)), lanes)[0:1]
        par[RATE : RATE + 1, 0:128] = exact(jnp.broadcast_to(al_ref[...], (8, 2 * HEADS)), lanes)[0:1]

    def body(core):
        pack(core, mine_x)
        pack(1 - core, give_x)

    def rest(core):
        pack_rest(core, mine_zo, mine_p)
        pack_rest(1 - core, give_zo, give_p)

    on_core(body)
    done(mine_x, give_x)
    even_seq = 1 - lax.rem(lax.axis_index("seq"), 2)
    rows_half = hid_half.shape[0]
    start = lax.axis_index("section") * rows_half
    for src, dst in ((hid_ref, hid_half), (cot_ref, cot_half)):

        def move(r, src=src, dst=dst):
            dst[at(r, 32), :] = src[even_seq, pl.ds(pl.multiple_of(start + r * 32, 32), 32), :]

        loop(rows_half // 32, move)
        done(dst)
    on_core(rest)


def k_pick(mine_x, got_x, mine_p, got_p, x0, x1, p0, p1):
    need()

    def body(core):
        for layer, (x, p) in enumerate(((x0, p0), (x1, p1))):
            x[...] = (mine_x, got_x)[layer ^ core][...]
            p[...] = (mine_p, got_p)[layer ^ core][...]

    on_core(body)


def k_pick_rest(mine_zo, got_zo, zo0, zo1):
    need()

    def body(core):
        zo0[...] = (mine_zo, got_zo)[core][...]
        zo1[...] = (mine_zo, got_zo)[1 - core][...]

    on_core(body)


def norm_rows(h, gain):
    scale = lax.rsqrt(jnp.mean(h * h, axis=1, keepdims=True) + EPS)
    return (h * scale * gain).astype(bf16)


def project(t, normed_ref, wx_ref, xb_ref, tail_ref):
    xb_ref[0:8, :] = jnp.zeros((8, XD), f32)

    def cols(c):
        xb_ref[8 : 8 + t, at(c, 384)] = nn(normed_ref[...], wx_ref[:, at(c, 384)])

    loop(XD // 384, cols)
    tail_ref[...] = xb_ref[t:, :XC]


def k_in(hid_ref, ga_ref, gb_ref, par_ref, *rest):
    *parts, h_ref, normed_ref, xb_ref, wx_ref, tail_ref = rest
    need(hid_ref, ga_ref, gb_ref, par_ref)
    t = h_ref.shape[0]
    half = t // 2
    odd = lax.rem(lax.axis_index("seq"), 2)
    core = lax.axis_index("section")
    copy_rows(h_ref, odd * half, hid_ref.at[odd])
    copy_rows(h_ref, (1 - odd) * half + core * (half // 2), ga_ref)
    copy_rows(h_ref, (1 - odd) * half + (1 - core) * (half // 2), gb_ref)

    def rows(r):
        normed_ref[at(r, R), :] = norm_rows(h_ref[at(r, R), :].astype(f32), par_ref[NORM : NORM + 1, :WIDTH])

    loop(t // R, rows)
    done(h_ref, normed_ref)
    need(*parts)
    place_rows(wx_ref, parts)
    done(wx_ref)
    project(t, normed_ref, wx_ref, xb_ref, tail_ref)


def k_mid(h_ref, p_ref, st_ref, msg_ref, par_ref, *rest):
    *parts, h1_ref, pt_ref, rs_ref, normed_ref, xb_ref, wx_ref, tail_ref = rest
    need(h_ref, p_ref, st_ref, msg_ref, par_ref)
    t = h_ref.shape[0]

    def rows(r):
        s = at(r, R)
        other = stats_in(msg_ref[s, WIDTH:])[0]
        rs = lax.rsqrt((st_ref[s, 0:128] + other) * (1.0 / INNER) + EPS)
        rs_ref[s, :] = rs
        p = p_ref[s, :] + msg_ref[s, :WIDTH].astype(f32)
        pt_ref[s, :] = p
        h1 = (h_ref[s, :].astype(f32) + rs[:, 0:1] * p).astype(bf16)
        h1_ref[s, :] = h1
        normed_ref[s, :] = norm_rows(h1.astype(f32), par_ref[NORM : NORM + 1, :WIDTH])

    loop(t // R, rows)
    done(h1_ref, pt_ref, rs_ref, normed_ref)
    need(*parts)
    place_rows(wx_ref, parts)
    done(wx_ref)
    project(t, normed_ref, wx_ref, xb_ref, tail_ref)


def k_z(normed_ref, *rest):
    *parts, z_ref, wz_ref, keep_ref, give_ref, o = rest
    need(*parts)
    place_rows(wz_ref, parts, slice(0, OWN))
    done(wz_ref)
    place_rows(o, parts, slice(OWN, 2 * OWN))

    def split(core):
        rows = keep_ref.shape[0]
        keep_ref[...] = o[core * rows : (core + 1) * rows, :]
        give_ref[...] = o[(1 - core) * rows : (2 - core) * rows, :]

    on_core(split)
    done(keep_ref, give_ref)
    need(normed_ref)

    def cols(c):
        z_ref[:, at(c, 384)] = nn(normed_ref[...], wz_ref[:, at(c, 384)])

    loop(OWN // 384, cols)


def k_front(xb_ref, before_ref, par_ref, act_ref, slope_ref, bc_ref, xdt_ref, dt_ref, cum_ref, s_ref, dec_ref, tot_ref, wide, edge):
    t = act_ref.shape[0]
    need()
    edge[0:8, :] = before_ref[...]
    edge[8:16, :] = jnp.zeros((8, XC), f32)

    def conv(c):
        cols = at(c, 128)
        w = par_ref[0:8, cols]
        total = w[4:5] + w[0:1] * xb_ref[pl.ds(5, t), cols]
        for k in range(1, 4):
            total = total + w[k : k + 1] * xb_ref[pl.ds(5 + k, t), cols]
        first = total[0:8]
        for k in range(4):
            first = first + w[k : k + 1] * edge[5 + k : 13 + k, cols]
        total = jnp.concatenate([first, total[8:]], axis=0)
        sg = sig(total)
        act = total * sg
        act_ref[:, cols] = act
        slope_ref[:, cols] = (sg + act * (1.0 - sg)).astype(bf16)

    loop(XC // 128, conv)
    bc_ref[...] = act_ref[:, OWN:].astype(bf16)
    done(act_ref, slope_ref, bc_ref)
    dt = softplus(xb_ref[8 : 8 + t, XC:] + par_ref[STEP : STEP + 1, 0:128])
    dt_ref[...] = dt
    done(dt_ref)
    rate = -jnp.exp(par_ref[RATE : RATE + 1, 0:128])
    spread = spread_matrix(OWN, HDIM)
    wide[...] = nn(thirds(dt), spread)

    def rows(r):
        s = at(r, R)
        xdt_ref[s, :] = (act_ref[s, :OWN] * wide[s, :]).astype(bf16)

    loop(t // R, rows)
    done(xdt_ref)
    for b in range(t // BLOCK):
        s = pl.ds(b * BLOCK, BLOCK)
        cum = running_sum(rate * dt[b * BLOCK : (b + 1) * BLOCK])
        cum_ref[s, :] = cum
        end = cum[BLOCK - 1 : BLOCK, :]
        dec_ref[8 * b : 8 * b + 8, :] = nn(thirds(jnp.exp(jnp.broadcast_to(end, (8, 128)))), spread)
        wide[s, :] = nn(thirds(jnp.exp(end - cum)), spread)
        bl = bc_ref[s, 0:STATE]

        def cols(c):
            decayed = (xdt_ref[s, at(c, 256)].astype(f32) * wide[s, at(c, 256)]).astype(bf16)
            s_ref[pl.ds(b * STATE, STATE), at(c, 256)] = tn(bl, decayed)

        loop(OWN // 256, cols)
    tot_ref[...] = (s_ref[STATE:, :] + dec_ref[8:9, :] * s_ref[:STATE, :]).astype(bf16)


def decay_tables(cum_ref, tall, flat):
    t = cum_ref.shape[0]
    parts = thirds(cum_ref[...])
    tall[...] = nn(parts, spread_matrix(HEADS * 128, 128))
    r, c = iotas((HEADS * 8, 128))
    pick = jnp.where(((c & 15) == r // 8) & (c < 48), 1.0, 0.0).astype(bf16)
    for b in range(t // 128):
        flat[b] = nt(pick, parts[b * 128 : (b + 1) * 128])


def k_within(cum_ref, bc_ref, xdt_ref, y_ref, tall, flat, scores):
    t = cum_ref.shape[0]
    need(cum_ref)
    decay_tables(cum_ref, tall, flat)
    blocks = t // BLOCK
    need(bc_ref, xdt_ref)
    for b in range(blocks):
        s = pl.ds(b * BLOCK, BLOCK)
        scores[s, :] = nt(bc_ref[s, STATE:], bc_ref[s, 0:STATE])
    r, c = iotas((128, 128))
    causal = r >= c
    lane = iotas((BLOCK, 128))[1]

    def pair(p):
        cols = at(p, 128)
        for b in range(blocks):
            o = b * BLOCK
            u = xdt_ref[pl.ds(o, BLOCK), cols]
            top = jnp.zeros((128, 128), f32)
            low = jnp.zeros((128, 128), f32)
            for a in range(2):
                head = 2 * p + a
                own = jnp.where((lane >= 64) == (a == 1), u, jnp.zeros_like(u))
                hc = at(head, 128)
                hr = pl.ds(pl.multiple_of(head * 8, 8), 8)
                t0, t1 = tall[pl.ds(o, 128), hc], tall[pl.ds(o + 128, 128), hc]
                u0, u1 = flat[2 * b, hr, :][0:1], flat[2 * b + 1, hr, :][0:1]
                sc = scores
                w00 = jnp.where(causal, sc[pl.ds(o, 128), 0:128] * jnp.exp(jnp.where(causal, t0 - u0, 0.0)), 0.0)
                w10 = sc[pl.ds(o + 128, 128), 0:128] * jnp.exp(t1 - u0)
                w11 = jnp.where(causal, sc[pl.ds(o + 128, 128), 128:] * jnp.exp(jnp.where(causal, t1 - u1, 0.0)), 0.0)
                top = top + nn(w00.astype(bf16), own[:128])
                low = low + nn(w10.astype(bf16), own[:128]) + nn(w11.astype(bf16), own[128:])
            y_ref[pl.ds(o, 128), cols] = top
            y_ref[pl.ds(o + 128, 128), cols] = low

    loop(OWN // 128, pair)


def k_out(first_layer, yw_ref, act_ref, bc_ref, cum_ref, cin_ref, s_ref, dec_ref, z_ref, par_ref, keep_ref, got_ref, *rest):
    if first_layer:
        y_ref, p_ref, msg_ref, st_ref, c_ref, wo_ref, wide, u_ref = rest
    else:
        cot_ref, ca_ref, cb_ref, y_ref, p_ref, msg_ref, st_ref, c_ref, wo_ref, g_ref, wide, u_ref = rest
    t = yw_ref.shape[0]
    half = WIDTH // 2
    shard = o_rows(keep_ref)

    def weights(core):
        for r in range(keep_ref.shape[0] // shard):
            for k in range(2):
                for src, side in ((keep_ref, core), (got_ref, 1 - core)):
                    wo_ref[(2 * r + k) * shard : (2 * r + k + 1) * shard, side * half : (side + 1) * half] = src[
                        r * shard : (r + 1) * shard, k * half : (k + 1) * half
                    ]

    need(keep_ref, got_ref)
    on_core(weights)
    done(wo_ref)
    need(bc_ref, cum_ref, cin_ref, s_ref, dec_ref)
    c_ref[0:STATE, :] = cin_ref[...].astype(f32)
    c_ref[STATE:, :] = s_ref[:STATE, :] + dec_ref[0:1, :] * c_ref[0:STATE, :]
    wide[...] = nn(thirds(jnp.exp(cum_ref[...])), spread_matrix(OWN, HDIM))
    for b in range(t // BLOCK):
        s = pl.ds(b * BLOCK, BLOCK)

        def cols(c):
            from_state = nn(bc_ref[s, STATE:], c_ref[pl.ds(b * STATE, STATE), at(c, 256)].astype(bf16))
            wide[s, at(c, 256)] = wide[s, at(c, 256)] * from_state

        loop(OWN // 256, cols)

    done(c_ref)
    need(yw_ref, act_ref, z_ref, par_ref)

    def rows(r):
        s = at(r, R)
        y = yw_ref[s, :] + wide[s, :] + par_ref[SKIP : SKIP + 1, :OWN] * act_ref[s, :OWN]
        y_ref[s, :] = y
        z = z_ref[s, :]
        gated = y * z * sig(z)
        u_ref[s, :] = (gated * par_ref[GATE : GATE + 1, :OWN]).astype(bf16)
        st_ref[s, 0:128] = jnp.broadcast_to(jnp.sum(gated * gated, axis=1, keepdims=True), (R, 128))

    loop(t // R, rows)
    done(y_ref)

    def project_out(c):
        p_ref[:, at(c, 256)] = nn(u_ref[...], wo_ref[:, at(c, 256)])

    loop(WIDTH // 256, project_out)
    done(p_ref)
    if first_layer:

        def send(r):
            s = at(r, R)
            msg_ref[s, :WIDTH] = p_ref[s, :].astype(bf16)
            v = st_ref[s, 0:128]
            msg_ref[s, WIDTH:] = stats_out(v, v)

        loop(t // R, send)
    else:
        odd = lax.rem(lax.axis_index("seq"), 2)
        need(cot_ref, ca_ref, cb_ref)
        copy_rows(g_ref, odd * (t // 2), cot_ref.at[odd])
        core = lax.axis_index("section")
        copy_rows(g_ref, (1 - odd) * (t // 2) + core * (t // 4), ca_ref)
        copy_rows(g_ref, (1 - odd) * (t // 2) + (1 - core) * (t // 4), cb_ref)
        done(g_ref)

        def dots(r):
            s = at(r, R)
            d = jnp.sum(p_ref[s, :] * g_ref[s, :].astype(f32), axis=1, keepdims=True)
            d = jnp.broadcast_to(d, (R, 128))
            st_ref[s, 128:256] = d
            msg_ref[s, half:] = stats_out(st_ref[s, 0:128], d)

        loop(t // R, dots)

        def send(core):
            msg_ref[:, :half] = p_ref[:, (1 - core) * half : (2 - core) * half].astype(bf16)

        on_core(send)


def o_rows(keep_ref):
    return keep_ref.shape[0] // (lax.axis_size("seq") // 2)


def k_final(h_ref, p_ref, st_ref, msg_ref, keep_ref, give_ref):
    need()
    half = WIDTH // 2
    rows_each = keep_ref.shape[0]
    odd = lax.rem(lax.axis_index("seq"), 2)

    def body(core):
        cols = slice(core * half, (core + 1) * half)

        def half_out(dst, start):
            def rows(r):
                s = pl.ds(pl.multiple_of(start + r * R, R), R)
                other = stats_in(msg_ref[s, half:])[0]
                rs = lax.rsqrt((st_ref[s, 0:1] + other) * (1.0 / INNER) + EPS)
                p = p_ref[s, cols] + msg_ref[s, :half].astype(f32)
                dst[at(r, R), :] = (h_ref[s, cols].astype(f32) + rs * p).astype(bf16)

            loop(rows_each // R, rows)

        half_out(keep_ref, odd * rows_each)
        half_out(give_ref, (1 - odd) * rows_each)

    on_core(body)


def kb_gate(g_ref, w_ref, y_ref, yw_ref, z_ref, act_ref, bc_ref, cum_ref, rs_ref, rd_ref, par_ref, dec_ref,
            qz_ref, dy_ref, df_ref, dca_ref, keep_ref, give_ref, d_ref, e_ref, small_ref, dgn, wide, gn):
    t = g_ref.shape[0]
    need(g_ref, w_ref)

    def back(c):
        dgn[:, at(c, 256)] = nt(g_ref[...], w_ref[at(c, 256), :])

    loop(OWN // 256, back)
    need(cum_ref)
    wide[...] = nn(thirds(jnp.exp(cum_ref[...])), spread_matrix(OWN, HDIM))
    small_ref[...] = jnp.zeros(small_ref.shape, f32)
    collect = collect_matrix()
    need()

    def rows(r):
        s = at(r, R)
        z, y, d, x = z_ref[s, :], y_ref[s, :], dgn[s, :], act_ref[s, :OWN]
        gg = par_ref[GATE : GATE + 1, :OWN]
        if rs_ref.shape[1] == 128:
            rs, rd = rs_ref[s, 0:1], rd_ref[s, 0:1]
        else:
            squares, dots = stats_in(rd_ref[s, WIDTH // 2 :])
            rs = lax.rsqrt((rs_ref[s, 0:1] + squares) * (1.0 / INNER) + EPS)
            rd = rs_ref[s, 128:129] + dots
        sg = sig(z)
        sz = z * sg
        gated = y * sz
        scaled = gated * rs
        small_ref[0:8, :] += fold(d * scaled)
        gn[s, :] = (scaled * gg).astype(bf16)
        dgated = rs * (gg * d) - gated * (rs * rs * rs * rd * (1.0 / INNER))
        dy = dgated * sz
        dy_ref[s, :] = dy
        qz_ref[s, :] = (dgated * y * (sg * (1.0 + z - sz))).astype(bf16)
        small_ref[8:16, :] += fold(dy * x)
        df_ref[s, :] = (wide[s, :] * dy).astype(bf16)
        yw = yw_ref[s, :]
        high, low = halves(dy.astype(bf16).astype(f32) * yw + dy * (y - yw - par_ref[SKIP : SKIP + 1, :OWN] * x))
        sums = nn(jnp.concatenate([high, low], axis=0), collect)
        dca_ref[s, :] = sums[:R] + sums[R:]

    loop(t // R, rows)
    done(dy_ref, qz_ref, df_ref, dca_ref, small_ref)
    for b in range(t // BLOCK):
        s = pl.ds(b * BLOCK, BLOCK)
        cl = bc_ref[s, STATE:]

        def cols(c):
            d_ref[pl.ds(b * STATE, STATE), at(c, 256)] = tn(cl, df_ref[s, at(c, 256)])

        loop(OWN // 256, cols)
    e_ref[...] = (d_ref[:STATE, :] + dec_ref[0:1, :] * d_ref[STATE:, :]).astype(bf16)

    done(d_ref, e_ref)
    half = WIDTH // 2

    def halves_of(core):
        def weight(c):
            dw = tn(gn[:, at(c, 256)], g_ref[...]).astype(bf16)
            keep_ref[at(c, 256), :] = dw[:, core * half : (core + 1) * half]
            give_ref[at(c, 256), :] = dw[:, (1 - core) * half : (2 - core) * half]

        loop(OWN // 256, weight)

    on_core(halves_of)


def kb_within(dy_ref, xdt_ref, cum_ref, bc_ref, df_ref, c_ref, dx_ref, dbc_ref, tall, flat, scores, ds):
    t = cum_ref.shape[0]
    need(cum_ref)
    decay_tables(cum_ref, tall, flat)
    blocks = t // BLOCK
    need(bc_ref, xdt_ref, dy_ref)
    for b in range(blocks):
        s = pl.ds(b * BLOCK, BLOCK)
        scores[s, :] = nt(bc_ref[s, STATE:], bc_ref[s, 0:STATE])
    ds[...] = jnp.zeros(ds.shape, f32)
    r, c = iotas((128, 128))
    causal = r >= c
    lane = iotas((BLOCK, 128))[1]

    def pair(p):
        cols = at(p, 128)
        for b in range(blocks):
            o = b * BLOCK
            u = xdt_ref[pl.ds(o, BLOCK), cols]
            g = dy_ref[pl.ds(o, BLOCK), cols].astype(bf16)
            top = jnp.zeros((128, 128), f32)
            low = jnp.zeros((128, 128), f32)
            for a in range(2):
                head = 2 * p + a
                own = jnp.where((lane >= 64) == (a == 1), g, jnp.zeros_like(g))
                hc = at(head, 128)
                hr = pl.ds(pl.multiple_of(head * 8, 8), 8)
                t0, t1 = tall[pl.ds(o, 128), hc], tall[pl.ds(o + 128, 128), hc]
                u0, u1 = flat[2 * b, hr, :][0:1], flat[2 * b + 1, hr, :][0:1]
                e00 = jnp.where(causal, jnp.exp(jnp.where(causal, t0 - u0, 0.0)), 0.0)
                e10 = jnp.exp(t1 - u0)
                e11 = jnp.where(causal, jnp.exp(jnp.where(causal, t1 - u1, 0.0)), 0.0)
                q0, q1 = pl.ds(o, 128), pl.ds(o + 128, 128)
                w00 = (scores[q0, 0:128] * e00).astype(bf16)
                w10 = (scores[q1, 0:128] * e10).astype(bf16)
                w11 = (scores[q1, 128:] * e11).astype(bf16)
                top = top + tn(w00, own[:128]) + tn(w10, own[128:])
                low = low + tn(w11, own[128:])
                ds[q0, 0:128] += nt(own[:128], u[:128]) * e00
                ds[q1, 0:128] += nt(own[128:], u[:128]) * e10
                ds[q1, 128:] += nt(own[128:], u[128:]) * e11
            dx_ref[pl.ds(o, 128), cols] = top
            dx_ref[pl.ds(o + 128, 128), cols] = low

    loop(OWN // 128, pair)
    done(dx_ref)
    need(df_ref, c_ref)
    for b in range(blocks):
        s = pl.ds(b * BLOCK, BLOCK)
        d = ds[s, :].astype(bf16)
        carried = c_ref[pl.ds(b * STATE, STATE), :].astype(bf16)
        dbc_ref[s, 0:STATE] = tn(d, bc_ref[s, STATE:])
        dbc_ref[s, STATE:] = nn(d, bc_ref[s, 0:STATE]) + nt(df_ref[s, :], carried)


def kb_front(gin_ref, d_ref, c_ref, dec_ref, bc_ref, xdt_ref, act_ref, xb_ref, slope_ref, before_ref, dt_ref, cum_ref, dxw_ref, dbc_ref,
             dy_ref, dca_ref, par_ref,
             dxb_ref, halo_ref, qdt_ref, small_ref, head_ref, gs, dd, te, dtw, dact, red, red2, ends, pad):
    t = act_ref.shape[0]
    blocks = t // BLOCK
    spread, collect = spread_matrix(OWN, HDIM), collect_matrix()
    need(gin_ref, d_ref, dec_ref)
    gs[STATE:, :] = gin_ref[...].astype(f32)
    gs[:STATE, :] = d_ref[STATE:, :] + dec_ref[8:9, :] * gs[STATE:, :]
    need(dbc_ref, dt_ref, c_ref, cum_ref, bc_ref, xdt_ref)
    dact[:, OWN:] = dbc_ref[...]
    dtw[...] = nn(thirds(dt_ref[...]), spread)
    for b in range(blocks):
        s = pl.ds(b * BLOCK, BLOCK)
        ss = pl.ds(b * STATE, STATE)
        end = cum_ref[pl.ds((b + 1) * BLOCK - 8, 8), :][7:8]
        te[s, :] = nn(thirds(jnp.exp(end - cum_ref[s, :])), spread)
        bl = bc_ref[s, 0:STATE]
        ends[8 * b : 8 * b + 8, :] = fold(gs[ss, :] * c_ref[ss, :]) * dec_ref[8 * b : 8 * b + 8, :]

        def cols(c):
            q = at(c, 256)
            low = gs[ss, q].astype(bf16)
            dd[s, q] = nn(bl, low)
            decayed = (xdt_ref[s, q].astype(f32) * te[s, q]).astype(bf16)
            dact[s, OWN : OWN + STATE] += nt(decayed, low)

        loop(OWN // 256, cols)
        if b == 0:
            need(dxw_ref, dy_ref, act_ref, par_ref)

        def rows(r):
            q = pl.ds(pl.multiple_of(b * BLOCK + r * R, R), R)
            w = dd[q, :] * te[q, :]
            ends[8 * b : 8 * b + 8, :] += fold(w * xdt_ref[q, :].astype(f32))
            dxdt = dxw_ref[q, :] + w
            dact[q, :OWN] = dxdt * dtw[q, :] + par_ref[SKIP : SKIP + 1, :OWN] * dy_ref[q, :]
            parts = [(dxdt * act_ref[q, :OWN]).astype(bf16), *halves(dxdt * xdt_ref[q, :].astype(f32))]
            sums = nn(jnp.concatenate(parts, axis=0), collect)
            red[q, :] = sums[:R]
            red2[q, :] = sums[R : 2 * R] + sums[2 * R :]

        loop(BLOCK // R, rows)
    need()
    high, low = halves(ends[...])
    at_end = nn(high, collect) + nn(low, collect)
    rate = -jnp.exp(par_ref[RATE : RATE + 1, 0:128])
    head_ref[...] = jnp.zeros(head_ref.shape, f32)
    for b in range(blocks):
        s = pl.ds(b * BLOCK, BLOCK)
        dt = dt_ref[s, :]
        total = running_sum(dca_ref[s, :] - red2[s, :], True)
        total = total + jnp.sum(at_end[8 * b : 8 * b + 8], axis=0, keepdims=True)
        ddt = red[s, :] + rate * total
        raw = xb_ref[pl.ds(8 + b * BLOCK, BLOCK), XC:] + par_ref[STEP : STEP + 1, 0:128]
        draw = ddt * jax.nn.sigmoid(raw)
        head_ref[0:8, :] += fold(draw)
        head_ref[8:16, :] += fold(rate * dt * total)
        lane = iotas(draw.shape)[1]
        qdt_ref[s, :] = jnp.where(lane < HEADS, draw, 0.0).astype(bf16)
    done(qdt_ref, head_ref)
    pad[0:8, :] = jnp.zeros((8, 128), f32)
    pad[8 + t :, :] = jnp.zeros((8, 128), f32)

    def conv(c):
        cols = at(c, 128)
        w = par_ref[0:8, cols]
        d = dact[:, cols] * slope_ref[:, cols].astype(f32)
        pad[8 : 8 + t, :] = d
        small_ref[32:40, cols] = fold(d)
        xb, before = xb_ref[:, cols], before_ref[:, cols]
        out = 0.0
        for k in range(4):
            later = pad[3 - k : 11 - k + t, :]
            out = out + w[k : k + 1] * later
            small_ref[8 * k : 8 * k + 8, cols] = fold(later * xb) + later[0:8] * before
        dxb_ref[:, cols] = out
        halo_ref[:, cols] = out[0:8]

    loop(XC // 128, conv)


def z_weight(dw_ref, first, normed_ref, qz_ref, okeep_ref, ogot_ref):
    def weight(c):
        dw_ref[at(c, 256), first : first + OWN] = tn(normed_ref[:, at(c, 256)], qz_ref[...]).astype(bf16)

    loop(WIDTH // 256, weight)
    n = lax.axis_size("seq")
    shard, half = WIDTH // n, WIDTH // 2
    need()

    def out(core):
        for j in range(n):
            src = okeep_ref if j // (n // 2) == core else ogot_ref
            for k in range(2):
                row, col = (2 * (j % (n // 2)) + k) * shard, first + OWN + k * half
                dw_ref[j * shard : (j + 1) * shard, col : col + half] = src[row : row + shard, :]

    on_core(out)


def kb_z_weight(normed_ref, qz_ref, okeep_ref, ogot_ref, *rest):
    *blocks, dw_ref = rest
    need(normed_ref, qz_ref)
    z_weight(dw_ref, 0, normed_ref, qz_ref, okeep_ref, ogot_ref)
    to_blocks(blocks, dw_ref)


CUT = 640


def kb_x_weight(normed_ref, q_ref, *rest):
    *parts, dw_ref = rest
    need()
    x_weight(normed_ref, q_ref, dw_ref)
    if len(parts) == 1:
        return copy_rows(parts[0], 0, dw_ref)
    me = lax.axis_index("seq")
    rows = WIDTH // 4
    first, last = slice(0, CUT), slice(CUT, XD)
    for ref, cols, ranks in zip(parts, (first, last, first, last), ((1, 3), (2, 3), (0, 2), (0, 1))):
        for k, bits in enumerate(ranks):
            start = (me ^ bits) * rows

            def move(r, ref=ref, cols=cols, k=k, start=start):
                ref[pl.ds(pl.multiple_of(k * rows + r * 48, 16), 48), :] = dw_ref[
                    pl.ds(pl.multiple_of(start + r * 48, 16), 48), cols
                ]

            loop(rows // 48, move)
        done(ref)


def k_phase(keep_a, keep_b, got_a, got_b, own_a, own_b, give_a, give_b):
    need()
    rows = own_a.shape[0]
    for keep, got, own, give in ((keep_a, got_a, own_a, give_a), (keep_b, got_b, own_b, give_b)):
        for dst, start in ((give, rows), (own, 0)):

            def move(r, keep=keep, got=got, dst=dst, start=start):
                s = pl.ds(pl.multiple_of(start + r * 48, 16), 48)
                dst[at(r, 48), :] = (keep[s, :].astype(f32) + got[s, :].astype(f32)).astype(bf16)

            loop(rows // 48, move)
            done(dst)


def to_blocks(blocks, dw):
    if len(blocks) == 1:
        return copy_rows(blocks[0], 0, dw)
    me = lax.axis_index("seq")
    rows = blocks[0].shape[0]
    for k in reversed(range(len(blocks))):
        block, start = blocks[k], (me ^ k) * rows

        def move(r, block=block, start=start):
            block[at(r, 48), :] = dw[pl.ds(pl.multiple_of(start + r * 48, 16), 48), :]

        loop(rows // 48, move)
        done(block)


def kb_z_normed(qz_ref, w_ref, dn_ref):
    need()

    def back(c):
        dn_ref[:, at(c, 256)] = nt(qz_ref[...], w_ref[at(c, 256), :])

    loop(WIDTH // 256, back)


def make_q(dxb_ref, ret_ref, qdt_ref, q):
    t = q.shape[0]

    def rows(r):
        q[at(r, R), :XC] = dxb_ref[pl.ds(pl.multiple_of(r * R, R) + 8, R), :].astype(bf16)

    loop(t // R, rows)
    q[t - 16 :, :XC] = (
        dxb_ref[t - 8 : t + 8, :] + jnp.concatenate([jnp.zeros((8, XC), f32), ret_ref[...]], axis=0)
    ).astype(bf16)
    q[:, XC:] = qdt_ref[...]


def x_normed(q_ref, dnz_ref, w_ref, dn_ref, dnb_ref):
    def back(c):
        cols = at(c, 256)
        d = dnz_ref[:, cols] + nt(q_ref[...], w_ref[cols, :])
        dn_ref[:, cols] = d
        dnb_ref[:, cols] = d.astype(bf16)

    loop(WIDTH // 256, back)


def x_weight(normed_ref, q_ref, dw_ref):
    def weight(c):
        dw_ref[at(c, 256), :] = tn(normed_ref[:, at(c, 256)], q_ref[...]).astype(bf16)

    loop(WIDTH // 256, weight)


def kb_x_normed(dxb_ref, ret_ref, qdt_ref, dnz_ref, w_ref, q_ref, dn_ref, dnb_ref):
    need(dxb_ref, ret_ref, qdt_ref)
    make_q(dxb_ref, ret_ref, qdt_ref, q_ref)
    done(q_ref)
    need()
    x_normed(q_ref, dnz_ref, w_ref, dn_ref, dnb_ref)


def kb_x_weight_first(normed_ref, dxb_ref, ret_ref, qdt_ref, q_ref, *rest):
    *blocks, dw = rest
    need()
    make_q(dxb_ref, ret_ref, qdt_ref, q_ref)
    done(q_ref)
    x_weight(normed_ref, q_ref, dw)
    to_blocks(blocks, dw)


def kb_x_normed_last(q_ref, dnz_ref, w_ref, dn_ref, dnb_ref):
    need()
    x_normed(q_ref, dnz_ref, w_ref, dn_ref, dnb_ref)


def kb_norm(h_ref, dn_ref, dr_ref, g_ref, par_ref, pt_ref, gh_ref, small_ref, rd_ref):
    t = h_ref.shape[0]
    need()
    small_ref[...] = jnp.zeros(small_ref.shape, f32)

    def rows(r):
        s = at(r, R)
        h = h_ref[s, :].astype(f32)
        d = dn_ref[s, :] + dr_ref[s, :].astype(f32)
        scale = lax.rsqrt(jnp.mean(h * h, axis=1, keepdims=True) + EPS)
        hs = h * scale
        small_ref[...] += fold(d * hs)
        gd = par_ref[NORM : NORM + 1, :WIDTH] * d
        back = scale * (gd - hs * jnp.mean(hs * gd, axis=1, keepdims=True))
        gh = (g_ref[s, :].astype(f32) + back).astype(bf16)
        gh_ref[s, :] = gh
        if rd_ref is not None:
            dot = jnp.sum(gh.astype(f32) * pt_ref[s, :], axis=1, keepdims=True)
            rd_ref[s, :] = jnp.broadcast_to(dot, (R, 128))

    loop(t // R, rows)


def kb_norm_last(h_ref, dn_ref, dr_ref, g_ref, par_ref, keep_ref, give_ref, small_ref, gh):
    kb_norm(h_ref, dn_ref, dr_ref, g_ref, par_ref, None, gh, small_ref, None)
    half = WIDTH // 2
    each = keep_ref.shape[0]
    odd = lax.rem(lax.axis_index("seq"), 2)

    def body(core):
        def rows(r):
            for dst, start in ((keep_ref, odd * each), (give_ref, (1 - odd) * each)):
                s = pl.ds(pl.multiple_of(start + r * R, R), R)
                dst[at(r, R), :] = gh[s, core * half : (core + 1) * half]

        loop(each // R, rows)

    on_core(body)


SMALL = 12


def k_small(*refs):
    *ins, out = refs
    need()
    out[...] = jnp.zeros(out.shape, f32)

    def total(x):
        return jnp.sum(x, axis=0, keepdims=True)

    for layer in range(2):
        a, b, c, d = ins[4 * layer : 4 * layer + 4]
        base = SMALL * layer
        for k in range(5):
            out[base + k : base + k + 1, :] = total(b[8 * k : 8 * k + 8, :])
        out[base + NORM : base + NORM + 1, :WIDTH] = total(d[...])
        out[base + GATE : base + GATE + 1, :OWN] = total(a[0:8, :])
        out[base + SKIP : base + SKIP + 1, :OWN] = total(a[8:16, :])
        out[base + STEP : base + STEP + 1, 0:128] = total(c[0:8, :])
        out[base + RATE : base + RATE + 1, 0:128] = total(c[8:16, :])


def k_small_out(mine_ref, got_ref, ng_ref, cw_ref, cb_ref, db_ref, al_ref, sk_ref, gg_ref):
    need()

    def body(core):
        base = SMALL * core
        cores = (mine_ref, got_ref) if core == 0 else (got_ref, mine_ref)
        ng_ref[...] = mine_ref[base + NORM : base + NORM + 1, :WIDTH]
        for c, src in enumerate(cores):
            cw_ref[:, c * OWN : (c + 1) * OWN] = src[base : base + 4, :OWN]
            cb_ref[:, c * OWN : (c + 1) * OWN] = src[base + BIAS : base + BIAS + 1, :OWN]
            gg_ref[:, c * OWN : (c + 1) * OWN] = src[base + GATE : base + GATE + 1, :OWN]
        a, b = cores
        cw_ref[:, INNER:] = a[base : base + 4, OWN:] + b[base : base + 4, OWN:]
        cb_ref[:, INNER:] = a[base + BIAS : base + BIAS + 1, OWN:] + b[base + BIAS : base + BIAS + 1, OWN:]
        r, c = iotas((128, 2 * HEADS))
        r2, c2 = iotas((OWN, 2 * HEADS))
        wide = lambda v: jnp.broadcast_to(v, (8, v.shape[1]))
        for ref, row in ((db_ref, STEP), (al_ref, RATE)):
            acc = jnp.zeros((8, 2 * HEADS), f32)
            for k, src in enumerate(cores):
                pick = jnp.where((r == c - k * HEADS) & (r < HEADS), 1.0, 0.0)
                acc = acc + exact(wide(src[base + row : base + row + 1, 0:128]), pick)
            ref[...] = acc[0:1]
        acc = jnp.zeros((8, 2 * HEADS), f32)
        for k, src in enumerate(cores):
            pick = jnp.where(r2 // HDIM == c2 - k * HEADS, 1.0, 0.0)
            acc = acc + exact(wide(src[base + SKIP : base + SKIP + 1, :OWN]), pick)
        sk_ref[...] = acc[0:1]

    on_core(body)


def in_place(refs, full):
    odd = lax.rem(lax.axis_index("dp"), 2)
    half = refs[0].shape[0]
    copy_rows(full, odd * half, refs[0])
    copy_rows(full, (1 - odd) * half, refs[1])


def k_home(m1_ref, o1_ref, mz_ref, oz_ref, mx_ref, ox_ref, give_ref, zo, x):
    need()

    def body(core):
        if core == 0:
            in_place((m1_ref, o1_ref), give_ref)
        else:
            in_place((mz_ref, oz_ref), zo)
            in_place((mx_ref, ox_ref), x)
            give_ref[:, :XD] = x[...]
            give_ref[:, XD:] = zo[...]

    on_core(body)


def k_grads(m1_ref, o1_ref, mz_ref, oz_ref, mx_ref, ox_ref, got_ref, gw_ref, go_ref, dw1, zo0, x0):
    need()
    rows, half = got_ref.shape[0], WIDTH // 2
    in_place((m1_ref, o1_ref), dw1)
    in_place((mz_ref, oz_ref), zo0)
    in_place((mx_ref, ox_ref), x0)

    def body(core):
        mine = (x0, zo0, 0) if core == 0 else (dw1, dw1, XD)
        other = (got_ref, got_ref, XD)
        cores = (mine, other) if core == 0 else (other, mine)
        for c, (x, zo, first) in enumerate(cores):
            gw_ref[:, c * OWN : (c + 1) * OWN] = zo[:, first : first + OWN].astype(f32)
            gw_ref[:, INNER + c * OWN : INNER + (c + 1) * OWN] = x[:, :OWN].astype(f32)
            for k in range(2):
                col = first + OWN + k * half
                go_ref[k * rows : (k + 1) * rows, c * half : (c + 1) * half] = zo[:, col : col + half].astype(f32)
        a, b = cores[0][0], cores[1][0]
        gw_ref[:, 2 * INNER : 2 * INNER + 2 * STATE] = a[:, OWN:XC].astype(f32) + b[:, OWN:XC].astype(f32)
        r, c = iotas((128, 2 * HEADS))
        acc = 0.0
        for k, x in enumerate((a, b)):
            pick = jnp.where((r == c - k * HEADS) & (r < HEADS), 1.0, 0.0).astype(bf16)
            acc = acc + nn(x[:, XC:XD], pick)
        gw_ref[:, INNER + CONV :] = acc

    on_core(body)


def across(x):
    return jax.tree.map(lambda a: lax.ppermute(a, "section", [(0, 1), (1, 0)]), x)


def flip(x, axis, bits):
    return lax.ppermute(x, axis, [(k, k ^ bits) for k in range(lax.axis_size(axis))])


def chain_step(x, steps, backward):
    n = lax.axis_size("seq")
    hop = -2 * steps if backward else 2 * steps
    return lax.ppermute(x, "seq", [(k, k + hop) for k in range(n) if 0 <= k + hop < n])


def chain(value, decay, backward):
    entered = chain_step(value, 1, backward)
    count = lax.axis_size("seq") // 2
    if count > 2:
        rate = chain_step(decay, 1, backward)
        total = entered.astype(f32)
        steps = 1
        while steps < count - 1:
            total = total + rate[0:1] * chain_step(total.astype(bf16), steps, backward).astype(f32)
            rate = rate * chain_step(rate, steps, backward)
            steps *= 2
        entered = total.astype(bf16)
    return entered


def gather_rows(x):
    n = lax.axis_size("seq")
    if n != 4:
        return [lax.all_gather(x, "seq", axis=0, tiled=True)]
    return [x, *[flip(x, "seq", k) for k in (1, 2, 3)]]


def gather_near(x):
    if lax.axis_size("seq") != 4:
        return gather_rows(x)
    return [x, flip(x, "seq", 1), flip(x, "seq", 2)]


def gather_across(parts, *release):
    if len(parts) == 1:
        return parts
    x, gx, gy = parts
    gx, gy, *_ = lax.optimization_barrier((gx, gy, *release))
    half = x.shape[0] // 2
    return [x, gx, gy, flip(gx[:half], "seq", 2), flip(gy[half:], "seq", 1)]


def k_sum(counts, *refs):
    *blocks, keep_ref, give_ref = refs
    starts = [sum(counts[:k]) for k in range(len(counts))]
    need()
    odd = lax.rem(lax.axis_index("dp"), 2)
    half = keep_ref.shape[0]
    for dst, start in ((give_ref, (1 - odd) * half), (keep_ref, odd * half)):

        def rows(r, dst=dst, start=start):
            s = pl.ds(pl.multiple_of(start + r * 16, 16), 16)
            first = 0
            for begin, count in zip(starts, counts):
                total = 0.0
                for ref in blocks[begin : begin + count]:
                    total = total + ref[s, :].astype(f32)
                dst[at(r, 16), first : first + total.shape[1]] = total.astype(dst.dtype)
                first += total.shape[1]

        loop(half // 16, rows)
        done(dst)


def k_add(a_ref, b_ref, out_ref):
    need()

    def rows(r):
        s = at(r, 16)
        out_ref[s, :] = (a_ref[s, :].astype(f32) + b_ref[s, :].astype(f32)).astype(bf16)

    loop(out_ref.shape[0] // 16, rows)


def send_blocks(blocks):
    if len(blocks) > 1:
        return [blocks[0]] + [flip(blocks[k], "seq", k) for k in (3, 2, 1)]
    return [lax.psum_scatter(blocks[0], "seq", scatter_dimension=0, tiled=True)]


def halved(groups, *pins):
    got = [b for group in groups for b in group]
    rows, width = got[0].shape[0], sum(group[0].shape[1] for group in groups)
    shape = (rows // 2, width)
    return run(
        functools.partial(k_sum, [len(group) for group in groups]), "sum", [(shape, f32, "a"), (shape, bf16, "a")],
        after(got[0], *pins), *got[1:],
    )


def paired(mine, got, *pins):
    return run(k_add, "add", [(got.shape, bf16, "a")], after(mine, *pins), got)[0]


def over_dp(keep, got, *pins, later=()):
    return further([paired(keep, got, *pins)], *later)


def further(mine, *later):
    (mine,), bit = mine, 2
    while bit < lax.axis_size("dp"):
        mine = paired(mine, flip(mine, "dp", bit), *later)
        bit *= 2
    return mine, flip(mine, "dp", 1)


def simple_dp():
    n = lax.axis_size("dp")
    return n == 1 or n & (n - 1) != 0


def summed_dp(keep, give, *pins, later=()):
    if not simple_dp():
        return over_dp(keep, flip(give, "dp", 1), *pins, later=later)
    odd = lax.axis_index("dp") % 2 == 1
    keep = keep.astype(bf16)
    low, high = jnp.where(odd, give, keep), jnp.where(odd, keep, give)
    low, high = lax.psum((low, high), "dp")
    return jnp.where(odd, high, low), jnp.where(odd, low, high)


def k_add_small(*refs):
    *ins, out_ref = refs
    need()
    if len(ins) == 2:
        out_ref[...] = ins[0][...] + ins[1][...]
    else:
        out_ref[...] = (ins[0][...] + ins[1][...]) + (ins[2][...] + ins[3][...])


def sum_small(x, axes):
    for axis in axes:
        n = lax.axis_size(axis)
        if n == 4:
            x = run(k_add_small, "add_small", [(x.shape, f32, "a")], x, *[flip(x, axis, k) for k in (1, 2, 3)])[0]
        elif n & (n - 1):
            x = lax.psum(x, axis)
        else:
            bit = 1
            while bit < n:
                x = run(k_add_small, "add_small", [(x.shape, f32, "a")], x, flip(x, axis, bit))[0]
                bit *= 2
    return x


def sum_small_dp(x):
    n = lax.axis_size("dp")
    if n & (n - 1):
        return lax.psum(x, "dp"), x
    half_way, bit = x, 1
    while bit < n:
        x = run(k_add_small, "add_small", [(x.shape, f32, "a")], x, flip(x, "dp", bit))[0]
        half_way = x if bit == 1 else half_way
        bit *= 2
    return x, half_way


def after(x, *others):
    return lax.optimization_barrier((x, *others))[0]


AHEAD = ["xdt", "cum", "bc", "c"], ["act", "xb", "slope", "dt"], ["wz", "wx"]
AHEAD_WEIGHT, AHEAD_NORM = ["y", "yw"], ["wo", "z", "act"]


def on_device(hidden_in, cotangent, norm_gain, in_weight, conv_weight, conv_bias, dt_bias, a_log, skip, gate_gain, out_weight):
    core = lax.axis_index("section")
    first = core == 0
    odd = lax.axis_index("seq") % 2
    even = odd == 0
    length = hidden_in.shape[1]
    t = 2 * length
    n = lax.axis_size("seq")
    shard = in_weight.shape[1]
    half = WIDTH // 2
    packed = XD + 2 * OWN

    def given(x):
        return lax.dynamic_index_in_dim(x, 1 - odd, 0, keepdims=False)

    def both_sequences(mine, give):
        got = flip(give, "seq", 1)
        return jnp.stack([jnp.where(even, mine, got), jnp.where(even, got, mine)])

    hid_half, cot_half, mine_x, give_x, mine_zo, give_zo, mine_p, give_p = run(
        k_prep, "prep",
        [((length // 2, WIDTH), bf16, "a"), ((length // 2, WIDTH), bf16, "a"), ((shard, XD), bf16, "v"),
         ((shard, XD), bf16, "a"), ((shard, 2 * OWN), bf16, "v"), ((shard, 2 * OWN), bf16, "a"),
         ((PARAMS, XC), f32, "v"), ((PARAMS, XC), f32, "a")],
        *[
            far_away(a)
            for a in (hidden_in, cotangent, in_weight[0], out_weight[0], norm_gain, conv_weight[0], conv_bias, dt_bias, a_log, skip, gate_gain)
        ],
    )
    x0, x1, par0, par1 = run(
        k_pick, "pick",
        [((shard, XD), bf16, "a"), ((shard, XD), bf16, "a"), ((PARAMS, XC), f32), ((PARAMS, XC), f32)],
        mine_x, across(give_x), mine_p, across(give_p),
    )
    zo0, zo1 = run(
        k_pick_rest, "pick_rest", [((shard, 2 * OWN), bf16, "a"), ((shard, 2 * OWN), bf16, "a")], mine_zo, across(give_zo)
    )
    params = [par0, par1]

    def half_given(x):
        return lax.dynamic_slice_in_dim(given(x), core * (length // 2), length // 2, 0)

    def both_halves(mine):
        got = flip(mine, "seq", 1)
        return got, across(got)

    ga, gb = both_halves(hid_half)
    give_cot = cot_half
    parts_x0 = gather_rows(after(x0, ga, give_cot))
    near_zo0 = gather_near(after(zo0, *parts_x0))

    saved = [{}, {}]

    def keeping(layer, soon):
        return "vh" if soon else "h"

    def named(layer, names, results, modes, stayed=()):
        soon, at_result = {}, 0
        for name, mode in zip(names, modes):
            for m in mode:
                value = results[at_result]
                at_result += 1
                if m != "h":
                    soon[name] = value
                if m == mode[-1]:
                    saved[layer][name] = value
        for name in stayed:
            saved[layer][name] = results[len(results) - len(stayed) + stayed.index(name)]
        return soon

    def scan_part(layer, x, tail, near_zo, before_front):
        par = params[layer]
        last = keeping(layer, False)
        before = chain_step(tail, 1, False)
        saved[layer]["before"] = before
        modes = ["v"] * 8 + ["a"]
        shapes = [((t, XC), f32), ((t, XC), bf16), ((t, 2 * STATE), bf16), ((t, OWN), bf16), ((t, 128), f32), ((t, 128), f32),
                  ((2 * STATE, OWN), f32), ((16, OWN), f32), ((STATE, OWN), bf16)]
        x |= named(
            layer, ["act", "slope", "bc", "xdt", "dt", "cum", "s", "dec", "tot"],
            run(
                k_front, "front", [(*shape, m) for shape, m in zip(shapes, modes)],
                x["xb"], after(before, *before_front), par, scratch=[((t, OWN), f32), ((16, XC), f32)],
            ),
            modes,
        )
        dec = saved[layer]["dec"]
        saved[layer]["decay"] = dec[:8] * dec[8:] if n > 4 else None
        entered = chain(x["tot"], saved[layer]["decay"], False)
        x |= named(
            layer, ["yw"],
            run(
                k_within, "within", [((t, OWN), f32, "v")], x["cum"], x["bc"], x["xdt"],
                scratch=[((t, HEADS * 128), f32), ((t // 128, HEADS * 8, 128), f32), ((t, BLOCK), f32)],
                stay=[x[k] for k in ("xb", "slope", "dt", "cum")],
            ),
            ["v"],
            ["xb", "slope", "dt", "cum"],
        )
        parts_zo = gather_across(near_zo, before)
        x["parts_zo"] = parts_zo
        modes = ["v", "h", "v", "p"]
        x |= named(
            layer, ["z", "wz", "keep", "give"],
            run(
                k_z, "gate_in",
                [((t, OWN), f32, modes[0]), ((WIDTH, OWN), bf16, modes[1]), ((WIDTH // 2, OWN), bf16, "v"),
                 ((WIDTH // 2, OWN), bf16, "p")],
                near(after(x["normed"], x["yw"], entered)), *parts_zo, scratch=[((WIDTH, OWN), bf16)],
                stay=[x[k] for k in ("normed", "xdt", "bc", "dec")],
            ),
            modes,
            ["normed", "xdt", "bc", "dec"],
        )
        ogot = across(x["give"])
        x["entered"] = entered
        cot_halves = [ca, cb] if layer else []
        ins = [x["yw"], x["act"], x["bc"], x["cum"], entered, x["s"], x["dec"], x["z"], par, x["keep"], ogot]
        kept = "v" if layer else "h"
        stayed = ["act"] if layer else ["act", "yw", "z"]
        modes = [kept, "h" if layer else "v", "p", "vh" if layer else "v", last, kept] + ["vh"] * layer
        shapes = [((t, OWN), f32), ((t, WIDTH), f32), ((t, half + 128 if layer else WIDTH + 128), bf16),
                  ((t, 256 if layer else 128), f32), ((2 * STATE, OWN), f32), ((OWN, WIDTH), bf16)]
        shapes += [((t, WIDTH), bf16)] * layer
        results = run(
            functools.partial(k_out, layer == 0), "out", [(*shape, m) for shape, m in zip(shapes, modes)],
            *ins, *([cotangent, *cot_halves] if layer else []), scratch=[((t, OWN), f32), ((t, OWN), bf16)],
            ahead=[] if layer else [saved[0]["h"]], stay=[x[k] for k in stayed],
        )
        x |= named(layer, ["y", "p", "msg", "st", "c", "wo", "g"][: len(modes)], results, modes, stayed)
        if layer == 0:
            x["h"] = results[-1 - len(stayed)]
        return x

    outs_in = [((t, WIDTH), bf16), ((t + 8, XD), f32), ((WIDTH, XD), bf16), ((8, XC), f32)]
    names_in = ["normed", "xb", "wx", "tail"]
    modes = ["h", "v", "v", "h", "a"]
    shapes = [((t, WIDTH), bf16), *outs_in]
    x = named(
        0, ["h", *names_in],
        run(k_in, "project", [(*shape, m) for shape, m in zip(shapes, modes)], hidden_in, ga, gb, par0, *parts_x0),
        modes,
    )
    tail0 = x["tail"]
    x = scan_part(0, x, tail0, near_zo0, [])
    parts_x1 = gather_across(gather_near(after(x1, x["entered"], x["yw"], *x["parts_zo"][3:])), x["msg"])
    msg = across(x["msg"])
    near_zo1 = gather_near(after(zo1, *parts_x1, *msg))
    modes = ["h", "h", "h", "v", "v", "h", "a"]
    shapes = [((t, WIDTH), bf16), ((t, WIDTH), f32), ((t, 128), f32), *outs_in]
    x = named(
        1, ["h", "pt", "rs", *names_in],
        run(
            k_mid, "middle", [(*shape, m) for shape, m in zip(shapes, modes)],
            x["h"], x["p"], x["st"], msg, par1, *parts_x1,
        ),
        modes,
    )
    h1_far, pt, rs0 = saved[1]["h"], saved[1]["pt"], saved[1]["rs"]
    tail1 = x["tail"]
    ca, cb = both_halves(after(give_cot, tail1))
    x = scan_part(1, x, x["tail"], near_zo1, near_zo1[1:])
    p1, st1, st1_far = saved[1]["p"], x["st"], saved[1]["st"]
    msg = across(x["msg"])
    count = 4 if n == 4 else 1

    ahead_zw, ahead_within, ahead_front = AHEAD

    def backward(layer, v, g, rs, rd, close=None, before_zw=(), before_zo=()):
        par = params[layer]
        v = dict(v)
        far = dict(v)

        def fetched(names, results):
            if names:
                v.update(zip(names, results[-len(names) :]))

        qz, dy, df, dca, okeep, ogive, d, e, small_a = run(
            kb_gate, "back_gate",
            [((t, OWN), bf16, "v"), ((t, OWN), f32, "v"), ((t, OWN), bf16, "v"), ((t, 128), f32, "v"),
             ((OWN, half), bf16, "v"), ((OWN, half), bf16, "p"), ((2 * STATE, OWN), f32, "v"),
             ((STATE, OWN), bf16, "a"), ((16, OWN), f32)],
            g, *[(close or v)[k] for k in ("wo", "y", "yw", "z", "act", "bc", "cum")], rs, rd, par, (close or v)["dec"],
            scratch=[((t, OWN), f32), ((t, OWN), f32), ((t, OWN), bf16)],
        )
        entered = chain(e, v["decay"], True)
        ogot = across(ogive)
        results = run(
            kb_z_weight, "back_zw", [((WIDTH // count, 2 * OWN), bf16, "a")] * count, v["normed"], qz, okeep,
            after(ogot, *before_zw),
            scratch=[((WIDTH, 2 * OWN), bf16)], ahead=[v[k] for k in ahead_zw],
        )
        zo = list(results[:count])
        beside_zw = [*zo]
        if layer:
            zo = [after(b, entered) for b in zo]
        fetched(ahead_zw, results)
        v["act"] = far["act"]
        dy = near(after(dy, *beside_zw))
        results = run(
            kb_within, "back_within", [((t, OWN), f32, "v"), ((t, 2 * STATE), f32, "v")],
            dy, v["xdt"], v["cum"], v["bc"], df, v["c"],
            scratch=[((t, HEADS * 128), f32), ((t // 128, HEADS * 8, 128), f32), ((t, BLOCK), f32), ((t, BLOCK), f32)],
            ahead=[v[k] for k in ahead_within],
        )
        dxw, dbc = results[:2]
        if layer == 0:
            dxw, dbc = near(*lax.optimization_barrier((dxw, dbc)))
            zo = [after(b, entered, dxw, *before_zo) for b in zo]
        fetched(ahead_within, results)
        results = run(
            kb_front, "back_front",
            [((t + 8, XC), f32, "v"), ((8, XC), f32, "a"), ((t, 128), bf16, "v"), ((40, XC), f32), ((16, 128), f32)],
            entered, d, v["c"], far["dec"], v["bc"], v["xdt"], v["act"], v["xb"], v["slope"], v["before"], v["dt"], v["cum"],
            dxw, dbc, dy, dca, par,
            scratch=[((2 * STATE, OWN), f32), ((t, OWN), f32), ((t, OWN), f32), ((t, OWN), f32), ((t, XC), f32),
                     ((t, 128), f32), ((t, 128), f32), ((16, OWN), f32), ((t + 16, 128), f32)],
            ahead=[v[k] for k in ahead_front],
        )
        dxb, halo, qdt, small_b, small_c = results[:5]
        fetched(ahead_front, results)
        ret = chain_step(halo, 1, True)
        dnz = run(kb_z_normed, "back_z", [((t, WIDTH), f32, "v")], near(after(qz, halo)), v["wz"])[0]
        return dxb, ret, qdt, dnz, zo, (small_a, small_b, small_c), v, (e, dbc, halo)

    shape_q, shape_n = ((t, XD), bf16, "v"), [((t, WIDTH), f32, "v"), ((t, WIDTH), bf16, "p")]
    x_blocks = [((WIDTH // count, XD), bf16, "a")] * count
    x_scratch = [((WIDTH, XD), bf16)]
    dxb, ret, qdt, dnz, zo1, small1, v1, _ = backward(1, saved[1], x["g"], st1, msg, x)
    got_zo1 = send_blocks(zo1)
    v0 = saved[0]
    early = []
    q, dn, dnb1, *fetched = run(
        kb_x_normed, "back_x", [shape_q, shape_n[0], ((t, WIDTH), bf16, "a")], dxb, ret, qdt, dnz, v1["wx"], ahead=[v0[k] for k in early]
    )
    v0.update(zip(early, fetched))
    dr = across(dnb1)
    shapes_x = [((2 * shard, CUT), bf16, "a"), ((2 * shard, XD - CUT), bf16, "a")] * 2
    x1 = run(
        kb_x_weight, "back_xw", shapes_x if count > 1 else [((WIDTH, XD), bf16, "a")], v1["normed"],
        near(after(q, dnb1, *got_zo1)), scratch=x_scratch, ahead=[*[v0[k] for k in AHEAD_WEIGHT], h1_far, pt],
    )
    *x1, h1_near, pt_near = x1
    v0.update(zip(AHEAD_WEIGHT, x1[-len(AHEAD_WEIGHT) :]))
    x1 = x1[: -len(AHEAD_WEIGHT)]
    got_x1 = [flip(x1[0], "seq", 1), flip(x1[1], "seq", 2)] if count > 1 else []

    def second_phase(*pins):
        if count == 1:
            return [[lax.psum_scatter(x1[0], "seq", scatter_dimension=0, tiled=True)]]
        own_a, own_b, give_a, give_b = run(
            k_phase, "phase", [((shard, CUT), bf16, "a"), ((shard, XD - CUT), bf16, "a")] * 2,
            after(x1[2], *pins), x1[3], *got_x1,
        )
        return [[own_a, flip(give_a, "seq", 2)], [own_b, flip(give_b, "seq", 1)]]

    phase = second_phase()
    early = AHEAD_NORM
    g0, g0_far, small_d1, rd0, *fetched = run(
        kb_norm, "back_norm", [((t, WIDTH), bf16, "vh"), ((8, WIDTH), f32), ((t, 128), f32, "v")],
        h1_near, dn, after(dr, *x1), saved[1]["g"], par1, pt_near, ahead=[v0[k] for k in early],
    )
    v0.update(zip(early, fetched))
    dxb, ret, qdt, dnz, zo0, small0, v0, (e0, dbc0, halo0) = backward(
        0, v0, g0, rs0, rd0, before_zw=phase[0][:1], before_zo=[p[-1] for p in phase]
    )
    got_zo0 = send_blocks(zo0)
    halves1 = halved([*phase, got_zo1], dbc0)
    over1 = [] if simple_dp() else [paired(halves1[0], flip(halves1[1], "dp", 1))]
    q, *x0 = run(kb_x_weight_first, "back_xw", [shape_q] + x_blocks, v0["normed"], dxb, after(ret, *over1, *got_zo0), qdt, scratch=x_scratch)
    got_x0 = send_blocks(x0)
    dn, dnb0 = run(kb_x_normed_last, "back_x", [shape_n[0], ((t, WIDTH), bf16, "a")], near(after(q, *x0)), dnz, v0["wx"])
    dr = across(dnb0)
    sum1 = further(over1, x0[0]) if over1 else summed_dp(*halves1)
    sum_zo0 = summed_dp(*halved([got_zo0], x0[0]))
    final = run(
        k_final, "final", [((length, half), bf16, "a"), ((length, half), bf16, "a")],
        h1_far, p1, st1_far, after(msg, dnb0),
    )
    hidden_out = both_sequences(*final)
    keep, give, small_d0 = run(
        kb_norm_last, "back_norm", [((length, half), bf16, "a"), ((length, half), bf16, "a"), ((8, WIDTH), f32)],
        saved[0]["h"], dn, dr, g0_far, par0, scratch=[((t, WIDTH), bf16)],
    )
    grad_in = both_sequences(keep, give)
    small = run(k_small, "small", [((2 * SMALL, XC), f32, "a")], *small0, small_d0, *small1, small_d1)[0]
    halves0 = halved([got_x0], final[0], keep, small)
    small = sum_small(small, ["seq"])
    first_small = small
    small, half_way = sum_small_dp(small)
    sum_x0 = summed_dp(*halves0, first_small, later=[half_way])
    sums = [*sum1, *sum_zo0, after(sum_x0[0], small), sum_x0[1]]
    heads = 2 * HEADS
    smalls = run(
        k_small_out, "small_out",
        [((1, WIDTH), f32, "a"), ((4, CONV), f32, "a"), ((1, CONV), f32, "a"), ((1, heads), f32, "a"), ((1, heads), f32, "a"), ((1, heads), f32, "a"),
         ((1, INNER), f32, "a")],
        small, across(small),
    )
    give = run(k_home, "home", [((shard, packed), bf16, "p")], *sums, scratch=[((shard, 2 * OWN), bf16), ((shard, XD), bf16)])[0]
    grad_w, grad_o = run(
        k_grads, "grads", [((shard, INNER + CONV + heads), f32, "a"), ((2 * shard, WIDTH), f32, "a")],
        *sums, across(give),
        scratch=[((shard, packed), bf16), ((shard, 2 * OWN), bf16), ((shard, XD), bf16)],
    )
    norm, taps, bias, dtb, rates, skips, gates = smalls
    return (hidden_out, grad_in, norm, grad_w[None], taps[None], bias, dtb, rates, skips, gates, grad_o[None])


def solution(mesh):
    by_section = P("section", None)
    rows = P("section", "seq", None)
    tokens = P("dp", "seq", None)
    taps = P("section", None, None)
    out = P("dp", "seq", "section")
    small = (by_section,) * 4
    return jax.shard_map(
        on_device,
        mesh=mesh,
        in_specs=(tokens, tokens, by_section, rows, taps, by_section, *small, rows),
        out_specs=(out, out, by_section, rows, taps, by_section, *small, rows),
        check_vma=False,
    )
```

```python
import functools

import jax
import jax.numpy as jnp
from jax import lax
from jax.experimental import pallas as pl
from jax.experimental.pallas import tpu as pltpu
from jax.sharding import PartitionSpec as P

HDIM = 64
STATE = 128
INNER = 1536
CONV = 1792
EPS = 1e-05
f32, bf16 = jnp.float32, jnp.bfloat16

WIDTH = 768
OWN = 768
HEADS = 12
XC = OWN + 2 * STATE
XD = XC + 128
R = 256
BLOCK = 256


def nn(a, b):
    return lax.dot_general(a, b, (((1,), (0,)), ((), ())), preferred_element_type=f32)


def nt(a, b):
    return lax.dot_general(a, b, (((1,), (1,)), ((), ())), preferred_element_type=f32)


def tn(a, b):
    return lax.dot_general(a, b, (((0,), (0,)), ((), ())), preferred_element_type=f32)


def loop(count, body):
    def step(k, carry):
        body(k)
        return carry

    lax.fori_loop(0, count, step, 0)


def at(k, size):
    return pl.ds(pl.multiple_of(k * size, size), size)


def iotas(shape):
    return lax.broadcasted_iota(jnp.int32, shape, 0), lax.broadcasted_iota(jnp.int32, shape, 1)


def spread_matrix(width, per):
    r, c = iotas((128, width))
    return jnp.where(((r & 15) == c // per) & (r < 48), 1.0, 0.0).astype(bf16)


def collect_matrix():
    r, c = iotas((OWN, 128))
    return jnp.where(((c & 15) == r // HDIM) & (c < 48), 1.0, 0.0).astype(bf16)


def thirds(v):
    high = v.astype(bf16).astype(f32)
    rest = v - high
    mid = rest.astype(bf16).astype(f32)
    lane = iotas(v.shape)[1]
    out = jnp.where(lane < 16, high, jnp.where(lane < 32, mid, rest - mid))
    return jnp.where(lane < 48, out, 0.0).astype(bf16)


def halves(v):
    high = v.astype(bf16)
    return high, (v - high.astype(f32)).astype(bf16)


def running_sum(v, backward=False):
    r, c = iotas((BLOCK, BLOCK))
    tri = jnp.where((c >= r) if backward else (r >= c), 1.0, 0.0).astype(bf16)
    high = v.astype(bf16)
    rest = v - high.astype(f32)
    mid = rest.astype(bf16)
    last = (rest - mid.astype(f32)).astype(bf16)
    return nn(tri, high) + nn(tri, mid) + nn(tri, last)


def sig(v):
    return 0.5 * jnp.tanh(0.5 * v) + 0.5


def softplus(v):
    e = jnp.exp(-jnp.abs(v))
    u = 1.0 + e
    small = u == 1.0
    return jnp.maximum(v, 0.0) + jnp.where(small, e, jnp.log(u) * e / jnp.where(small, 1.0, u - 1.0))


def fold(v):
    return jnp.sum(v.reshape(v.shape[0] // 8, 8, v.shape[1]), axis=0)


def copy_rows(dst, start, src, cols=None):
    rows = src.shape[0]
    step = next(k for k in (48, 32, 16, 8, rows) if rows % k == 0)

    def move(r):
        place = pl.ds(pl.multiple_of(start + r * step, 16), step)
        if cols is None:
            dst[place, :] = src[at(r, step), :]
        else:
            dst[place, :] = src[at(r, step), cols]

    loop(rows // step, move)


def place_rows(dst, parts, cols=None):
    if len(parts) == 1:
        return copy_rows(dst, 0, parts[0], cols)
    me = lax.axis_index("seq")
    rows = parts[0].shape[0]
    for k in range(min(len(parts), 4)):
        copy_rows(dst, (me ^ k) * rows, parts[k], cols)
    if len(parts) > 4:
        copy_rows(dst, (me ^ 3) * rows + rows // 2, parts[4], cols)


def on_core(body):
    me = lax.axis_index("section")
    for core in range(2):
        pl.when(me == core)(lambda core=core: body(core))


def exact(a, b):
    return lax.dot_general(
        a, b, (((1,), (0,)), ((), ())), preferred_element_type=f32, precision=lax.Precision.HIGHEST
    )


def stats_out(a, b):
    lane = iotas(a.shape)[1]
    v = jnp.where(lane < 64, a, b)
    high = v.astype(bf16).astype(f32)
    rest = v - high
    mid = rest.astype(bf16).astype(f32)
    l = lane & 63
    out = jnp.where(l < 16, high, jnp.where(l < 32, mid, rest - mid))
    return jnp.where(l < 48, out, 0.0).astype(bf16)


def stats_in(v):
    v = v.astype(f32)
    lane = iotas(v.shape)[1]
    a = jnp.sum(jnp.where(lane < 64, v, 0.0), axis=1, keepdims=True)
    b = jnp.sum(jnp.where(lane < 64, 0.0, v), axis=1, keepdims=True)
    return a * (1.0 / 16), b * (1.0 / 16)


class Copies:

    def __init__(self, pairs_in, pairs_ahead, pairs_out, sems_in, sems_out):
        self.waiting, self.ready, self.started, self.ahead = {}, {}, [], []
        for k, (far, near, whole) in enumerate(pairs_in):
            copy = pltpu.make_async_copy(far, near, sems_in.at[k])
            copy.start()
            self.waiting.setdefault(id(whole), []).append(copy)
        for k, (far, near) in enumerate(pairs_ahead):
            copy = pltpu.make_async_copy(far, near, sems_in.at[len(pairs_in) + k])
            copy.start()
            self.ahead.append(copy)
        for k, (far, near, whole) in enumerate(pairs_out):
            self.ready.setdefault(id(whole), []).append(pltpu.make_async_copy(near, far, sems_out.at[k]))

    def need(self, refs):
        for key in [id(r) for r in refs] if refs else list(self.waiting):
            for copy in self.waiting.pop(key, ()):
                copy.wait()

    def done(self, refs):
        for key in [id(r) for r in refs] if refs else list(self.ready):
            for copy in self.ready.pop(key, ()):
                copy.start()
                self.started.append(copy)


COPIES = []


def need(*refs):
    COPIES[-1].need(refs)


def done(*refs):
    COPIES[-1].done(refs)


FAR = []
NEAR = []


def near(*arrays):
    NEAR.extend(arrays)
    return arrays if len(arrays) > 1 else arrays[0]


def far_away(array):
    FAR.append(array)
    return array


def run(kernel, name, outs, *ins, scratch=(), ahead=(), stay=()):
    far, close = pl.BlockSpec(memory_space=pltpu.HBM), pl.BlockSpec(memory_space=pltpu.VMEM)
    loose = pl.BlockSpec(memory_space=pl.ANY)
    modes = [o[2] if len(o) > 2 else "h" for o in outs]
    units = [m for mode in modes for m in mode] + ["v"] * len(ahead) + ["h"] * len(stay)
    shapes, specs = [], []
    for (shape, dtype, *_), mode in zip(outs, modes):
        for m in mode:
            if m == "p":
                shapes += [jax.ShapeDtypeStruct((shape[0] // 2, *shape[1:]), dtype)] * 2
                specs += [loose] * 2
            else:
                space = dict(v=pltpu.VMEM, h=pltpu.HBM, a=jax.ShapeDtypeStruct)[m]
                shapes.append(space(shape, dtype))
                specs.append(dict(v=close, h=far, a=loose)[m])
    for a in ahead:
        shapes.append(pltpu.VMEM(a.shape, a.dtype))
        specs.append(close)
    for a in stay:
        shapes.append(pltpu.HBM(a.shape, a.dtype))
        specs.append(far)
    groups = [a if isinstance(a, (tuple, list)) else (a,) for a in (*ins, *ahead, *stay)]
    flat = [a for group in groups for a in group]
    held = [any(a is k for k in NEAR) for a in flat]
    kept = [any(a is k for k in FAR) for a in flat]
    flat = [
        pltpu.with_memory_space_constraint(a, pltpu.VMEM if h else pltpu.HBM) if h or k else a
        for a, h, k in zip(flat, held, kept)
    ]
    n_in, n_out, n_own = len(flat), len(shapes), sum(len(group) for group in groups[: len(ins)])
    buffers = [
        pltpu.VMEM((sum(a.shape[0] for a in group), *group[0].shape[1:]), group[0].dtype)
        for group in groups[: len(ins)]
        if not any(group[0] is k for k in NEAR)
    ]
    buffers += [pltpu.VMEM(shape, dtype) for (shape, dtype, *_), mode in zip(outs, modes) if "v" not in mode]

    def body(*refs):
        given, made, rest = list(refs[:n_in]), list(refs[n_in : n_in + n_out]), list(refs[n_in + n_out :])
        pairs_in, pairs_out, vin, vout = [], [], [], []
        pairs_ahead = list(zip(given[n_own:], made[n_out - len(ahead) - len(stay) :]))
        at_ref = 0
        for group in groups[: len(ins)]:
            if held[at_ref]:
                vin.append(given[at_ref])
            else:
                vin.append(rest.pop(0))
                start = 0
                for k, part in enumerate(group):
                    rows = part.shape[0]
                    place = vin[-1] if len(group) == 1 else vin[-1].at[pl.ds(start, rows)]
                    pairs_in.append((given[at_ref + k], place, vin[-1]))
                    start += rows
            at_ref += len(group)
        for mode in modes:
            vout.append(made.pop(0) if "v" in mode else rest.pop(0))
            if mode == "p":
                rows = vout[-1].shape[0] // 2
                for k in range(2):
                    pairs_out.append((made.pop(0), vout[-1].at[pl.ds(k * rows, rows)], vout[-1]))
            elif mode != "v":
                pairs_out.append((made.pop(0), vout[-1], vout[-1]))
        *extra, sems_in, sems_out = rest
        copies = Copies(pairs_in, pairs_ahead, pairs_out, sems_in, sems_out)
        COPIES.append(copies)
        kernel(*vin, *vout, *extra)
        need()
        done()
        for copy in [*copies.ahead, *copies.started]:
            copy.wait()
        COPIES.pop()

    results = list(
        pl.pallas_call(
            body,
            name=name,
            out_shape=shapes,
            in_specs=[close if h else far if k else loose for h, k in zip(held, kept)],
            out_specs=specs,
            scratch_shapes=[
                *buffers,
                *[pltpu.VMEM(s, d) for s, d in scratch],
                pltpu.SemaphoreType.DMA((max(n_in, 1),)),
                pltpu.SemaphoreType.DMA((max(n_out, 1),)),
            ],
            compiler_params=pltpu.CompilerParams(vmem_limit_bytes=MIB * 2**20),
            cost_estimate=pl.CostEstimate(flops=1, bytes_accessed=1, transcendentals=0),
        )(*flat)
    )
    grouped = []
    for unit in units:
        if unit == "p":
            grouped.append((results.pop(0), results.pop(0)))
            continue
        grouped.append(results.pop(0))
        if unit != "a":
            (NEAR if unit == "v" else FAR).append(grouped[-1])
    return grouped


MIB = 24


TAPS, BIAS, NORM, GATE, SKIP, STEP, RATE = 0, 4, 5, 6, 7, 8, 9
PARAMS = 16


def k_prep(hid_ref, cot_ref, w_ref, o_ref, ng_ref, cw_ref, cb_ref, db_ref, al_ref, sk_ref, gg_ref, hid_half, cot_half, mine_x, give_x, mine_zo, give_zo, mine_p, give_p):
    need()
    rows = w_ref.shape[0]
    half = WIDTH // 2
    r24, c24 = iotas((2 * HEADS, 128))
    rk, ck = iotas((2 * HEADS, OWN))

    def pack(core, out):
        own = core * OWN
        out[:, 0:OWN] = w_ref[:, INNER + own : INNER + own + OWN]
        out[:, OWN:XC] = w_ref[:, 2 * INNER : 2 * INNER + 2 * STATE]
        pick = ((c24 & 15) == r24 - core * HEADS) & (c24 < 48)
        steps = w_ref[:, INNER + CONV : INNER + CONV + 2 * HEADS]
        out[:, XC:XD] = nn(steps, jnp.where(pick, 1.0, 0.0).astype(bf16)).astype(bf16)

    def pack_rest(core, out, par):
        own = core * OWN
        pick = ((c24 & 15) == r24 - core * HEADS) & (c24 < 48)
        out[:, 0:OWN] = w_ref[:, own : own + OWN]
        for t in range(2):
            at_lane = OWN + t * half
            out[:, at_lane : at_lane + half] = o_ref[t * rows : (t + 1) * rows, core * half : (core + 1) * half]
        par[...] = jnp.zeros(par.shape, f32)
        par[TAPS : TAPS + 4, :OWN] = cw_ref[:, own : own + OWN]
        par[TAPS : TAPS + 4, OWN:] = cw_ref[:, INNER:]
        par[BIAS : BIAS + 1, :OWN] = cb_ref[:, own : own + OWN]
        par[BIAS : BIAS + 1, OWN:] = cb_ref[:, INNER:]
        par[NORM : NORM + 1, :WIDTH] = ng_ref[...]
        par[GATE : GATE + 1, :OWN] = gg_ref[:, own : own + OWN]
        spread = jnp.where(rk - core * HEADS == ck // HDIM, 1.0, 0.0)
        par[SKIP : SKIP + 1, :OWN] = exact(jnp.broadcast_to(sk_ref[...], (8, 2 * HEADS)), spread)[0:1]
        lanes = jnp.where(pick, 1.0, 0.0)
        par[STEP : STEP + 1, 0:128] = exact(jnp.broadcast_to(db_ref[...], (8, 2 * HEADS)), lanes)[0:1]
        par[RATE : RATE + 1, 0:128] = exact(jnp.broadcast_to(al_ref[...], (8, 2 * HEADS)), lanes)[0:1]

    def body(core):
        pack(core, mine_x)
        pack(1 - core, give_x)

    def rest(core):
        pack_rest(core, mine_zo, mine_p)
        pack_rest(1 - core, give_zo, give_p)

    on_core(body)
    done(mine_x, give_x)
    even_seq = 1 - lax.rem(lax.axis_index("seq"), 2)
    rows_half = hid_half.shape[0]
    start = lax.axis_index("section") * rows_half
    for src, dst in ((hid_ref, hid_half), (cot_ref, cot_half)):

        def move(r, src=src, dst=dst):
            dst[at(r, 32), :] = src[even_seq, pl.ds(pl.multiple_of(start + r * 32, 32), 32), :]

        loop(rows_half // 32, move)
        done(dst)
    on_core(rest)


def k_pick(mine_x, got_x, mine_p, got_p, x0, x1, p0, p1):
    need()

    def body(core):
        for layer, (x, p) in enumerate(((x0, p0), (x1, p1))):
            x[...] = (mine_x, got_x)[layer ^ core][...]
            p[...] = (mine_p, got_p)[layer ^ core][...]

    on_core(body)


def k_pick_rest(mine_zo, got_zo, zo0, zo1):
    need()

    def body(core):
        zo0[...] = (mine_zo, got_zo)[core][...]
        zo1[...] = (mine_zo, got_zo)[1 - core][...]

    on_core(body)


def norm_rows(h, gain):
    scale = lax.rsqrt(jnp.mean(h * h, axis=1, keepdims=True) + EPS)
    return (h * scale * gain).astype(bf16)


def project(t, normed_ref, wx_ref, xb_ref, tail_ref):
    xb_ref[0:8, :] = jnp.zeros((8, XD), f32)

    def cols(c):
        xb_ref[8 : 8 + t, at(c, 384)] = nn(normed_ref[...], wx_ref[:, at(c, 384)])

    loop(XD // 384, cols)
    tail_ref[...] = xb_ref[t:, :XC]


def k_in(hid_ref, ga_ref, gb_ref, par_ref, *rest):
    *parts, h_ref, normed_ref, xb_ref, wx_ref, tail_ref = rest
    need(hid_ref, ga_ref, gb_ref, par_ref)
    t = h_ref.shape[0]
    half = t // 2
    odd = lax.rem(lax.axis_index("seq"), 2)
    core = lax.axis_index("section")
    copy_rows(h_ref, odd * half, hid_ref.at[odd])
    copy_rows(h_ref, (1 - odd) * half + core * (half // 2), ga_ref)
    copy_rows(h_ref, (1 - odd) * half + (1 - core) * (half // 2), gb_ref)

    def rows(r):
        normed_ref[at(r, R), :] = norm_rows(h_ref[at(r, R), :].astype(f32), par_ref[NORM : NORM + 1, :WIDTH])

    loop(t // R, rows)
    done(h_ref, normed_ref)
    need(*parts)
    place_rows(wx_ref, parts)
    done(wx_ref)
    project(t, normed_ref, wx_ref, xb_ref, tail_ref)


def k_mid(h_ref, p_ref, st_ref, msg_ref, par_ref, *rest):
    *parts, h1_ref, pt_ref, rs_ref, normed_ref, xb_ref, wx_ref, tail_ref = rest
    need(h_ref, p_ref, st_ref, msg_ref, par_ref)
    t = h_ref.shape[0]

    def rows(r):
        s = at(r, R)
        other = stats_in(msg_ref[s, WIDTH:])[0]
        rs = lax.rsqrt((st_ref[s, 0:128] + other) * (1.0 / INNER) + EPS)
        rs_ref[s, :] = rs
        p = p_ref[s, :] + msg_ref[s, :WIDTH].astype(f32)
        pt_ref[s, :] = p
        h1 = (h_ref[s, :].astype(f32) + rs[:, 0:1] * p).astype(bf16)
        h1_ref[s, :] = h1
        normed_ref[s, :] = norm_rows(h1.astype(f32), par_ref[NORM : NORM + 1, :WIDTH])

    loop(t // R, rows)
    done(h1_ref, pt_ref, rs_ref, normed_ref)
    need(*parts)
    place_rows(wx_ref, parts)
    done(wx_ref)
    project(t, normed_ref, wx_ref, xb_ref, tail_ref)


def k_z(normed_ref, *rest):
    *parts, z_ref, wz_ref, keep_ref, give_ref, o = rest
    need(*parts)
    place_rows(wz_ref, parts, slice(0, OWN))
    done(wz_ref)
    place_rows(o, parts, slice(OWN, 2 * OWN))

    def split(core):
        rows = keep_ref.shape[0]
        keep_ref[...] = o[core * rows : (core + 1) * rows, :]
        give_ref[...] = o[(1 - core) * rows : (2 - core) * rows, :]

    on_core(split)
    done(keep_ref, give_ref)
    need(normed_ref)

    def cols(c):
        z_ref[:, at(c, 384)] = nn(normed_ref[...], wz_ref[:, at(c, 384)])

    loop(OWN // 384, cols)


def k_front(xb_ref, before_ref, par_ref, act_ref, slope_ref, bc_ref, xdt_ref, dt_ref, cum_ref, s_ref, dec_ref, tot_ref, wide, edge):
    t = act_ref.shape[0]
    need()
    edge[0:8, :] = before_ref[...]
    edge[8:16, :] = jnp.zeros((8, XC), f32)

    def conv(c):
        cols = at(c, 128)
        w = par_ref[0:8, cols]
        total = w[4:5] + w[0:1] * xb_ref[pl.ds(5, t), cols]
        for k in range(1, 4):
            total = total + w[k : k + 1] * xb_ref[pl.ds(5 + k, t), cols]
        first = total[0:8]
        for k in range(4):
            first = first + w[k : k + 1] * edge[5 + k : 13 + k, cols]
        total = jnp.concatenate([first, total[8:]], axis=0)
        sg = sig(total)
        act = total * sg
        act_ref[:, cols] = act
        slope_ref[:, cols] = (sg + act * (1.0 - sg)).astype(bf16)

    loop(XC // 128, conv)
    bc_ref[...] = act_ref[:, OWN:].astype(bf16)
    done(act_ref, slope_ref, bc_ref)
    dt = softplus(xb_ref[8 : 8 + t, XC:] + par_ref[STEP : STEP + 1, 0:128])
    dt_ref[...] = dt
    done(dt_ref)
    rate = -jnp.exp(par_ref[RATE : RATE + 1, 0:128])
    spread = spread_matrix(OWN, HDIM)
    wide[...] = nn(thirds(dt), spread)

    def rows(r):
        s = at(r, R)
        xdt_ref[s, :] = (act_ref[s, :OWN] * wide[s, :]).astype(bf16)

    loop(t // R, rows)
    done(xdt_ref)
    for b in range(t // BLOCK):
        s = pl.ds(b * BLOCK, BLOCK)
        cum = running_sum(rate * dt[b * BLOCK : (b + 1) * BLOCK])
        cum_ref[s, :] = cum
        end = cum[BLOCK - 1 : BLOCK, :]
        dec_ref[8 * b : 8 * b + 8, :] = nn(thirds(jnp.exp(jnp.broadcast_to(end, (8, 128)))), spread)
        wide[s, :] = nn(thirds(jnp.exp(end - cum)), spread)
        bl = bc_ref[s, 0:STATE]

        def cols(c):
            decayed = (xdt_ref[s, at(c, 256)].astype(f32) * wide[s, at(c, 256)]).astype(bf16)
            s_ref[pl.ds(b * STATE, STATE), at(c, 256)] = tn(bl, decayed)

        loop(OWN // 256, cols)
    tot_ref[...] = (s_ref[STATE:, :] + dec_ref[8:9, :] * s_ref[:STATE, :]).astype(bf16)


def decay_tables(cum_ref, tall, flat):
    t = cum_ref.shape[0]
    parts = thirds(cum_ref[...])
    tall[...] = nn(parts, spread_matrix(HEADS * 128, 128))
    r, c = iotas((HEADS * 8, 128))
    pick = jnp.where(((c & 15) == r // 8) & (c < 48), 1.0, 0.0).astype(bf16)
    for b in range(t // 128):
        flat[b] = nt(pick, parts[b * 128 : (b + 1) * 128])


def k_within(cum_ref, bc_ref, xdt_ref, y_ref, tall, flat, scores):
    t = cum_ref.shape[0]
    need(cum_ref)
    decay_tables(cum_ref, tall, flat)
    blocks = t // BLOCK
    need(bc_ref, xdt_ref)
    for b in range(blocks):
        s = pl.ds(b * BLOCK, BLOCK)
        scores[s, :] = nt(bc_ref[s, STATE:], bc_ref[s, 0:STATE])
    r, c = iotas((128, 128))
    causal = r >= c
    lane = iotas((BLOCK, 128))[1]

    def pair(p):
        cols = at(p, 128)
        for b in range(blocks):
            o = b * BLOCK
            u = xdt_ref[pl.ds(o, BLOCK), cols]
            top = jnp.zeros((128, 128), f32)
            low = jnp.zeros((128, 128), f32)
            for a in range(2):
                head = 2 * p + a
                own = jnp.where((lane >= 64) == (a == 1), u, jnp.zeros_like(u))
                hc = at(head, 128)
                hr = pl.ds(pl.multiple_of(head * 8, 8), 8)
                t0, t1 = tall[pl.ds(o, 128), hc], tall[pl.ds(o + 128, 128), hc]
                u0, u1 = flat[2 * b, hr, :][0:1], flat[2 * b + 1, hr, :][0:1]
                sc = scores
                w00 = jnp.where(causal, sc[pl.ds(o, 128), 0:128] * jnp.exp(jnp.where(causal, t0 - u0, 0.0)), 0.0)
                w10 = sc[pl.ds(o + 128, 128), 0:128] * jnp.exp(t1 - u0)
                w11 = jnp.where(causal, sc[pl.ds(o + 128, 128), 128:] * jnp.exp(jnp.where(causal, t1 - u1, 0.0)), 0.0)
                top = top + nn(w00.astype(bf16), own[:128])
                low = low + nn(w10.astype(bf16), own[:128]) + nn(w11.astype(bf16), own[128:])
            y_ref[pl.ds(o, 128), cols] = top
            y_ref[pl.ds(o + 128, 128), cols] = low

    loop(OWN // 128, pair)


def k_out(first_layer, yw_ref, act_ref, bc_ref, cum_ref, cin_ref, s_ref, dec_ref, z_ref, par_ref, keep_ref, got_ref, *rest):
    if first_layer:
        y_ref, p_ref, msg_ref, st_ref, c_ref, wo_ref, wide, u_ref = rest
    else:
        cot_ref, ca_ref, cb_ref, y_ref, p_ref, msg_ref, st_ref, c_ref, wo_ref, g_ref, wide, u_ref = rest
    t = yw_ref.shape[0]
    half = WIDTH // 2
    shard = o_rows(keep_ref)

    def weights(core):
        for r in range(keep_ref.shape[0] // shard):
            for k in range(2):
                for src, side in ((keep_ref, core), (got_ref, 1 - core)):
                    wo_ref[(2 * r + k) * shard : (2 * r + k + 1) * shard, side * half : (side + 1) * half] = src[
                        r * shard : (r + 1) * shard, k * half : (k + 1) * half
                    ]

    need(keep_ref, got_ref)
    on_core(weights)
    done(wo_ref)
    need(bc_ref, cum_ref, cin_ref, s_ref, dec_ref)
    c_ref[0:STATE, :] = cin_ref[...].astype(f32)
    c_ref[STATE:, :] = s_ref[:STATE, :] + dec_ref[0:1, :] * c_ref[0:STATE, :]
    wide[...] = nn(thirds(jnp.exp(cum_ref[...])), spread_matrix(OWN, HDIM))
    for b in range(t // BLOCK):
        s = pl.ds(b * BLOCK, BLOCK)

        def cols(c):
            from_state = nn(bc_ref[s, STATE:], c_ref[pl.ds(b * STATE, STATE), at(c, 256)].astype(bf16))
            wide[s, at(c, 256)] = wide[s, at(c, 256)] * from_state

        loop(OWN // 256, cols)

    done(c_ref)
    need(yw_ref, act_ref, z_ref, par_ref)

    def rows(r):
        s = at(r, R)
        y = yw_ref[s, :] + wide[s, :] + par_ref[SKIP : SKIP + 1, :OWN] * act_ref[s, :OWN]
        y_ref[s, :] = y
        z = z_ref[s, :]
        gated = y * z * sig(z)
        u_ref[s, :] = (gated * par_ref[GATE : GATE + 1, :OWN]).astype(bf16)
        st_ref[s, 0:128] = jnp.broadcast_to(jnp.sum(gated * gated, axis=1, keepdims=True), (R, 128))

    loop(t // R, rows)
    done(y_ref)

    def project_out(c):
        p_ref[:, at(c, 256)] = nn(u_ref[...], wo_ref[:, at(c, 256)])

    loop(WIDTH // 256, project_out)
    done(p_ref)
    if first_layer:

        def send(r):
            s = at(r, R)
            msg_ref[s, :WIDTH] = p_ref[s, :].astype(bf16)
            v = st_ref[s, 0:128]
            msg_ref[s, WIDTH:] = stats_out(v, v)

        loop(t // R, send)
    else:
        odd = lax.rem(lax.axis_index("seq"), 2)
        need(cot_ref, ca_ref, cb_ref)
        copy_rows(g_ref, odd * (t // 2), cot_ref.at[odd])
        core = lax.axis_index("section")
        copy_rows(g_ref, (1 - odd) * (t // 2) + core * (t // 4), ca_ref)
        copy_rows(g_ref, (1 - odd) * (t // 2) + (1 - core) * (t // 4), cb_ref)
        done(g_ref)

        def dots(r):
            s = at(r, R)
            d = jnp.sum(p_ref[s, :] * g_ref[s, :].astype(f32), axis=1, keepdims=True)
            d = jnp.broadcast_to(d, (R, 128))
            st_ref[s, 128:256] = d
            msg_ref[s, half:] = stats_out(st_ref[s, 0:128], d)

        loop(t // R, dots)

        def send(core):
            msg_ref[:, :half] = p_ref[:, (1 - core) * half : (2 - core) * half].astype(bf16)

        on_core(send)


def o_rows(keep_ref):
    return keep_ref.shape[0] // (lax.axis_size("seq") // 2)


def k_final(h_ref, p_ref, st_ref, msg_ref, keep_ref, give_ref):
    need()
    half = WIDTH // 2
    rows_each = keep_ref.shape[0]
    odd = lax.rem(lax.axis_index("seq"), 2)

    def body(core):
        cols = slice(core * half, (core + 1) * half)

        def half_out(dst, start):
            def rows(r):
                s = pl.ds(pl.multiple_of(start + r * R, R), R)
                other = stats_in(msg_ref[s, half:])[0]
                rs = lax.rsqrt((st_ref[s, 0:1] + other) * (1.0 / INNER) + EPS)
                p = p_ref[s, cols] + msg_ref[s, :half].astype(f32)
                dst[at(r, R), :] = (h_ref[s, cols].astype(f32) + rs * p).astype(bf16)

            loop(rows_each // R, rows)

        half_out(keep_ref, odd * rows_each)
        half_out(give_ref, (1 - odd) * rows_each)

    on_core(body)


def kb_gate(g_ref, w_ref, y_ref, yw_ref, z_ref, act_ref, bc_ref, cum_ref, rs_ref, rd_ref, par_ref, dec_ref,
            qz_ref, dy_ref, df_ref, dca_ref, keep_ref, give_ref, d_ref, e_ref, small_ref, dgn, wide, gn):
    t = g_ref.shape[0]
    need(g_ref, w_ref)

    def back(c):
        dgn[:, at(c, 256)] = nt(g_ref[...], w_ref[at(c, 256), :])

    loop(OWN // 256, back)
    need(cum_ref)
    wide[...] = nn(thirds(jnp.exp(cum_ref[...])), spread_matrix(OWN, HDIM))
    small_ref[...] = jnp.zeros(small_ref.shape, f32)
    collect = collect_matrix()
    need()

    def rows(r):
        s = at(r, R)
        z, y, d, x = z_ref[s, :], y_ref[s, :], dgn[s, :], act_ref[s, :OWN]
        gg = par_ref[GATE : GATE + 1, :OWN]
        if rs_ref.shape[1] == 128:
            rs, rd = rs_ref[s, 0:1], rd_ref[s, 0:1]
        else:
            squares, dots = stats_in(rd_ref[s, WIDTH // 2 :])
            rs = lax.rsqrt((rs_ref[s, 0:1] + squares) * (1.0 / INNER) + EPS)
            rd = rs_ref[s, 128:129] + dots
        sg = sig(z)
        sz = z * sg
        gated = y * sz
        scaled = gated * rs
        small_ref[0:8, :] += fold(d * scaled)
        gn[s, :] = (scaled * gg).astype(bf16)
        dgated = rs * (gg * d) - gated * (rs * rs * rs * rd * (1.0 / INNER))
        dy = dgated * sz
        dy_ref[s, :] = dy
        qz_ref[s, :] = (dgated * y * (sg * (1.0 + z - sz))).astype(bf16)
        small_ref[8:16, :] += fold(dy * x)
        df_ref[s, :] = (wide[s, :] * dy).astype(bf16)
        yw = yw_ref[s, :]
        high, low = halves(dy.astype(bf16).astype(f32) * yw + dy * (y - yw - par_ref[SKIP : SKIP + 1, :OWN] * x))
        sums = nn(jnp.concatenate([high, low], axis=0), collect)
        dca_ref[s, :] = sums[:R] + sums[R:]

    loop(t // R, rows)
    done(dy_ref, qz_ref, df_ref, dca_ref, small_ref)
    for b in range(t // BLOCK):
        s = pl.ds(b * BLOCK, BLOCK)
        cl = bc_ref[s, STATE:]

        def cols(c):
            d_ref[pl.ds(b * STATE, STATE), at(c, 256)] = tn(cl, df_ref[s, at(c, 256)])

        loop(OWN // 256, cols)
    e_ref[...] = (d_ref[:STATE, :] + dec_ref[0:1, :] * d_ref[STATE:, :]).astype(bf16)

    done(d_ref, e_ref)
    half = WIDTH // 2

    def halves_of(core):
        def weight(c):
            dw = tn(gn[:, at(c, 256)], g_ref[...]).astype(bf16)
            keep_ref[at(c, 256), :] = dw[:, core * half : (core + 1) * half]
            give_ref[at(c, 256), :] = dw[:, (1 - core) * half : (2 - core) * half]

        loop(OWN // 256, weight)

    on_core(halves_of)


def kb_within(dy_ref, xdt_ref, cum_ref, bc_ref, df_ref, c_ref, dx_ref, dbc_ref, tall, flat, scores, ds):
    t = cum_ref.shape[0]
    need(cum_ref)
    decay_tables(cum_ref, tall, flat)
    blocks = t // BLOCK
    need(bc_ref, xdt_ref, dy_ref)
    for b in range(blocks):
        s = pl.ds(b * BLOCK, BLOCK)
        scores[s, :] = nt(bc_ref[s, STATE:], bc_ref[s, 0:STATE])
    ds[...] = jnp.zeros(ds.shape, f32)
    r, c = iotas((128, 128))
    causal = r >= c
    lane = iotas((BLOCK, 128))[1]

    def pair(p):
        cols = at(p, 128)
        for b in range(blocks):
            o = b * BLOCK
            u = xdt_ref[pl.ds(o, BLOCK), cols]
            g = dy_ref[pl.ds(o, BLOCK), cols].astype(bf16)
            top = jnp.zeros((128, 128), f32)
            low = jnp.zeros((128, 128), f32)
            for a in range(2):
                head = 2 * p + a
                own = jnp.where((lane >= 64) == (a == 1), g, jnp.zeros_like(g))
                hc = at(head, 128)
                hr = pl.ds(pl.multiple_of(head * 8, 8), 8)
                t0, t1 = tall[pl.ds(o, 128), hc], tall[pl.ds(o + 128, 128), hc]
                u0, u1 = flat[2 * b, hr, :][0:1], flat[2 * b + 1, hr, :][0:1]
                e00 = jnp.where(causal, jnp.exp(jnp.where(causal, t0 - u0, 0.0)), 0.0)
                e10 = jnp.exp(t1 - u0)
                e11 = jnp.where(causal, jnp.exp(jnp.where(causal, t1 - u1, 0.0)), 0.0)
                q0, q1 = pl.ds(o, 128), pl.ds(o + 128, 128)
                w00 = (scores[q0, 0:128] * e00).astype(bf16)
                w10 = (scores[q1, 0:128] * e10).astype(bf16)
                w11 = (scores[q1, 128:] * e11).astype(bf16)
                top = top + tn(w00, own[:128]) + tn(w10, own[128:])
                low = low + tn(w11, own[128:])
                ds[q0, 0:128] += nt(own[:128], u[:128]) * e00
                ds[q1, 0:128] += nt(own[128:], u[:128]) * e10
                ds[q1, 128:] += nt(own[128:], u[128:]) * e11
            dx_ref[pl.ds(o, 128), cols] = top
            dx_ref[pl.ds(o + 128, 128), cols] = low

    loop(OWN // 128, pair)
    done(dx_ref)
    need(df_ref, c_ref)
    for b in range(blocks):
        s = pl.ds(b * BLOCK, BLOCK)
        d = ds[s, :].astype(bf16)
        carried = c_ref[pl.ds(b * STATE, STATE), :].astype(bf16)
        dbc_ref[s, 0:STATE] = tn(d, bc_ref[s, STATE:])
        dbc_ref[s, STATE:] = nn(d, bc_ref[s, 0:STATE]) + nt(df_ref[s, :], carried)


def kb_front(gin_ref, d_ref, c_ref, dec_ref, bc_ref, xdt_ref, act_ref, xb_ref, slope_ref, before_ref, dt_ref, cum_ref, dxw_ref, dbc_ref,
             dy_ref, dca_ref, par_ref,
             dxb_ref, halo_ref, qdt_ref, small_ref, head_ref, gs, dd, te, dtw, dact, red, red2, ends, pad):
    t = act_ref.shape[0]
    blocks = t // BLOCK
    spread, collect = spread_matrix(OWN, HDIM), collect_matrix()
    need(gin_ref, d_ref, dec_ref)
    gs[STATE:, :] = gin_ref[...].astype(f32)
    gs[:STATE, :] = d_ref[STATE:, :] + dec_ref[8:9, :] * gs[STATE:, :]
    need(dbc_ref, dt_ref, c_ref, cum_ref, bc_ref, xdt_ref)
    dact[:, OWN:] = dbc_ref[...]
    dtw[...] = nn(thirds(dt_ref[...]), spread)
    for b in range(blocks):
        s = pl.ds(b * BLOCK, BLOCK)
        ss = pl.ds(b * STATE, STATE)
        end = cum_ref[pl.ds((b + 1) * BLOCK - 8, 8), :][7:8]
        te[s, :] = nn(thirds(jnp.exp(end - cum_ref[s, :])), spread)
        bl = bc_ref[s, 0:STATE]
        ends[8 * b : 8 * b + 8, :] = fold(gs[ss, :] * c_ref[ss, :]) * dec_ref[8 * b : 8 * b + 8, :]

        def cols(c):
            q = at(c, 256)
            low = gs[ss, q].astype(bf16)
            dd[s, q] = nn(bl, low)
            decayed = (xdt_ref[s, q].astype(f32) * te[s, q]).astype(bf16)
            dact[s, OWN : OWN + STATE] += nt(decayed, low)

        loop(OWN // 256, cols)
        if b == 0:
            need(dxw_ref, dy_ref, act_ref, par_ref)

        def rows(r):
            q = pl.ds(pl.multiple_of(b * BLOCK + r * R, R), R)
            w = dd[q, :] * te[q, :]
            ends[8 * b : 8 * b + 8, :] += fold(w * xdt_ref[q, :].astype(f32))
            dxdt = dxw_ref[q, :] + w
            dact[q, :OWN] = dxdt * dtw[q, :] + par_ref[SKIP : SKIP + 1, :OWN] * dy_ref[q, :]
            parts = [(dxdt * act_ref[q, :OWN]).astype(bf16), *halves(dxdt * xdt_ref[q, :].astype(f32))]
            sums = nn(jnp.concatenate(parts, axis=0), collect)
            red[q, :] = sums[:R]
            red2[q, :] = sums[R : 2 * R] + sums[2 * R :]

        loop(BLOCK // R, rows)
    need()
    high, low = halves(ends[...])
    at_end = nn(high, collect) + nn(low, collect)
    rate = -jnp.exp(par_ref[RATE : RATE + 1, 0:128])
    head_ref[...] = jnp.zeros(head_ref.shape, f32)
    for b in range(blocks):
        s = pl.ds(b * BLOCK, BLOCK)
        dt = dt_ref[s, :]
        total = running_sum(dca_ref[s, :] - red2[s, :], True)
        total = total + jnp.sum(at_end[8 * b : 8 * b + 8], axis=0, keepdims=True)
        ddt = red[s, :] + rate * total
        raw = xb_ref[pl.ds(8 + b * BLOCK, BLOCK), XC:] + par_ref[STEP : STEP + 1, 0:128]
        draw = ddt * jax.nn.sigmoid(raw)
        head_ref[0:8, :] += fold(draw)
        head_ref[8:16, :] += fold(rate * dt * total)
        lane = iotas(draw.shape)[1]
        qdt_ref[s, :] = jnp.where(lane < HEADS, draw, 0.0).astype(bf16)
    done(qdt_ref, head_ref)
    pad[0:8, :] = jnp.zeros((8, 128), f32)
    pad[8 + t :, :] = jnp.zeros((8, 128), f32)

    def conv(c):
        cols = at(c, 128)
        w = par_ref[0:8, cols]
        d = dact[:, cols] * slope_ref[:, cols].astype(f32)
        pad[8 : 8 + t, :] = d
        small_ref[32:40, cols] = fold(d)
        xb, before = xb_ref[:, cols], before_ref[:, cols]
        out = 0.0
        for k in range(4):
            later = pad[3 - k : 11 - k + t, :]
            out = out + w[k : k + 1] * later
            small_ref[8 * k : 8 * k + 8, cols] = fold(later * xb) + later[0:8] * before
        dxb_ref[:, cols] = out
        halo_ref[:, cols] = out[0:8]

    loop(XC // 128, conv)


def z_weight(dw_ref, first, normed_ref, qz_ref, okeep_ref, ogot_ref):
    def weight(c):
        dw_ref[at(c, 256), first : first + OWN] = tn(normed_ref[:, at(c, 256)], qz_ref[...]).astype(bf16)

    loop(WIDTH // 256, weight)
    n = lax.axis_size("seq")
    shard, half = WIDTH // n, WIDTH // 2
    need()

    def out(core):
        for j in range(n):
            src = okeep_ref if j // (n // 2) == core else ogot_ref
            for k in range(2):
                row, col = (2 * (j % (n // 2)) + k) * shard, first + OWN + k * half
                dw_ref[j * shard : (j + 1) * shard, col : col + half] = src[row : row + shard, :]

    on_core(out)


def kb_z_weight(normed_ref, qz_ref, okeep_ref, ogot_ref, *rest):
    *blocks, dw_ref = rest
    need(normed_ref, qz_ref)
    z_weight(dw_ref, 0, normed_ref, qz_ref, okeep_ref, ogot_ref)
    to_blocks(blocks, dw_ref)


CUT = 640


def kb_x_weight(normed_ref, q_ref, *rest):
    *parts, dw_ref = rest
    need()
    x_weight(normed_ref, q_ref, dw_ref)
    if len(parts) == 1:
        return copy_rows(parts[0], 0, dw_ref)
    me = lax.axis_index("seq")
    rows = WIDTH // 4
    first, last = slice(0, CUT), slice(CUT, XD)
    for ref, cols, ranks in zip(parts, (first, last, first, last), ((1, 3), (2, 3), (0, 2), (0, 1))):
        for k, bits in enumerate(ranks):
            start = (me ^ bits) * rows

            def move(r, ref=ref, cols=cols, k=k, start=start):
                ref[pl.ds(pl.multiple_of(k * rows + r * 48, 16), 48), :] = dw_ref[
                    pl.ds(pl.multiple_of(start + r * 48, 16), 48), cols
                ]

            loop(rows // 48, move)
        done(ref)


def k_phase(keep_a, keep_b, got_a, got_b, own_a, own_b, give_a, give_b):
    need()
    rows = own_a.shape[0]
    for keep, got, own, give in ((keep_a, got_a, own_a, give_a), (keep_b, got_b, own_b, give_b)):
        for dst, start in ((give, rows), (own, 0)):

            def move(r, keep=keep, got=got, dst=dst, start=start):
                s = pl.ds(pl.multiple_of(start + r * 48, 16), 48)
                dst[at(r, 48), :] = (keep[s, :].astype(f32) + got[s, :].astype(f32)).astype(bf16)

            loop(rows // 48, move)
            done(dst)


def to_blocks(blocks, dw):
    if len(blocks) == 1:
        return copy_rows(blocks[0], 0, dw)
    me = lax.axis_index("seq")
    rows = blocks[0].shape[0]
    for k in reversed(range(len(blocks))):
        block, start = blocks[k], (me ^ k) * rows

        def move(r, block=block, start=start):
            block[at(r, 48), :] = dw[pl.ds(pl.multiple_of(start + r * 48, 16), 48), :]

        loop(rows // 48, move)
        done(block)


def kb_z_normed(qz_ref, w_ref, dn_ref):
    need()

    def back(c):
        dn_ref[:, at(c, 256)] = nt(qz_ref[...], w_ref[at(c, 256), :])

    loop(WIDTH // 256, back)


def make_q(dxb_ref, ret_ref, qdt_ref, q):
    t = q.shape[0]

    def rows(r):
        q[at(r, R), :XC] = dxb_ref[pl.ds(pl.multiple_of(r * R, R) + 8, R), :].astype(bf16)

    loop(t // R, rows)
    q[t - 16 :, :XC] = (
        dxb_ref[t - 8 : t + 8, :] + jnp.concatenate([jnp.zeros((8, XC), f32), ret_ref[...]], axis=0)
    ).astype(bf16)
    q[:, XC:] = qdt_ref[...]


def x_normed(q_ref, dnz_ref, w_ref, dn_ref, dnb_ref):
    def back(c):
        cols = at(c, 256)
        d = dnz_ref[:, cols] + nt(q_ref[...], w_ref[cols, :])
        dn_ref[:, cols] = d
        dnb_ref[:, cols] = d.astype(bf16)

    loop(WIDTH // 256, back)


def x_weight(normed_ref, q_ref, dw_ref):
    def weight(c):
        dw_ref[at(c, 256), :] = tn(normed_ref[:, at(c, 256)], q_ref[...]).astype(bf16)

    loop(WIDTH // 256, weight)


def kb_x_normed(dxb_ref, ret_ref, qdt_ref, dnz_ref, w_ref, q_ref, dn_ref, dnb_ref):
    need(dxb_ref, ret_ref, qdt_ref)
    make_q(dxb_ref, ret_ref, qdt_ref, q_ref)
    done(q_ref)
    need()
    x_normed(q_ref, dnz_ref, w_ref, dn_ref, dnb_ref)


def kb_x_weight_first(normed_ref, dxb_ref, ret_ref, qdt_ref, q_ref, *rest):
    *blocks, dw = rest
    need()
    make_q(dxb_ref, ret_ref, qdt_ref, q_ref)
    done(q_ref)
    x_weight(normed_ref, q_ref, dw)
    to_blocks(blocks, dw)


def kb_x_normed_last(q_ref, dnz_ref, w_ref, dn_ref, dnb_ref):
    need()
    x_normed(q_ref, dnz_ref, w_ref, dn_ref, dnb_ref)


def kb_norm(h_ref, dn_ref, dr_ref, g_ref, par_ref, pt_ref, gh_ref, small_ref, rd_ref):
    t = h_ref.shape[0]
    need()
    small_ref[...] = jnp.zeros(small_ref.shape, f32)

    def rows(r):
        s = at(r, R)
        h = h_ref[s, :].astype(f32)
        d = dn_ref[s, :] + dr_ref[s, :].astype(f32)
        scale = lax.rsqrt(jnp.mean(h * h, axis=1, keepdims=True) + EPS)
        hs = h * scale
        small_ref[...] += fold(d * hs)
        gd = par_ref[NORM : NORM + 1, :WIDTH] * d
        back = scale * (gd - hs * jnp.mean(hs * gd, axis=1, keepdims=True))
        gh = (g_ref[s, :].astype(f32) + back).astype(bf16)
        gh_ref[s, :] = gh
        if rd_ref is not None:
            dot = jnp.sum(gh.astype(f32) * pt_ref[s, :], axis=1, keepdims=True)
            rd_ref[s, :] = jnp.broadcast_to(dot, (R, 128))

    loop(t // R, rows)


def kb_norm_last(h_ref, dn_ref, dr_ref, g_ref, par_ref, keep_ref, give_ref, small_ref, gh):
    kb_norm(h_ref, dn_ref, dr_ref, g_ref, par_ref, None, gh, small_ref, None)
    half = WIDTH // 2
    each = keep_ref.shape[0]
    odd = lax.rem(lax.axis_index("seq"), 2)

    def body(core):
        def rows(r):
            for dst, start in ((keep_ref, odd * each), (give_ref, (1 - odd) * each)):
                s = pl.ds(pl.multiple_of(start + r * R, R), R)
                dst[at(r, R), :] = gh[s, core * half : (core + 1) * half]

        loop(each // R, rows)

    on_core(body)


SMALL = 12


def k_small(*refs):
    *ins, out = refs
    need()
    out[...] = jnp.zeros(out.shape, f32)

    def total(x):
        return jnp.sum(x, axis=0, keepdims=True)

    for layer in range(2):
        a, b, c, d = ins[4 * layer : 4 * layer + 4]
        base = SMALL * layer
        for k in range(5):
            out[base + k : base + k + 1, :] = total(b[8 * k : 8 * k + 8, :])
        out[base + NORM : base + NORM + 1, :WIDTH] = total(d[...])
        out[base + GATE : base + GATE + 1, :OWN] = total(a[0:8, :])
        out[base + SKIP : base + SKIP + 1, :OWN] = total(a[8:16, :])
        out[base + STEP : base + STEP + 1, 0:128] = total(c[0:8, :])
        out[base + RATE : base + RATE + 1, 0:128] = total(c[8:16, :])


def k_small_out(mine_ref, got_ref, ng_ref, cw_ref, cb_ref, db_ref, al_ref, sk_ref, gg_ref):
    need()

    def body(core):
        base = SMALL * core
        cores = (mine_ref, got_ref) if core == 0 else (got_ref, mine_ref)
        ng_ref[...] = mine_ref[base + NORM : base + NORM + 1, :WIDTH]
        for c, src in enumerate(cores):
            cw_ref[:, c * OWN : (c + 1) * OWN] = src[base : base + 4, :OWN]
            cb_ref[:, c * OWN : (c + 1) * OWN] = src[base + BIAS : base + BIAS + 1, :OWN]
            gg_ref[:, c * OWN : (c + 1) * OWN] = src[base + GATE : base + GATE + 1, :OWN]
        a, b = cores
        cw_ref[:, INNER:] = a[base : base + 4, OWN:] + b[base : base + 4, OWN:]
        cb_ref[:, INNER:] = a[base + BIAS : base + BIAS + 1, OWN:] + b[base + BIAS : base + BIAS + 1, OWN:]
        r, c = iotas((128, 2 * HEADS))
        r2, c2 = iotas((OWN, 2 * HEADS))
        wide = lambda v: jnp.broadcast_to(v, (8, v.shape[1]))
        for ref, row in ((db_ref, STEP), (al_ref, RATE)):
            acc = jnp.zeros((8, 2 * HEADS), f32)
            for k, src in enumerate(cores):
                pick = jnp.where((r == c - k * HEADS) & (r < HEADS), 1.0, 0.0)
                acc = acc + exact(wide(src[base + row : base + row + 1, 0:128]), pick)
            ref[...] = acc[0:1]
        acc = jnp.zeros((8, 2 * HEADS), f32)
        for k, src in enumerate(cores):
            pick = jnp.where(r2 // HDIM == c2 - k * HEADS, 1.0, 0.0)
            acc = acc + exact(wide(src[base + SKIP : base + SKIP + 1, :OWN]), pick)
        sk_ref[...] = acc[0:1]

    on_core(body)


def in_place(refs, full):
    if len(refs) == 1:
        return copy_rows(full, 0, refs[0])
    odd = lax.rem(lax.axis_index("dp"), 2)
    half = refs[0].shape[0]
    copy_rows(full, odd * half, refs[0])
    copy_rows(full, (1 - odd) * half, refs[1])


def k_home(*refs):
    *halves_all, give_ref, zo, x = refs
    per = len(halves_all) // 3
    first, second, third = halves_all[:per], halves_all[per : 2 * per], halves_all[2 * per :]
    need()

    def body(core):
        if core == 0:
            in_place(first, give_ref)
        else:
            in_place(second, zo)
            in_place(third, x)
            give_ref[:, :XD] = x[...]
            give_ref[:, XD:] = zo[...]

    on_core(body)


def k_grads(*refs):
    *halves_all, got_ref, gw_ref, go_ref, dw1, zo0, x0 = refs
    per = len(halves_all) // 3
    first_halves, second, third = halves_all[:per], halves_all[per : 2 * per], halves_all[2 * per :]
    need()
    rows, half = got_ref.shape[0], WIDTH // 2

    def body(core):
        if core:
            in_place(first_halves, dw1)
        else:
            in_place(second, zo0)
            in_place(third, x0)
        mine = (x0, zo0, 0) if core == 0 else (dw1, dw1, XD)
        other = (got_ref, got_ref, XD)
        cores = (mine, other) if core == 0 else (other, mine)
        for c, (x, zo, first) in enumerate(cores):
            for k in range(2):
                col = first + OWN + k * half
                go_ref[k * rows : (k + 1) * rows, c * half : (c + 1) * half] = zo[:, col : col + half].astype(f32)

    def rest(core):
        mine = (x0, zo0, 0) if core == 0 else (dw1, dw1, XD)
        other = (got_ref, got_ref, XD)
        cores = (mine, other) if core == 0 else (other, mine)
        for c, (x, zo, first) in enumerate(cores):
            gw_ref[:, c * OWN : (c + 1) * OWN] = zo[:, first : first + OWN].astype(f32)
            gw_ref[:, INNER + c * OWN : INNER + (c + 1) * OWN] = x[:, :OWN].astype(f32)
        a, b = cores[0][0], cores[1][0]
        gw_ref[:, 2 * INNER : 2 * INNER + 2 * STATE] = a[:, OWN:XC].astype(f32) + b[:, OWN:XC].astype(f32)
        r, c = iotas((128, 2 * HEADS))
        acc = 0.0
        for k, x in enumerate((a, b)):
            pick = jnp.where((r == c - k * HEADS) & (r < HEADS), 1.0, 0.0).astype(bf16)
            acc = acc + nn(x[:, XC:XD], pick)
        gw_ref[:, INNER + CONV :] = acc

    on_core(body)
    done(go_ref)
    on_core(rest)


def across(x):
    return jax.tree.map(lambda a: lax.ppermute(a, "section", [(0, 1), (1, 0)]), x)


def flip(x, axis, bits):
    return lax.ppermute(x, axis, [(k, k ^ bits) for k in range(lax.axis_size(axis))])


def chain_step(x, steps, backward):
    n = lax.axis_size("seq")
    hop = -2 * steps if backward else 2 * steps
    return lax.ppermute(x, "seq", [(k, k + hop) for k in range(n) if 0 <= k + hop < n])


def chain(value, decay, backward):
    entered = chain_step(value, 1, backward)
    count = lax.axis_size("seq") // 2
    if count > 2:
        rate = chain_step(decay, 1, backward)
        total = entered.astype(f32)
        steps = 1
        while steps < count - 1:
            total = total + rate[0:1] * chain_step(total.astype(bf16), steps, backward).astype(f32)
            rate = rate * chain_step(rate, steps, backward)
            steps *= 2
        entered = total.astype(bf16)
    return entered


def gather_rows(x):
    n = lax.axis_size("seq")
    if n != 4:
        return [lax.all_gather(x, "seq", axis=0, tiled=True)]
    return [x, *[flip(x, "seq", k) for k in (1, 2, 3)]]


def gather_near(x):
    if lax.axis_size("seq") != 4:
        return gather_rows(x)
    return [x, flip(x, "seq", 1), flip(x, "seq", 2)]


def gather_across(parts, *release):
    if len(parts) == 1:
        return parts
    x, gx, gy = parts
    gx, gy, *_ = lax.optimization_barrier((gx, gy, *release))
    half = x.shape[0] // 2
    return [x, gx, gy, flip(gx[:half], "seq", 2), flip(gy[half:], "seq", 1)]


def k_sum(counts, *refs):
    *blocks, keep_ref, give_ref = refs
    starts = [sum(counts[:k]) for k in range(len(counts))]
    need()
    odd = lax.rem(lax.axis_index("dp"), 2)
    half = keep_ref.shape[0]
    step = 48 if half % 48 == 0 else half
    for dst, start in ((give_ref, (1 - odd) * half), (keep_ref, odd * half)):

        def rows(r, dst=dst, start=start):
            s = pl.ds(pl.multiple_of(start + r * step, 16), step)
            first = 0
            for begin, count in zip(starts, counts):
                total = 0.0
                for ref in blocks[begin : begin + count]:
                    total = total + ref[s, :].astype(f32)
                dst[at(r, step), first : first + total.shape[1]] = total.astype(dst.dtype)
                first += total.shape[1]

        loop(half // step, rows)
        done(dst)


def k_add(a_ref, b_ref, out_ref):
    need()

    def rows(r):
        s = at(r, 16)
        out_ref[s, :] = (a_ref[s, :].astype(f32) + b_ref[s, :].astype(f32)).astype(bf16)

    loop(out_ref.shape[0] // 16, rows)


def send_blocks(blocks):
    if len(blocks) > 1:
        return [blocks[0]] + [flip(blocks[k], "seq", k) for k in (3, 2, 1)]
    return [lax.psum_scatter(blocks[0], "seq", scatter_dimension=0, tiled=True)]


def whole_sum(groups):
    total = jnp.concatenate([sum(b.astype(f32) for b in group) for group in groups], axis=1)
    return [lax.psum(total.astype(bf16), "dp")]


def halved(groups, *pins):
    got = [b for group in groups for b in group]
    rows, width = got[0].shape[0], sum(group[0].shape[1] for group in groups)
    shape = (rows // 2, width)
    return run(
        functools.partial(k_sum, [len(group) for group in groups]), "sum", [(shape, f32, "a"), (shape, bf16, "a")],
        after(got[0], *pins), *got[1:],
    )


def paired(mine, got, *pins):
    return run(k_add, "add", [(got.shape, bf16, "a")], after(mine, *pins), got)[0]


def over_dp(keep, got, *pins, later=()):
    return further([paired(keep, got, *pins)], *later)


def further(mine, *later):
    (mine,), bit = mine, 2
    while bit < lax.axis_size("dp"):
        mine = paired(mine, flip(mine, "dp", bit), *later)
        bit *= 2
    return mine, flip(mine, "dp", 1)


def simple_dp(rows):
    n = lax.axis_size("dp")
    return n == 1 or n & (n - 1) != 0 or rows % 32 != 0


def summed_dp(groups, *pins, before=(), later=()):
    if simple_dp(groups[0][0].shape[0]):
        return whole_sum(groups)
    keep, give = halved(groups, *before)
    return over_dp(keep, flip(give, "dp", 1), *pins, later=later)


def k_add_small(*refs):
    *ins, out_ref = refs
    need()
    if len(ins) == 2:
        out_ref[...] = ins[0][...] + ins[1][...]
    else:
        out_ref[...] = (ins[0][...] + ins[1][...]) + (ins[2][...] + ins[3][...])


def sum_small(x, axes):
    for axis in axes:
        n = lax.axis_size(axis)
        if n == 4:
            x = run(k_add_small, "add_small", [(x.shape, f32, "a")], x, *[flip(x, axis, k) for k in (1, 2, 3)])[0]
        elif n & (n - 1):
            x = lax.psum(x, axis)
        else:
            bit = 1
            while bit < n:
                x = run(k_add_small, "add_small", [(x.shape, f32, "a")], x, flip(x, axis, bit))[0]
                bit *= 2
    return x


def sum_small_dp(x):
    n = lax.axis_size("dp")
    if n & (n - 1):
        return lax.psum(x, "dp"), x
    half_way, bit = x, 1
    while bit < n:
        x = run(k_add_small, "add_small", [(x.shape, f32, "a")], x, flip(x, "dp", bit))[0]
        half_way = x if bit == 1 else half_way
        bit *= 2
    return x, half_way


def after(x, *others):
    return lax.optimization_barrier((x, *others))[0]


AHEAD = ["xdt", "cum", "bc", "c"], ["act", "xb", "slope", "dt"], ["wz", "wx"]
AHEAD_WEIGHT, AHEAD_NORM = ["y", "yw"], ["wo", "z", "act"]


def on_device(hidden_in, cotangent, norm_gain, in_weight, conv_weight, conv_bias, dt_bias, a_log, skip, gate_gain, out_weight):
    core = lax.axis_index("section")
    first = core == 0
    odd = lax.axis_index("seq") % 2
    even = odd == 0
    length = hidden_in.shape[1]
    t = 2 * length
    n = lax.axis_size("seq")
    shard = in_weight.shape[1]
    half = WIDTH // 2
    packed = XD + 2 * OWN

    def given(x):
        return lax.dynamic_index_in_dim(x, 1 - odd, 0, keepdims=False)

    def both_sequences(mine, give):
        got = flip(give, "seq", 1)
        return jnp.stack([jnp.where(even, mine, got), jnp.where(even, got, mine)])

    hid_half, cot_half, mine_x, give_x, mine_zo, give_zo, mine_p, give_p = run(
        k_prep, "prep",
        [((length // 2, WIDTH), bf16, "a"), ((length // 2, WIDTH), bf16, "a"), ((shard, XD), bf16, "v"),
         ((shard, XD), bf16, "a"), ((shard, 2 * OWN), bf16, "v"), ((shard, 2 * OWN), bf16, "a"),
         ((PARAMS, XC), f32, "v"), ((PARAMS, XC), f32, "a")],
        *[
            far_away(a)
            for a in (hidden_in, cotangent, in_weight[0], out_weight[0], norm_gain, conv_weight[0], conv_bias, dt_bias, a_log, skip, gate_gain)
        ],
    )
    x0, x1, par0, par1 = run(
        k_pick, "pick",
        [((shard, XD), bf16, "a"), ((shard, XD), bf16, "a"), ((PARAMS, XC), f32), ((PARAMS, XC), f32)],
        mine_x, across(give_x), mine_p, across(give_p),
    )
    zo0, zo1 = run(
        k_pick_rest, "pick_rest", [((shard, 2 * OWN), bf16, "a"), ((shard, 2 * OWN), bf16, "a")], mine_zo, across(give_zo)
    )
    params = [par0, par1]

    def half_given(x):
        return lax.dynamic_slice_in_dim(given(x), core * (length // 2), length // 2, 0)

    def both_halves(mine):
        got = flip(mine, "seq", 1)
        return got, across(got)

    ga, gb = both_halves(hid_half)
    give_cot = cot_half
    parts_x0 = gather_rows(after(x0, ga, give_cot))
    near_zo0 = gather_near(after(zo0, *parts_x0))

    saved = [{}, {}]

    def keeping(layer, soon):
        return "vh" if soon else "h"

    def named(layer, names, results, modes, stayed=()):
        soon, at_result = {}, 0
        for name, mode in zip(names, modes):
            for m in mode:
                value = results[at_result]
                at_result += 1
                if m != "h":
                    soon[name] = value
                if m == mode[-1]:
                    saved[layer][name] = value
        for name in stayed:
            saved[layer][name] = results[len(results) - len(stayed) + stayed.index(name)]
        return soon

    def scan_part(layer, x, tail, near_zo, before_front):
        par = params[layer]
        last = keeping(layer, False)
        before = chain_step(tail, 1, False)
        saved[layer]["before"] = before
        modes = ["v"] * 8 + ["a"]
        shapes = [((t, XC), f32), ((t, XC), bf16), ((t, 2 * STATE), bf16), ((t, OWN), bf16), ((t, 128), f32), ((t, 128), f32),
                  ((2 * STATE, OWN), f32), ((16, OWN), f32), ((STATE, OWN), bf16)]
        x |= named(
            layer, ["act", "slope", "bc", "xdt", "dt", "cum", "s", "dec", "tot"],
            run(
                k_front, "front", [(*shape, m) for shape, m in zip(shapes, modes)],
                x["xb"], after(before, *before_front), par, scratch=[((t, OWN), f32), ((16, XC), f32)],
            ),
            modes,
        )
        dec = saved[layer]["dec"]
        saved[layer]["decay"] = dec[:8] * dec[8:] if n > 4 else None
        entered = chain(x["tot"], saved[layer]["decay"], False)
        x |= named(
            layer, ["yw"],
            run(
                k_within, "within", [((t, OWN), f32, "v")], x["cum"], x["bc"], x["xdt"],
                scratch=[((t, HEADS * 128), f32), ((t // 128, HEADS * 8, 128), f32), ((t, BLOCK), f32)],
                stay=[x[k] for k in ("xb", "slope", "dt", "cum")],
            ),
            ["v"],
            ["xb", "slope", "dt", "cum"],
        )
        parts_zo = gather_across(near_zo, before)
        x["parts_zo"] = parts_zo
        modes = ["v", "h", "v", "p"]
        x |= named(
            layer, ["z", "wz", "keep", "give"],
            run(
                k_z, "gate_in",
                [((t, OWN), f32, modes[0]), ((WIDTH, OWN), bf16, modes[1]), ((WIDTH // 2, OWN), bf16, "v"),
                 ((WIDTH // 2, OWN), bf16, "p")],
                near(after(x["normed"], x["yw"], entered)), *parts_zo, scratch=[((WIDTH, OWN), bf16)],
                stay=[x[k] for k in ("normed", "xdt", "bc", "dec")],
            ),
            modes,
            ["normed", "xdt", "bc", "dec"],
        )
        ogot = across(x["give"])
        x["entered"] = entered
        cot_halves = [ca, cb] if layer else []
        ins = [x["yw"], x["act"], x["bc"], x["cum"], entered, x["s"], x["dec"], x["z"], par, x["keep"], ogot]
        kept = "v" if layer else "h"
        stayed = ["act"] if layer else ["act", "yw", "z"]
        modes = [kept, "h" if layer else "v", "p", "vh" if layer else "v", last, kept] + ["vh"] * layer
        shapes = [((t, OWN), f32), ((t, WIDTH), f32), ((t, half + 128 if layer else WIDTH + 128), bf16),
                  ((t, 256 if layer else 128), f32), ((2 * STATE, OWN), f32), ((OWN, WIDTH), bf16)]
        shapes += [((t, WIDTH), bf16)] * layer
        results = run(
            functools.partial(k_out, layer == 0), "out", [(*shape, m) for shape, m in zip(shapes, modes)],
            *ins, *([cotangent, *cot_halves] if layer else []), scratch=[((t, OWN), f32), ((t, OWN), bf16)],
            ahead=[] if layer else [saved[0]["h"]], stay=[x[k] for k in stayed],
        )
        x |= named(layer, ["y", "p", "msg", "st", "c", "wo", "g"][: len(modes)], results, modes, stayed)
        if layer == 0:
            x["h"] = results[-1 - len(stayed)]
        return x

    outs_in = [((t, WIDTH), bf16), ((t + 8, XD), f32), ((WIDTH, XD), bf16), ((8, XC), f32)]
    names_in = ["normed", "xb", "wx", "tail"]
    modes = ["h", "v", "v", "h", "a"]
    shapes = [((t, WIDTH), bf16), *outs_in]
    x = named(
        0, ["h", *names_in],
        run(k_in, "project", [(*shape, m) for shape, m in zip(shapes, modes)], hidden_in, ga, gb, par0, *parts_x0),
        modes,
    )
    tail0 = x["tail"]
    x = scan_part(0, x, tail0, near_zo0, [])
    parts_x1 = gather_across(gather_near(after(x1, x["entered"], x["yw"], *x["parts_zo"][3:])), x["msg"])
    msg = across(x["msg"])
    near_zo1 = gather_near(after(zo1, *parts_x1, *msg))
    modes = ["h", "h", "h", "v", "v", "h", "a"]
    shapes = [((t, WIDTH), bf16), ((t, WIDTH), f32), ((t, 128), f32), *outs_in]
    x = named(
        1, ["h", "pt", "rs", *names_in],
        run(
            k_mid, "middle", [(*shape, m) for shape, m in zip(shapes, modes)],
            x["h"], x["p"], x["st"], msg, par1, *parts_x1,
        ),
        modes,
    )
    h1_far, pt, rs0 = saved[1]["h"], saved[1]["pt"], saved[1]["rs"]
    tail1 = x["tail"]
    ca, cb = both_halves(after(give_cot, tail1))
    x = scan_part(1, x, x["tail"], near_zo1, near_zo1[1:])
    p1, st1, st1_far = saved[1]["p"], x["st"], saved[1]["st"]
    msg = across(x["msg"])
    count = 4 if n == 4 else 1

    ahead_zw, ahead_within, ahead_front = AHEAD

    def backward(layer, v, g, rs, rd, close=None, before_zw=(), before_zo=()):
        par = params[layer]
        v = dict(v)
        far = dict(v)

        def fetched(names, results):
            if names:
                v.update(zip(names, results[-len(names) :]))

        qz, dy, df, dca, okeep, ogive, d, e, small_a = run(
            kb_gate, "back_gate",
            [((t, OWN), bf16, "v"), ((t, OWN), f32, "v"), ((t, OWN), bf16, "v"), ((t, 128), f32, "v"),
             ((OWN, half), bf16, "v"), ((OWN, half), bf16, "p"), ((2 * STATE, OWN), f32, "v"),
             ((STATE, OWN), bf16, "a"), ((16, OWN), f32)],
            g, *[(close or v)[k] for k in ("wo", "y", "yw", "z", "act", "bc", "cum")], rs, rd, par, (close or v)["dec"],
            scratch=[((t, OWN), f32), ((t, OWN), f32), ((t, OWN), bf16)],
        )
        entered = chain(e, v["decay"], True)
        ogot = across(ogive)
        results = run(
            kb_z_weight, "back_zw", [((WIDTH // count, 2 * OWN), bf16, "a")] * count, v["normed"], qz, okeep,
            after(ogot, *before_zw),
            scratch=[((WIDTH, 2 * OWN), bf16)], ahead=[v[k] for k in ahead_zw],
        )
        zo = list(results[:count])
        beside_zw = [*zo]
        if layer:
            zo = [after(b, entered) for b in zo]
        fetched(ahead_zw, results)
        v["act"] = far["act"]
        dy = near(after(dy, *beside_zw))
        results = run(
            kb_within, "back_within", [((t, OWN), f32, "v"), ((t, 2 * STATE), f32, "v")],
            dy, v["xdt"], v["cum"], v["bc"], df, v["c"],
            scratch=[((t, HEADS * 128), f32), ((t // 128, HEADS * 8, 128), f32), ((t, BLOCK), f32), ((t, BLOCK), f32)],
            ahead=[v[k] for k in ahead_within],
        )
        dxw, dbc = results[:2]
        if layer == 0:
            dxw, dbc = near(*lax.optimization_barrier((dxw, dbc)))
            zo = [after(b, entered, dxw, *before_zo) for b in zo]
        fetched(ahead_within, results)
        results = run(
            kb_front, "back_front",
            [((t + 8, XC), f32, "v"), ((8, XC), f32, "a"), ((t, 128), bf16, "v"), ((40, XC), f32), ((16, 128), f32)],
            entered, d, v["c"], far["dec"], v["bc"], v["xdt"], v["act"], v["xb"], v["slope"], v["before"], v["dt"], v["cum"],
            dxw, dbc, dy, dca, par,
            scratch=[((2 * STATE, OWN), f32), ((t, OWN), f32), ((t, OWN), f32), ((t, OWN), f32), ((t, XC), f32),
                     ((t, 128), f32), ((t, 128), f32), ((16, OWN), f32), ((t + 16, 128), f32)],
            ahead=[v[k] for k in ahead_front],
        )
        dxb, halo, qdt, small_b, small_c = results[:5]
        fetched(ahead_front, results)
        ret = chain_step(halo, 1, True)
        dnz = run(kb_z_normed, "back_z", [((t, WIDTH), f32, "v")], near(after(qz, halo)), v["wz"])[0]
        return dxb, ret, qdt, dnz, zo, (small_a, small_b, small_c), v, (e, dbc, halo)

    shape_q, shape_n = ((t, XD), bf16, "v"), [((t, WIDTH), f32, "v"), ((t, WIDTH), bf16, "p")]
    x_blocks = [((WIDTH // count, XD), bf16, "a")] * count
    x_scratch = [((WIDTH, XD), bf16)]
    dxb, ret, qdt, dnz, zo1, small1, v1, _ = backward(1, saved[1], x["g"], st1, msg, x)
    got_zo1 = send_blocks(zo1)
    v0 = saved[0]
    early = []
    q, dn, dnb1, *fetched = run(
        kb_x_normed, "back_x", [shape_q, shape_n[0], ((t, WIDTH), bf16, "a")], dxb, ret, qdt, dnz, v1["wx"], ahead=[v0[k] for k in early]
    )
    v0.update(zip(early, fetched))
    dr = across(dnb1)
    shapes_x = [((2 * shard, CUT), bf16, "a"), ((2 * shard, XD - CUT), bf16, "a")] * 2
    x1 = run(
        kb_x_weight, "back_xw", shapes_x if count > 1 else [((WIDTH, XD), bf16, "a")], v1["normed"],
        near(after(q, dnb1, *got_zo1)), scratch=x_scratch, ahead=[*[v0[k] for k in AHEAD_WEIGHT], h1_far, pt],
    )
    *x1, h1_near, pt_near = x1
    v0.update(zip(AHEAD_WEIGHT, x1[-len(AHEAD_WEIGHT) :]))
    x1 = x1[: -len(AHEAD_WEIGHT)]
    got_x1 = [flip(x1[0], "seq", 1), flip(x1[1], "seq", 2)] if count > 1 else []

    def second_phase(*pins):
        if count == 1:
            return [[lax.psum_scatter(x1[0], "seq", scatter_dimension=0, tiled=True)]]
        own_a, own_b, give_a, give_b = run(
            k_phase, "phase", [((shard, CUT), bf16, "a"), ((shard, XD - CUT), bf16, "a")] * 2,
            after(x1[2], *pins), x1[3], *got_x1,
        )
        return [[own_a, flip(give_a, "seq", 2)], [own_b, flip(give_b, "seq", 1)]]

    phase = second_phase()
    early = AHEAD_NORM
    g0, g0_far, small_d1, rd0, *fetched = run(
        kb_norm, "back_norm", [((t, WIDTH), bf16, "vh"), ((8, WIDTH), f32), ((t, 128), f32, "v")],
        h1_near, dn, after(dr, *x1), saved[1]["g"], par1, pt_near, ahead=[v0[k] for k in early],
    )
    v0.update(zip(early, fetched))
    dxb, ret, qdt, dnz, zo0, small0, v0, (e0, dbc0, halo0) = backward(
        0, v0, g0, rs0, rd0, before_zw=phase[0][:1], before_zo=[p[-1] for p in phase]
    )
    got_zo0 = send_blocks(zo0)
    simple = simple_dp(shard)
    halves1 = [] if simple else halved([*phase, got_zo1], dbc0)
    over1 = [] if simple else [paired(halves1[0], flip(halves1[1], "dp", 1))]
    q, *x0 = run(kb_x_weight_first, "back_xw", [shape_q] + x_blocks, v0["normed"], dxb, after(ret, *over1, *got_zo0), qdt, scratch=x_scratch)
    got_x0 = send_blocks(x0)
    dn, dnb0 = run(kb_x_normed_last, "back_x", [shape_n[0], ((t, WIDTH), bf16, "a")], near(after(q, *x0)), dnz, v0["wx"])
    dr = across(dnb0)
    sum1 = whole_sum([*phase, got_zo1]) if simple else further(over1, x0[0])
    sum_zo0 = summed_dp([got_zo0], before=[x0[0]])
    final = run(
        k_final, "final", [((length, half), bf16, "a"), ((length, half), bf16, "a")],
        h1_far, p1, st1_far, after(msg, dnb0),
    )
    hidden_out = both_sequences(*final)
    keep, give, small_d0 = run(
        kb_norm_last, "back_norm", [((length, half), bf16, "a"), ((length, half), bf16, "a"), ((8, WIDTH), f32)],
        saved[0]["h"], dn, dr, g0_far, par0, scratch=[((t, WIDTH), bf16)],
    )
    grad_in = both_sequences(keep, give)
    small = run(k_small, "small", [((2 * SMALL, XC), f32, "a")], *small0, small_d0, *small1, small_d1)[0]
    halves0 = [] if simple else halved([got_x0], final[0], keep, small)
    small = sum_small(small, ["seq"])
    first_small = small
    small, half_way = sum_small_dp(small)
    if simple:
        sum_x0 = whole_sum([got_x0])
    else:
        sum_x0 = over_dp(halves0[0], flip(halves0[1], "dp", 1), first_small, later=[half_way])
    sums = [*sum1, *sum_zo0, after(sum_x0[0], small), *sum_x0[1:]]
    heads = 2 * HEADS
    smalls = run(
        k_small_out, "small_out",
        [((1, WIDTH), f32, "a"), ((4, CONV), f32, "a"), ((1, CONV), f32, "a"), ((1, heads), f32, "a"), ((1, heads), f32, "a"), ((1, heads), f32, "a"),
         ((1, INNER), f32, "a")],
        small, across(small),
    )
    give = run(k_home, "home", [((shard, packed), bf16, "p")], *sums, scratch=[((shard, 2 * OWN), bf16), ((shard, XD), bf16)])[0]
    grad_w, grad_o = run(
        k_grads, "grads", [((shard, INNER + CONV + heads), f32, "a"), ((2 * shard, WIDTH), f32, "a")],
        *sums, across(give),
        scratch=[((shard, packed), bf16), ((shard, 2 * OWN), bf16), ((shard, XD), bf16)],
    )
    norm, taps, bias, dtb, rates, skips, gates = smalls
    return (hidden_out, grad_in, norm, grad_w[None], taps[None], bias, dtb, rates, skips, gates, grad_o[None])


def solution(mesh):
    by_section = P("section", None)
    rows = P("section", "seq", None)
    tokens = P("dp", "seq", None)
    taps = P("section", None, None)
    out = P("dp", "seq", "section")
    small = (by_section,) * 4
    return jax.shard_map(
        on_device,
        mesh=mesh,
        in_specs=(tokens, tokens, by_section, rows, taps, by_section, *small, rows),
        out_specs=(out, out, by_section, rows, taps, by_section, *small, rows),
        check_vma=False,
    )
```

```python
import functools

import jax
import jax.numpy as jnp
from jax import lax
from jax.experimental import pallas as pl
from jax.experimental.pallas import tpu as pltpu
from jax.sharding import PartitionSpec as P

HDIM = 64
STATE = 128
INNER = 1536
CONV = 1792
EPS = 1e-05
f32, bf16 = jnp.float32, jnp.bfloat16

WIDTH = 768
OWN = 768
HEADS = 12
XC = OWN + 2 * STATE
XD = XC + 128
R = 256
BLOCK = 256


def nn(a, b):
    return lax.dot_general(a, b, (((1,), (0,)), ((), ())), preferred_element_type=f32)


def nt(a, b):
    return lax.dot_general(a, b, (((1,), (1,)), ((), ())), preferred_element_type=f32)


def tn(a, b):
    return lax.dot_general(a, b, (((0,), (0,)), ((), ())), preferred_element_type=f32)


def loop(count, body):
    def step(k, carry):
        body(k)
        return carry

    lax.fori_loop(0, count, step, 0)


def at(k, size):
    return pl.ds(pl.multiple_of(k * size, size), size)


def iotas(shape):
    return lax.broadcasted_iota(jnp.int32, shape, 0), lax.broadcasted_iota(jnp.int32, shape, 1)


def spread_matrix(width, per):
    r, c = iotas((128, width))
    return jnp.where(((r & 15) == c // per) & (r < 48), 1.0, 0.0).astype(bf16)


def collect_matrix():
    r, c = iotas((OWN, 128))
    return jnp.where(((c & 15) == r // HDIM) & (c < 48), 1.0, 0.0).astype(bf16)


def thirds(v):
    high = v.astype(bf16).astype(f32)
    rest = v - high
    mid = rest.astype(bf16).astype(f32)
    lane = iotas(v.shape)[1]
    out = jnp.where(lane < 16, high, jnp.where(lane < 32, mid, rest - mid))
    return jnp.where(lane < 48, out, 0.0).astype(bf16)


def halves(v):
    high = v.astype(bf16)
    return high, (v - high.astype(f32)).astype(bf16)


def running_sum(v, backward=False):
    r, c = iotas((BLOCK, BLOCK))
    tri = jnp.where((c >= r) if backward else (r >= c), 1.0, 0.0).astype(bf16)
    high = v.astype(bf16)
    rest = v - high.astype(f32)
    mid = rest.astype(bf16)
    last = (rest - mid.astype(f32)).astype(bf16)
    return nn(tri, high) + nn(tri, mid) + nn(tri, last)


def sig(v):
    return 0.5 * jnp.tanh(0.5 * v) + 0.5


def softplus(v):
    e = jnp.exp(-jnp.abs(v))
    u = 1.0 + e
    small = u == 1.0
    return jnp.maximum(v, 0.0) + jnp.where(small, e, jnp.log(u) * e / jnp.where(small, 1.0, u - 1.0))


def fold(v):
    return jnp.sum(v.reshape(v.shape[0] // 8, 8, v.shape[1]), axis=0)


def copy_rows(dst, start, src, cols=None):
    rows = src.shape[0]
    step = next(k for k in (48, 32, 16, 8, rows) if rows % k == 0)

    def move(r):
        place = pl.ds(pl.multiple_of(start + r * step, 16), step)
        if cols is None:
            dst[place, :] = src[at(r, step), :]
        else:
            dst[place, :] = src[at(r, step), cols]

    loop(rows // step, move)


def place_rows(dst, parts, cols=None):
    if len(parts) == 1:
        return copy_rows(dst, 0, parts[0], cols)
    me = lax.axis_index("seq")
    rows = parts[0].shape[0]
    for k in range(min(len(parts), 4)):
        copy_rows(dst, (me ^ k) * rows, parts[k], cols)
    if len(parts) > 4:
        copy_rows(dst, (me ^ 3) * rows + rows // 2, parts[4], cols)


def on_core(body):
    me = lax.axis_index("section")
    for core in range(2):
        pl.when(me == core)(lambda core=core: body(core))


def exact(a, b):
    return lax.dot_general(
        a, b, (((1,), (0,)), ((), ())), preferred_element_type=f32, precision=lax.Precision.HIGHEST
    )


def stats_out(a, b):
    lane = iotas(a.shape)[1]
    v = jnp.where(lane < 64, a, b)
    high = v.astype(bf16).astype(f32)
    rest = v - high
    mid = rest.astype(bf16).astype(f32)
    l = lane & 63
    out = jnp.where(l < 16, high, jnp.where(l < 32, mid, rest - mid))
    return jnp.where(l < 48, out, 0.0).astype(bf16)


def stats_in(v):
    v = v.astype(f32)
    lane = iotas(v.shape)[1]
    a = jnp.sum(jnp.where(lane < 64, v, 0.0), axis=1, keepdims=True)
    b = jnp.sum(jnp.where(lane < 64, 0.0, v), axis=1, keepdims=True)
    return a * (1.0 / 16), b * (1.0 / 16)


class Copies:

    def __init__(self, pairs_in, pairs_ahead, pairs_out, sems_in, sems_out):
        self.waiting, self.ready, self.started, self.ahead = {}, {}, [], []
        for k, (far, near, whole) in enumerate(pairs_in):
            copy = pltpu.make_async_copy(far, near, sems_in.at[k])
            copy.start()
            self.waiting.setdefault(id(whole), []).append(copy)
        for k, (far, near) in enumerate(pairs_ahead):
            copy = pltpu.make_async_copy(far, near, sems_in.at[len(pairs_in) + k])
            copy.start()
            self.ahead.append(copy)
        for k, (far, near, whole) in enumerate(pairs_out):
            self.ready.setdefault(id(whole), []).append(pltpu.make_async_copy(near, far, sems_out.at[k]))

    def need(self, refs):
        for key in [id(r) for r in refs] if refs else list(self.waiting):
            for copy in self.waiting.pop(key, ()):
                copy.wait()

    def done(self, refs):
        for key in [id(r) for r in refs] if refs else list(self.ready):
            for copy in self.ready.pop(key, ()):
                copy.start()
                self.started.append(copy)


COPIES = []


def need(*refs):
    COPIES[-1].need(refs)


def done(*refs):
    COPIES[-1].done(refs)


FAR = []
NEAR = []


def near(*arrays):
    NEAR.extend(arrays)
    return arrays if len(arrays) > 1 else arrays[0]


def far_away(array):
    FAR.append(array)
    return array


def run(kernel, name, outs, *ins, scratch=(), ahead=(), stay=()):
    far, close = pl.BlockSpec(memory_space=pltpu.HBM), pl.BlockSpec(memory_space=pltpu.VMEM)
    loose = pl.BlockSpec(memory_space=pl.ANY)
    modes = [o[2] if len(o) > 2 else "h" for o in outs]
    units = [m for mode in modes for m in mode] + ["v"] * len(ahead) + ["h"] * len(stay)
    shapes, specs = [], []
    for (shape, dtype, *_), mode in zip(outs, modes):
        for m in mode:
            if m == "p":
                shapes += [jax.ShapeDtypeStruct((shape[0] // 2, *shape[1:]), dtype)] * 2
                specs += [loose] * 2
            else:
                space = dict(v=pltpu.VMEM, h=pltpu.HBM, a=jax.ShapeDtypeStruct)[m]
                shapes.append(space(shape, dtype))
                specs.append(dict(v=close, h=far, a=loose)[m])
    for a in ahead:
        shapes.append(pltpu.VMEM(a.shape, a.dtype))
        specs.append(close)
    for a in stay:
        shapes.append(pltpu.HBM(a.shape, a.dtype))
        specs.append(far)
    groups = [a if isinstance(a, (tuple, list)) else (a,) for a in (*ins, *ahead, *stay)]
    flat = [a for group in groups for a in group]
    held = [any(a is k for k in NEAR) for a in flat]
    kept = [any(a is k for k in FAR) for a in flat]
    flat = [
        pltpu.with_memory_space_constraint(a, pltpu.VMEM if h else pltpu.HBM) if h or k else a
        for a, h, k in zip(flat, held, kept)
    ]
    n_in, n_out, n_own = len(flat), len(shapes), sum(len(group) for group in groups[: len(ins)])
    buffers = [
        pltpu.VMEM((sum(a.shape[0] for a in group), *group[0].shape[1:]), group[0].dtype)
        for group in groups[: len(ins)]
        if not any(group[0] is k for k in NEAR)
    ]
    buffers += [pltpu.VMEM(shape, dtype) for (shape, dtype, *_), mode in zip(outs, modes) if "v" not in mode]

    def body(*refs):
        given, made, rest = list(refs[:n_in]), list(refs[n_in : n_in + n_out]), list(refs[n_in + n_out :])
        pairs_in, pairs_out, vin, vout = [], [], [], []
        pairs_ahead = list(zip(given[n_own:], made[n_out - len(ahead) - len(stay) :]))
        at_ref = 0
        for group in groups[: len(ins)]:
            if held[at_ref]:
                vin.append(given[at_ref])
            else:
                vin.append(rest.pop(0))
                start = 0
                for k, part in enumerate(group):
                    rows = part.shape[0]
                    place = vin[-1] if len(group) == 1 else vin[-1].at[pl.ds(start, rows)]
                    pairs_in.append((given[at_ref + k], place, vin[-1]))
                    start += rows
            at_ref += len(group)
        for mode in modes:
            vout.append(made.pop(0) if "v" in mode else rest.pop(0))
            if mode == "p":
                rows = vout[-1].shape[0] // 2
                for k in range(2):
                    pairs_out.append((made.pop(0), vout[-1].at[pl.ds(k * rows, rows)], vout[-1]))
            elif mode != "v":
                pairs_out.append((made.pop(0), vout[-1], vout[-1]))
        *extra, sems_in, sems_out = rest
        copies = Copies(pairs_in, pairs_ahead, pairs_out, sems_in, sems_out)
        COPIES.append(copies)
        kernel(*vin, *vout, *extra)
        need()
        done()
        for copy in [*copies.ahead, *copies.started]:
            copy.wait()
        COPIES.pop()

    results = list(
        pl.pallas_call(
            body,
            name=name,
            out_shape=shapes,
            in_specs=[close if h else far if k else loose for h, k in zip(held, kept)],
            out_specs=specs,
            scratch_shapes=[
                *buffers,
                *[pltpu.VMEM(s, d) for s, d in scratch],
                pltpu.SemaphoreType.DMA((max(n_in, 1),)),
                pltpu.SemaphoreType.DMA((max(n_out, 1),)),
            ],
            compiler_params=pltpu.CompilerParams(vmem_limit_bytes=MIB * 2**20),
            cost_estimate=pl.CostEstimate(flops=1, bytes_accessed=1, transcendentals=0),
        )(*flat)
    )
    grouped = []
    for unit in units:
        if unit == "p":
            grouped.append((results.pop(0), results.pop(0)))
            continue
        grouped.append(results.pop(0))
        if unit != "a":
            (NEAR if unit == "v" else FAR).append(grouped[-1])
    return grouped


MIB = 24


TAPS, BIAS, NORM, GATE, SKIP, STEP, RATE = 0, 4, 5, 6, 7, 8, 9
PARAMS = 16


def k_prep(hid_ref, cot_ref, w_ref, o_ref, ng_ref, cw_ref, cb_ref, db_ref, al_ref, sk_ref, gg_ref, hid_half, cot_half, mine_x, give_x, mine_zo, give_zo, mine_p, give_p):
    need()
    rows = w_ref.shape[0]
    half = WIDTH // 2
    r24, c24 = iotas((2 * HEADS, 128))
    rk, ck = iotas((2 * HEADS, OWN))

    def pack(core, out):
        own = core * OWN
        out[:, 0:OWN] = w_ref[:, INNER + own : INNER + own + OWN]
        out[:, OWN:XC] = w_ref[:, 2 * INNER : 2 * INNER + 2 * STATE]
        pick = ((c24 & 15) == r24 - core * HEADS) & (c24 < 48)
        steps = w_ref[:, INNER + CONV : INNER + CONV + 2 * HEADS]
        out[:, XC:XD] = nn(steps, jnp.where(pick, 1.0, 0.0).astype(bf16)).astype(bf16)

    def pack_rest(core, out, par):
        own = core * OWN
        pick = ((c24 & 15) == r24 - core * HEADS) & (c24 < 48)
        out[:, 0:OWN] = w_ref[:, own : own + OWN]
        for t in range(2):
            at_lane = OWN + t * half
            out[:, at_lane : at_lane + half] = o_ref[t * rows : (t + 1) * rows, core * half : (core + 1) * half]
        par[...] = jnp.zeros(par.shape, f32)
        par[TAPS : TAPS + 4, :OWN] = cw_ref[:, own : own + OWN]
        par[TAPS : TAPS + 4, OWN:] = cw_ref[:, INNER:]
        par[BIAS : BIAS + 1, :OWN] = cb_ref[:, own : own + OWN]
        par[BIAS : BIAS + 1, OWN:] = cb_ref[:, INNER:]
        par[NORM : NORM + 1, :WIDTH] = ng_ref[...]
        par[GATE : GATE + 1, :OWN] = gg_ref[:, own : own + OWN]
        spread = jnp.where(rk - core * HEADS == ck // HDIM, 1.0, 0.0)
        par[SKIP : SKIP + 1, :OWN] = exact(jnp.broadcast_to(sk_ref[...], (8, 2 * HEADS)), spread)[0:1]
        lanes = jnp.where(pick, 1.0, 0.0)
        par[STEP : STEP + 1, 0:128] = exact(jnp.broadcast_to(db_ref[...], (8, 2 * HEADS)), lanes)[0:1]
        par[RATE : RATE + 1, 0:128] = exact(jnp.broadcast_to(al_ref[...], (8, 2 * HEADS)), lanes)[0:1]

    def body(core):
        pack(core, mine_x)
        pack(1 - core, give_x)

    def rest(core):
        pack_rest(core, mine_zo, mine_p)
        pack_rest(1 - core, give_zo, give_p)

    on_core(body)
    done(mine_x, give_x)
    even_seq = 1 - lax.rem(lax.axis_index("seq"), 2)
    rows_half = hid_half.shape[0]
    start = lax.axis_index("section") * rows_half
    for src, dst in ((hid_ref, hid_half), (cot_ref, cot_half)):

        def move(r, src=src, dst=dst):
            dst[at(r, 32), :] = src[even_seq, pl.ds(pl.multiple_of(start + r * 32, 32), 32), :]

        loop(rows_half // 32, move)
        done(dst)
    on_core(rest)


def k_pick(mine_x, got_x, mine_p, got_p, x0, x1, p0, p1):
    need()

    def body(core):
        for layer, (x, p) in enumerate(((x0, p0), (x1, p1))):
            x[...] = (mine_x, got_x)[layer ^ core][...]
            p[...] = (mine_p, got_p)[layer ^ core][...]

    on_core(body)


def k_pick_rest(mine_zo, got_zo, zo0, zo1):
    need()

    def body(core):
        zo0[...] = (mine_zo, got_zo)[core][...]
        zo1[...] = (mine_zo, got_zo)[1 - core][...]

    on_core(body)


def norm_rows(h, gain):
    scale = lax.rsqrt(jnp.mean(h * h, axis=1, keepdims=True) + EPS)
    return (h * scale * gain).astype(bf16)


def project(t, normed_ref, wx_ref, xb_ref, tail_ref):
    xb_ref[0:8, :] = jnp.zeros((8, XD), f32)

    def cols(c):
        xb_ref[8 : 8 + t, :] = nn(normed_ref[...], wx_ref[...])

    loop(1, cols)
    tail_ref[...] = xb_ref[t:, :XC]


def k_in(hid_ref, ga_ref, gb_ref, par_ref, *rest):
    *parts, h_ref, normed_ref, xb_ref, wx_ref, tail_ref = rest
    need(hid_ref, ga_ref, gb_ref, par_ref)
    t = h_ref.shape[0]
    half = t // 2
    odd = lax.rem(lax.axis_index("seq"), 2)
    core = lax.axis_index("section")
    copy_rows(h_ref, odd * half, hid_ref.at[odd])
    copy_rows(h_ref, (1 - odd) * half + core * (half // 2), ga_ref)
    copy_rows(h_ref, (1 - odd) * half + (1 - core) * (half // 2), gb_ref)

    def rows(r):
        normed_ref[at(r, R), :] = norm_rows(h_ref[at(r, R), :].astype(f32), par_ref[NORM : NORM + 1, :WIDTH])

    loop(t // R, rows)
    done(h_ref, normed_ref)
    need(*parts)
    place_rows(wx_ref, parts)
    done(wx_ref)
    project(t, normed_ref, wx_ref, xb_ref, tail_ref)


def k_mid(h_ref, p_ref, st_ref, msg_ref, par_ref, *rest):
    *parts, h1_ref, pt_ref, rs_ref, normed_ref, xb_ref, wx_ref, tail_ref = rest
    need(h_ref, p_ref, st_ref, msg_ref, par_ref)
    t = h_ref.shape[0]

    def rows(r):
        s = at(r, R)
        other = stats_in(msg_ref[s, WIDTH:])[0]
        rs = lax.rsqrt((st_ref[s, 0:128] + other) * (1.0 / INNER) + EPS)
        rs_ref[s, :] = rs
        p = p_ref[s, :] + msg_ref[s, :WIDTH].astype(f32)
        pt_ref[s, :] = p
        h1 = (h_ref[s, :].astype(f32) + rs[:, 0:1] * p).astype(bf16)
        h1_ref[s, :] = h1
        normed_ref[s, :] = norm_rows(h1.astype(f32), par_ref[NORM : NORM + 1, :WIDTH])

    loop(t // R, rows)
    done(h1_ref, pt_ref, rs_ref, normed_ref)
    need(*parts)
    place_rows(wx_ref, parts)
    done(wx_ref)
    project(t, normed_ref, wx_ref, xb_ref, tail_ref)


def k_z(normed_ref, *rest):
    *parts, z_ref, wz_ref, keep_ref, give_ref, o = rest
    need(*parts)
    place_rows(wz_ref, parts, slice(0, OWN))
    done(wz_ref)
    place_rows(o, parts, slice(OWN, 2 * OWN))

    def split(core):
        rows = keep_ref.shape[0]
        keep_ref[...] = o[core * rows : (core + 1) * rows, :]
        give_ref[...] = o[(1 - core) * rows : (2 - core) * rows, :]

    on_core(split)
    done(keep_ref, give_ref)
    need(normed_ref)

    def cols(c):
        z_ref[:, at(c, 768)] = nn(normed_ref[...], wz_ref[:, at(c, 768)])

    loop(OWN // 768, cols)


def k_front(xb_ref, before_ref, par_ref, act_ref, slope_ref, bc_ref, xdt_ref, dt_ref, cum_ref, s_ref, dec_ref, tot_ref, wide, edge):
    t = act_ref.shape[0]
    need()
    edge[0:8, :] = before_ref[...]
    edge[8:16, :] = jnp.zeros((8, XC), f32)

    def conv(c):
        cols = at(c, 128)
        w = par_ref[0:8, cols]
        total = w[4:5] + w[0:1] * xb_ref[pl.ds(5, t), cols]
        for k in range(1, 4):
            total = total + w[k : k + 1] * xb_ref[pl.ds(5 + k, t), cols]
        first = total[0:8]
        for k in range(4):
            first = first + w[k : k + 1] * edge[5 + k : 13 + k, cols]
        total = jnp.concatenate([first, total[8:]], axis=0)
        sg = sig(total)
        act = total * sg
        act_ref[:, cols] = act
        slope_ref[:, cols] = (sg + act * (1.0 - sg)).astype(bf16)

    loop(XC // 128, conv)
    bc_ref[...] = act_ref[:, OWN:].astype(bf16)
    done(act_ref, slope_ref, bc_ref)
    dt = softplus(xb_ref[8 : 8 + t, XC:] + par_ref[STEP : STEP + 1, 0:128])
    dt_ref[...] = dt
    done(dt_ref)
    rate = -jnp.exp(par_ref[RATE : RATE + 1, 0:128])
    spread = spread_matrix(OWN, HDIM)
    wide[...] = nn(thirds(dt), spread)

    def rows(r):
        s = at(r, R)
        xdt_ref[s, :] = (act_ref[s, :OWN] * wide[s, :]).astype(bf16)

    loop(t // R, rows)
    done(xdt_ref)
    for b in range(t // BLOCK):
        s = pl.ds(b * BLOCK, BLOCK)
        cum = running_sum(rate * dt[b * BLOCK : (b + 1) * BLOCK])
        cum_ref[s, :] = cum
        end = cum[BLOCK - 1 : BLOCK, :]
        dec_ref[8 * b : 8 * b + 8, :] = nn(thirds(jnp.exp(jnp.broadcast_to(end, (8, 128)))), spread)
        wide[s, :] = nn(thirds(jnp.exp(end - cum)), spread)
        bl = bc_ref[s, 0:STATE]

        def cols(c):
            decayed = (xdt_ref[s, at(c, 768)].astype(f32) * wide[s, at(c, 768)]).astype(bf16)
            s_ref[pl.ds(b * STATE, STATE), at(c, 768)] = tn(bl, decayed)

        loop(OWN // 768, cols)
    tot_ref[...] = (s_ref[STATE:, :] + dec_ref[8:9, :] * s_ref[:STATE, :]).astype(bf16)


def decay_tables(cum_ref, tall, flat):
    t = cum_ref.shape[0]
    parts = thirds(cum_ref[...])
    tall[...] = nn(parts, spread_matrix(HEADS * 128, 128))
    r, c = iotas((HEADS * 8, 128))
    pick = jnp.where(((c & 15) == r // 8) & (c < 48), 1.0, 0.0).astype(bf16)
    for b in range(t // 128):
        flat[b] = nt(pick, parts[b * 128 : (b + 1) * 128])


def k_within(cum_ref, bc_ref, xdt_ref, y_ref, tall, flat, scores):
    t = cum_ref.shape[0]
    need(cum_ref)
    decay_tables(cum_ref, tall, flat)
    blocks = t // BLOCK
    need(bc_ref, xdt_ref)
    for b in range(blocks):
        s = pl.ds(b * BLOCK, BLOCK)
        scores[s, :] = nt(bc_ref[s, STATE:], bc_ref[s, 0:STATE])
    r, c = iotas((128, 128))
    causal = r >= c
    lane = iotas((BLOCK, 128))[1]

    def pair(p):
        cols = at(p, 128)
        for b in range(blocks):
            o = b * BLOCK
            u = xdt_ref[pl.ds(o, BLOCK), cols]
            top = jnp.zeros((128, 128), f32)
            low = jnp.zeros((128, 128), f32)
            for a in range(2):
                head = 2 * p + a
                own = jnp.where((lane >= 64) == (a == 1), u, jnp.zeros_like(u))
                hc = at(head, 128)
                hr = pl.ds(pl.multiple_of(head * 8, 8), 8)
                t0, t1 = tall[pl.ds(o, 128), hc], tall[pl.ds(o + 128, 128), hc]
                u0, u1 = flat[2 * b, hr, :][0:1], flat[2 * b + 1, hr, :][0:1]
                sc = scores
                w00 = jnp.where(causal, sc[pl.ds(o, 128), 0:128] * jnp.exp(jnp.where(causal, t0 - u0, 0.0)), 0.0)
                w10 = sc[pl.ds(o + 128, 128), 0:128] * jnp.exp(t1 - u0)
                w11 = jnp.where(causal, sc[pl.ds(o + 128, 128), 128:] * jnp.exp(jnp.where(causal, t1 - u1, 0.0)), 0.0)
                top = top + nn(w00.astype(bf16), own[:128])
                low = low + nn(w10.astype(bf16), own[:128]) + nn(w11.astype(bf16), own[128:])
            y_ref[pl.ds(o, 128), cols] = top
            y_ref[pl.ds(o + 128, 128), cols] = low

    loop(OWN // 128, pair)


def k_out(first_layer, yw_ref, act_ref, bc_ref, cum_ref, cin_ref, s_ref, dec_ref, z_ref, par_ref, keep_ref, got_ref, *rest):
    if first_layer:
        y_ref, p_ref, msg_ref, st_ref, c_ref, wo_ref, wide, u_ref = rest
    else:
        cot_ref, ca_ref, cb_ref, y_ref, p_ref, msg_ref, st_ref, c_ref, wo_ref, g_ref, wide, u_ref = rest
    t = yw_ref.shape[0]
    half = WIDTH // 2
    shard = o_rows(keep_ref)

    def weights(core):
        for r in range(keep_ref.shape[0] // shard):
            for k in range(2):
                for src, side in ((keep_ref, core), (got_ref, 1 - core)):
                    wo_ref[(2 * r + k) * shard : (2 * r + k + 1) * shard, side * half : (side + 1) * half] = src[
                        r * shard : (r + 1) * shard, k * half : (k + 1) * half
                    ]

    need(keep_ref, got_ref)
    on_core(weights)
    done(wo_ref)
    need(bc_ref, cum_ref, cin_ref, s_ref, dec_ref)
    c_ref[0:STATE, :] = cin_ref[...].astype(f32)
    c_ref[STATE:, :] = s_ref[:STATE, :] + dec_ref[0:1, :] * c_ref[0:STATE, :]
    wide[...] = nn(thirds(jnp.exp(cum_ref[...])), spread_matrix(OWN, HDIM))
    for b in range(t // BLOCK):
        s = pl.ds(b * BLOCK, BLOCK)

        def cols(c):
            from_state = nn(bc_ref[s, STATE:], c_ref[pl.ds(b * STATE, STATE), at(c, 768)].astype(bf16))
            wide[s, at(c, 768)] = wide[s, at(c, 768)] * from_state

        loop(OWN // 768, cols)

    done(c_ref)
    need(yw_ref, act_ref, z_ref, par_ref)

    def rows(r):
        s = at(r, R)
        y = yw_ref[s, :] + wide[s, :] + par_ref[SKIP : SKIP + 1, :OWN] * act_ref[s, :OWN]
        y_ref[s, :] = y
        z = z_ref[s, :]
        gated = y * z * sig(z)
        u_ref[s, :] = (gated * par_ref[GATE : GATE + 1, :OWN]).astype(bf16)
        st_ref[s, 0:128] = jnp.broadcast_to(jnp.sum(gated * gated, axis=1, keepdims=True), (R, 128))

    loop(t // R, rows)
    done(y_ref)

    def project_out(c):
        p_ref[:, at(c, 768)] = nn(u_ref[...], wo_ref[:, at(c, 768)])

    loop(WIDTH // 768, project_out)
    done(p_ref)
    if first_layer:

        def send(r):
            s = at(r, R)
            msg_ref[s, :WIDTH] = p_ref[s, :].astype(bf16)
            v = st_ref[s, 0:128]
            msg_ref[s, WIDTH:] = stats_out(v, v)

        loop(t // R, send)
    else:
        odd = lax.rem(lax.axis_index("seq"), 2)
        need(cot_ref, ca_ref, cb_ref)
        copy_rows(g_ref, odd * (t // 2), cot_ref.at[odd])
        core = lax.axis_index("section")
        copy_rows(g_ref, (1 - odd) * (t // 2) + core * (t // 4), ca_ref)
        copy_rows(g_ref, (1 - odd) * (t // 2) + (1 - core) * (t // 4), cb_ref)
        done(g_ref)

        def dots(r):
            s = at(r, R)
            d = jnp.sum(p_ref[s, :] * g_ref[s, :].astype(f32), axis=1, keepdims=True)
            d = jnp.broadcast_to(d, (R, 128))
            st_ref[s, 128:256] = d
            msg_ref[s, half:] = stats_out(st_ref[s, 0:128], d)

        loop(t // R, dots)

        def send(core):
            msg_ref[:, :half] = p_ref[:, (1 - core) * half : (2 - core) * half].astype(bf16)

        on_core(send)


def o_rows(keep_ref):
    return keep_ref.shape[0] // (lax.axis_size("seq") // 2)


def k_final(h_ref, p_ref, st_ref, msg_ref, keep_ref, give_ref):
    need()
    half = WIDTH // 2
    rows_each = keep_ref.shape[0]
    odd = lax.rem(lax.axis_index("seq"), 2)

    def body(core):
        cols = slice(core * half, (core + 1) * half)

        def half_out(dst, start):
            def rows(r):
                s = pl.ds(pl.multiple_of(start + r * R, R), R)
                other = stats_in(msg_ref[s, half:])[0]
                rs = lax.rsqrt((st_ref[s, 0:1] + other) * (1.0 / INNER) + EPS)
                p = p_ref[s, cols] + msg_ref[s, :half].astype(f32)
                dst[at(r, R), :] = (h_ref[s, cols].astype(f32) + rs * p).astype(bf16)

            loop(rows_each // R, rows)

        half_out(keep_ref, odd * rows_each)
        half_out(give_ref, (1 - odd) * rows_each)

    on_core(body)


def kb_gate(g_ref, w_ref, y_ref, yw_ref, z_ref, act_ref, bc_ref, cum_ref, rs_ref, rd_ref, par_ref, dec_ref,
            qz_ref, dy_ref, df_ref, dca_ref, keep_ref, give_ref, d_ref, e_ref, small_ref, dgn, wide, gn):
    t = g_ref.shape[0]
    need(g_ref, w_ref)

    def back(c):
        dgn[:, at(c, 768)] = nt(g_ref[...], w_ref[at(c, 768), :])

    loop(OWN // 768, back)
    need(cum_ref)
    wide[...] = nn(thirds(jnp.exp(cum_ref[...])), spread_matrix(OWN, HDIM))
    small_ref[...] = jnp.zeros(small_ref.shape, f32)
    collect = collect_matrix()
    need()

    def rows(r):
        s = at(r, R)
        z, y, d, x = z_ref[s, :], y_ref[s, :], dgn[s, :], act_ref[s, :OWN]
        gg = par_ref[GATE : GATE + 1, :OWN]
        if rs_ref.shape[1] == 128:
            rs, rd = rs_ref[s, 0:1], rd_ref[s, 0:1]
        else:
            squares, dots = stats_in(rd_ref[s, WIDTH // 2 :])
            rs = lax.rsqrt((rs_ref[s, 0:1] + squares) * (1.0 / INNER) + EPS)
            rd = rs_ref[s, 128:129] + dots
        sg = sig(z)
        sz = z * sg
        gated = y * sz
        scaled = gated * rs
        small_ref[0:8, :] += fold(d * scaled)
        gn[s, :] = (scaled * gg).astype(bf16)
        dgated = rs * (gg * d) - gated * (rs * rs * rs * rd * (1.0 / INNER))
        dy = dgated * sz
        dy_ref[s, :] = dy
        qz_ref[s, :] = (dgated * y * (sg * (1.0 + z - sz))).astype(bf16)
        small_ref[8:16, :] += fold(dy * x)
        df_ref[s, :] = (wide[s, :] * dy).astype(bf16)
        yw = yw_ref[s, :]
        high, low = halves(dy.astype(bf16).astype(f32) * yw + dy * (y - yw - par_ref[SKIP : SKIP + 1, :OWN] * x))
        sums = nn(jnp.concatenate([high, low], axis=0), collect)
        dca_ref[s, :] = sums[:R] + sums[R:]

    loop(t // R, rows)
    done(dy_ref, qz_ref, df_ref, dca_ref, small_ref)
    for b in range(t // BLOCK):
        s = pl.ds(b * BLOCK, BLOCK)
        cl = bc_ref[s, STATE:]

        def cols(c):
            d_ref[pl.ds(b * STATE, STATE), at(c, 768)] = tn(cl, df_ref[s, at(c, 768)])

        loop(OWN // 768, cols)
    e_ref[...] = (d_ref[:STATE, :] + dec_ref[0:1, :] * d_ref[STATE:, :]).astype(bf16)

    done(d_ref, e_ref)
    half = WIDTH // 2

    def halves_of(core):
        def weight(c):
            dw = tn(gn[:, at(c, 768)], g_ref[...]).astype(bf16)
            keep_ref[at(c, 768), :] = dw[:, core * half : (core + 1) * half]
            give_ref[at(c, 768), :] = dw[:, (1 - core) * half : (2 - core) * half]

        loop(OWN // 768, weight)

    on_core(halves_of)


def kb_within(dy_ref, xdt_ref, cum_ref, bc_ref, df_ref, c_ref, dx_ref, dbc_ref, tall, flat, scores, ds):
    t = cum_ref.shape[0]
    need(cum_ref)
    decay_tables(cum_ref, tall, flat)
    blocks = t // BLOCK
    need(bc_ref, xdt_ref, dy_ref)
    for b in range(blocks):
        s = pl.ds(b * BLOCK, BLOCK)
        scores[s, :] = nt(bc_ref[s, STATE:], bc_ref[s, 0:STATE])
    ds[...] = jnp.zeros(ds.shape, f32)
    r, c = iotas((128, 128))
    causal = r >= c
    lane = iotas((BLOCK, 128))[1]

    def pair(p):
        cols = at(p, 128)
        for b in range(blocks):
            o = b * BLOCK
            u = xdt_ref[pl.ds(o, BLOCK), cols]
            g = dy_ref[pl.ds(o, BLOCK), cols].astype(bf16)
            top = jnp.zeros((128, 128), f32)
            low = jnp.zeros((128, 128), f32)
            for a in range(2):
                head = 2 * p + a
                own = jnp.where((lane >= 64) == (a == 1), g, jnp.zeros_like(g))
                hc = at(head, 128)
                hr = pl.ds(pl.multiple_of(head * 8, 8), 8)
                t0, t1 = tall[pl.ds(o, 128), hc], tall[pl.ds(o + 128, 128), hc]
                u0, u1 = flat[2 * b, hr, :][0:1], flat[2 * b + 1, hr, :][0:1]
                e00 = jnp.where(causal, jnp.exp(jnp.where(causal, t0 - u0, 0.0)), 0.0)
                e10 = jnp.exp(t1 - u0)
                e11 = jnp.where(causal, jnp.exp(jnp.where(causal, t1 - u1, 0.0)), 0.0)
                q0, q1 = pl.ds(o, 128), pl.ds(o + 128, 128)
                w00 = (scores[q0, 0:128] * e00).astype(bf16)
                w10 = (scores[q1, 0:128] * e10).astype(bf16)
                w11 = (scores[q1, 128:] * e11).astype(bf16)
                top = top + tn(w00, own[:128]) + tn(w10, own[128:])
                low = low + tn(w11, own[128:])
                ds[q0, 0:128] += nt(own[:128], u[:128]) * e00
                ds[q1, 0:128] += nt(own[128:], u[:128]) * e10
                ds[q1, 128:] += nt(own[128:], u[128:]) * e11
            dx_ref[pl.ds(o, 128), cols] = top
            dx_ref[pl.ds(o + 128, 128), cols] = low

    loop(OWN // 128, pair)
    done(dx_ref)
    need(df_ref, c_ref)
    for b in range(blocks):
        s = pl.ds(b * BLOCK, BLOCK)
        d = ds[s, :].astype(bf16)
        carried = c_ref[pl.ds(b * STATE, STATE), :].astype(bf16)
        dbc_ref[s, 0:STATE] = tn(d, bc_ref[s, STATE:])
        dbc_ref[s, STATE:] = nn(d, bc_ref[s, 0:STATE]) + nt(df_ref[s, :], carried)


def kb_front(gin_ref, d_ref, c_ref, dec_ref, bc_ref, xdt_ref, act_ref, xb_ref, slope_ref, before_ref, dt_ref, cum_ref, dxw_ref, dbc_ref,
             dy_ref, dca_ref, par_ref,
             dxb_ref, halo_ref, qdt_ref, small_ref, head_ref, gs, dd, te, dtw, dact, red, red2, ends, pad):
    t = act_ref.shape[0]
    blocks = t // BLOCK
    spread, collect = spread_matrix(OWN, HDIM), collect_matrix()
    need(gin_ref, d_ref, dec_ref)
    gs[STATE:, :] = gin_ref[...].astype(f32)
    gs[:STATE, :] = d_ref[STATE:, :] + dec_ref[8:9, :] * gs[STATE:, :]
    need(dbc_ref, dt_ref, c_ref, cum_ref, bc_ref, xdt_ref)
    dact[:, OWN:] = dbc_ref[...]
    dtw[...] = nn(thirds(dt_ref[...]), spread)
    for b in range(blocks):
        s = pl.ds(b * BLOCK, BLOCK)
        ss = pl.ds(b * STATE, STATE)
        end = cum_ref[pl.ds((b + 1) * BLOCK - 8, 8), :][7:8]
        te[s, :] = nn(thirds(jnp.exp(end - cum_ref[s, :])), spread)
        bl = bc_ref[s, 0:STATE]
        ends[8 * b : 8 * b + 8, :] = fold(gs[ss, :] * c_ref[ss, :]) * dec_ref[8 * b : 8 * b + 8, :]

        def cols(c):
            q = at(c, 768)
            low = gs[ss, q].astype(bf16)
            dd[s, q] = nn(bl, low)
            decayed = (xdt_ref[s, q].astype(f32) * te[s, q]).astype(bf16)
            dact[s, OWN : OWN + STATE] += nt(decayed, low)

        loop(OWN // 768, cols)
        if b == 0:
            need(dxw_ref, dy_ref, act_ref, par_ref)

        def rows(r):
            q = pl.ds(pl.multiple_of(b * BLOCK + r * R, R), R)
            w = dd[q, :] * te[q, :]
            ends[8 * b : 8 * b + 8, :] += fold(w * xdt_ref[q, :].astype(f32))
            dxdt = dxw_ref[q, :] + w
            dact[q, :OWN] = dxdt * dtw[q, :] + par_ref[SKIP : SKIP + 1, :OWN] * dy_ref[q, :]
            parts = [(dxdt * act_ref[q, :OWN]).astype(bf16), *halves(dxdt * xdt_ref[q, :].astype(f32))]
            sums = nn(jnp.concatenate(parts, axis=0), collect)
            red[q, :] = sums[:R]
            red2[q, :] = sums[R : 2 * R] + sums[2 * R :]

        loop(BLOCK // R, rows)
    need()
    high, low = halves(ends[...])
    at_end = nn(high, collect) + nn(low, collect)
    rate = -jnp.exp(par_ref[RATE : RATE + 1, 0:128])
    head_ref[...] = jnp.zeros(head_ref.shape, f32)
    for b in range(blocks):
        s = pl.ds(b * BLOCK, BLOCK)
        dt = dt_ref[s, :]
        total = running_sum(dca_ref[s, :] - red2[s, :], True)
        total = total + jnp.sum(at_end[8 * b : 8 * b + 8], axis=0, keepdims=True)
        ddt = red[s, :] + rate * total
        raw = xb_ref[pl.ds(8 + b * BLOCK, BLOCK), XC:] + par_ref[STEP : STEP + 1, 0:128]
        draw = ddt * jax.nn.sigmoid(raw)
        head_ref[0:8, :] += fold(draw)
        head_ref[8:16, :] += fold(rate * dt * total)
        lane = iotas(draw.shape)[1]
        qdt_ref[s, :] = jnp.where(lane < HEADS, draw, 0.0).astype(bf16)
    done(qdt_ref, head_ref)
    pad[0:8, :] = jnp.zeros((8, 128), f32)
    pad[8 + t :, :] = jnp.zeros((8, 128), f32)

    def conv(c):
        cols = at(c, 128)
        w = par_ref[0:8, cols]
        d = dact[:, cols] * slope_ref[:, cols].astype(f32)
        pad[8 : 8 + t, :] = d
        small_ref[32:40, cols] = fold(d)
        xb, before = xb_ref[:, cols], before_ref[:, cols]
        out = 0.0
        for k in range(4):
            later = pad[3 - k : 11 - k + t, :]
            out = out + w[k : k + 1] * later
            small_ref[8 * k : 8 * k + 8, cols] = fold(later * xb) + later[0:8] * before
        dxb_ref[:, cols] = out
        halo_ref[:, cols] = out[0:8]

    loop(XC // 128, conv)


def z_weight(dw_ref, first, normed_ref, qz_ref, okeep_ref, ogot_ref):
    def weight(c):
        dw_ref[at(c, 768), first : first + OWN] = tn(normed_ref[:, at(c, 768)], qz_ref[...]).astype(bf16)

    loop(WIDTH // 768, weight)
    n = lax.axis_size("seq")
    shard, half = WIDTH // n, WIDTH // 2
    need()

    def out(core):
        for j in range(n):
            src = okeep_ref if j // (n // 2) == core else ogot_ref
            for k in range(2):
                row, col = (2 * (j % (n // 2)) + k) * shard, first + OWN + k * half
                dw_ref[j * shard : (j + 1) * shard, col : col + half] = src[row : row + shard, :]

    on_core(out)


def kb_z_weight(normed_ref, qz_ref, okeep_ref, ogot_ref, *rest):
    *blocks, dw_ref = rest
    need(normed_ref, qz_ref)
    z_weight(dw_ref, 0, normed_ref, qz_ref, okeep_ref, ogot_ref)
    to_blocks(blocks, dw_ref)


CUT = 640


def kb_x_weight(normed_ref, q_ref, *rest):
    *parts, dw_ref = rest
    need()
    x_weight(normed_ref, q_ref, dw_ref)
    if len(parts) == 1:
        return copy_rows(parts[0], 0, dw_ref)
    me = lax.axis_index("seq")
    rows = WIDTH // 4
    first, last = slice(0, CUT), slice(CUT, XD)
    for ref, cols, ranks in zip(parts, (first, last, first, last), ((1, 3), (2, 3), (0, 2), (0, 1))):
        for k, bits in enumerate(ranks):
            start = (me ^ bits) * rows

            def move(r, ref=ref, cols=cols, k=k, start=start):
                ref[pl.ds(pl.multiple_of(k * rows + r * 48, 16), 48), :] = dw_ref[
                    pl.ds(pl.multiple_of(start + r * 48, 16), 48), cols
                ]

            loop(rows // 48, move)
        done(ref)


def k_phase(keep_a, keep_b, got_a, got_b, own_a, own_b, give_a, give_b):
    need()
    rows = own_a.shape[0]
    for keep, got, own, give in ((keep_a, got_a, own_a, give_a), (keep_b, got_b, own_b, give_b)):
        for dst, start in ((give, rows), (own, 0)):

            def move(r, keep=keep, got=got, dst=dst, start=start):
                s = pl.ds(pl.multiple_of(start + r * 48, 16), 48)
                dst[at(r, 48), :] = (keep[s, :].astype(f32) + got[s, :].astype(f32)).astype(bf16)

            loop(rows // 48, move)
            done(dst)


def to_blocks(blocks, dw):
    if len(blocks) == 1:
        return copy_rows(blocks[0], 0, dw)
    me = lax.axis_index("seq")
    rows = blocks[0].shape[0]
    for k in reversed(range(len(blocks))):
        block, start = blocks[k], (me ^ k) * rows

        def move(r, block=block, start=start):
            block[at(r, 48), :] = dw[pl.ds(pl.multiple_of(start + r * 48, 16), 48), :]

        loop(rows // 48, move)
        done(block)


def kb_z_normed(qz_ref, w_ref, dn_ref):
    need()

    def back(c):
        dn_ref[:, at(c, 768)] = nt(qz_ref[...], w_ref[at(c, 768), :])

    loop(WIDTH // 768, back)


def make_q(dxb_ref, ret_ref, qdt_ref, q):
    t = q.shape[0]

    def rows(r):
        q[at(r, R), :XC] = dxb_ref[pl.ds(pl.multiple_of(r * R, R) + 8, R), :].astype(bf16)

    loop(t // R, rows)
    q[t - 16 :, :XC] = (
        dxb_ref[t - 8 : t + 8, :] + jnp.concatenate([jnp.zeros((8, XC), f32), ret_ref[...]], axis=0)
    ).astype(bf16)
    q[:, XC:] = qdt_ref[...]


def x_normed(q_ref, dnz_ref, w_ref, dn_ref, dnb_ref):
    def back(c):
        cols = at(c, 768)
        d = dnz_ref[:, cols] + nt(q_ref[...], w_ref[cols, :])
        dn_ref[:, cols] = d
        dnb_ref[:, cols] = d.astype(bf16)

    loop(WIDTH // 768, back)


def x_weight(normed_ref, q_ref, dw_ref):
    def weight(c):
        dw_ref[at(c, 768), :] = tn(normed_ref[:, at(c, 768)], q_ref[...]).astype(bf16)

    loop(WIDTH // 768, weight)


def kb_x_normed(dxb_ref, ret_ref, qdt_ref, dnz_ref, w_ref, q_ref, dn_ref, dnb_ref):
    need(dxb_ref, ret_ref, qdt_ref)
    make_q(dxb_ref, ret_ref, qdt_ref, q_ref)
    done(q_ref)
    need()
    x_normed(q_ref, dnz_ref, w_ref, dn_ref, dnb_ref)


def kb_x_weight_first(normed_ref, dxb_ref, ret_ref, qdt_ref, q_ref, *rest):
    *blocks, dw = rest
    need()
    make_q(dxb_ref, ret_ref, qdt_ref, q_ref)
    done(q_ref)
    x_weight(normed_ref, q_ref, dw)
    to_blocks(blocks, dw)


def kb_x_normed_last(q_ref, dnz_ref, w_ref, dn_ref, dnb_ref):
    need()
    x_normed(q_ref, dnz_ref, w_ref, dn_ref, dnb_ref)


def kb_norm(h_ref, dn_ref, dr_ref, g_ref, par_ref, pt_ref, gh_ref, small_ref, rd_ref):
    t = h_ref.shape[0]
    need()
    small_ref[...] = jnp.zeros(small_ref.shape, f32)

    def rows(r):
        s = at(r, R)
        h = h_ref[s, :].astype(f32)
        d = dn_ref[s, :] + dr_ref[s, :].astype(f32)
        scale = lax.rsqrt(jnp.mean(h * h, axis=1, keepdims=True) + EPS)
        hs = h * scale
        small_ref[...] += fold(d * hs)
        gd = par_ref[NORM : NORM + 1, :WIDTH] * d
        back = scale * (gd - hs * jnp.mean(hs * gd, axis=1, keepdims=True))
        gh = (g_ref[s, :].astype(f32) + back).astype(bf16)
        gh_ref[s, :] = gh
        if rd_ref is not None:
            dot = jnp.sum(gh.astype(f32) * pt_ref[s, :], axis=1, keepdims=True)
            rd_ref[s, :] = jnp.broadcast_to(dot, (R, 128))

    loop(t // R, rows)


def kb_norm_last(h_ref, dn_ref, dr_ref, g_ref, par_ref, keep_ref, give_ref, small_ref, gh):
    kb_norm(h_ref, dn_ref, dr_ref, g_ref, par_ref, None, gh, small_ref, None)
    half = WIDTH // 2
    each = keep_ref.shape[0]
    odd = lax.rem(lax.axis_index("seq"), 2)

    def body(core):
        def rows(r):
            for dst, start in ((keep_ref, odd * each), (give_ref, (1 - odd) * each)):
                s = pl.ds(pl.multiple_of(start + r * R, R), R)
                dst[at(r, R), :] = gh[s, core * half : (core + 1) * half]

        loop(each // R, rows)

    on_core(body)


SMALL = 12


def k_small(*refs):
    *ins, out = refs
    need()
    out[...] = jnp.zeros(out.shape, f32)

    def total(x):
        return jnp.sum(x, axis=0, keepdims=True)

    for layer in range(2):
        a, b, c, d = ins[4 * layer : 4 * layer + 4]
        base = SMALL * layer
        for k in range(5):
            out[base + k : base + k + 1, :] = total(b[8 * k : 8 * k + 8, :])
        out[base + NORM : base + NORM + 1, :WIDTH] = total(d[...])
        out[base + GATE : base + GATE + 1, :OWN] = total(a[0:8, :])
        out[base + SKIP : base + SKIP + 1, :OWN] = total(a[8:16, :])
        out[base + STEP : base + STEP + 1, 0:128] = total(c[0:8, :])
        out[base + RATE : base + RATE + 1, 0:128] = total(c[8:16, :])


def k_small_out(mine_ref, got_ref, ng_ref, cw_ref, cb_ref, db_ref, al_ref, sk_ref, gg_ref):
    need()

    def body(core):
        base = SMALL * core
        cores = (mine_ref, got_ref) if core == 0 else (got_ref, mine_ref)
        ng_ref[...] = mine_ref[base + NORM : base + NORM + 1, :WIDTH]
        for c, src in enumerate(cores):
            cw_ref[:, c * OWN : (c + 1) * OWN] = src[base : base + 4, :OWN]
            cb_ref[:, c * OWN : (c + 1) * OWN] = src[base + BIAS : base + BIAS + 1, :OWN]
            gg_ref[:, c * OWN : (c + 1) * OWN] = src[base + GATE : base + GATE + 1, :OWN]
        a, b = cores
        cw_ref[:, INNER:] = a[base : base + 4, OWN:] + b[base : base + 4, OWN:]
        cb_ref[:, INNER:] = a[base + BIAS : base + BIAS + 1, OWN:] + b[base + BIAS : base + BIAS + 1, OWN:]
        r, c = iotas((128, 2 * HEADS))
        r2, c2 = iotas((OWN, 2 * HEADS))
        wide = lambda v: jnp.broadcast_to(v, (8, v.shape[1]))
        for ref, row in ((db_ref, STEP), (al_ref, RATE)):
            acc = jnp.zeros((8, 2 * HEADS), f32)
            for k, src in enumerate(cores):
                pick = jnp.where((r == c - k * HEADS) & (r < HEADS), 1.0, 0.0)
                acc = acc + exact(wide(src[base + row : base + row + 1, 0:128]), pick)
            ref[...] = acc[0:1]
        acc = jnp.zeros((8, 2 * HEADS), f32)
        for k, src in enumerate(cores):
            pick = jnp.where(r2 // HDIM == c2 - k * HEADS, 1.0, 0.0)
            acc = acc + exact(wide(src[base + SKIP : base + SKIP + 1, :OWN]), pick)
        sk_ref[...] = acc[0:1]

    on_core(body)


def in_place(refs, full):
    if len(refs) == 1:
        return copy_rows(full, 0, refs[0])
    odd = lax.rem(lax.axis_index("dp"), 2)
    half = refs[0].shape[0]
    copy_rows(full, odd * half, refs[0])
    copy_rows(full, (1 - odd) * half, refs[1])


def k_home(*refs):
    *halves_all, give_ref, zo, x = refs
    per = len(halves_all) // 3
    first, second, third = halves_all[:per], halves_all[per : 2 * per], halves_all[2 * per :]
    need()

    def body(core):
        if core == 0:
            in_place(first, give_ref)
        else:
            in_place(second, zo)
            in_place(third, x)
            give_ref[:, :XD] = x[...]
            give_ref[:, XD:] = zo[...]

    on_core(body)


def k_grads(*refs):
    *halves_all, got_ref, gw_ref, go_ref, dw1, zo0, x0 = refs
    per = len(halves_all) // 3
    first_halves, second, third = halves_all[:per], halves_all[per : 2 * per], halves_all[2 * per :]
    need()
    rows, half = got_ref.shape[0], WIDTH // 2

    def body(core):
        if core:
            in_place(first_halves, dw1)
        else:
            in_place(second, zo0)
            in_place(third, x0)
        mine = (x0, zo0, 0) if core == 0 else (dw1, dw1, XD)
        other = (got_ref, got_ref, XD)
        cores = (mine, other) if core == 0 else (other, mine)
        for c, (x, zo, first) in enumerate(cores):
            for k in range(2):
                col = first + OWN + k * half
                go_ref[k * rows : (k + 1) * rows, c * half : (c + 1) * half] = zo[:, col : col + half].astype(f32)

    def rest(core):
        mine = (x0, zo0, 0) if core == 0 else (dw1, dw1, XD)
        other = (got_ref, got_ref, XD)
        cores = (mine, other) if core == 0 else (other, mine)
        for c, (x, zo, first) in enumerate(cores):
            gw_ref[:, c * OWN : (c + 1) * OWN] = zo[:, first : first + OWN].astype(f32)
            gw_ref[:, INNER + c * OWN : INNER + (c + 1) * OWN] = x[:, :OWN].astype(f32)
        a, b = cores[0][0], cores[1][0]
        gw_ref[:, 2 * INNER : 2 * INNER + 2 * STATE] = a[:, OWN:XC].astype(f32) + b[:, OWN:XC].astype(f32)
        r, c = iotas((128, 2 * HEADS))
        acc = 0.0
        for k, x in enumerate((a, b)):
            pick = jnp.where((r == c - k * HEADS) & (r < HEADS), 1.0, 0.0).astype(bf16)
            acc = acc + nn(x[:, XC:XD], pick)
        gw_ref[:, INNER + CONV :] = acc

    on_core(body)
    done(go_ref)
    on_core(rest)


def across(x):
    return jax.tree.map(lambda a: lax.ppermute(a, "section", [(0, 1), (1, 0)]), x)


def flip(x, axis, bits):
    return lax.ppermute(x, axis, [(k, k ^ bits) for k in range(lax.axis_size(axis))])


def chain_step(x, steps, backward):
    n = lax.axis_size("seq")
    hop = -2 * steps if backward else 2 * steps
    return lax.ppermute(x, "seq", [(k, k + hop) for k in range(n) if 0 <= k + hop < n])


def chain(value, decay, backward):
    entered = chain_step(value, 1, backward)
    count = lax.axis_size("seq") // 2
    if count > 2:
        rate = chain_step(decay, 1, backward)
        total = entered.astype(f32)
        steps = 1
        while steps < count - 1:
            total = total + rate[0:1] * chain_step(total.astype(bf16), steps, backward).astype(f32)
            rate = rate * chain_step(rate, steps, backward)
            steps *= 2
        entered = total.astype(bf16)
    return entered


def gather_rows(x):
    n = lax.axis_size("seq")
    if n != 4:
        return [lax.all_gather(x, "seq", axis=0, tiled=True)]
    return [x, *[flip(x, "seq", k) for k in (1, 2, 3)]]


def gather_near(x):
    if lax.axis_size("seq") != 4:
        return gather_rows(x)
    return [x, flip(x, "seq", 1), flip(x, "seq", 2)]


def gather_across(parts, *release):
    if len(parts) == 1:
        return parts
    x, gx, gy = parts
    gx, gy, *_ = lax.optimization_barrier((gx, gy, *release))
    half = x.shape[0] // 2
    return [x, gx, gy, flip(gx[:half], "seq", 2), flip(gy[half:], "seq", 1)]


def k_sum(counts, *refs):
    *blocks, keep_ref, give_ref = refs
    starts = [sum(counts[:k]) for k in range(len(counts))]
    need()
    odd = lax.rem(lax.axis_index("dp"), 2)
    half = keep_ref.shape[0]
    step = 48 if half % 48 == 0 else half
    for dst, start in ((give_ref, (1 - odd) * half), (keep_ref, odd * half)):

        def rows(r, dst=dst, start=start):
            s = pl.ds(pl.multiple_of(start + r * step, 16), step)
            first = 0
            for begin, count in zip(starts, counts):
                total = 0.0
                for ref in blocks[begin : begin + count]:
                    total = total + ref[s, :].astype(f32)
                dst[at(r, step), first : first + total.shape[1]] = total.astype(dst.dtype)
                first += total.shape[1]

        loop(half // step, rows)
        done(dst)


def k_add(a_ref, b_ref, out_ref):
    need()

    def rows(r):
        s = at(r, 16)
        out_ref[s, :] = (a_ref[s, :].astype(f32) + b_ref[s, :].astype(f32)).astype(bf16)

    loop(out_ref.shape[0] // 16, rows)


def send_blocks(blocks):
    if len(blocks) > 1:
        return [blocks[0]] + [flip(blocks[k], "seq", k) for k in (3, 2, 1)]
    return [lax.psum_scatter(blocks[0], "seq", scatter_dimension=0, tiled=True)]


def whole_sum(groups):
    total = jnp.concatenate([sum(b.astype(f32) for b in group) for group in groups], axis=1)
    return [lax.psum(total.astype(bf16), "dp")]


def halved(groups, *pins):
    got = [b for group in groups for b in group]
    rows, width = got[0].shape[0], sum(group[0].shape[1] for group in groups)
    shape = (rows // 2, width)
    return run(
        functools.partial(k_sum, [len(group) for group in groups]), "sum", [(shape, f32, "a"), (shape, bf16, "a")],
        after(got[0], *pins), *got[1:],
    )


def paired(mine, got, *pins):
    return run(k_add, "add", [(got.shape, bf16, "a")], after(mine, *pins), got)[0]


def over_dp(keep, got, *pins, later=()):
    return further([paired(keep, got, *pins)], *later)


def further(mine, *later):
    (mine,), bit = mine, 2
    while bit < lax.axis_size("dp"):
        mine = paired(mine, flip(mine, "dp", bit), *later)
        bit *= 2
    return mine, flip(mine, "dp", 1)


def simple_dp(rows):
    n = lax.axis_size("dp")
    return n == 1 or n & (n - 1) != 0 or rows % 32 != 0


def summed_dp(groups, *pins, before=(), later=()):
    if simple_dp(groups[0][0].shape[0]):
        return whole_sum(groups)
    keep, give = halved(groups, *before)
    return over_dp(keep, flip(give, "dp", 1), *pins, later=later)


def k_add_small(*refs):
    *ins, out_ref = refs
    need()
    if len(ins) == 2:
        out_ref[...] = ins[0][...] + ins[1][...]
    else:
        out_ref[...] = (ins[0][...] + ins[1][...]) + (ins[2][...] + ins[3][...])


def sum_small(x, axes):
    for axis in axes:
        n = lax.axis_size(axis)
        if n == 4:
            x = run(k_add_small, "add_small", [(x.shape, f32, "a")], x, *[flip(x, axis, k) for k in (1, 2, 3)])[0]
        elif n & (n - 1):
            x = lax.psum(x, axis)
        else:
            bit = 1
            while bit < n:
                x = run(k_add_small, "add_small", [(x.shape, f32, "a")], x, flip(x, axis, bit))[0]
                bit *= 2
    return x


def sum_small_dp(x):
    n = lax.axis_size("dp")
    if n & (n - 1):
        return lax.psum(x, "dp"), x
    half_way, bit = x, 1
    while bit < n:
        x = run(k_add_small, "add_small", [(x.shape, f32, "a")], x, flip(x, "dp", bit))[0]
        half_way = x if bit == 1 else half_way
        bit *= 2
    return x, half_way


def after(x, *others):
    return lax.optimization_barrier((x, *others))[0]


AHEAD = ["xdt", "cum", "bc", "c"], ["act", "xb", "slope", "dt"], ["wz", "wx"]
AHEAD_WEIGHT, AHEAD_NORM = ["y", "yw"], ["wo", "z", "act"]


def on_device(hidden_in, cotangent, norm_gain, in_weight, conv_weight, conv_bias, dt_bias, a_log, skip, gate_gain, out_weight):
    core = lax.axis_index("section")
    first = core == 0
    odd = lax.axis_index("seq") % 2
    even = odd == 0
    length = hidden_in.shape[1]
    t = 2 * length
    n = lax.axis_size("seq")
    shard = in_weight.shape[1]
    half = WIDTH // 2
    packed = XD + 2 * OWN

    def given(x):
        return lax.dynamic_index_in_dim(x, 1 - odd, 0, keepdims=False)

    def both_sequences(mine, give):
        got = flip(give, "seq", 1)
        return jnp.stack([jnp.where(even, mine, got), jnp.where(even, got, mine)])

    hid_half, cot_half, mine_x, give_x, mine_zo, give_zo, mine_p, give_p = run(
        k_prep, "prep",
        [((length // 2, WIDTH), bf16, "a"), ((length // 2, WIDTH), bf16, "a"), ((shard, XD), bf16, "v"),
         ((shard, XD), bf16, "a"), ((shard, 2 * OWN), bf16, "v"), ((shard, 2 * OWN), bf16, "a"),
         ((PARAMS, XC), f32, "v"), ((PARAMS, XC), f32, "a")],
        *[
            far_away(a)
            for a in (hidden_in, cotangent, in_weight[0], out_weight[0], norm_gain, conv_weight[0], conv_bias, dt_bias, a_log, skip, gate_gain)
        ],
    )
    x0, x1, par0, par1 = run(
        k_pick, "pick",
        [((shard, XD), bf16, "a"), ((shard, XD), bf16, "a"), ((PARAMS, XC), f32), ((PARAMS, XC), f32)],
        mine_x, across(give_x), mine_p, across(give_p),
    )
    zo0, zo1 = run(
        k_pick_rest, "pick_rest", [((shard, 2 * OWN), bf16, "a"), ((shard, 2 * OWN), bf16, "a")], mine_zo, across(give_zo)
    )
    params = [par0, par1]

    def half_given(x):
        return lax.dynamic_slice_in_dim(given(x), core * (length // 2), length // 2, 0)

    def both_halves(mine):
        got = flip(mine, "seq", 1)
        return got, across(got)

    ga, gb = both_halves(hid_half)
    give_cot = cot_half
    parts_x0 = gather_rows(after(x0, ga, give_cot))
    near_zo0 = gather_near(after(zo0, *parts_x0))

    saved = [{}, {}]

    def keeping(layer, soon):
        return "vh" if soon else "h"

    def named(layer, names, results, modes, stayed=()):
        soon, at_result = {}, 0
        for name, mode in zip(names, modes):
            for m in mode:
                value = results[at_result]
                at_result += 1
                if m != "h":
                    soon[name] = value
                if m == mode[-1]:
                    saved[layer][name] = value
        for name in stayed:
            saved[layer][name] = results[len(results) - len(stayed) + stayed.index(name)]
        return soon

    def scan_part(layer, x, tail, near_zo, before_front):
        par = params[layer]
        last = keeping(layer, False)
        before = chain_step(tail, 1, False)
        saved[layer]["before"] = before
        modes = ["v"] * 8 + ["a"]
        shapes = [((t, XC), f32), ((t, XC), bf16), ((t, 2 * STATE), bf16), ((t, OWN), bf16), ((t, 128), f32), ((t, 128), f32),
                  ((2 * STATE, OWN), f32), ((16, OWN), f32), ((STATE, OWN), bf16)]
        x |= named(
            layer, ["act", "slope", "bc", "xdt", "dt", "cum", "s", "dec", "tot"],
            run(
                k_front, "front", [(*shape, m) for shape, m in zip(shapes, modes)],
                x["xb"], after(before, *before_front), par, scratch=[((t, OWN), f32), ((16, XC), f32)],
            ),
            modes,
        )
        dec = saved[layer]["dec"]
        saved[layer]["decay"] = dec[:8] * dec[8:] if n > 4 else None
        entered = chain(x["tot"], saved[layer]["decay"], False)
        x |= named(
            layer, ["yw"],
            run(
                k_within, "within", [((t, OWN), f32, "v")], x["cum"], x["bc"], x["xdt"],
                scratch=[((t, HEADS * 128), f32), ((t // 128, HEADS * 8, 128), f32), ((t, BLOCK), f32)],
                stay=[x[k] for k in ("xb", "slope", "dt", "cum")],
            ),
            ["v"],
            ["xb", "slope", "dt", "cum"],
        )
        parts_zo = gather_across(near_zo, before)
        x["parts_zo"] = parts_zo
        modes = ["v", "h", "v", "p"]
        x |= named(
            layer, ["z", "wz", "keep", "give"],
            run(
                k_z, "gate_in",
                [((t, OWN), f32, modes[0]), ((WIDTH, OWN), bf16, modes[1]), ((WIDTH // 2, OWN), bf16, "v"),
                 ((WIDTH // 2, OWN), bf16, "p")],
                near(after(x["normed"], x["yw"], entered)), *parts_zo, scratch=[((WIDTH, OWN), bf16)],
                stay=[x[k] for k in ("normed", "xdt", "bc", "dec")],
            ),
            modes,
            ["normed", "xdt", "bc", "dec"],
        )
        ogot = across(x["give"])
        x["entered"] = entered
        cot_halves = [ca, cb] if layer else []
        ins = [x["yw"], x["act"], x["bc"], x["cum"], entered, x["s"], x["dec"], x["z"], par, x["keep"], ogot]
        kept = "v" if layer else "h"
        stayed = ["act"] if layer else ["act", "yw", "z"]
        modes = [kept, "h" if layer else "v", "p", "vh" if layer else "v", last, kept] + ["vh"] * layer
        shapes = [((t, OWN), f32), ((t, WIDTH), f32), ((t, half + 128 if layer else WIDTH + 128), bf16),
                  ((t, 256 if layer else 128), f32), ((2 * STATE, OWN), f32), ((OWN, WIDTH), bf16)]
        shapes += [((t, WIDTH), bf16)] * layer
        results = run(
            functools.partial(k_out, layer == 0), "out", [(*shape, m) for shape, m in zip(shapes, modes)],
            *ins, *([cotangent, *cot_halves] if layer else []), scratch=[((t, OWN), f32), ((t, OWN), bf16)],
            ahead=[] if layer else [saved[0]["h"]], stay=[x[k] for k in stayed],
        )
        x |= named(layer, ["y", "p", "msg", "st", "c", "wo", "g"][: len(modes)], results, modes, stayed)
        if layer == 0:
            x["h"] = results[-1 - len(stayed)]
        return x

    outs_in = [((t, WIDTH), bf16), ((t + 8, XD), f32), ((WIDTH, XD), bf16), ((8, XC), f32)]
    names_in = ["normed", "xb", "wx", "tail"]
    modes = ["h", "v", "v", "h", "a"]
    shapes = [((t, WIDTH), bf16), *outs_in]
    x = named(
        0, ["h", *names_in],
        run(k_in, "project", [(*shape, m) for shape, m in zip(shapes, modes)], hidden_in, ga, gb, par0, *parts_x0),
        modes,
    )
    tail0 = x["tail"]
    x = scan_part(0, x, tail0, near_zo0, [])
    parts_x1 = gather_across(gather_near(after(x1, x["entered"], x["yw"], *x["parts_zo"][3:])), x["msg"])
    msg = across(x["msg"])
    near_zo1 = gather_near(after(zo1, *parts_x1, *msg))
    modes = ["h", "h", "h", "v", "v", "h", "a"]
    shapes = [((t, WIDTH), bf16), ((t, WIDTH), f32), ((t, 128), f32), *outs_in]
    x = named(
        1, ["h", "pt", "rs", *names_in],
        run(
            k_mid, "middle", [(*shape, m) for shape, m in zip(shapes, modes)],
            x["h"], x["p"], x["st"], msg, par1, *parts_x1,
        ),
        modes,
    )
    h1_far, pt, rs0 = saved[1]["h"], saved[1]["pt"], saved[1]["rs"]
    tail1 = x["tail"]
    ca, cb = both_halves(after(give_cot, tail1))
    x = scan_part(1, x, x["tail"], near_zo1, near_zo1[1:])
    p1, st1, st1_far = saved[1]["p"], x["st"], saved[1]["st"]
    msg = across(x["msg"])
    count = 4 if n == 4 else 1

    ahead_zw, ahead_within, ahead_front = AHEAD

    def backward(layer, v, g, rs, rd, close=None, before_zw=(), before_zo=()):
        par = params[layer]
        v = dict(v)
        far = dict(v)

        def fetched(names, results):
            if names:
                v.update(zip(names, results[-len(names) :]))

        qz, dy, df, dca, okeep, ogive, d, e, small_a = run(
            kb_gate, "back_gate",
            [((t, OWN), bf16, "v"), ((t, OWN), f32, "v"), ((t, OWN), bf16, "v"), ((t, 128), f32, "v"),
             ((OWN, half), bf16, "v"), ((OWN, half), bf16, "p"), ((2 * STATE, OWN), f32, "v"),
             ((STATE, OWN), bf16, "a"), ((16, OWN), f32)],
            g, *[(close or v)[k] for k in ("wo", "y", "yw", "z", "act", "bc", "cum")], rs, rd, par, (close or v)["dec"],
            scratch=[((t, OWN), f32), ((t, OWN), f32), ((t, OWN), bf16)],
        )
        entered = chain(e, v["decay"], True)
        ogot = across(ogive)
        results = run(
            kb_z_weight, "back_zw", [((WIDTH // count, 2 * OWN), bf16, "a")] * count, v["normed"], qz, okeep,
            after(ogot, *before_zw),
            scratch=[((WIDTH, 2 * OWN), bf16)], ahead=[v[k] for k in ahead_zw],
        )
        zo = list(results[:count])
        beside_zw = [*zo]
        if layer:
            zo = [after(b, entered) for b in zo]
        fetched(ahead_zw, results)
        v["act"] = far["act"]
        dy = near(after(dy, *beside_zw))
        results = run(
            kb_within, "back_within", [((t, OWN), f32, "v"), ((t, 2 * STATE), f32, "v")],
            dy, v["xdt"], v["cum"], v["bc"], df, v["c"],
            scratch=[((t, HEADS * 128), f32), ((t // 128, HEADS * 8, 128), f32), ((t, BLOCK), f32), ((t, BLOCK), f32)],
            ahead=[v[k] for k in ahead_within],
        )
        dxw, dbc = results[:2]
        if layer == 0:
            dxw, dbc = near(*lax.optimization_barrier((dxw, dbc)))
            zo = [after(b, entered, dxw, *before_zo) for b in zo]
        fetched(ahead_within, results)
        results = run(
            kb_front, "back_front",
            [((t + 8, XC), f32, "v"), ((8, XC), f32, "a"), ((t, 128), bf16, "v"), ((40, XC), f32), ((16, 128), f32)],
            entered, d, v["c"], far["dec"], v["bc"], v["xdt"], v["act"], v["xb"], v["slope"], v["before"], v["dt"], v["cum"],
            dxw, dbc, dy, dca, par,
            scratch=[((2 * STATE, OWN), f32), ((t, OWN), f32), ((t, OWN), f32), ((t, OWN), f32), ((t, XC), f32),
                     ((t, 128), f32), ((t, 128), f32), ((16, OWN), f32), ((t + 16, 128), f32)],
            ahead=[v[k] for k in ahead_front],
        )
        dxb, halo, qdt, small_b, small_c = results[:5]
        fetched(ahead_front, results)
        ret = chain_step(halo, 1, True)
        dnz = run(kb_z_normed, "back_z", [((t, WIDTH), f32, "v")], near(after(qz, halo)), v["wz"])[0]
        return dxb, ret, qdt, dnz, zo, (small_a, small_b, small_c), v, (e, dbc, halo)

    shape_q, shape_n = ((t, XD), bf16, "v"), [((t, WIDTH), f32, "v"), ((t, WIDTH), bf16, "p")]
    x_blocks = [((WIDTH // count, XD), bf16, "a")] * count
    x_scratch = [((WIDTH, XD), bf16)]
    dxb, ret, qdt, dnz, zo1, small1, v1, _ = backward(1, saved[1], x["g"], st1, msg, x)
    got_zo1 = send_blocks(zo1)
    v0 = saved[0]
    early = []
    q, dn, dnb1, *fetched = run(
        kb_x_normed, "back_x", [shape_q, shape_n[0], ((t, WIDTH), bf16, "a")], dxb, ret, qdt, dnz, v1["wx"], ahead=[v0[k] for k in early]
    )
    v0.update(zip(early, fetched))
    dr = across(dnb1)
    shapes_x = [((2 * shard, CUT), bf16, "a"), ((2 * shard, XD - CUT), bf16, "a")] * 2
    x1 = run(
        kb_x_weight, "back_xw", shapes_x if count > 1 else [((WIDTH, XD), bf16, "a")], v1["normed"],
        near(after(q, dnb1, *got_zo1)), scratch=x_scratch, ahead=[*[v0[k] for k in AHEAD_WEIGHT], h1_far, pt],
    )
    *x1, h1_near, pt_near = x1
    v0.update(zip(AHEAD_WEIGHT, x1[-len(AHEAD_WEIGHT) :]))
    x1 = x1[: -len(AHEAD_WEIGHT)]
    got_x1 = [flip(x1[0], "seq", 1), flip(x1[1], "seq", 2)] if count > 1 else []

    def second_phase(*pins):
        if count == 1:
            return [[lax.psum_scatter(x1[0], "seq", scatter_dimension=0, tiled=True)]]
        own_a, own_b, give_a, give_b = run(
            k_phase, "phase", [((shard, CUT), bf16, "a"), ((shard, XD - CUT), bf16, "a")] * 2,
            after(x1[2], *pins), x1[3], *got_x1,
        )
        return [[own_a, flip(give_a, "seq", 2)], [own_b, flip(give_b, "seq", 1)]]

    phase = second_phase()
    early = AHEAD_NORM
    g0, g0_far, small_d1, rd0, *fetched = run(
        kb_norm, "back_norm", [((t, WIDTH), bf16, "vh"), ((8, WIDTH), f32), ((t, 128), f32, "v")],
        h1_near, dn, after(dr, *x1), saved[1]["g"], par1, pt_near, ahead=[v0[k] for k in early],
    )
    v0.update(zip(early, fetched))
    dxb, ret, qdt, dnz, zo0, small0, v0, (e0, dbc0, halo0) = backward(
        0, v0, g0, rs0, rd0, before_zw=phase[0][:1], before_zo=[p[-1] for p in phase]
    )
    got_zo0 = send_blocks(zo0)
    simple = simple_dp(shard)
    halves1 = [] if simple else halved([*phase, got_zo1], dbc0)
    over1 = [] if simple else [paired(halves1[0], flip(halves1[1], "dp", 1))]
    q, *x0 = run(kb_x_weight_first, "back_xw", [shape_q] + x_blocks, v0["normed"], dxb, after(ret, *over1, *got_zo0), qdt, scratch=x_scratch)
    got_x0 = send_blocks(x0)
    dn, dnb0 = run(kb_x_normed_last, "back_x", [shape_n[0], ((t, WIDTH), bf16, "a")], near(after(q, *x0)), dnz, v0["wx"])
    dr = across(dnb0)
    sum1 = whole_sum([*phase, got_zo1]) if simple else further(over1, x0[0])
    sum_zo0 = summed_dp([got_zo0], before=[x0[0]])
    final = run(
        k_final, "final", [((length, half), bf16, "a"), ((length, half), bf16, "a")],
        h1_far, p1, st1_far, after(msg, dnb0),
    )
    hidden_out = both_sequences(*final)
    keep, give, small_d0 = run(
        kb_norm_last, "back_norm", [((length, half), bf16, "a"), ((length, half), bf16, "a"), ((8, WIDTH), f32)],
        saved[0]["h"], dn, dr, g0_far, par0, scratch=[((t, WIDTH), bf16)],
    )
    grad_in = both_sequences(keep, give)
    small = run(k_small, "small", [((2 * SMALL, XC), f32, "a")], *small0, small_d0, *small1, small_d1)[0]
    halves0 = [] if simple else halved([got_x0], final[0], keep, small)
    small = sum_small(small, ["seq"])
    first_small = small
    small, half_way = sum_small_dp(small)
    if simple:
        sum_x0 = whole_sum([got_x0])
    else:
        sum_x0 = over_dp(halves0[0], flip(halves0[1], "dp", 1), first_small, later=[half_way])
    sums = [*sum1, *sum_zo0, after(sum_x0[0], small), *sum_x0[1:]]
    heads = 2 * HEADS
    smalls = run(
        k_small_out, "small_out",
        [((1, WIDTH), f32, "a"), ((4, CONV), f32, "a"), ((1, CONV), f32, "a"), ((1, heads), f32, "a"), ((1, heads), f32, "a"), ((1, heads), f32, "a"),
         ((1, INNER), f32, "a")],
        small, across(small),
    )
    give = run(k_home, "home", [((shard, packed), bf16, "p")], *sums, scratch=[((shard, 2 * OWN), bf16), ((shard, XD), bf16)])[0]
    grad_w, grad_o = run(
        k_grads, "grads", [((shard, INNER + CONV + heads), f32, "a"), ((2 * shard, WIDTH), f32, "a")],
        *sums, across(give),
        scratch=[((shard, packed), bf16), ((shard, 2 * OWN), bf16), ((shard, XD), bf16)],
    )
    norm, taps, bias, dtb, rates, skips, gates = smalls
    return (hidden_out, grad_in, norm, grad_w[None], taps[None], bias, dtb, rates, skips, gates, grad_o[None])


def solution(mesh):
    by_section = P("section", None)
    rows = P("section", "seq", None)
    tokens = P("dp", "seq", None)
    taps = P("section", None, None)
    out = P("dp", "seq", "section")
    small = (by_section,) * 4
    return jax.shard_map(
        on_device,
        mesh=mesh,
        in_specs=(tokens, tokens, by_section, rows, taps, by_section, *small, rows),
        out_specs=(out, out, by_section, rows, taps, by_section, *small, rows),
        check_vma=False,
    )
```

```python
import functools

import jax
import jax.numpy as jnp
from jax import lax
from jax.experimental import pallas as pl
from jax.experimental.pallas import tpu as pltpu
from jax.sharding import PartitionSpec as P

HDIM = 64
STATE = 128
INNER = 1536
CONV = 1792
EPS = 1e-05
f32, bf16 = jnp.float32, jnp.bfloat16

WIDTH = 768
OWN = 768
HEADS = 12
XC = OWN + 2 * STATE
XD = XC + 128
R = 256
BLOCK = 256


def nn(a, b):
    return lax.dot_general(a, b, (((1,), (0,)), ((), ())), preferred_element_type=f32)


def nt(a, b):
    return lax.dot_general(a, b, (((1,), (1,)), ((), ())), preferred_element_type=f32)


def tn(a, b):
    return lax.dot_general(a, b, (((0,), (0,)), ((), ())), preferred_element_type=f32)


def loop(count, body, unroll=True):
    def step(k, carry):
        body(k)
        return carry

    lax.fori_loop(0, count, step, 0, unroll=unroll and count <= 8)


def at(k, size):
    return pl.ds(pl.multiple_of(k * size, size), size)


def iotas(shape):
    return lax.broadcasted_iota(jnp.int32, shape, 0), lax.broadcasted_iota(jnp.int32, shape, 1)


def spread_matrix(width, per):
    r, c = iotas((128, width))
    return jnp.where(((r & 15) == c // per) & (r < 48), 1.0, 0.0).astype(bf16)


def collect_matrix():
    r, c = iotas((OWN, 128))
    return jnp.where(((c & 15) == r // HDIM) & (c < 48), 1.0, 0.0).astype(bf16)


def thirds(v):
    high = v.astype(bf16).astype(f32)
    rest = v - high
    mid = rest.astype(bf16).astype(f32)
    lane = iotas(v.shape)[1]
    out = jnp.where(lane < 16, high, jnp.where(lane < 32, mid, rest - mid))
    return jnp.where(lane < 48, out, 0.0).astype(bf16)


def halves(v):
    high = v.astype(bf16)
    return high, (v - high.astype(f32)).astype(bf16)


def running_sum(v, backward=False):
    r, c = iotas((BLOCK, BLOCK))
    tri = jnp.where((c >= r) if backward else (r >= c), 1.0, 0.0).astype(bf16)
    high = v.astype(bf16)
    rest = v - high.astype(f32)
    mid = rest.astype(bf16)
    last = (rest - mid.astype(f32)).astype(bf16)
    return nn(tri, high) + nn(tri, mid) + nn(tri, last)


def sig(v):
    return 0.5 * jnp.tanh(0.5 * v) + 0.5


def softplus(v):
    e = jnp.exp(-jnp.abs(v))
    u = 1.0 + e
    small = u == 1.0
    return jnp.maximum(v, 0.0) + jnp.where(small, e, jnp.log(u) * e / jnp.where(small, 1.0, u - 1.0))


def fold(v):
    return jnp.sum(v.reshape(v.shape[0] // 8, 8, v.shape[1]), axis=0)


def copy_rows(dst, start, src, cols=None):
    rows = src.shape[0]
    step = next(k for k in (48, 32, 16, 8, rows) if rows % k == 0)

    def move(r):
        place = pl.ds(pl.multiple_of(start + r * step, 16), step)
        if cols is None:
            dst[place, :] = src[at(r, step), :]
        else:
            dst[place, :] = src[at(r, step), cols]

    loop(rows // step, move)


def place_rows(dst, parts, cols=None):
    if len(parts) == 1:
        return copy_rows(dst, 0, parts[0], cols)
    me = lax.axis_index("seq")
    rows = parts[0].shape[0]
    for k in range(min(len(parts), 4)):
        copy_rows(dst, (me ^ k) * rows, parts[k], cols)
    if len(parts) > 4:
        copy_rows(dst, (me ^ 3) * rows + rows // 2, parts[4], cols)


def on_core(body):
    me = lax.axis_index("section")
    for core in range(2):
        pl.when(me == core)(lambda core=core: body(core))


def exact(a, b):
    return lax.dot_general(
        a, b, (((1,), (0,)), ((), ())), preferred_element_type=f32, precision=lax.Precision.HIGHEST
    )


def stats_out(a, b):
    lane = iotas(a.shape)[1]
    v = jnp.where(lane < 64, a, b)
    high = v.astype(bf16).astype(f32)
    rest = v - high
    mid = rest.astype(bf16).astype(f32)
    l = lane & 63
    out = jnp.where(l < 16, high, jnp.where(l < 32, mid, rest - mid))
    return jnp.where(l < 48, out, 0.0).astype(bf16)


def stats_in(v):
    v = v.astype(f32)
    lane = iotas(v.shape)[1]
    a = jnp.sum(jnp.where(lane < 64, v, 0.0), axis=1, keepdims=True)
    b = jnp.sum(jnp.where(lane < 64, 0.0, v), axis=1, keepdims=True)
    return a * (1.0 / 16), b * (1.0 / 16)


class Copies:

    def __init__(self, pairs_in, pairs_ahead, pairs_out, sems_in, sems_out):
        self.waiting, self.ready, self.started, self.ahead = {}, {}, [], []
        for k, (far, near, whole) in enumerate(pairs_in):
            copy = pltpu.make_async_copy(far, near, sems_in.at[k])
            copy.start()
            self.waiting.setdefault(id(whole), []).append(copy)
        for k, (far, near) in enumerate(pairs_ahead):
            copy = pltpu.make_async_copy(far, near, sems_in.at[len(pairs_in) + k])
            copy.start()
            self.ahead.append(copy)
        for k, (far, near, whole) in enumerate(pairs_out):
            self.ready.setdefault(id(whole), []).append(pltpu.make_async_copy(near, far, sems_out.at[k]))

    def need(self, refs):
        for key in [id(r) for r in refs] if refs else list(self.waiting):
            for copy in self.waiting.pop(key, ()):
                copy.wait()

    def done(self, refs):
        for key in [id(r) for r in refs] if refs else list(self.ready):
            for copy in self.ready.pop(key, ()):
                copy.start()
                self.started.append(copy)


COPIES = []


def need(*refs):
    COPIES[-1].need(refs)


def done(*refs):
    COPIES[-1].done(refs)


FAR = []
NEAR = []


def near(*arrays):
    NEAR.extend(arrays)
    return arrays if len(arrays) > 1 else arrays[0]


def far_away(array):
    FAR.append(array)
    return array


def run(kernel, name, outs, *ins, scratch=(), ahead=(), stay=()):
    far, close = pl.BlockSpec(memory_space=pltpu.HBM), pl.BlockSpec(memory_space=pltpu.VMEM)
    loose = pl.BlockSpec(memory_space=pl.ANY)
    modes = [o[2] if len(o) > 2 else "h" for o in outs]
    units = [m for mode in modes for m in mode] + ["v"] * len(ahead) + ["h"] * len(stay)
    shapes, specs = [], []
    for (shape, dtype, *_), mode in zip(outs, modes):
        for m in mode:
            if m == "p":
                shapes += [jax.ShapeDtypeStruct((shape[0] // 2, *shape[1:]), dtype)] * 2
                specs += [loose] * 2
            else:
                space = dict(v=pltpu.VMEM, h=pltpu.HBM, a=jax.ShapeDtypeStruct)[m]
                shapes.append(space(shape, dtype))
                specs.append(dict(v=close, h=far, a=loose)[m])
    for a in ahead:
        shapes.append(pltpu.VMEM(a.shape, a.dtype))
        specs.append(close)
    for a in stay:
        shapes.append(pltpu.HBM(a.shape, a.dtype))
        specs.append(far)
    groups = [a if isinstance(a, (tuple, list)) else (a,) for a in (*ins, *ahead, *stay)]
    flat = [a for group in groups for a in group]
    held = [any(a is k for k in NEAR) for a in flat]
    kept = [any(a is k for k in FAR) for a in flat]
    flat = [
        pltpu.with_memory_space_constraint(a, pltpu.VMEM if h else pltpu.HBM) if h or k else a
        for a, h, k in zip(flat, held, kept)
    ]
    n_in, n_out, n_own = len(flat), len(shapes), sum(len(group) for group in groups[: len(ins)])
    buffers = [
        pltpu.VMEM((sum(a.shape[0] for a in group), *group[0].shape[1:]), group[0].dtype)
        for group in groups[: len(ins)]
        if not any(group[0] is k for k in NEAR)
    ]
    buffers += [pltpu.VMEM(shape, dtype) for (shape, dtype, *_), mode in zip(outs, modes) if "v" not in mode]

    def body(*refs):
        given, made, rest = list(refs[:n_in]), list(refs[n_in : n_in + n_out]), list(refs[n_in + n_out :])
        pairs_in, pairs_out, vin, vout = [], [], [], []
        pairs_ahead = list(zip(given[n_own:], made[n_out - len(ahead) - len(stay) :]))
        at_ref = 0
        for group in groups[: len(ins)]:
            if held[at_ref]:
                vin.append(given[at_ref])
            else:
                vin.append(rest.pop(0))
                start = 0
                for k, part in enumerate(group):
                    rows = part.shape[0]
                    place = vin[-1] if len(group) == 1 else vin[-1].at[pl.ds(start, rows)]
                    pairs_in.append((given[at_ref + k], place, vin[-1]))
                    start += rows
            at_ref += len(group)
        for mode in modes:
            vout.append(made.pop(0) if "v" in mode else rest.pop(0))
            if mode == "p":
                rows = vout[-1].shape[0] // 2
                for k in range(2):
                    pairs_out.append((made.pop(0), vout[-1].at[pl.ds(k * rows, rows)], vout[-1]))
            elif mode != "v":
                pairs_out.append((made.pop(0), vout[-1], vout[-1]))
        *extra, sems_in, sems_out = rest
        copies = Copies(pairs_in, pairs_ahead, pairs_out, sems_in, sems_out)
        COPIES.append(copies)
        kernel(*vin, *vout, *extra)
        need()
        done()
        for copy in [*copies.ahead, *copies.started]:
            copy.wait()
        COPIES.pop()

    results = list(
        pl.pallas_call(
            body,
            name=name,
            out_shape=shapes,
            in_specs=[close if h else far if k else loose for h, k in zip(held, kept)],
            out_specs=specs,
            scratch_shapes=[
                *buffers,
                *[pltpu.VMEM(s, d) for s, d in scratch],
                pltpu.SemaphoreType.DMA((max(n_in, 1),)),
                pltpu.SemaphoreType.DMA((max(n_out, 1),)),
            ],
            compiler_params=pltpu.CompilerParams(vmem_limit_bytes=MIB * 2**20),
            cost_estimate=pl.CostEstimate(flops=1, bytes_accessed=1, transcendentals=0),
        )(*flat)
    )
    grouped = []
    for unit in units:
        if unit == "p":
            grouped.append((results.pop(0), results.pop(0)))
            continue
        grouped.append(results.pop(0))
        if unit != "a":
            (NEAR if unit == "v" else FAR).append(grouped[-1])
    return grouped


MIB = 24


TAPS, BIAS, NORM, GATE, SKIP, STEP, RATE = 0, 4, 5, 6, 7, 8, 9
PARAMS = 16


def k_prep(hid_ref, cot_ref, w_ref, o_ref, ng_ref, cw_ref, cb_ref, db_ref, al_ref, sk_ref, gg_ref, hid_half, cot_half, mine_x, give_x, mine_zo, give_zo, mine_p, give_p):
    need()
    rows = w_ref.shape[0]
    half = WIDTH // 2
    r24, c24 = iotas((2 * HEADS, 128))
    rk, ck = iotas((2 * HEADS, OWN))

    def pack(core, out):
        own = core * OWN
        out[:, 0:OWN] = w_ref[:, INNER + own : INNER + own + OWN]
        out[:, OWN:XC] = w_ref[:, 2 * INNER : 2 * INNER + 2 * STATE]
        pick = ((c24 & 15) == r24 - core * HEADS) & (c24 < 48)
        steps = w_ref[:, INNER + CONV : INNER + CONV + 2 * HEADS]
        out[:, XC:XD] = nn(steps, jnp.where(pick, 1.0, 0.0).astype(bf16)).astype(bf16)

    def pack_rest(core, out, par):
        own = core * OWN
        pick = ((c24 & 15) == r24 - core * HEADS) & (c24 < 48)
        out[:, 0:OWN] = w_ref[:, own : own + OWN]
        for t in range(2):
            at_lane = OWN + t * half
            out[:, at_lane : at_lane + half] = o_ref[t * rows : (t + 1) * rows, core * half : (core + 1) * half]
        par[...] = jnp.zeros(par.shape, f32)
        par[TAPS : TAPS + 4, :OWN] = cw_ref[:, own : own + OWN]
        par[TAPS : TAPS + 4, OWN:] = cw_ref[:, INNER:]
        par[BIAS : BIAS + 1, :OWN] = cb_ref[:, own : own + OWN]
        par[BIAS : BIAS + 1, OWN:] = cb_ref[:, INNER:]
        par[NORM : NORM + 1, :WIDTH] = ng_ref[...]
        par[GATE : GATE + 1, :OWN] = gg_ref[:, own : own + OWN]
        spread = jnp.where(rk - core * HEADS == ck // HDIM, 1.0, 0.0)
        par[SKIP : SKIP + 1, :OWN] = exact(jnp.broadcast_to(sk_ref[...], (8, 2 * HEADS)), spread)[0:1]
        lanes = jnp.where(pick, 1.0, 0.0)
        par[STEP : STEP + 1, 0:128] = exact(jnp.broadcast_to(db_ref[...], (8, 2 * HEADS)), lanes)[0:1]
        par[RATE : RATE + 1, 0:128] = exact(jnp.broadcast_to(al_ref[...], (8, 2 * HEADS)), lanes)[0:1]

    def body(core):
        pack(core, mine_x)
        pack(1 - core, give_x)

    def rest(core):
        pack_rest(core, mine_zo, mine_p)
        pack_rest(1 - core, give_zo, give_p)

    on_core(body)
    done(mine_x, give_x)
    even_seq = 1 - lax.rem(lax.axis_index("seq"), 2)
    rows_half = hid_half.shape[0]
    start = lax.axis_index("section") * rows_half
    for src, dst in ((hid_ref, hid_half), (cot_ref, cot_half)):

        def move(r, src=src, dst=dst):
            dst[at(r, 32), :] = src[even_seq, pl.ds(pl.multiple_of(start + r * 32, 32), 32), :]

        loop(rows_half // 32, move)
        done(dst)
    on_core(rest)


def k_pick(mine_x, got_x, mine_p, got_p, x0, x1, p0, p1):
    need()

    def body(core):
        for layer, (x, p) in enumerate(((x0, p0), (x1, p1))):
            x[...] = (mine_x, got_x)[layer ^ core][...]
            p[...] = (mine_p, got_p)[layer ^ core][...]

    on_core(body)


def k_pick_rest(mine_zo, got_zo, zo0, zo1):
    need()

    def body(core):
        zo0[...] = (mine_zo, got_zo)[core][...]
        zo1[...] = (mine_zo, got_zo)[1 - core][...]

    on_core(body)


def norm_rows(h, gain):
    scale = lax.rsqrt(jnp.mean(h * h, axis=1, keepdims=True) + EPS)
    return (h * scale * gain).astype(bf16)


def project(t, normed_ref, wx_ref, xb_ref, tail_ref):
    xb_ref[0:8, :] = jnp.zeros((8, XD), f32)

    def cols(c):
        xb_ref[8 : 8 + t, :] = nn(normed_ref[...], wx_ref[...])

    loop(1, cols)
    tail_ref[...] = xb_ref[t:, :XC]


def k_in(hid_ref, ga_ref, gb_ref, par_ref, *rest):
    *parts, h_ref, normed_ref, xb_ref, wx_ref, tail_ref = rest
    need(hid_ref, ga_ref, gb_ref, par_ref)
    t = h_ref.shape[0]
    half = t // 2
    odd = lax.rem(lax.axis_index("seq"), 2)
    core = lax.axis_index("section")
    copy_rows(h_ref, odd * half, hid_ref.at[odd])
    copy_rows(h_ref, (1 - odd) * half + core * (half // 2), ga_ref)
    copy_rows(h_ref, (1 - odd) * half + (1 - core) * (half // 2), gb_ref)

    def rows(r):
        normed_ref[at(r, R), :] = norm_rows(h_ref[at(r, R), :].astype(f32), par_ref[NORM : NORM + 1, :WIDTH])

    loop(t // R, rows)
    done(h_ref, normed_ref)
    need(*parts)
    place_rows(wx_ref, parts)
    done(wx_ref)
    project(t, normed_ref, wx_ref, xb_ref, tail_ref)


def k_mid(h_ref, p_ref, st_ref, msg_ref, par_ref, *rest):
    *parts, h1_ref, pt_ref, rs_ref, normed_ref, xb_ref, wx_ref, tail_ref = rest
    need(h_ref, p_ref, st_ref, msg_ref, par_ref)
    t = h_ref.shape[0]

    def rows(r):
        s = at(r, R)
        other = stats_in(msg_ref[s, WIDTH:])[0]
        rs = lax.rsqrt((st_ref[s, 0:128] + other) * (1.0 / INNER) + EPS)
        rs_ref[s, :] = rs
        p = p_ref[s, :] + msg_ref[s, :WIDTH].astype(f32)
        pt_ref[s, :] = p
        h1 = (h_ref[s, :].astype(f32) + rs[:, 0:1] * p).astype(bf16)
        h1_ref[s, :] = h1
        normed_ref[s, :] = norm_rows(h1.astype(f32), par_ref[NORM : NORM + 1, :WIDTH])

    loop(t // R, rows)
    done(h1_ref, pt_ref, rs_ref, normed_ref)
    need(*parts)
    place_rows(wx_ref, parts)
    done(wx_ref)
    project(t, normed_ref, wx_ref, xb_ref, tail_ref)


def k_z(normed_ref, *rest):
    *parts, z_ref, wz_ref, keep_ref, give_ref, o = rest
    need(*parts)
    place_rows(wz_ref, parts, slice(0, OWN))
    done(wz_ref)
    place_rows(o, parts, slice(OWN, 2 * OWN))

    def split(core):
        rows = keep_ref.shape[0]
        keep_ref[...] = o[core * rows : (core + 1) * rows, :]
        give_ref[...] = o[(1 - core) * rows : (2 - core) * rows, :]

    on_core(split)
    done(keep_ref, give_ref)
    need(normed_ref)

    def cols(c):
        z_ref[:, at(c, 768)] = nn(normed_ref[...], wz_ref[:, at(c, 768)])

    loop(OWN // 768, cols)


def k_front(xb_ref, before_ref, par_ref, act_ref, slope_ref, bc_ref, xdt_ref, dt_ref, cum_ref, s_ref, dec_ref, tot_ref, wide, edge):
    t = act_ref.shape[0]
    need()
    edge[0:8, :] = before_ref[...]
    edge[8:16, :] = jnp.zeros((8, XC), f32)

    def conv(c):
        cols = at(c, 128)
        w = par_ref[0:8, cols]
        total = w[4:5] + w[0:1] * xb_ref[pl.ds(5, t), cols]
        for k in range(1, 4):
            total = total + w[k : k + 1] * xb_ref[pl.ds(5 + k, t), cols]
        first = total[0:8]
        for k in range(4):
            first = first + w[k : k + 1] * edge[5 + k : 13 + k, cols]
        total = jnp.concatenate([first, total[8:]], axis=0)
        sg = sig(total)
        act = total * sg
        act_ref[:, cols] = act
        slope_ref[:, cols] = (sg + act * (1.0 - sg)).astype(bf16)

    loop(XC // 128, conv)
    bc_ref[...] = act_ref[:, OWN:].astype(bf16)
    done(act_ref, slope_ref, bc_ref)
    dt = softplus(xb_ref[8 : 8 + t, XC:] + par_ref[STEP : STEP + 1, 0:128])
    dt_ref[...] = dt
    done(dt_ref)
    rate = -jnp.exp(par_ref[RATE : RATE + 1, 0:128])
    spread = spread_matrix(OWN, HDIM)
    wide[...] = nn(thirds(dt), spread)

    def rows(r):
        s = at(r, R)
        xdt_ref[s, :] = (act_ref[s, :OWN] * wide[s, :]).astype(bf16)

    loop(t // R, rows)
    done(xdt_ref)
    for b in range(t // BLOCK):
        s = pl.ds(b * BLOCK, BLOCK)
        cum = running_sum(rate * dt[b * BLOCK : (b + 1) * BLOCK])
        cum_ref[s, :] = cum
        end = cum[BLOCK - 1 : BLOCK, :]
        dec_ref[8 * b : 8 * b + 8, :] = nn(thirds(jnp.exp(jnp.broadcast_to(end, (8, 128)))), spread)
        wide[s, :] = nn(thirds(jnp.exp(end - cum)), spread)
        bl = bc_ref[s, 0:STATE]

        def cols(c):
            decayed = (xdt_ref[s, at(c, 768)].astype(f32) * wide[s, at(c, 768)]).astype(bf16)
            s_ref[pl.ds(b * STATE, STATE), at(c, 768)] = tn(bl, decayed)

        loop(OWN // 768, cols)
    tot_ref[...] = (s_ref[STATE:, :] + dec_ref[8:9, :] * s_ref[:STATE, :]).astype(bf16)


def decay_tables(cum_ref, tall, flat):
    t = cum_ref.shape[0]
    parts = thirds(cum_ref[...])
    tall[...] = nn(parts, spread_matrix(HEADS * 128, 128))
    r, c = iotas((HEADS * 8, 128))
    pick = jnp.where(((c & 15) == r // 8) & (c < 48), 1.0, 0.0).astype(bf16)
    for b in range(t // 128):
        flat[b] = nt(pick, parts[b * 128 : (b + 1) * 128])


def k_within(cum_ref, bc_ref, xdt_ref, y_ref, tall, flat, scores):
    t = cum_ref.shape[0]
    need(cum_ref)
    decay_tables(cum_ref, tall, flat)
    blocks = t // BLOCK
    need(bc_ref, xdt_ref)
    for b in range(blocks):
        s = pl.ds(b * BLOCK, BLOCK)
        scores[s, :] = nt(bc_ref[s, STATE:], bc_ref[s, 0:STATE])
    r, c = iotas((128, 128))
    causal = r >= c
    lane = iotas((BLOCK, 128))[1]

    def pair(p):
        cols = at(p, 128)
        for b in range(blocks):
            o = b * BLOCK
            u = xdt_ref[pl.ds(o, BLOCK), cols]
            top = jnp.zeros((128, 128), f32)
            low = jnp.zeros((128, 128), f32)
            for a in range(2):
                head = 2 * p + a
                own = jnp.where((lane >= 64) == (a == 1), u, jnp.zeros_like(u))
                hc = at(head, 128)
                hr = pl.ds(pl.multiple_of(head * 8, 8), 8)
                t0, t1 = tall[pl.ds(o, 128), hc], tall[pl.ds(o + 128, 128), hc]
                u0, u1 = flat[2 * b, hr, :][0:1], flat[2 * b + 1, hr, :][0:1]
                sc = scores
                w00 = jnp.where(causal, sc[pl.ds(o, 128), 0:128] * jnp.exp(jnp.where(causal, t0 - u0, 0.0)), 0.0)
                w10 = sc[pl.ds(o + 128, 128), 0:128] * jnp.exp(t1 - u0)
                w11 = jnp.where(causal, sc[pl.ds(o + 128, 128), 128:] * jnp.exp(jnp.where(causal, t1 - u1, 0.0)), 0.0)
                top = top + nn(w00.astype(bf16), own[:128])
                low = low + nn(w10.astype(bf16), own[:128]) + nn(w11.astype(bf16), own[128:])
            y_ref[pl.ds(o, 128), cols] = top
            y_ref[pl.ds(o + 128, 128), cols] = low

    loop(OWN // 128, pair)


def k_out(first_layer, yw_ref, act_ref, bc_ref, cum_ref, cin_ref, s_ref, dec_ref, z_ref, par_ref, keep_ref, got_ref, *rest):
    if first_layer:
        y_ref, p_ref, msg_ref, st_ref, c_ref, wo_ref, wide, u_ref = rest
    else:
        cot_ref, ca_ref, cb_ref, y_ref, p_ref, msg_ref, st_ref, c_ref, wo_ref, g_ref, wide, u_ref = rest
    t = yw_ref.shape[0]
    half = WIDTH // 2
    shard = o_rows(keep_ref)

    def weights(core):
        for r in range(keep_ref.shape[0] // shard):
            for k in range(2):
                for src, side in ((keep_ref, core), (got_ref, 1 - core)):
                    wo_ref[(2 * r + k) * shard : (2 * r + k + 1) * shard, side * half : (side + 1) * half] = src[
                        r * shard : (r + 1) * shard, k * half : (k + 1) * half
                    ]

    need(keep_ref, got_ref)
    on_core(weights)
    done(wo_ref)
    need(bc_ref, cum_ref, cin_ref, s_ref, dec_ref)
    c_ref[0:STATE, :] = cin_ref[...].astype(f32)
    c_ref[STATE:, :] = s_ref[:STATE, :] + dec_ref[0:1, :] * c_ref[0:STATE, :]
    wide[...] = nn(thirds(jnp.exp(cum_ref[...])), spread_matrix(OWN, HDIM))
    for b in range(t // BLOCK):
        s = pl.ds(b * BLOCK, BLOCK)

        def cols(c):
            from_state = nn(bc_ref[s, STATE:], c_ref[pl.ds(b * STATE, STATE), at(c, 768)].astype(bf16))
            wide[s, at(c, 768)] = wide[s, at(c, 768)] * from_state

        loop(OWN // 768, cols)

    done(c_ref)
    need(yw_ref, act_ref, z_ref, par_ref)

    def rows(r):
        s = at(r, R)
        y = yw_ref[s, :] + wide[s, :] + par_ref[SKIP : SKIP + 1, :OWN] * act_ref[s, :OWN]
        y_ref[s, :] = y
        z = z_ref[s, :]
        gated = y * z * sig(z)
        u_ref[s, :] = (gated * par_ref[GATE : GATE + 1, :OWN]).astype(bf16)
        st_ref[s, 0:128] = jnp.broadcast_to(jnp.sum(gated * gated, axis=1, keepdims=True), (R, 128))

    loop(t // R, rows)
    done(y_ref)

    def project_out(c):
        p_ref[:, at(c, 768)] = nn(u_ref[...], wo_ref[:, at(c, 768)])

    loop(WIDTH // 768, project_out)
    done(p_ref)
    if first_layer:

        def send(r):
            s = at(r, R)
            msg_ref[s, :WIDTH] = p_ref[s, :].astype(bf16)
            v = st_ref[s, 0:128]
            msg_ref[s, WIDTH:] = stats_out(v, v)

        loop(t // R, send)
    else:
        odd = lax.rem(lax.axis_index("seq"), 2)
        need(cot_ref, ca_ref, cb_ref)
        copy_rows(g_ref, odd * (t // 2), cot_ref.at[odd])
        core = lax.axis_index("section")
        copy_rows(g_ref, (1 - odd) * (t // 2) + core * (t // 4), ca_ref)
        copy_rows(g_ref, (1 - odd) * (t // 2) + (1 - core) * (t // 4), cb_ref)
        done(g_ref)

        def dots(r):
            s = at(r, R)
            d = jnp.sum(p_ref[s, :] * g_ref[s, :].astype(f32), axis=1, keepdims=True)
            d = jnp.broadcast_to(d, (R, 128))
            st_ref[s, 128:256] = d
            msg_ref[s, half:] = stats_out(st_ref[s, 0:128], d)

        loop(t // R, dots)

        def send(core):
            msg_ref[:, :half] = p_ref[:, (1 - core) * half : (2 - core) * half].astype(bf16)

        on_core(send)


def o_rows(keep_ref):
    return keep_ref.shape[0] // (lax.axis_size("seq") // 2)


def k_final(h_ref, p_ref, st_ref, msg_ref, keep_ref, give_ref):
    need()
    half = WIDTH // 2
    rows_each = keep_ref.shape[0]
    odd = lax.rem(lax.axis_index("seq"), 2)

    def body(core):
        cols = slice(core * half, (core + 1) * half)

        def half_out(dst, start):
            def rows(r):
                s = pl.ds(pl.multiple_of(start + r * R, R), R)
                other = stats_in(msg_ref[s, half:])[0]
                rs = lax.rsqrt((st_ref[s, 0:1] + other) * (1.0 / INNER) + EPS)
                p = p_ref[s, cols] + msg_ref[s, :half].astype(f32)
                dst[at(r, R), :] = (h_ref[s, cols].astype(f32) + rs * p).astype(bf16)

            loop(rows_each // R, rows)

        half_out(keep_ref, odd * rows_each)
        half_out(give_ref, (1 - odd) * rows_each)

    on_core(body)


def kb_gate(g_ref, w_ref, y_ref, yw_ref, z_ref, act_ref, bc_ref, cum_ref, rs_ref, rd_ref, par_ref, dec_ref,
            qz_ref, dy_ref, df_ref, dca_ref, keep_ref, give_ref, d_ref, e_ref, small_ref, dgn, wide, gn):
    t = g_ref.shape[0]
    need(g_ref, w_ref)

    def back(c):
        dgn[:, at(c, 768)] = nt(g_ref[...], w_ref[at(c, 768), :])

    loop(OWN // 768, back)
    need(cum_ref)
    wide[...] = nn(thirds(jnp.exp(cum_ref[...])), spread_matrix(OWN, HDIM))
    small_ref[...] = jnp.zeros(small_ref.shape, f32)
    collect = collect_matrix()
    need()

    def rows(r):
        s = at(r, R)
        z, y, d, x = z_ref[s, :], y_ref[s, :], dgn[s, :], act_ref[s, :OWN]
        gg = par_ref[GATE : GATE + 1, :OWN]
        if rs_ref.shape[1] == 128:
            rs, rd = rs_ref[s, 0:1], rd_ref[s, 0:1]
        else:
            squares, dots = stats_in(rd_ref[s, WIDTH // 2 :])
            rs = lax.rsqrt((rs_ref[s, 0:1] + squares) * (1.0 / INNER) + EPS)
            rd = rs_ref[s, 128:129] + dots
        sg = sig(z)
        sz = z * sg
        gated = y * sz
        scaled = gated * rs
        small_ref[0:8, :] += fold(d * scaled)
        gn[s, :] = (scaled * gg).astype(bf16)
        dgated = rs * (gg * d) - gated * (rs * rs * rs * rd * (1.0 / INNER))
        dy = dgated * sz
        dy_ref[s, :] = dy
        qz_ref[s, :] = (dgated * y * (sg * (1.0 + z - sz))).astype(bf16)
        small_ref[8:16, :] += fold(dy * x)
        df_ref[s, :] = (wide[s, :] * dy).astype(bf16)
        yw = yw_ref[s, :]
        high, low = halves(dy.astype(bf16).astype(f32) * yw + dy * (y - yw - par_ref[SKIP : SKIP + 1, :OWN] * x))
        sums = nn(jnp.concatenate([high, low], axis=0), collect)
        dca_ref[s, :] = sums[:R] + sums[R:]

    loop(t // R, rows)
    done(dy_ref, qz_ref, df_ref, dca_ref, small_ref)
    for b in range(t // BLOCK):
        s = pl.ds(b * BLOCK, BLOCK)
        cl = bc_ref[s, STATE:]

        def cols(c):
            d_ref[pl.ds(b * STATE, STATE), at(c, 768)] = tn(cl, df_ref[s, at(c, 768)])

        loop(OWN // 768, cols)
    e_ref[...] = (d_ref[:STATE, :] + dec_ref[0:1, :] * d_ref[STATE:, :]).astype(bf16)

    done(d_ref, e_ref)
    half = WIDTH // 2

    def halves_of(core):
        def weight(c):
            dw = tn(gn[:, at(c, 768)], g_ref[...]).astype(bf16)
            keep_ref[at(c, 768), :] = dw[:, core * half : (core + 1) * half]
            give_ref[at(c, 768), :] = dw[:, (1 - core) * half : (2 - core) * half]

        loop(OWN // 768, weight)

    on_core(halves_of)


def kb_within(dy_ref, xdt_ref, cum_ref, bc_ref, df_ref, c_ref, dx_ref, dbc_ref, tall, flat, scores, ds):
    t = cum_ref.shape[0]
    need(cum_ref)
    decay_tables(cum_ref, tall, flat)
    blocks = t // BLOCK
    need(bc_ref, xdt_ref, dy_ref)
    for b in range(blocks):
        s = pl.ds(b * BLOCK, BLOCK)
        scores[s, :] = nt(bc_ref[s, STATE:], bc_ref[s, 0:STATE])
    ds[...] = jnp.zeros(ds.shape, f32)
    r, c = iotas((128, 128))
    causal = r >= c
    lane = iotas((BLOCK, 128))[1]

    def pair(p):
        cols = at(p, 128)
        for b in range(blocks):
            o = b * BLOCK
            u = xdt_ref[pl.ds(o, BLOCK), cols]
            g = dy_ref[pl.ds(o, BLOCK), cols].astype(bf16)
            top = jnp.zeros((128, 128), f32)
            low = jnp.zeros((128, 128), f32)
            for a in range(2):
                head = 2 * p + a
                own = jnp.where((lane >= 64) == (a == 1), g, jnp.zeros_like(g))
                hc = at(head, 128)
                hr = pl.ds(pl.multiple_of(head * 8, 8), 8)
                t0, t1 = tall[pl.ds(o, 128), hc], tall[pl.ds(o + 128, 128), hc]
                u0, u1 = flat[2 * b, hr, :][0:1], flat[2 * b + 1, hr, :][0:1]
                e00 = jnp.where(causal, jnp.exp(jnp.where(causal, t0 - u0, 0.0)), 0.0)
                e10 = jnp.exp(t1 - u0)
                e11 = jnp.where(causal, jnp.exp(jnp.where(causal, t1 - u1, 0.0)), 0.0)
                q0, q1 = pl.ds(o, 128), pl.ds(o + 128, 128)
                w00 = (scores[q0, 0:128] * e00).astype(bf16)
                w10 = (scores[q1, 0:128] * e10).astype(bf16)
                w11 = (scores[q1, 128:] * e11).astype(bf16)
                top = top + tn(w00, own[:128]) + tn(w10, own[128:])
                low = low + tn(w11, own[128:])
                ds[q0, 0:128] += nt(own[:128], u[:128]) * e00
                ds[q1, 0:128] += nt(own[128:], u[:128]) * e10
                ds[q1, 128:] += nt(own[128:], u[128:]) * e11
            dx_ref[pl.ds(o, 128), cols] = top
            dx_ref[pl.ds(o + 128, 128), cols] = low

    loop(OWN // 128, pair, False)
    done(dx_ref)
    need(df_ref, c_ref)
    for b in range(blocks):
        s = pl.ds(b * BLOCK, BLOCK)
        d = ds[s, :].astype(bf16)
        carried = c_ref[pl.ds(b * STATE, STATE), :].astype(bf16)
        dbc_ref[s, 0:STATE] = tn(d, bc_ref[s, STATE:])
        dbc_ref[s, STATE:] = nn(d, bc_ref[s, 0:STATE]) + nt(df_ref[s, :], carried)


def kb_front(gin_ref, d_ref, c_ref, dec_ref, bc_ref, xdt_ref, act_ref, xb_ref, slope_ref, before_ref, dt_ref, cum_ref, dxw_ref, dbc_ref,
             dy_ref, dca_ref, par_ref,
             dxb_ref, halo_ref, qdt_ref, small_ref, head_ref, gs, dd, te, dtw, dact, red, red2, ends, pad):
    t = act_ref.shape[0]
    blocks = t // BLOCK
    spread, collect = spread_matrix(OWN, HDIM), collect_matrix()
    need(gin_ref, d_ref, dec_ref)
    gs[STATE:, :] = gin_ref[...].astype(f32)
    gs[:STATE, :] = d_ref[STATE:, :] + dec_ref[8:9, :] * gs[STATE:, :]
    need(dbc_ref, dt_ref, c_ref, cum_ref, bc_ref, xdt_ref)
    dact[:, OWN:] = dbc_ref[...]
    dtw[...] = nn(thirds(dt_ref[...]), spread)
    for b in range(blocks):
        s = pl.ds(b * BLOCK, BLOCK)
        ss = pl.ds(b * STATE, STATE)
        end = cum_ref[pl.ds((b + 1) * BLOCK - 8, 8), :][7:8]
        te[s, :] = nn(thirds(jnp.exp(end - cum_ref[s, :])), spread)
        bl = bc_ref[s, 0:STATE]
        ends[8 * b : 8 * b + 8, :] = fold(gs[ss, :] * c_ref[ss, :]) * dec_ref[8 * b : 8 * b + 8, :]

        def cols(c):
            q = at(c, 768)
            low = gs[ss, q].astype(bf16)
            dd[s, q] = nn(bl, low)
            decayed = (xdt_ref[s, q].astype(f32) * te[s, q]).astype(bf16)
            dact[s, OWN : OWN + STATE] += nt(decayed, low)

        loop(OWN // 768, cols)
        if b == 0:
            need(dxw_ref, dy_ref, act_ref, par_ref)

        def rows(r):
            q = pl.ds(pl.multiple_of(b * BLOCK + r * R, R), R)
            w = dd[q, :] * te[q, :]
            ends[8 * b : 8 * b + 8, :] += fold(w * xdt_ref[q, :].astype(f32))
            dxdt = dxw_ref[q, :] + w
            dact[q, :OWN] = dxdt * dtw[q, :] + par_ref[SKIP : SKIP + 1, :OWN] * dy_ref[q, :]
            parts = [(dxdt * act_ref[q, :OWN]).astype(bf16), *halves(dxdt * xdt_ref[q, :].astype(f32))]
            sums = nn(jnp.concatenate(parts, axis=0), collect)
            red[q, :] = sums[:R]
            red2[q, :] = sums[R : 2 * R] + sums[2 * R :]

        loop(BLOCK // R, rows)
    need()
    high, low = halves(ends[...])
    at_end = nn(high, collect) + nn(low, collect)
    rate = -jnp.exp(par_ref[RATE : RATE + 1, 0:128])
    head_ref[...] = jnp.zeros(head_ref.shape, f32)
    for b in range(blocks):
        s = pl.ds(b * BLOCK, BLOCK)
        dt = dt_ref[s, :]
        total = running_sum(dca_ref[s, :] - red2[s, :], True)
        total = total + jnp.sum(at_end[8 * b : 8 * b + 8], axis=0, keepdims=True)
        ddt = red[s, :] + rate * total
        raw = xb_ref[pl.ds(8 + b * BLOCK, BLOCK), XC:] + par_ref[STEP : STEP + 1, 0:128]
        draw = ddt * jax.nn.sigmoid(raw)
        head_ref[0:8, :] += fold(draw)
        head_ref[8:16, :] += fold(rate * dt * total)
        lane = iotas(draw.shape)[1]
        qdt_ref[s, :] = jnp.where(lane < HEADS, draw, 0.0).astype(bf16)
    done(qdt_ref, head_ref)
    pad[0:8, :] = jnp.zeros((8, 128), f32)
    pad[8 + t :, :] = jnp.zeros((8, 128), f32)

    def conv(c):
        cols = at(c, 128)
        w = par_ref[0:8, cols]
        d = dact[:, cols] * slope_ref[:, cols].astype(f32)
        pad[8 : 8 + t, :] = d
        small_ref[32:40, cols] = fold(d)
        xb, before = xb_ref[:, cols], before_ref[:, cols]
        out = 0.0
        for k in range(4):
            later = pad[3 - k : 11 - k + t, :]
            out = out + w[k : k + 1] * later
            small_ref[8 * k : 8 * k + 8, cols] = fold(later * xb) + later[0:8] * before
        dxb_ref[:, cols] = out
        halo_ref[:, cols] = out[0:8]

    loop(XC // 128, conv)


def z_weight(dw_ref, first, normed_ref, qz_ref, okeep_ref, ogot_ref):
    def weight(c):
        dw_ref[at(c, 768), first : first + OWN] = tn(normed_ref[:, at(c, 768)], qz_ref[...]).astype(bf16)

    loop(WIDTH // 768, weight)
    n = lax.axis_size("seq")
    shard, half = WIDTH // n, WIDTH // 2
    need()

    def out(core):
        for j in range(n):
            src = okeep_ref if j // (n // 2) == core else ogot_ref
            for k in range(2):
                row, col = (2 * (j % (n // 2)) + k) * shard, first + OWN + k * half
                dw_ref[j * shard : (j + 1) * shard, col : col + half] = src[row : row + shard, :]

    on_core(out)


def kb_z_weight(normed_ref, qz_ref, okeep_ref, ogot_ref, *rest):
    *blocks, dw_ref = rest
    need(normed_ref, qz_ref)
    z_weight(dw_ref, 0, normed_ref, qz_ref, okeep_ref, ogot_ref)
    to_blocks(blocks, dw_ref)


CUT = 640


def kb_x_weight(normed_ref, q_ref, *rest):
    *parts, dw_ref = rest
    need()
    x_weight(normed_ref, q_ref, dw_ref)
    if len(parts) == 1:
        return copy_rows(parts[0], 0, dw_ref)
    me = lax.axis_index("seq")
    rows = WIDTH // 4
    first, last = slice(0, CUT), slice(CUT, XD)
    for ref, cols, ranks in zip(parts, (first, last, first, last), ((1, 3), (2, 3), (0, 2), (0, 1))):
        for k, bits in enumerate(ranks):
            start = (me ^ bits) * rows

            def move(r, ref=ref, cols=cols, k=k, start=start):
                ref[pl.ds(pl.multiple_of(k * rows + r * 48, 16), 48), :] = dw_ref[
                    pl.ds(pl.multiple_of(start + r * 48, 16), 48), cols
                ]

            loop(rows // 48, move)
        done(ref)


def k_phase(keep_a, keep_b, got_a, got_b, own_a, own_b, give_a, give_b):
    need()
    rows = own_a.shape[0]
    for keep, got, own, give in ((keep_a, got_a, own_a, give_a), (keep_b, got_b, own_b, give_b)):
        for dst, start in ((give, rows), (own, 0)):

            def move(r, keep=keep, got=got, dst=dst, start=start):
                s = pl.ds(pl.multiple_of(start + r * 48, 16), 48)
                dst[at(r, 48), :] = (keep[s, :].astype(f32) + got[s, :].astype(f32)).astype(bf16)

            loop(rows // 48, move)
            done(dst)


def to_blocks(blocks, dw):
    if len(blocks) == 1:
        return copy_rows(blocks[0], 0, dw)
    me = lax.axis_index("seq")
    rows = blocks[0].shape[0]
    for k in reversed(range(len(blocks))):
        block, start = blocks[k], (me ^ k) * rows

        def move(r, block=block, start=start):
            block[at(r, 48), :] = dw[pl.ds(pl.multiple_of(start + r * 48, 16), 48), :]

        loop(rows // 48, move)
        done(block)


def kb_z_normed(qz_ref, w_ref, dn_ref):
    need()

    def back(c):
        dn_ref[:, at(c, 768)] = nt(qz_ref[...], w_ref[at(c, 768), :])

    loop(WIDTH // 768, back)


def make_q(dxb_ref, ret_ref, qdt_ref, q):
    t = q.shape[0]

    def rows(r):
        q[at(r, R), :XC] = dxb_ref[pl.ds(pl.multiple_of(r * R, R) + 8, R), :].astype(bf16)

    loop(t // R, rows)
    q[t - 16 :, :XC] = (
        dxb_ref[t - 8 : t + 8, :] + jnp.concatenate([jnp.zeros((8, XC), f32), ret_ref[...]], axis=0)
    ).astype(bf16)
    q[:, XC:] = qdt_ref[...]


def x_normed(q_ref, dnz_ref, w_ref, dn_ref, dnb_ref):
    def back(c):
        cols = at(c, 768)
        d = dnz_ref[:, cols] + nt(q_ref[...], w_ref[cols, :])
        dn_ref[:, cols] = d
        dnb_ref[:, cols] = d.astype(bf16)

    loop(WIDTH // 768, back)


def x_weight(normed_ref, q_ref, dw_ref):
    def weight(c):
        dw_ref[at(c, 768), :] = tn(normed_ref[:, at(c, 768)], q_ref[...]).astype(bf16)

    loop(WIDTH // 768, weight)


def kb_x_normed(dxb_ref, ret_ref, qdt_ref, dnz_ref, w_ref, q_ref, dn_ref, dnb_ref):
    need(dxb_ref, ret_ref, qdt_ref)
    make_q(dxb_ref, ret_ref, qdt_ref, q_ref)
    done(q_ref)
    need()
    x_normed(q_ref, dnz_ref, w_ref, dn_ref, dnb_ref)


def kb_x_weight_first(normed_ref, dxb_ref, ret_ref, qdt_ref, q_ref, *rest):
    *blocks, dw = rest
    need()
    make_q(dxb_ref, ret_ref, qdt_ref, q_ref)
    done(q_ref)
    x_weight(normed_ref, q_ref, dw)
    to_blocks(blocks, dw)


def kb_x_normed_last(q_ref, dnz_ref, w_ref, dn_ref, dnb_ref):
    need()
    x_normed(q_ref, dnz_ref, w_ref, dn_ref, dnb_ref)


def kb_norm(h_ref, dn_ref, dr_ref, g_ref, par_ref, pt_ref, gh_ref, small_ref, rd_ref):
    t = h_ref.shape[0]
    need()
    small_ref[...] = jnp.zeros(small_ref.shape, f32)

    def rows(r):
        s = at(r, R)
        h = h_ref[s, :].astype(f32)
        d = dn_ref[s, :] + dr_ref[s, :].astype(f32)
        scale = lax.rsqrt(jnp.mean(h * h, axis=1, keepdims=True) + EPS)
        hs = h * scale
        small_ref[...] += fold(d * hs)
        gd = par_ref[NORM : NORM + 1, :WIDTH] * d
        back = scale * (gd - hs * jnp.mean(hs * gd, axis=1, keepdims=True))
        gh = (g_ref[s, :].astype(f32) + back).astype(bf16)
        gh_ref[s, :] = gh
        if rd_ref is not None:
            dot = jnp.sum(gh.astype(f32) * pt_ref[s, :], axis=1, keepdims=True)
            rd_ref[s, :] = jnp.broadcast_to(dot, (R, 128))

    loop(t // R, rows)


def kb_norm_last(h_ref, dn_ref, dr_ref, g_ref, par_ref, keep_ref, give_ref, small_ref, gh):
    kb_norm(h_ref, dn_ref, dr_ref, g_ref, par_ref, None, gh, small_ref, None)
    half = WIDTH // 2
    each = keep_ref.shape[0]
    odd = lax.rem(lax.axis_index("seq"), 2)

    def body(core):
        def rows(r):
            for dst, start in ((keep_ref, odd * each), (give_ref, (1 - odd) * each)):
                s = pl.ds(pl.multiple_of(start + r * R, R), R)
                dst[at(r, R), :] = gh[s, core * half : (core + 1) * half]

        loop(each // R, rows)

    on_core(body)


SMALL = 12


def k_small(*refs):
    *ins, out = refs
    need()
    out[...] = jnp.zeros(out.shape, f32)

    def total(x):
        return jnp.sum(x, axis=0, keepdims=True)

    for layer in range(2):
        a, b, c, d = ins[4 * layer : 4 * layer + 4]
        base = SMALL * layer
        for k in range(5):
            out[base + k : base + k + 1, :] = total(b[8 * k : 8 * k + 8, :])
        out[base + NORM : base + NORM + 1, :WIDTH] = total(d[...])
        out[base + GATE : base + GATE + 1, :OWN] = total(a[0:8, :])
        out[base + SKIP : base + SKIP + 1, :OWN] = total(a[8:16, :])
        out[base + STEP : base + STEP + 1, 0:128] = total(c[0:8, :])
        out[base + RATE : base + RATE + 1, 0:128] = total(c[8:16, :])


def k_small_out(mine_ref, got_ref, ng_ref, cw_ref, cb_ref, db_ref, al_ref, sk_ref, gg_ref):
    need()

    def body(core):
        base = SMALL * core
        cores = (mine_ref, got_ref) if core == 0 else (got_ref, mine_ref)
        ng_ref[...] = mine_ref[base + NORM : base + NORM + 1, :WIDTH]
        for c, src in enumerate(cores):
            cw_ref[:, c * OWN : (c + 1) * OWN] = src[base : base + 4, :OWN]
            cb_ref[:, c * OWN : (c + 1) * OWN] = src[base + BIAS : base + BIAS + 1, :OWN]
            gg_ref[:, c * OWN : (c + 1) * OWN] = src[base + GATE : base + GATE + 1, :OWN]
        a, b = cores
        cw_ref[:, INNER:] = a[base : base + 4, OWN:] + b[base : base + 4, OWN:]
        cb_ref[:, INNER:] = a[base + BIAS : base + BIAS + 1, OWN:] + b[base + BIAS : base + BIAS + 1, OWN:]
        r, c = iotas((128, 2 * HEADS))
        r2, c2 = iotas((OWN, 2 * HEADS))
        wide = lambda v: jnp.broadcast_to(v, (8, v.shape[1]))
        for ref, row in ((db_ref, STEP), (al_ref, RATE)):
            acc = jnp.zeros((8, 2 * HEADS), f32)
            for k, src in enumerate(cores):
                pick = jnp.where((r == c - k * HEADS) & (r < HEADS), 1.0, 0.0)
                acc = acc + exact(wide(src[base + row : base + row + 1, 0:128]), pick)
            ref[...] = acc[0:1]
        acc = jnp.zeros((8, 2 * HEADS), f32)
        for k, src in enumerate(cores):
            pick = jnp.where(r2 // HDIM == c2 - k * HEADS, 1.0, 0.0)
            acc = acc + exact(wide(src[base + SKIP : base + SKIP + 1, :OWN]), pick)
        sk_ref[...] = acc[0:1]

    on_core(body)


def in_place(refs, full):
    if len(refs) == 1:
        return copy_rows(full, 0, refs[0])
    odd = lax.rem(lax.axis_index("dp"), 2)
    half = refs[0].shape[0]
    copy_rows(full, odd * half, refs[0])
    copy_rows(full, (1 - odd) * half, refs[1])


def k_home(*refs):
    *halves_all, give_ref, zo, x = refs
    per = len(halves_all) // 3
    first, second, third = halves_all[:per], halves_all[per : 2 * per], halves_all[2 * per :]
    need()

    def body(core):
        if core == 0:
            in_place(first, give_ref)
        else:
            in_place(second, zo)
            in_place(third, x)
            give_ref[:, :XD] = x[...]
            give_ref[:, XD:] = zo[...]

    on_core(body)


def k_grads(*refs):
    *halves_all, got_ref, gw_ref, go_ref, dw1, zo0, x0 = refs
    per = len(halves_all) // 3
    first_halves, second, third = halves_all[:per], halves_all[per : 2 * per], halves_all[2 * per :]
    need()
    rows, half = got_ref.shape[0], WIDTH // 2

    def body(core):
        if core:
            in_place(first_halves, dw1)
        else:
            in_place(second, zo0)
            in_place(third, x0)
        mine = (x0, zo0, 0) if core == 0 else (dw1, dw1, XD)
        other = (got_ref, got_ref, XD)
        cores = (mine, other) if core == 0 else (other, mine)
        for c, (x, zo, first) in enumerate(cores):
            for k in range(2):
                col = first + OWN + k * half
                go_ref[k * rows : (k + 1) * rows, c * half : (c + 1) * half] = zo[:, col : col + half].astype(f32)

    def rest(core):
        mine = (x0, zo0, 0) if core == 0 else (dw1, dw1, XD)
        other = (got_ref, got_ref, XD)
        cores = (mine, other) if core == 0 else (other, mine)
        for c, (x, zo, first) in enumerate(cores):
            gw_ref[:, c * OWN : (c + 1) * OWN] = zo[:, first : first + OWN].astype(f32)
            gw_ref[:, INNER + c * OWN : INNER + (c + 1) * OWN] = x[:, :OWN].astype(f32)
        a, b = cores[0][0], cores[1][0]
        gw_ref[:, 2 * INNER : 2 * INNER + 2 * STATE] = a[:, OWN:XC].astype(f32) + b[:, OWN:XC].astype(f32)
        r, c = iotas((128, 2 * HEADS))
        acc = 0.0
        for k, x in enumerate((a, b)):
            pick = jnp.where((r == c - k * HEADS) & (r < HEADS), 1.0, 0.0).astype(bf16)
            acc = acc + nn(x[:, XC:XD], pick)
        gw_ref[:, INNER + CONV :] = acc

    on_core(body)
    done(go_ref)
    on_core(rest)


def across(x):
    return jax.tree.map(lambda a: lax.ppermute(a, "section", [(0, 1), (1, 0)]), x)


def flip(x, axis, bits):
    return lax.ppermute(x, axis, [(k, k ^ bits) for k in range(lax.axis_size(axis))])


def chain_step(x, steps, backward):
    n = lax.axis_size("seq")
    hop = -2 * steps if backward else 2 * steps
    return lax.ppermute(x, "seq", [(k, k + hop) for k in range(n) if 0 <= k + hop < n])


def chain(value, decay, backward):
    entered = chain_step(value, 1, backward)
    count = lax.axis_size("seq") // 2
    if count > 2:
        rate = chain_step(decay, 1, backward)
        total = entered.astype(f32)
        steps = 1
        while steps < count - 1:
            total = total + rate[0:1] * chain_step(total.astype(bf16), steps, backward).astype(f32)
            rate = rate * chain_step(rate, steps, backward)
            steps *= 2
        entered = total.astype(bf16)
    return entered


def gather_rows(x):
    n = lax.axis_size("seq")
    if n != 4:
        return [lax.all_gather(x, "seq", axis=0, tiled=True)]
    return [x, *[flip(x, "seq", k) for k in (1, 2, 3)]]


def gather_near(x):
    if lax.axis_size("seq") != 4:
        return gather_rows(x)
    return [x, flip(x, "seq", 1), flip(x, "seq", 2)]


def gather_across(parts, *release):
    if len(parts) == 1:
        return parts
    x, gx, gy = parts
    gx, gy, *_ = lax.optimization_barrier((gx, gy, *release))
    half = x.shape[0] // 2
    return [x, gx, gy, flip(gx[:half], "seq", 2), flip(gy[half:], "seq", 1)]


def k_sum(counts, *refs):
    *blocks, keep_ref, give_ref = refs
    starts = [sum(counts[:k]) for k in range(len(counts))]
    need()
    odd = lax.rem(lax.axis_index("dp"), 2)
    half = keep_ref.shape[0]
    step = 48 if half % 48 == 0 else half
    for dst, start in ((give_ref, (1 - odd) * half), (keep_ref, odd * half)):

        def rows(r, dst=dst, start=start):
            s = pl.ds(pl.multiple_of(start + r * step, 16), step)
            first = 0
            for begin, count in zip(starts, counts):
                total = 0.0
                for ref in blocks[begin : begin + count]:
                    total = total + ref[s, :].astype(f32)
                dst[at(r, step), first : first + total.shape[1]] = total.astype(dst.dtype)
                first += total.shape[1]

        loop(half // step, rows)
        done(dst)


def k_add(a_ref, b_ref, out_ref):
    need()

    def rows(r):
        s = at(r, 16)
        out_ref[s, :] = (a_ref[s, :].astype(f32) + b_ref[s, :].astype(f32)).astype(bf16)

    loop(out_ref.shape[0] // 16, rows)


def send_blocks(blocks):
    if len(blocks) > 1:
        return [blocks[0]] + [flip(blocks[k], "seq", k) for k in (3, 2, 1)]
    return [lax.psum_scatter(blocks[0], "seq", scatter_dimension=0, tiled=True)]


def whole_sum(groups):
    total = jnp.concatenate([sum(b.astype(f32) for b in group) for group in groups], axis=1)
    return [lax.psum(total.astype(bf16), "dp")]


def halved(groups, *pins):
    got = [b for group in groups for b in group]
    rows, width = got[0].shape[0], sum(group[0].shape[1] for group in groups)
    shape = (rows // 2, width)
    return run(
        functools.partial(k_sum, [len(group) for group in groups]), "sum", [(shape, f32, "a"), (shape, bf16, "a")],
        after(got[0], *pins), *got[1:],
    )


def paired(mine, got, *pins):
    return run(k_add, "add", [(got.shape, bf16, "a")], after(mine, *pins), got)[0]


def over_dp(keep, got, *pins, later=()):
    return further([paired(keep, got, *pins)], *later)


def further(mine, *later):
    (mine,), bit = mine, 2
    while bit < lax.axis_size("dp"):
        mine = paired(mine, flip(mine, "dp", bit), *later)
        bit *= 2
    return mine, flip(mine, "dp", 1)


def simple_dp(rows):
    n = lax.axis_size("dp")
    return n == 1 or n & (n - 1) != 0 or rows % 32 != 0


def summed_dp(groups, *pins, before=(), later=()):
    if simple_dp(groups[0][0].shape[0]):
        return whole_sum(groups)
    keep, give = halved(groups, *before)
    return over_dp(keep, flip(give, "dp", 1), *pins, later=later)


def k_add_small(*refs):
    *ins, out_ref = refs
    need()
    if len(ins) == 2:
        out_ref[...] = ins[0][...] + ins[1][...]
    else:
        out_ref[...] = (ins[0][...] + ins[1][...]) + (ins[2][...] + ins[3][...])


def sum_small(x, axes):
    for axis in axes:
        n = lax.axis_size(axis)
        if n == 4:
            x = run(k_add_small, "add_small", [(x.shape, f32, "a")], x, *[flip(x, axis, k) for k in (1, 2, 3)])[0]
        elif n & (n - 1):
            x = lax.psum(x, axis)
        else:
            bit = 1
            while bit < n:
                x = run(k_add_small, "add_small", [(x.shape, f32, "a")], x, flip(x, axis, bit))[0]
                bit *= 2
    return x


def sum_small_dp(x):
    n = lax.axis_size("dp")
    if n & (n - 1):
        return lax.psum(x, "dp"), x
    half_way, bit = x, 1
    while bit < n:
        x = run(k_add_small, "add_small", [(x.shape, f32, "a")], x, flip(x, "dp", bit))[0]
        half_way = x if bit == 1 else half_way
        bit *= 2
    return x, half_way


def after(x, *others):
    return lax.optimization_barrier((x, *others))[0]


AHEAD = ["xdt", "cum", "bc", "c"], ["act", "xb", "slope", "dt"], ["wz", "wx"]
AHEAD_WEIGHT, AHEAD_NORM = ["y", "yw"], ["wo", "z", "act"]


def on_device(hidden_in, cotangent, norm_gain, in_weight, conv_weight, conv_bias, dt_bias, a_log, skip, gate_gain, out_weight):
    core = lax.axis_index("section")
    first = core == 0
    odd = lax.axis_index("seq") % 2
    even = odd == 0
    length = hidden_in.shape[1]
    t = 2 * length
    n = lax.axis_size("seq")
    shard = in_weight.shape[1]
    half = WIDTH // 2
    packed = XD + 2 * OWN

    def given(x):
        return lax.dynamic_index_in_dim(x, 1 - odd, 0, keepdims=False)

    def both_sequences(mine, give):
        got = flip(give, "seq", 1)
        return jnp.stack([jnp.where(even, mine, got), jnp.where(even, got, mine)])

    hid_half, cot_half, mine_x, give_x, mine_zo, give_zo, mine_p, give_p = run(
        k_prep, "prep",
        [((length // 2, WIDTH), bf16, "a"), ((length // 2, WIDTH), bf16, "a"), ((shard, XD), bf16, "v"),
         ((shard, XD), bf16, "a"), ((shard, 2 * OWN), bf16, "v"), ((shard, 2 * OWN), bf16, "a"),
         ((PARAMS, XC), f32, "v"), ((PARAMS, XC), f32, "a")],
        *[
            far_away(a)
            for a in (hidden_in, cotangent, in_weight[0], out_weight[0], norm_gain, conv_weight[0], conv_bias, dt_bias, a_log, skip, gate_gain)
        ],
    )
    x0, x1, par0, par1 = run(
        k_pick, "pick",
        [((shard, XD), bf16, "a"), ((shard, XD), bf16, "a"), ((PARAMS, XC), f32), ((PARAMS, XC), f32)],
        mine_x, across(give_x), mine_p, across(give_p),
    )
    zo0, zo1 = run(
        k_pick_rest, "pick_rest", [((shard, 2 * OWN), bf16, "a"), ((shard, 2 * OWN), bf16, "a")], mine_zo, across(give_zo)
    )
    params = [par0, par1]

    def half_given(x):
        return lax.dynamic_slice_in_dim(given(x), core * (length // 2), length // 2, 0)

    def both_halves(mine):
        got = flip(mine, "seq", 1)
        return got, across(got)

    ga, gb = both_halves(hid_half)
    give_cot = cot_half
    parts_x0 = gather_rows(after(x0, ga, give_cot))
    near_zo0 = gather_near(after(zo0, *parts_x0))

    saved = [{}, {}]

    def keeping(layer, soon):
        return "vh" if soon else "h"

    def named(layer, names, results, modes, stayed=()):
        soon, at_result = {}, 0
        for name, mode in zip(names, modes):
            for m in mode:
                value = results[at_result]
                at_result += 1
                if m != "h":
                    soon[name] = value
                if m == mode[-1]:
                    saved[layer][name] = value
        for name in stayed:
            saved[layer][name] = results[len(results) - len(stayed) + stayed.index(name)]
        return soon

    def scan_part(layer, x, tail, near_zo, before_front):
        par = params[layer]
        last = keeping(layer, False)
        before = chain_step(tail, 1, False)
        saved[layer]["before"] = before
        modes = ["v"] * 8 + ["a"]
        shapes = [((t, XC), f32), ((t, XC), bf16), ((t, 2 * STATE), bf16), ((t, OWN), bf16), ((t, 128), f32), ((t, 128), f32),
                  ((2 * STATE, OWN), f32), ((16, OWN), f32), ((STATE, OWN), bf16)]
        x |= named(
            layer, ["act", "slope", "bc", "xdt", "dt", "cum", "s", "dec", "tot"],
            run(
                k_front, "front", [(*shape, m) for shape, m in zip(shapes, modes)],
                x["xb"], after(before, *before_front), par, scratch=[((t, OWN), f32), ((16, XC), f32)],
            ),
            modes,
        )
        dec = saved[layer]["dec"]
        saved[layer]["decay"] = dec[:8] * dec[8:] if n > 4 else None
        entered = chain(x["tot"], saved[layer]["decay"], False)
        x |= named(
            layer, ["yw"],
            run(
                k_within, "within", [((t, OWN), f32, "v")], x["cum"], x["bc"], x["xdt"],
                scratch=[((t, HEADS * 128), f32), ((t // 128, HEADS * 8, 128), f32), ((t, BLOCK), f32)],
                stay=[x[k] for k in ("xb", "slope", "dt", "cum")],
            ),
            ["v"],
            ["xb", "slope", "dt", "cum"],
        )
        parts_zo = gather_across(near_zo, before)
        x["parts_zo"] = parts_zo
        modes = ["v", "h", "v", "p"]
        x |= named(
            layer, ["z", "wz", "keep", "give"],
            run(
                k_z, "gate_in",
                [((t, OWN), f32, modes[0]), ((WIDTH, OWN), bf16, modes[1]), ((WIDTH // 2, OWN), bf16, "v"),
                 ((WIDTH // 2, OWN), bf16, "p")],
                near(after(x["normed"], x["yw"], entered)), *parts_zo, scratch=[((WIDTH, OWN), bf16)],
                stay=[x[k] for k in ("normed", "xdt", "bc", "dec")],
            ),
            modes,
            ["normed", "xdt", "bc", "dec"],
        )
        ogot = across(x["give"])
        x["entered"] = entered
        cot_halves = [ca, cb] if layer else []
        ins = [x["yw"], x["act"], x["bc"], x["cum"], entered, x["s"], x["dec"], x["z"], par, x["keep"], ogot]
        kept = "v" if layer else "h"
        stayed = ["act"] if layer else ["act", "yw", "z"]
        modes = [kept, "h" if layer else "v", "p", "vh" if layer else "v", last, kept] + ["vh"] * layer
        shapes = [((t, OWN), f32), ((t, WIDTH), f32), ((t, half + 128 if layer else WIDTH + 128), bf16),
                  ((t, 256 if layer else 128), f32), ((2 * STATE, OWN), f32), ((OWN, WIDTH), bf16)]
        shapes += [((t, WIDTH), bf16)] * layer
        results = run(
            functools.partial(k_out, layer == 0), "out", [(*shape, m) for shape, m in zip(shapes, modes)],
            *ins, *([cotangent, *cot_halves] if layer else []), scratch=[((t, OWN), f32), ((t, OWN), bf16)],
            ahead=[] if layer else [saved[0]["h"]], stay=[x[k] for k in stayed],
        )
        x |= named(layer, ["y", "p", "msg", "st", "c", "wo", "g"][: len(modes)], results, modes, stayed)
        if layer == 0:
            x["h"] = results[-1 - len(stayed)]
        return x

    outs_in = [((t, WIDTH), bf16), ((t + 8, XD), f32), ((WIDTH, XD), bf16), ((8, XC), f32)]
    names_in = ["normed", "xb", "wx", "tail"]
    modes = ["h", "v", "v", "h", "a"]
    shapes = [((t, WIDTH), bf16), *outs_in]
    x = named(
        0, ["h", *names_in],
        run(k_in, "project", [(*shape, m) for shape, m in zip(shapes, modes)], hidden_in, ga, gb, par0, *parts_x0),
        modes,
    )
    tail0 = x["tail"]
    x = scan_part(0, x, tail0, near_zo0, [])
    parts_x1 = gather_across(gather_near(after(x1, x["entered"], x["yw"], *x["parts_zo"][3:])), x["msg"])
    msg = across(x["msg"])
    near_zo1 = gather_near(after(zo1, *parts_x1, *msg))
    modes = ["h", "h", "h", "v", "v", "h", "a"]
    shapes = [((t, WIDTH), bf16), ((t, WIDTH), f32), ((t, 128), f32), *outs_in]
    x = named(
        1, ["h", "pt", "rs", *names_in],
        run(
            k_mid, "middle", [(*shape, m) for shape, m in zip(shapes, modes)],
            x["h"], x["p"], x["st"], msg, par1, *parts_x1,
        ),
        modes,
    )
    h1_far, pt, rs0 = saved[1]["h"], saved[1]["pt"], saved[1]["rs"]
    tail1 = x["tail"]
    ca, cb = both_halves(after(give_cot, tail1))
    x = scan_part(1, x, x["tail"], near_zo1, near_zo1[1:])
    p1, st1, st1_far = saved[1]["p"], x["st"], saved[1]["st"]
    msg = across(x["msg"])
    count = 4 if n == 4 else 1

    ahead_zw, ahead_within, ahead_front = AHEAD

    def backward(layer, v, g, rs, rd, close=None, before_zw=(), before_zo=()):
        par = params[layer]
        v = dict(v)
        far = dict(v)

        def fetched(names, results):
            if names:
                v.update(zip(names, results[-len(names) :]))

        qz, dy, df, dca, okeep, ogive, d, e, small_a = run(
            kb_gate, "back_gate",
            [((t, OWN), bf16, "v"), ((t, OWN), f32, "v"), ((t, OWN), bf16, "v"), ((t, 128), f32, "v"),
             ((OWN, half), bf16, "v"), ((OWN, half), bf16, "p"), ((2 * STATE, OWN), f32, "v"),
             ((STATE, OWN), bf16, "a"), ((16, OWN), f32)],
            g, *[(close or v)[k] for k in ("wo", "y", "yw", "z", "act", "bc", "cum")], rs, rd, par, (close or v)["dec"],
            scratch=[((t, OWN), f32), ((t, OWN), f32), ((t, OWN), bf16)],
        )
        entered = chain(e, v["decay"], True)
        ogot = across(ogive)
        results = run(
            kb_z_weight, "back_zw", [((WIDTH // count, 2 * OWN), bf16, "a")] * count, v["normed"], qz, okeep,
            after(ogot, *before_zw),
            scratch=[((WIDTH, 2 * OWN), bf16)], ahead=[v[k] for k in ahead_zw],
        )
        zo = list(results[:count])
        beside_zw = [*zo]
        if layer:
            zo = [after(b, entered) for b in zo]
        fetched(ahead_zw, results)
        v["act"] = far["act"]
        dy = near(after(dy, *beside_zw))
        results = run(
            kb_within, "back_within", [((t, OWN), f32, "v"), ((t, 2 * STATE), f32, "v")],
            dy, v["xdt"], v["cum"], v["bc"], df, v["c"],
            scratch=[((t, HEADS * 128), f32), ((t // 128, HEADS * 8, 128), f32), ((t, BLOCK), f32), ((t, BLOCK), f32)],
            ahead=[v[k] for k in ahead_within],
        )
        dxw, dbc = results[:2]
        if layer == 0:
            dxw, dbc = near(*lax.optimization_barrier((dxw, dbc)))
            zo = [after(b, entered, dxw, *before_zo) for b in zo]
        fetched(ahead_within, results)
        results = run(
            kb_front, "back_front",
            [((t + 8, XC), f32, "v"), ((8, XC), f32, "a"), ((t, 128), bf16, "v"), ((40, XC), f32), ((16, 128), f32)],
            entered, d, v["c"], far["dec"], v["bc"], v["xdt"], v["act"], v["xb"], v["slope"], v["before"], v["dt"], v["cum"],
            dxw, dbc, dy, dca, par,
            scratch=[((2 * STATE, OWN), f32), ((t, OWN), f32), ((t, OWN), f32), ((t, OWN), f32), ((t, XC), f32),
                     ((t, 128), f32), ((t, 128), f32), ((16, OWN), f32), ((t + 16, 128), f32)],
            ahead=[v[k] for k in ahead_front],
        )
        dxb, halo, qdt, small_b, small_c = results[:5]
        fetched(ahead_front, results)
        ret = chain_step(halo, 1, True)
        dnz = run(kb_z_normed, "back_z", [((t, WIDTH), f32, "v")], near(after(qz, halo)), v["wz"])[0]
        return dxb, ret, qdt, dnz, zo, (small_a, small_b, small_c), v, (e, dbc, halo)

    shape_q, shape_n = ((t, XD), bf16, "v"), [((t, WIDTH), f32, "v"), ((t, WIDTH), bf16, "p")]
    x_blocks = [((WIDTH // count, XD), bf16, "a")] * count
    x_scratch = [((WIDTH, XD), bf16)]
    dxb, ret, qdt, dnz, zo1, small1, v1, _ = backward(1, saved[1], x["g"], st1, msg, x)
    got_zo1 = send_blocks(zo1)
    v0 = saved[0]
    early = []
    q, dn, dnb1, *fetched = run(
        kb_x_normed, "back_x", [shape_q, shape_n[0], ((t, WIDTH), bf16, "a")], dxb, ret, qdt, dnz, v1["wx"], ahead=[v0[k] for k in early]
    )
    v0.update(zip(early, fetched))
    dr = across(dnb1)
    shapes_x = [((2 * shard, CUT), bf16, "a"), ((2 * shard, XD - CUT), bf16, "a")] * 2
    x1 = run(
        kb_x_weight, "back_xw", shapes_x if count > 1 else [((WIDTH, XD), bf16, "a")], v1["normed"],
        near(after(q, dnb1, *got_zo1)), scratch=x_scratch, ahead=[*[v0[k] for k in AHEAD_WEIGHT], h1_far, pt],
    )
    *x1, h1_near, pt_near = x1
    v0.update(zip(AHEAD_WEIGHT, x1[-len(AHEAD_WEIGHT) :]))
    x1 = x1[: -len(AHEAD_WEIGHT)]
    got_x1 = [flip(x1[0], "seq", 1), flip(x1[1], "seq", 2)] if count > 1 else []

    def second_phase(*pins):
        if count == 1:
            return [[lax.psum_scatter(x1[0], "seq", scatter_dimension=0, tiled=True)]]
        own_a, own_b, give_a, give_b = run(
            k_phase, "phase", [((shard, CUT), bf16, "a"), ((shard, XD - CUT), bf16, "a")] * 2,
            after(x1[2], *pins), x1[3], *got_x1,
        )
        return [[own_a, flip(give_a, "seq", 2)], [own_b, flip(give_b, "seq", 1)]]

    phase = second_phase()
    early = AHEAD_NORM
    g0, g0_far, small_d1, rd0, *fetched = run(
        kb_norm, "back_norm", [((t, WIDTH), bf16, "vh"), ((8, WIDTH), f32), ((t, 128), f32, "v")],
        h1_near, dn, after(dr, *x1), saved[1]["g"], par1, pt_near, ahead=[v0[k] for k in early],
    )
    v0.update(zip(early, fetched))
    dxb, ret, qdt, dnz, zo0, small0, v0, (e0, dbc0, halo0) = backward(
        0, v0, g0, rs0, rd0, before_zw=phase[0][:1], before_zo=[p[-1] for p in phase]
    )
    got_zo0 = send_blocks(zo0)
    simple = simple_dp(shard)
    halves1 = [] if simple else halved([*phase, got_zo1], dbc0)
    over1 = [] if simple else [paired(halves1[0], flip(halves1[1], "dp", 1))]
    q, *x0 = run(kb_x_weight_first, "back_xw", [shape_q] + x_blocks, v0["normed"], dxb, after(ret, *over1, *got_zo0), qdt, scratch=x_scratch)
    got_x0 = send_blocks(x0)
    dn, dnb0 = run(kb_x_normed_last, "back_x", [shape_n[0], ((t, WIDTH), bf16, "a")], near(after(q, *x0)), dnz, v0["wx"])
    dr = across(dnb0)
    sum1 = whole_sum([*phase, got_zo1]) if simple else further(over1, x0[0])
    sum_zo0 = summed_dp([got_zo0], before=[x0[0]])
    final = run(
        k_final, "final", [((length, half), bf16, "a"), ((length, half), bf16, "a")],
        h1_far, p1, st1_far, after(msg, dnb0),
    )
    hidden_out = both_sequences(*final)
    keep, give, small_d0 = run(
        kb_norm_last, "back_norm", [((length, half), bf16, "a"), ((length, half), bf16, "a"), ((8, WIDTH), f32)],
        saved[0]["h"], dn, dr, g0_far, par0, scratch=[((t, WIDTH), bf16)],
    )
    grad_in = both_sequences(keep, give)
    small = run(k_small, "small", [((2 * SMALL, XC), f32, "a")], *small0, small_d0, *small1, small_d1)[0]
    halves0 = [] if simple else halved([got_x0], final[0], keep, small)
    small = sum_small(small, ["seq"])
    first_small = small
    small, half_way = sum_small_dp(small)
    if simple:
        sum_x0 = whole_sum([got_x0])
    else:
        sum_x0 = over_dp(halves0[0], flip(halves0[1], "dp", 1), first_small, later=[half_way])
    sums = [*sum1, *sum_zo0, after(sum_x0[0], small), *sum_x0[1:]]
    heads = 2 * HEADS
    smalls = run(
        k_small_out, "small_out",
        [((1, WIDTH), f32, "a"), ((4, CONV), f32, "a"), ((1, CONV), f32, "a"), ((1, heads), f32, "a"), ((1, heads), f32, "a"), ((1, heads), f32, "a"),
         ((1, INNER), f32, "a")],
        small, across(small),
    )
    give = run(k_home, "home", [((shard, packed), bf16, "p")], *sums, scratch=[((shard, 2 * OWN), bf16), ((shard, XD), bf16)])[0]
    grad_w, grad_o = run(
        k_grads, "grads", [((shard, INNER + CONV + heads), f32, "a"), ((2 * shard, WIDTH), f32, "a")],
        *sums, across(give),
        scratch=[((shard, packed), bf16), ((shard, 2 * OWN), bf16), ((shard, XD), bf16)],
    )
    norm, taps, bias, dtb, rates, skips, gates = smalls
    return (hidden_out, grad_in, norm, grad_w[None], taps[None], bias, dtb, rates, skips, gates, grad_o[None])


def solution(mesh):
    by_section = P("section", None)
    rows = P("section", "seq", None)
    tokens = P("dp", "seq", None)
    taps = P("section", None, None)
    out = P("dp", "seq", "section")
    small = (by_section,) * 4
    return jax.shard_map(
        on_device,
        mesh=mesh,
        in_specs=(tokens, tokens, by_section, rows, taps, by_section, *small, rows),
        out_specs=(out, out, by_section, rows, taps, by_section, *small, rows),
        check_vma=False,
    )
```

```python
import functools

import jax
import jax.numpy as jnp
from jax import lax
from jax.experimental import pallas as pl
from jax.experimental.pallas import tpu as pltpu
from jax.sharding import PartitionSpec as P

HDIM = 64
STATE = 128
INNER = 1536
CONV = 1792
EPS = 1e-05
f32, bf16 = jnp.float32, jnp.bfloat16

WIDTH = 768
OWN = 768
HEADS = 12
XC = OWN + 2 * STATE
XD = XC + 128
R = 256
BLOCK = 256


def nn(a, b):
    return lax.dot_general(a, b, (((1,), (0,)), ((), ())), preferred_element_type=f32)


def nt(a, b):
    return lax.dot_general(a, b, (((1,), (1,)), ((), ())), preferred_element_type=f32)


def tn(a, b):
    return lax.dot_general(a, b, (((0,), (0,)), ((), ())), preferred_element_type=f32)


def loop(count, body, unroll=True):
    def step(k, carry):
        body(k)
        return carry

    lax.fori_loop(0, count, step, 0, unroll=unroll and count <= 8)


def at(k, size):
    return pl.ds(pl.multiple_of(k * size, size), size)


def iotas(shape):
    return lax.broadcasted_iota(jnp.int32, shape, 0), lax.broadcasted_iota(jnp.int32, shape, 1)


def spread_matrix(width, per):
    r, c = iotas((128, width))
    return jnp.where(((r & 15) == c // per) & (r < 48), 1.0, 0.0).astype(bf16)


def collect_matrix():
    r, c = iotas((OWN, 128))
    return jnp.where(((c & 15) == r // HDIM) & (c < 48), 1.0, 0.0).astype(bf16)


def thirds(v):
    high = v.astype(bf16).astype(f32)
    rest = v - high
    mid = rest.astype(bf16).astype(f32)
    lane = iotas(v.shape)[1]
    out = jnp.where(lane < 16, high, jnp.where(lane < 32, mid, rest - mid))
    return jnp.where(lane < 48, out, 0.0).astype(bf16)


def halves(v):
    high = v.astype(bf16)
    return high, (v - high.astype(f32)).astype(bf16)


def running_sum(v, backward=False):
    r, c = iotas((BLOCK, BLOCK))
    tri = jnp.where((c >= r) if backward else (r >= c), 1.0, 0.0).astype(bf16)
    high = v.astype(bf16)
    rest = v - high.astype(f32)
    mid = rest.astype(bf16)
    last = (rest - mid.astype(f32)).astype(bf16)
    return nn(tri, high) + nn(tri, mid) + nn(tri, last)


def sig(v):
    return 0.5 * jnp.tanh(0.5 * v) + 0.5


def softplus(v):
    e = jnp.exp(-jnp.abs(v))
    u = 1.0 + e
    small = u == 1.0
    return jnp.maximum(v, 0.0) + jnp.where(small, e, jnp.log(u) * e / jnp.where(small, 1.0, u - 1.0))


def fold(v):
    return jnp.sum(v.reshape(v.shape[0] // 8, 8, v.shape[1]), axis=0)


def copy_rows(dst, start, src, cols=None):
    rows = src.shape[0]
    step = next(k for k in (48, 32, 16, 8, rows) if rows % k == 0)

    def move(r):
        place = pl.ds(pl.multiple_of(start + r * step, 16), step)
        if cols is None:
            dst[place, :] = src[at(r, step), :]
        else:
            dst[place, :] = src[at(r, step), cols]

    loop(rows // step, move, False)


def place_rows(dst, parts, cols=None):
    if len(parts) == 1:
        return copy_rows(dst, 0, parts[0], cols)
    me = lax.axis_index("seq")
    rows = parts[0].shape[0]
    for k in range(min(len(parts), 4)):
        copy_rows(dst, (me ^ k) * rows, parts[k], cols)
    if len(parts) > 4:
        copy_rows(dst, (me ^ 3) * rows + rows // 2, parts[4], cols)


def on_core(body):
    me = lax.axis_index("section")
    for core in range(2):
        pl.when(me == core)(lambda core=core: body(core))


def exact(a, b):
    return lax.dot_general(
        a, b, (((1,), (0,)), ((), ())), preferred_element_type=f32, precision=lax.Precision.HIGHEST
    )


def stats_out(a, b):
    lane = iotas(a.shape)[1]
    v = jnp.where(lane < 64, a, b)
    high = v.astype(bf16).astype(f32)
    rest = v - high
    mid = rest.astype(bf16).astype(f32)
    l = lane & 63
    out = jnp.where(l < 16, high, jnp.where(l < 32, mid, rest - mid))
    return jnp.where(l < 48, out, 0.0).astype(bf16)


def stats_in(v):
    v = v.astype(f32)
    lane = iotas(v.shape)[1]
    a = jnp.sum(jnp.where(lane < 64, v, 0.0), axis=1, keepdims=True)
    b = jnp.sum(jnp.where(lane < 64, 0.0, v), axis=1, keepdims=True)
    return a * (1.0 / 16), b * (1.0 / 16)


class Copies:

    def __init__(self, pairs_in, pairs_ahead, pairs_out, sems_in, sems_out):
        self.waiting, self.ready, self.started, self.ahead = {}, {}, [], []
        for k, (far, near, whole) in enumerate(pairs_in):
            copy = pltpu.make_async_copy(far, near, sems_in.at[k])
            copy.start()
            self.waiting.setdefault(id(whole), []).append(copy)
        for k, (far, near) in enumerate(pairs_ahead):
            copy = pltpu.make_async_copy(far, near, sems_in.at[len(pairs_in) + k])
            copy.start()
            self.ahead.append(copy)
        for k, (far, near, whole) in enumerate(pairs_out):
            self.ready.setdefault(id(whole), []).append(pltpu.make_async_copy(near, far, sems_out.at[k]))

    def need(self, refs):
        for key in [id(r) for r in refs] if refs else list(self.waiting):
            for copy in self.waiting.pop(key, ()):
                copy.wait()

    def done(self, refs):
        for key in [id(r) for r in refs] if refs else list(self.ready):
            for copy in self.ready.pop(key, ()):
                copy.start()
                self.started.append(copy)


COPIES = []


def need(*refs):
    COPIES[-1].need(refs)


def done(*refs):
    COPIES[-1].done(refs)


FAR = []
NEAR = []


def near(*arrays):
    NEAR.extend(arrays)
    return arrays if len(arrays) > 1 else arrays[0]


def far_away(array):
    FAR.append(array)
    return array


def run(kernel, name, outs, *ins, scratch=(), ahead=(), stay=()):
    far, close = pl.BlockSpec(memory_space=pltpu.HBM), pl.BlockSpec(memory_space=pltpu.VMEM)
    loose = pl.BlockSpec(memory_space=pl.ANY)
    modes = [o[2] if len(o) > 2 else "h" for o in outs]
    units = [m for mode in modes for m in mode] + ["v"] * len(ahead) + ["h"] * len(stay)
    shapes, specs = [], []
    for (shape, dtype, *_), mode in zip(outs, modes):
        for m in mode:
            if m == "p":
                shapes += [jax.ShapeDtypeStruct((shape[0] // 2, *shape[1:]), dtype)] * 2
                specs += [loose] * 2
            else:
                space = dict(v=pltpu.VMEM, h=pltpu.HBM, a=jax.ShapeDtypeStruct)[m]
                shapes.append(space(shape, dtype))
                specs.append(dict(v=close, h=far, a=loose)[m])
    for a in ahead:
        shapes.append(pltpu.VMEM(a.shape, a.dtype))
        specs.append(close)
    for a in stay:
        shapes.append(pltpu.HBM(a.shape, a.dtype))
        specs.append(far)
    groups = [a if isinstance(a, (tuple, list)) else (a,) for a in (*ins, *ahead, *stay)]
    flat = [a for group in groups for a in group]
    held = [any(a is k for k in NEAR) for a in flat]
    kept = [any(a is k for k in FAR) for a in flat]
    flat = [
        pltpu.with_memory_space_constraint(a, pltpu.VMEM if h else pltpu.HBM) if h or k else a
        for a, h, k in zip(flat, held, kept)
    ]
    n_in, n_out, n_own = len(flat), len(shapes), sum(len(group) for group in groups[: len(ins)])
    buffers = [
        pltpu.VMEM((sum(a.shape[0] for a in group), *group[0].shape[1:]), group[0].dtype)
        for group in groups[: len(ins)]
        if not any(group[0] is k for k in NEAR)
    ]
    buffers += [pltpu.VMEM(shape, dtype) for (shape, dtype, *_), mode in zip(outs, modes) if "v" not in mode]

    def body(*refs):
        given, made, rest = list(refs[:n_in]), list(refs[n_in : n_in + n_out]), list(refs[n_in + n_out :])
        pairs_in, pairs_out, vin, vout = [], [], [], []
        pairs_ahead = list(zip(given[n_own:], made[n_out - len(ahead) - len(stay) :]))
        at_ref = 0
        for group in groups[: len(ins)]:
            if held[at_ref]:
                vin.append(given[at_ref])
            else:
                vin.append(rest.pop(0))
                start = 0
                for k, part in enumerate(group):
                    rows = part.shape[0]
                    place = vin[-1] if len(group) == 1 else vin[-1].at[pl.ds(start, rows)]
                    pairs_in.append((given[at_ref + k], place, vin[-1]))
                    start += rows
            at_ref += len(group)
        for mode in modes:
            vout.append(made.pop(0) if "v" in mode else rest.pop(0))
            if mode == "p":
                rows = vout[-1].shape[0] // 2
                for k in range(2):
                    pairs_out.append((made.pop(0), vout[-1].at[pl.ds(k * rows, rows)], vout[-1]))
            elif mode != "v":
                pairs_out.append((made.pop(0), vout[-1], vout[-1]))
        *extra, sems_in, sems_out = rest
        copies = Copies(pairs_in, pairs_ahead, pairs_out, sems_in, sems_out)
        COPIES.append(copies)
        kernel(*vin, *vout, *extra)
        need()
        done()
        for copy in [*copies.ahead, *copies.started]:
            copy.wait()
        COPIES.pop()

    results = list(
        pl.pallas_call(
            body,
            name=name,
            out_shape=shapes,
            in_specs=[close if h else far if k else loose for h, k in zip(held, kept)],
            out_specs=specs,
            scratch_shapes=[
                *buffers,
                *[pltpu.VMEM(s, d) for s, d in scratch],
                pltpu.SemaphoreType.DMA((max(n_in, 1),)),
                pltpu.SemaphoreType.DMA((max(n_out, 1),)),
            ],
            compiler_params=pltpu.CompilerParams(vmem_limit_bytes=MIB * 2**20),
            cost_estimate=pl.CostEstimate(flops=1, bytes_accessed=1, transcendentals=0),
        )(*flat)
    )
    grouped = []
    for unit in units:
        if unit == "p":
            grouped.append((results.pop(0), results.pop(0)))
            continue
        grouped.append(results.pop(0))
        if unit != "a":
            (NEAR if unit == "v" else FAR).append(grouped[-1])
    return grouped


MIB = 24


TAPS, BIAS, NORM, GATE, SKIP, STEP, RATE = 0, 4, 5, 6, 7, 8, 9
PARAMS = 16


def k_prep(hid_ref, cot_ref, w_ref, o_ref, ng_ref, cw_ref, cb_ref, db_ref, al_ref, sk_ref, gg_ref, hid_half, cot_half, mine_x, give_x, mine_zo, give_zo, mine_p, give_p):
    need()
    rows = w_ref.shape[0]
    half = WIDTH // 2
    r24, c24 = iotas((2 * HEADS, 128))
    rk, ck = iotas((2 * HEADS, OWN))

    def pack(core, out):
        own = core * OWN
        out[:, 0:OWN] = w_ref[:, INNER + own : INNER + own + OWN]
        out[:, OWN:XC] = w_ref[:, 2 * INNER : 2 * INNER + 2 * STATE]
        pick = ((c24 & 15) == r24 - core * HEADS) & (c24 < 48)
        steps = w_ref[:, INNER + CONV : INNER + CONV + 2 * HEADS]
        out[:, XC:XD] = nn(steps, jnp.where(pick, 1.0, 0.0).astype(bf16)).astype(bf16)

    def pack_rest(core, out, par):
        own = core * OWN
        pick = ((c24 & 15) == r24 - core * HEADS) & (c24 < 48)
        out[:, 0:OWN] = w_ref[:, own : own + OWN]
        for t in range(2):
            at_lane = OWN + t * half
            out[:, at_lane : at_lane + half] = o_ref[t * rows : (t + 1) * rows, core * half : (core + 1) * half]
        par[...] = jnp.zeros(par.shape, f32)
        par[TAPS : TAPS + 4, :OWN] = cw_ref[:, own : own + OWN]
        par[TAPS : TAPS + 4, OWN:] = cw_ref[:, INNER:]
        par[BIAS : BIAS + 1, :OWN] = cb_ref[:, own : own + OWN]
        par[BIAS : BIAS + 1, OWN:] = cb_ref[:, INNER:]
        par[NORM : NORM + 1, :WIDTH] = ng_ref[...]
        par[GATE : GATE + 1, :OWN] = gg_ref[:, own : own + OWN]
        spread = jnp.where(rk - core * HEADS == ck // HDIM, 1.0, 0.0)
        par[SKIP : SKIP + 1, :OWN] = exact(jnp.broadcast_to(sk_ref[...], (8, 2 * HEADS)), spread)[0:1]
        lanes = jnp.where(pick, 1.0, 0.0)
        par[STEP : STEP + 1, 0:128] = exact(jnp.broadcast_to(db_ref[...], (8, 2 * HEADS)), lanes)[0:1]
        par[RATE : RATE + 1, 0:128] = exact(jnp.broadcast_to(al_ref[...], (8, 2 * HEADS)), lanes)[0:1]

    def body(core):
        pack(core, mine_x)
        pack(1 - core, give_x)

    def rest(core):
        pack_rest(core, mine_zo, mine_p)
        pack_rest(1 - core, give_zo, give_p)

    on_core(body)
    done(mine_x, give_x)
    even_seq = 1 - lax.rem(lax.axis_index("seq"), 2)
    rows_half = hid_half.shape[0]
    start = lax.axis_index("section") * rows_half
    for src, dst in ((hid_ref, hid_half), (cot_ref, cot_half)):

        def move(r, src=src, dst=dst):
            dst[at(r, 32), :] = src[even_seq, pl.ds(pl.multiple_of(start + r * 32, 32), 32), :]

        loop(rows_half // 32, move)
        done(dst)
    on_core(rest)


def k_pick(mine_x, got_x, mine_p, got_p, x0, x1, p0, p1):
    need()

    def body(core):
        for layer, (x, p) in enumerate(((x0, p0), (x1, p1))):
            x[...] = (mine_x, got_x)[layer ^ core][...]
            p[...] = (mine_p, got_p)[layer ^ core][...]

    on_core(body)


def k_pick_rest(mine_zo, got_zo, zo0, zo1):
    need()

    def body(core):
        zo0[...] = (mine_zo, got_zo)[core][...]
        zo1[...] = (mine_zo, got_zo)[1 - core][...]

    on_core(body)


def norm_rows(h, gain):
    scale = lax.rsqrt(jnp.mean(h * h, axis=1, keepdims=True) + EPS)
    return (h * scale * gain).astype(bf16)


def project(t, normed_ref, wx_ref, xb_ref, tail_ref):
    xb_ref[0:8, :] = jnp.zeros((8, XD), f32)

    def cols(c):
        xb_ref[8 : 8 + t, :] = nn(normed_ref[...], wx_ref[...])

    loop(1, cols)
    tail_ref[...] = xb_ref[t:, :XC]


def k_in(hid_ref, ga_ref, gb_ref, par_ref, *rest):
    *parts, h_ref, normed_ref, xb_ref, wx_ref, tail_ref = rest
    need(hid_ref, ga_ref, gb_ref, par_ref)
    t = h_ref.shape[0]
    half = t // 2
    odd = lax.rem(lax.axis_index("seq"), 2)
    core = lax.axis_index("section")
    copy_rows(h_ref, odd * half, hid_ref.at[odd])
    copy_rows(h_ref, (1 - odd) * half + core * (half // 2), ga_ref)
    copy_rows(h_ref, (1 - odd) * half + (1 - core) * (half // 2), gb_ref)

    def rows(r):
        normed_ref[at(r, R), :] = norm_rows(h_ref[at(r, R), :].astype(f32), par_ref[NORM : NORM + 1, :WIDTH])

    loop(t // R, rows)
    done(h_ref, normed_ref)
    need(*parts)
    place_rows(wx_ref, parts)
    done(wx_ref)
    project(t, normed_ref, wx_ref, xb_ref, tail_ref)


def k_mid(h_ref, p_ref, st_ref, msg_ref, par_ref, *rest):
    *parts, h1_ref, pt_ref, rs_ref, normed_ref, xb_ref, wx_ref, tail_ref = rest
    need(h_ref, p_ref, st_ref, msg_ref, par_ref)
    t = h_ref.shape[0]

    def rows(r):
        s = at(r, R)
        other = stats_in(msg_ref[s, WIDTH:])[0]
        rs = lax.rsqrt((st_ref[s, 0:128] + other) * (1.0 / INNER) + EPS)
        rs_ref[s, :] = rs
        p = p_ref[s, :] + msg_ref[s, :WIDTH].astype(f32)
        pt_ref[s, :] = p
        h1 = (h_ref[s, :].astype(f32) + rs[:, 0:1] * p).astype(bf16)
        h1_ref[s, :] = h1
        normed_ref[s, :] = norm_rows(h1.astype(f32), par_ref[NORM : NORM + 1, :WIDTH])

    loop(t // R, rows)
    done(h1_ref, pt_ref, rs_ref, normed_ref)
    need(*parts)
    place_rows(wx_ref, parts)
    done(wx_ref)
    project(t, normed_ref, wx_ref, xb_ref, tail_ref)


def k_z(normed_ref, *rest):
    *parts, z_ref, wz_ref, keep_ref, give_ref, o = rest
    need(*parts)
    place_rows(wz_ref, parts, slice(0, OWN))
    done(wz_ref)
    place_rows(o, parts, slice(OWN, 2 * OWN))

    def split(core):
        rows = keep_ref.shape[0]
        keep_ref[...] = o[core * rows : (core + 1) * rows, :]
        give_ref[...] = o[(1 - core) * rows : (2 - core) * rows, :]

    on_core(split)
    done(keep_ref, give_ref)
    need(normed_ref)

    def cols(c):
        z_ref[:, at(c, 768)] = nn(normed_ref[...], wz_ref[:, at(c, 768)])

    loop(OWN // 768, cols)


def k_front(xb_ref, before_ref, par_ref, act_ref, slope_ref, bc_ref, xdt_ref, dt_ref, cum_ref, s_ref, dec_ref, tot_ref, wide, edge):
    t = act_ref.shape[0]
    need()
    edge[0:8, :] = before_ref[...]
    edge[8:16, :] = jnp.zeros((8, XC), f32)

    def conv(c):
        cols = at(c, 128)
        w = par_ref[0:8, cols]
        total = w[4:5] + w[0:1] * xb_ref[pl.ds(5, t), cols]
        for k in range(1, 4):
            total = total + w[k : k + 1] * xb_ref[pl.ds(5 + k, t), cols]
        first = total[0:8]
        for k in range(4):
            first = first + w[k : k + 1] * edge[5 + k : 13 + k, cols]
        total = jnp.concatenate([first, total[8:]], axis=0)
        sg = sig(total)
        act = total * sg
        act_ref[:, cols] = act
        slope_ref[:, cols] = (sg + act * (1.0 - sg)).astype(bf16)

    loop(XC // 128, conv)
    bc_ref[...] = act_ref[:, OWN:].astype(bf16)
    done(act_ref, slope_ref, bc_ref)
    dt = softplus(xb_ref[8 : 8 + t, XC:] + par_ref[STEP : STEP + 1, 0:128])
    dt_ref[...] = dt
    done(dt_ref)
    rate = -jnp.exp(par_ref[RATE : RATE + 1, 0:128])
    spread = spread_matrix(OWN, HDIM)
    wide[...] = nn(thirds(dt), spread)

    def rows(r):
        s = at(r, R)
        xdt_ref[s, :] = (act_ref[s, :OWN] * wide[s, :]).astype(bf16)

    loop(t // R, rows)
    done(xdt_ref)
    for b in range(t // BLOCK):
        s = pl.ds(b * BLOCK, BLOCK)
        cum = running_sum(rate * dt[b * BLOCK : (b + 1) * BLOCK])
        cum_ref[s, :] = cum
        end = cum[BLOCK - 1 : BLOCK, :]
        dec_ref[8 * b : 8 * b + 8, :] = nn(thirds(jnp.exp(jnp.broadcast_to(end, (8, 128)))), spread)
        wide[s, :] = nn(thirds(jnp.exp(end - cum)), spread)
        bl = bc_ref[s, 0:STATE]

        def cols(c):
            decayed = (xdt_ref[s, at(c, 768)].astype(f32) * wide[s, at(c, 768)]).astype(bf16)
            s_ref[pl.ds(b * STATE, STATE), at(c, 768)] = tn(bl, decayed)

        loop(OWN // 768, cols)
    tot_ref[...] = (s_ref[STATE:, :] + dec_ref[8:9, :] * s_ref[:STATE, :]).astype(bf16)


def decay_tables(cum_ref, tall, flat):
    t = cum_ref.shape[0]
    parts = thirds(cum_ref[...])
    tall[...] = nn(parts, spread_matrix(HEADS * 128, 128))
    r, c = iotas((HEADS * 8, 128))
    pick = jnp.where(((c & 15) == r // 8) & (c < 48), 1.0, 0.0).astype(bf16)
    for b in range(t // 128):
        flat[b] = nt(pick, parts[b * 128 : (b + 1) * 128])


def k_within(cum_ref, bc_ref, xdt_ref, y_ref, tall, flat, scores):
    t = cum_ref.shape[0]
    need(cum_ref)
    decay_tables(cum_ref, tall, flat)
    blocks = t // BLOCK
    need(bc_ref, xdt_ref)
    for b in range(blocks):
        s = pl.ds(b * BLOCK, BLOCK)
        scores[s, :] = nt(bc_ref[s, STATE:], bc_ref[s, 0:STATE])
    r, c = iotas((128, 128))
    causal = r >= c
    lane = iotas((BLOCK, 128))[1]

    def pair(p):
        cols = at(p, 128)
        for b in range(blocks):
            o = b * BLOCK
            u = xdt_ref[pl.ds(o, BLOCK), cols]
            top = jnp.zeros((128, 128), f32)
            low = jnp.zeros((128, 128), f32)
            for a in range(2):
                head = 2 * p + a
                own = jnp.where((lane >= 64) == (a == 1), u, jnp.zeros_like(u))
                hc = at(head, 128)
                hr = pl.ds(pl.multiple_of(head * 8, 8), 8)
                t0, t1 = tall[pl.ds(o, 128), hc], tall[pl.ds(o + 128, 128), hc]
                u0, u1 = flat[2 * b, hr, :][0:1], flat[2 * b + 1, hr, :][0:1]
                sc = scores
                w00 = jnp.where(causal, sc[pl.ds(o, 128), 0:128] * jnp.exp(jnp.where(causal, t0 - u0, 0.0)), 0.0)
                w10 = sc[pl.ds(o + 128, 128), 0:128] * jnp.exp(t1 - u0)
                w11 = jnp.where(causal, sc[pl.ds(o + 128, 128), 128:] * jnp.exp(jnp.where(causal, t1 - u1, 0.0)), 0.0)
                top = top + nn(w00.astype(bf16), own[:128])
                low = low + nn(w10.astype(bf16), own[:128]) + nn(w11.astype(bf16), own[128:])
            y_ref[pl.ds(o, 128), cols] = top
            y_ref[pl.ds(o + 128, 128), cols] = low

    loop(OWN // 128, pair)


def k_out(first_layer, yw_ref, act_ref, bc_ref, cum_ref, cin_ref, s_ref, dec_ref, z_ref, par_ref, keep_ref, got_ref, *rest):
    if first_layer:
        y_ref, p_ref, msg_ref, st_ref, c_ref, wo_ref, wide, u_ref = rest
    else:
        cot_ref, ca_ref, cb_ref, y_ref, p_ref, msg_ref, st_ref, c_ref, wo_ref, g_ref, wide, u_ref = rest
    t = yw_ref.shape[0]
    half = WIDTH // 2
    shard = o_rows(keep_ref)

    def weights(core):
        for r in range(keep_ref.shape[0] // shard):
            for k in range(2):
                for src, side in ((keep_ref, core), (got_ref, 1 - core)):
                    wo_ref[(2 * r + k) * shard : (2 * r + k + 1) * shard, side * half : (side + 1) * half] = src[
                        r * shard : (r + 1) * shard, k * half : (k + 1) * half
                    ]

    need(keep_ref, got_ref)
    on_core(weights)
    done(wo_ref)
    need(bc_ref, cum_ref, cin_ref, s_ref, dec_ref)
    c_ref[0:STATE, :] = cin_ref[...].astype(f32)
    c_ref[STATE:, :] = s_ref[:STATE, :] + dec_ref[0:1, :] * c_ref[0:STATE, :]
    wide[...] = nn(thirds(jnp.exp(cum_ref[...])), spread_matrix(OWN, HDIM))
    for b in range(t // BLOCK):
        s = pl.ds(b * BLOCK, BLOCK)

        def cols(c):
            from_state = nn(bc_ref[s, STATE:], c_ref[pl.ds(b * STATE, STATE), at(c, 768)].astype(bf16))
            wide[s, at(c, 768)] = wide[s, at(c, 768)] * from_state

        loop(OWN // 768, cols)

    done(c_ref)
    need(yw_ref, act_ref, z_ref, par_ref)

    def rows(r):
        s = at(r, R)
        y = yw_ref[s, :] + wide[s, :] + par_ref[SKIP : SKIP + 1, :OWN] * act_ref[s, :OWN]
        y_ref[s, :] = y
        z = z_ref[s, :]
        gated = y * z * sig(z)
        u_ref[s, :] = (gated * par_ref[GATE : GATE + 1, :OWN]).astype(bf16)
        st_ref[s, 0:128] = jnp.broadcast_to(jnp.sum(gated * gated, axis=1, keepdims=True), (R, 128))

    loop(t // R, rows)
    done(y_ref)

    def project_out(c):
        p_ref[:, at(c, 768)] = nn(u_ref[...], wo_ref[:, at(c, 768)])

    loop(WIDTH // 768, project_out)
    done(p_ref)
    if first_layer:

        def send(r):
            s = at(r, R)
            msg_ref[s, :WIDTH] = p_ref[s, :].astype(bf16)
            v = st_ref[s, 0:128]
            msg_ref[s, WIDTH:] = stats_out(v, v)

        loop(t // R, send)
    else:
        odd = lax.rem(lax.axis_index("seq"), 2)
        need(cot_ref, ca_ref, cb_ref)
        copy_rows(g_ref, odd * (t // 2), cot_ref.at[odd])
        core = lax.axis_index("section")
        copy_rows(g_ref, (1 - odd) * (t // 2) + core * (t // 4), ca_ref)
        copy_rows(g_ref, (1 - odd) * (t // 2) + (1 - core) * (t // 4), cb_ref)
        done(g_ref)

        def dots(r):
            s = at(r, R)
            d = jnp.sum(p_ref[s, :] * g_ref[s, :].astype(f32), axis=1, keepdims=True)
            d = jnp.broadcast_to(d, (R, 128))
            st_ref[s, 128:256] = d
            msg_ref[s, half:] = stats_out(st_ref[s, 0:128], d)

        loop(t // R, dots)

        def send(core):
            msg_ref[:, :half] = p_ref[:, (1 - core) * half : (2 - core) * half].astype(bf16)

        on_core(send)


def o_rows(keep_ref):
    return keep_ref.shape[0] // (lax.axis_size("seq") // 2)


def k_final(h_ref, p_ref, st_ref, msg_ref, keep_ref, give_ref):
    need()
    half = WIDTH // 2
    rows_each = keep_ref.shape[0]
    odd = lax.rem(lax.axis_index("seq"), 2)

    def body(core):
        cols = slice(core * half, (core + 1) * half)

        def half_out(dst, start):
            def rows(r):
                s = pl.ds(pl.multiple_of(start + r * R, R), R)
                other = stats_in(msg_ref[s, half:])[0]
                rs = lax.rsqrt((st_ref[s, 0:1] + other) * (1.0 / INNER) + EPS)
                p = p_ref[s, cols] + msg_ref[s, :half].astype(f32)
                dst[at(r, R), :] = (h_ref[s, cols].astype(f32) + rs * p).astype(bf16)

            loop(rows_each // R, rows)

        half_out(keep_ref, odd * rows_each)
        half_out(give_ref, (1 - odd) * rows_each)

    on_core(body)


def kb_gate(g_ref, w_ref, y_ref, yw_ref, z_ref, act_ref, bc_ref, cum_ref, rs_ref, rd_ref, par_ref, dec_ref,
            qz_ref, dy_ref, df_ref, dca_ref, keep_ref, give_ref, d_ref, e_ref, small_ref, dgn, wide, gn):
    t = g_ref.shape[0]
    need(g_ref, w_ref)

    def back(c):
        dgn[:, at(c, 768)] = nt(g_ref[...], w_ref[at(c, 768), :])

    loop(OWN // 768, back)
    need(cum_ref)
    wide[...] = nn(thirds(jnp.exp(cum_ref[...])), spread_matrix(OWN, HDIM))
    small_ref[...] = jnp.zeros(small_ref.shape, f32)
    collect = collect_matrix()
    need()

    def rows(r):
        s = at(r, R)
        z, y, d, x = z_ref[s, :], y_ref[s, :], dgn[s, :], act_ref[s, :OWN]
        gg = par_ref[GATE : GATE + 1, :OWN]
        if rs_ref.shape[1] == 128:
            rs, rd = rs_ref[s, 0:1], rd_ref[s, 0:1]
        else:
            squares, dots = stats_in(rd_ref[s, WIDTH // 2 :])
            rs = lax.rsqrt((rs_ref[s, 0:1] + squares) * (1.0 / INNER) + EPS)
            rd = rs_ref[s, 128:129] + dots
        sg = sig(z)
        sz = z * sg
        gated = y * sz
        scaled = gated * rs
        small_ref[0:8, :] += fold(d * scaled)
        gn[s, :] = (scaled * gg).astype(bf16)
        dgated = rs * (gg * d) - gated * (rs * rs * rs * rd * (1.0 / INNER))
        dy = dgated * sz
        dy_ref[s, :] = dy
        qz_ref[s, :] = (dgated * y * (sg * (1.0 + z - sz))).astype(bf16)
        small_ref[8:16, :] += fold(dy * x)
        df_ref[s, :] = (wide[s, :] * dy).astype(bf16)
        yw = yw_ref[s, :]
        high, low = halves(dy.astype(bf16).astype(f32) * yw + dy * (y - yw - par_ref[SKIP : SKIP + 1, :OWN] * x))
        sums = nn(jnp.concatenate([high, low], axis=0), collect)
        dca_ref[s, :] = sums[:R] + sums[R:]

    loop(t // R, rows)
    done(dy_ref, qz_ref, df_ref, dca_ref, small_ref)
    for b in range(t // BLOCK):
        s = pl.ds(b * BLOCK, BLOCK)
        cl = bc_ref[s, STATE:]

        def cols(c):
            d_ref[pl.ds(b * STATE, STATE), at(c, 768)] = tn(cl, df_ref[s, at(c, 768)])

        loop(OWN // 768, cols)
    e_ref[...] = (d_ref[:STATE, :] + dec_ref[0:1, :] * d_ref[STATE:, :]).astype(bf16)

    done(d_ref, e_ref)
    half = WIDTH // 2

    def halves_of(core):
        def weight(c):
            dw = tn(gn[:, at(c, 768)], g_ref[...]).astype(bf16)
            keep_ref[at(c, 768), :] = dw[:, core * half : (core + 1) * half]
            give_ref[at(c, 768), :] = dw[:, (1 - core) * half : (2 - core) * half]

        loop(OWN // 768, weight)

    on_core(halves_of)


def kb_within(dy_ref, xdt_ref, cum_ref, bc_ref, df_ref, c_ref, dx_ref, dbc_ref, tall, flat, scores, ds):
    t = cum_ref.shape[0]
    need(cum_ref)
    decay_tables(cum_ref, tall, flat)
    blocks = t // BLOCK
    need(bc_ref, xdt_ref, dy_ref)
    for b in range(blocks):
        s = pl.ds(b * BLOCK, BLOCK)
        scores[s, :] = nt(bc_ref[s, STATE:], bc_ref[s, 0:STATE])
    ds[...] = jnp.zeros(ds.shape, f32)
    r, c = iotas((128, 128))
    causal = r >= c
    lane = iotas((BLOCK, 128))[1]

    def pair(p):
        cols = at(p, 128)
        for b in range(blocks):
            o = b * BLOCK
            u = xdt_ref[pl.ds(o, BLOCK), cols]
            g = dy_ref[pl.ds(o, BLOCK), cols].astype(bf16)
            top = jnp.zeros((128, 128), f32)
            low = jnp.zeros((128, 128), f32)
            for a in range(2):
                head = 2 * p + a
                own = jnp.where((lane >= 64) == (a == 1), g, jnp.zeros_like(g))
                hc = at(head, 128)
                hr = pl.ds(pl.multiple_of(head * 8, 8), 8)
                t0, t1 = tall[pl.ds(o, 128), hc], tall[pl.ds(o + 128, 128), hc]
                u0, u1 = flat[2 * b, hr, :][0:1], flat[2 * b + 1, hr, :][0:1]
                e00 = jnp.where(causal, jnp.exp(jnp.where(causal, t0 - u0, 0.0)), 0.0)
                e10 = jnp.exp(t1 - u0)
                e11 = jnp.where(causal, jnp.exp(jnp.where(causal, t1 - u1, 0.0)), 0.0)
                q0, q1 = pl.ds(o, 128), pl.ds(o + 128, 128)
                w00 = (scores[q0, 0:128] * e00).astype(bf16)
                w10 = (scores[q1, 0:128] * e10).astype(bf16)
                w11 = (scores[q1, 128:] * e11).astype(bf16)
                top = top + tn(w00, own[:128]) + tn(w10, own[128:])
                low = low + tn(w11, own[128:])
                ds[q0, 0:128] += nt(own[:128], u[:128]) * e00
                ds[q1, 0:128] += nt(own[128:], u[:128]) * e10
                ds[q1, 128:] += nt(own[128:], u[128:]) * e11
            dx_ref[pl.ds(o, 128), cols] = top
            dx_ref[pl.ds(o + 128, 128), cols] = low

    loop(OWN // 128, pair, False)
    done(dx_ref)
    need(df_ref, c_ref)
    for b in range(blocks):
        s = pl.ds(b * BLOCK, BLOCK)
        d = ds[s, :].astype(bf16)
        carried = c_ref[pl.ds(b * STATE, STATE), :].astype(bf16)
        dbc_ref[s, 0:STATE] = tn(d, bc_ref[s, STATE:])
        dbc_ref[s, STATE:] = nn(d, bc_ref[s, 0:STATE]) + nt(df_ref[s, :], carried)


def kb_front(gin_ref, d_ref, c_ref, dec_ref, bc_ref, xdt_ref, act_ref, xb_ref, slope_ref, before_ref, dt_ref, cum_ref, dxw_ref, dbc_ref,
             dy_ref, dca_ref, par_ref,
             dxb_ref, halo_ref, qdt_ref, small_ref, head_ref, gs, dd, te, dtw, dact, red, red2, ends, pad):
    t = act_ref.shape[0]
    blocks = t // BLOCK
    spread, collect = spread_matrix(OWN, HDIM), collect_matrix()
    need(gin_ref, d_ref, dec_ref)
    gs[STATE:, :] = gin_ref[...].astype(f32)
    gs[:STATE, :] = d_ref[STATE:, :] + dec_ref[8:9, :] * gs[STATE:, :]
    need(dbc_ref, dt_ref, c_ref, cum_ref, bc_ref, xdt_ref)
    dact[:, OWN:] = dbc_ref[...]
    dtw[...] = nn(thirds(dt_ref[...]), spread)
    for b in range(blocks):
        s = pl.ds(b * BLOCK, BLOCK)
        ss = pl.ds(b * STATE, STATE)
        end = cum_ref[pl.ds((b + 1) * BLOCK - 8, 8), :][7:8]
        te[s, :] = nn(thirds(jnp.exp(end - cum_ref[s, :])), spread)
        bl = bc_ref[s, 0:STATE]
        ends[8 * b : 8 * b + 8, :] = fold(gs[ss, :] * c_ref[ss, :]) * dec_ref[8 * b : 8 * b + 8, :]

        def cols(c):
            q = at(c, 768)
            low = gs[ss, q].astype(bf16)
            dd[s, q] = nn(bl, low)
            decayed = (xdt_ref[s, q].astype(f32) * te[s, q]).astype(bf16)
            dact[s, OWN : OWN + STATE] += nt(decayed, low)

        loop(OWN // 768, cols)
        if b == 0:
            need(dxw_ref, dy_ref, act_ref, par_ref)

        def rows(r):
            q = pl.ds(pl.multiple_of(b * BLOCK + r * R, R), R)
            w = dd[q, :] * te[q, :]
            ends[8 * b : 8 * b + 8, :] += fold(w * xdt_ref[q, :].astype(f32))
            dxdt = dxw_ref[q, :] + w
            dact[q, :OWN] = dxdt * dtw[q, :] + par_ref[SKIP : SKIP + 1, :OWN] * dy_ref[q, :]
            parts = [(dxdt * act_ref[q, :OWN]).astype(bf16), *halves(dxdt * xdt_ref[q, :].astype(f32))]
            sums = nn(jnp.concatenate(parts, axis=0), collect)
            red[q, :] = sums[:R]
            red2[q, :] = sums[R : 2 * R] + sums[2 * R :]

        loop(BLOCK // R, rows)
    need()
    high, low = halves(ends[...])
    at_end = nn(high, collect) + nn(low, collect)
    rate = -jnp.exp(par_ref[RATE : RATE + 1, 0:128])
    head_ref[...] = jnp.zeros(head_ref.shape, f32)
    for b in range(blocks):
        s = pl.ds(b * BLOCK, BLOCK)
        dt = dt_ref[s, :]
        total = running_sum(dca_ref[s, :] - red2[s, :], True)
        total = total + jnp.sum(at_end[8 * b : 8 * b + 8], axis=0, keepdims=True)
        ddt = red[s, :] + rate * total
        raw = xb_ref[pl.ds(8 + b * BLOCK, BLOCK), XC:] + par_ref[STEP : STEP + 1, 0:128]
        draw = ddt * jax.nn.sigmoid(raw)
        head_ref[0:8, :] += fold(draw)
        head_ref[8:16, :] += fold(rate * dt * total)
        lane = iotas(draw.shape)[1]
        qdt_ref[s, :] = jnp.where(lane < HEADS, draw, 0.0).astype(bf16)
    done(qdt_ref, head_ref)
    pad[0:8, :] = jnp.zeros((8, 128), f32)
    pad[8 + t :, :] = jnp.zeros((8, 128), f32)

    def conv(c):
        cols = at(c, 128)
        w = par_ref[0:8, cols]
        d = dact[:, cols] * slope_ref[:, cols].astype(f32)
        pad[8 : 8 + t, :] = d
        small_ref[32:40, cols] = fold(d)
        xb, before = xb_ref[:, cols], before_ref[:, cols]
        out = 0.0
        for k in range(4):
            later = pad[3 - k : 11 - k + t, :]
            out = out + w[k : k + 1] * later
            small_ref[8 * k : 8 * k + 8, cols] = fold(later * xb) + later[0:8] * before
        dxb_ref[:, cols] = out
        halo_ref[:, cols] = out[0:8]

    loop(XC // 128, conv)


def z_weight(dw_ref, first, normed_ref, qz_ref, okeep_ref, ogot_ref):
    def weight(c):
        dw_ref[at(c, 768), first : first + OWN] = tn(normed_ref[:, at(c, 768)], qz_ref[...]).astype(bf16)

    loop(WIDTH // 768, weight)
    n = lax.axis_size("seq")
    shard, half = WIDTH // n, WIDTH // 2
    need()

    def out(core):
        for j in range(n):
            src = okeep_ref if j // (n // 2) == core else ogot_ref
            for k in range(2):
                row, col = (2 * (j % (n // 2)) + k) * shard, first + OWN + k * half
                dw_ref[j * shard : (j + 1) * shard, col : col + half] = src[row : row + shard, :]

    on_core(out)


def kb_z_weight(normed_ref, qz_ref, okeep_ref, ogot_ref, *rest):
    *blocks, dw_ref = rest
    need(normed_ref, qz_ref)
    z_weight(dw_ref, 0, normed_ref, qz_ref, okeep_ref, ogot_ref)
    to_blocks(blocks, dw_ref)


CUT = 640


def kb_x_weight(normed_ref, q_ref, *rest):
    *parts, dw_ref = rest
    need()
    x_weight(normed_ref, q_ref, dw_ref)
    if len(parts) == 1:
        return copy_rows(parts[0], 0, dw_ref)
    me = lax.axis_index("seq")
    rows = WIDTH // 4
    first, last = slice(0, CUT), slice(CUT, XD)
    for ref, cols, ranks in zip(parts, (first, last, first, last), ((1, 3), (2, 3), (0, 2), (0, 1))):
        for k, bits in enumerate(ranks):
            start = (me ^ bits) * rows

            def move(r, ref=ref, cols=cols, k=k, start=start):
                ref[pl.ds(pl.multiple_of(k * rows + r * 48, 16), 48), :] = dw_ref[
                    pl.ds(pl.multiple_of(start + r * 48, 16), 48), cols
                ]

            loop(rows // 48, move, False)
        done(ref)


def k_phase(keep_a, keep_b, got_a, got_b, own_a, own_b, give_a, give_b):
    need()
    rows = own_a.shape[0]
    for keep, got, own, give in ((keep_a, got_a, own_a, give_a), (keep_b, got_b, own_b, give_b)):
        for dst, start in ((give, rows), (own, 0)):

            def move(r, keep=keep, got=got, dst=dst, start=start):
                s = pl.ds(pl.multiple_of(start + r * 48, 16), 48)
                dst[at(r, 48), :] = (keep[s, :].astype(f32) + got[s, :].astype(f32)).astype(bf16)

            loop(rows // 48, move, False)
            done(dst)


def to_blocks(blocks, dw):
    if len(blocks) == 1:
        return copy_rows(blocks[0], 0, dw)
    me = lax.axis_index("seq")
    rows = blocks[0].shape[0]
    for k in reversed(range(len(blocks))):
        block, start = blocks[k], (me ^ k) * rows

        def move(r, block=block, start=start):
            block[at(r, 48), :] = dw[pl.ds(pl.multiple_of(start + r * 48, 16), 48), :]

        loop(rows // 48, move, False)
        done(block)


def kb_z_normed(qz_ref, w_ref, dn_ref):
    need()

    def back(c):
        dn_ref[:, at(c, 768)] = nt(qz_ref[...], w_ref[at(c, 768), :])

    loop(WIDTH // 768, back)


def make_q(dxb_ref, ret_ref, qdt_ref, q):
    t = q.shape[0]

    def rows(r):
        q[at(r, R), :XC] = dxb_ref[pl.ds(pl.multiple_of(r * R, R) + 8, R), :].astype(bf16)

    loop(t // R, rows)
    q[t - 16 :, :XC] = (
        dxb_ref[t - 8 : t + 8, :] + jnp.concatenate([jnp.zeros((8, XC), f32), ret_ref[...]], axis=0)
    ).astype(bf16)
    q[:, XC:] = qdt_ref[...]


def x_normed(q_ref, dnz_ref, w_ref, dn_ref, dnb_ref):
    def back(c):
        cols = at(c, 768)
        d = dnz_ref[:, cols] + nt(q_ref[...], w_ref[cols, :])
        dn_ref[:, cols] = d
        dnb_ref[:, cols] = d.astype(bf16)

    loop(WIDTH // 768, back)


def x_weight(normed_ref, q_ref, dw_ref):
    def weight(c):
        dw_ref[at(c, 768), :] = tn(normed_ref[:, at(c, 768)], q_ref[...]).astype(bf16)

    loop(WIDTH // 768, weight)


def kb_x_normed(dxb_ref, ret_ref, qdt_ref, dnz_ref, w_ref, q_ref, dn_ref, dnb_ref):
    need(dxb_ref, ret_ref, qdt_ref)
    make_q(dxb_ref, ret_ref, qdt_ref, q_ref)
    done(q_ref)
    need()
    x_normed(q_ref, dnz_ref, w_ref, dn_ref, dnb_ref)


def kb_x_weight_first(normed_ref, dxb_ref, ret_ref, qdt_ref, q_ref, *rest):
    *blocks, dw = rest
    need()
    make_q(dxb_ref, ret_ref, qdt_ref, q_ref)
    done(q_ref)
    x_weight(normed_ref, q_ref, dw)
    to_blocks(blocks, dw)


def kb_x_normed_last(q_ref, dnz_ref, w_ref, dn_ref, dnb_ref):
    need()
    x_normed(q_ref, dnz_ref, w_ref, dn_ref, dnb_ref)


def kb_norm(h_ref, dn_ref, dr_ref, g_ref, par_ref, pt_ref, gh_ref, small_ref, rd_ref):
    t = h_ref.shape[0]
    need()
    small_ref[...] = jnp.zeros(small_ref.shape, f32)

    def rows(r):
        s = at(r, R)
        h = h_ref[s, :].astype(f32)
        d = dn_ref[s, :] + dr_ref[s, :].astype(f32)
        scale = lax.rsqrt(jnp.mean(h * h, axis=1, keepdims=True) + EPS)
        hs = h * scale
        small_ref[...] += fold(d * hs)
        gd = par_ref[NORM : NORM + 1, :WIDTH] * d
        back = scale * (gd - hs * jnp.mean(hs * gd, axis=1, keepdims=True))
        gh = (g_ref[s, :].astype(f32) + back).astype(bf16)
        gh_ref[s, :] = gh
        if rd_ref is not None:
            dot = jnp.sum(gh.astype(f32) * pt_ref[s, :], axis=1, keepdims=True)
            rd_ref[s, :] = jnp.broadcast_to(dot, (R, 128))

    loop(t // R, rows)


def kb_norm_last(h_ref, dn_ref, dr_ref, g_ref, par_ref, keep_ref, give_ref, small_ref, gh):
    kb_norm(h_ref, dn_ref, dr_ref, g_ref, par_ref, None, gh, small_ref, None)
    half = WIDTH // 2
    each = keep_ref.shape[0]
    odd = lax.rem(lax.axis_index("seq"), 2)

    def body(core):
        def rows(r):
            for dst, start in ((keep_ref, odd * each), (give_ref, (1 - odd) * each)):
                s = pl.ds(pl.multiple_of(start + r * R, R), R)
                dst[at(r, R), :] = gh[s, core * half : (core + 1) * half]

        loop(each // R, rows)

    on_core(body)


SMALL = 12


def k_small(*refs):
    *ins, out = refs
    need()
    out[...] = jnp.zeros(out.shape, f32)

    def total(x):
        return jnp.sum(x, axis=0, keepdims=True)

    for layer in range(2):
        a, b, c, d = ins[4 * layer : 4 * layer + 4]
        base = SMALL * layer
        for k in range(5):
            out[base + k : base + k + 1, :] = total(b[8 * k : 8 * k + 8, :])
        out[base + NORM : base + NORM + 1, :WIDTH] = total(d[...])
        out[base + GATE : base + GATE + 1, :OWN] = total(a[0:8, :])
        out[base + SKIP : base + SKIP + 1, :OWN] = total(a[8:16, :])
        out[base + STEP : base + STEP + 1, 0:128] = total(c[0:8, :])
        out[base + RATE : base + RATE + 1, 0:128] = total(c[8:16, :])


def k_small_out(mine_ref, got_ref, ng_ref, cw_ref, cb_ref, db_ref, al_ref, sk_ref, gg_ref):
    need()

    def body(core):
        base = SMALL * core
        cores = (mine_ref, got_ref) if core == 0 else (got_ref, mine_ref)
        ng_ref[...] = mine_ref[base + NORM : base + NORM + 1, :WIDTH]
        for c, src in enumerate(cores):
            cw_ref[:, c * OWN : (c + 1) * OWN] = src[base : base + 4, :OWN]
            cb_ref[:, c * OWN : (c + 1) * OWN] = src[base + BIAS : base + BIAS + 1, :OWN]
            gg_ref[:, c * OWN : (c + 1) * OWN] = src[base + GATE : base + GATE + 1, :OWN]
        a, b = cores
        cw_ref[:, INNER:] = a[base : base + 4, OWN:] + b[base : base + 4, OWN:]
        cb_ref[:, INNER:] = a[base + BIAS : base + BIAS + 1, OWN:] + b[base + BIAS : base + BIAS + 1, OWN:]
        r, c = iotas((128, 2 * HEADS))
        r2, c2 = iotas((OWN, 2 * HEADS))
        wide = lambda v: jnp.broadcast_to(v, (8, v.shape[1]))
        for ref, row in ((db_ref, STEP), (al_ref, RATE)):
            acc = jnp.zeros((8, 2 * HEADS), f32)
            for k, src in enumerate(cores):
                pick = jnp.where((r == c - k * HEADS) & (r < HEADS), 1.0, 0.0)
                acc = acc + exact(wide(src[base + row : base + row + 1, 0:128]), pick)
            ref[...] = acc[0:1]
        acc = jnp.zeros((8, 2 * HEADS), f32)
        for k, src in enumerate(cores):
            pick = jnp.where(r2 // HDIM == c2 - k * HEADS, 1.0, 0.0)
            acc = acc + exact(wide(src[base + SKIP : base + SKIP + 1, :OWN]), pick)
        sk_ref[...] = acc[0:1]

    on_core(body)


def in_place(refs, full):
    if len(refs) == 1:
        return copy_rows(full, 0, refs[0])
    odd = lax.rem(lax.axis_index("dp"), 2)
    half = refs[0].shape[0]
    copy_rows(full, odd * half, refs[0])
    copy_rows(full, (1 - odd) * half, refs[1])


def k_home(*refs):
    *halves_all, give_ref, zo, x = refs
    per = len(halves_all) // 3
    first, second, third = halves_all[:per], halves_all[per : 2 * per], halves_all[2 * per :]
    need()

    def body(core):
        if core == 0:
            in_place(first, give_ref)
        else:
            in_place(second, zo)
            in_place(third, x)
            give_ref[:, :XD] = x[...]
            give_ref[:, XD:] = zo[...]

    on_core(body)


def k_grads(*refs):
    *halves_all, got_ref, gw_ref, go_ref, dw1, zo0, x0 = refs
    per = len(halves_all) // 3
    first_halves, second, third = halves_all[:per], halves_all[per : 2 * per], halves_all[2 * per :]
    need()
    rows, half = got_ref.shape[0], WIDTH // 2

    def body(core):
        if core:
            in_place(first_halves, dw1)
        else:
            in_place(second, zo0)
            in_place(third, x0)
        mine = (x0, zo0, 0) if core == 0 else (dw1, dw1, XD)
        other = (got_ref, got_ref, XD)
        cores = (mine, other) if core == 0 else (other, mine)
        for c, (x, zo, first) in enumerate(cores):
            for k in range(2):
                col = first + OWN + k * half
                go_ref[k * rows : (k + 1) * rows, c * half : (c + 1) * half] = zo[:, col : col + half].astype(f32)

    def rest(core):
        mine = (x0, zo0, 0) if core == 0 else (dw1, dw1, XD)
        other = (got_ref, got_ref, XD)
        cores = (mine, other) if core == 0 else (other, mine)
        for c, (x, zo, first) in enumerate(cores):
            gw_ref[:, c * OWN : (c + 1) * OWN] = zo[:, first : first + OWN].astype(f32)
            gw_ref[:, INNER + c * OWN : INNER + (c + 1) * OWN] = x[:, :OWN].astype(f32)
        a, b = cores[0][0], cores[1][0]
        gw_ref[:, 2 * INNER : 2 * INNER + 2 * STATE] = a[:, OWN:XC].astype(f32) + b[:, OWN:XC].astype(f32)
        r, c = iotas((128, 2 * HEADS))
        acc = 0.0
        for k, x in enumerate((a, b)):
            pick = jnp.where((r == c - k * HEADS) & (r < HEADS), 1.0, 0.0).astype(bf16)
            acc = acc + nn(x[:, XC:XD], pick)
        gw_ref[:, INNER + CONV :] = acc

    on_core(body)
    done(go_ref)
    on_core(rest)


def across(x):
    return jax.tree.map(lambda a: lax.ppermute(a, "section", [(0, 1), (1, 0)]), x)


def flip(x, axis, bits):
    return lax.ppermute(x, axis, [(k, k ^ bits) for k in range(lax.axis_size(axis))])


def chain_step(x, steps, backward):
    n = lax.axis_size("seq")
    hop = -2 * steps if backward else 2 * steps
    return lax.ppermute(x, "seq", [(k, k + hop) for k in range(n) if 0 <= k + hop < n])


def chain(value, decay, backward):
    entered = chain_step(value, 1, backward)
    count = lax.axis_size("seq") // 2
    if count > 2:
        rate = chain_step(decay, 1, backward)
        total = entered.astype(f32)
        steps = 1
        while steps < count - 1:
            total = total + rate[0:1] * chain_step(total.astype(bf16), steps, backward).astype(f32)
            rate = rate * chain_step(rate, steps, backward)
            steps *= 2
        entered = total.astype(bf16)
    return entered


def gather_rows(x):
    n = lax.axis_size("seq")
    if n != 4:
        return [lax.all_gather(x, "seq", axis=0, tiled=True)]
    return [x, *[flip(x, "seq", k) for k in (1, 2, 3)]]


def gather_near(x):
    if lax.axis_size("seq") != 4:
        return gather_rows(x)
    return [x, flip(x, "seq", 1), flip(x, "seq", 2)]


def gather_across(parts, *release):
    if len(parts) == 1:
        return parts
    x, gx, gy = parts
    gx, gy, *_ = lax.optimization_barrier((gx, gy, *release))
    half = x.shape[0] // 2
    return [x, gx, gy, flip(gx[:half], "seq", 2), flip(gy[half:], "seq", 1)]


def k_sum(counts, *refs):
    *blocks, keep_ref, give_ref = refs
    starts = [sum(counts[:k]) for k in range(len(counts))]
    need()
    odd = lax.rem(lax.axis_index("dp"), 2)
    half = keep_ref.shape[0]
    step = 48 if half % 48 == 0 else half
    for dst, start in ((give_ref, (1 - odd) * half), (keep_ref, odd * half)):

        def rows(r, dst=dst, start=start):
            s = pl.ds(pl.multiple_of(start + r * step, 16), step)
            first = 0
            for begin, count in zip(starts, counts):
                total = 0.0
                for ref in blocks[begin : begin + count]:
                    total = total + ref[s, :].astype(f32)
                dst[at(r, step), first : first + total.shape[1]] = total.astype(dst.dtype)
                first += total.shape[1]

        loop(half // step, rows)
        done(dst)


def k_add(a_ref, b_ref, out_ref):
    need()

    def rows(r):
        s = at(r, 16)
        out_ref[s, :] = (a_ref[s, :].astype(f32) + b_ref[s, :].astype(f32)).astype(bf16)

    loop(out_ref.shape[0] // 16, rows)


def send_blocks(blocks):
    if len(blocks) > 1:
        return [blocks[0]] + [flip(blocks[k], "seq", k) for k in (3, 2, 1)]
    return [lax.psum_scatter(blocks[0], "seq", scatter_dimension=0, tiled=True)]


def whole_sum(groups):
    total = jnp.concatenate([sum(b.astype(f32) for b in group) for group in groups], axis=1)
    return [lax.psum(total.astype(bf16), "dp")]


def halved(groups, *pins):
    got = [b for group in groups for b in group]
    rows, width = got[0].shape[0], sum(group[0].shape[1] for group in groups)
    shape = (rows // 2, width)
    return run(
        functools.partial(k_sum, [len(group) for group in groups]), "sum", [(shape, f32, "a"), (shape, bf16, "a")],
        after(got[0], *pins), *got[1:],
    )


def paired(mine, got, *pins):
    return run(k_add, "add", [(got.shape, bf16, "a")], after(mine, *pins), got)[0]


def over_dp(keep, got, *pins, later=()):
    return further([paired(keep, got, *pins)], *later)


def further(mine, *later):
    (mine,), bit = mine, 2
    while bit < lax.axis_size("dp"):
        mine = paired(mine, flip(mine, "dp", bit), *later)
        bit *= 2
    return mine, flip(mine, "dp", 1)


def simple_dp(rows):
    n = lax.axis_size("dp")
    return n == 1 or n & (n - 1) != 0 or rows % 32 != 0


def summed_dp(groups, *pins, before=(), later=()):
    if simple_dp(groups[0][0].shape[0]):
        return whole_sum(groups)
    keep, give = halved(groups, *before)
    return over_dp(keep, flip(give, "dp", 1), *pins, later=later)


def k_add_small(*refs):
    *ins, out_ref = refs
    need()
    if len(ins) == 2:
        out_ref[...] = ins[0][...] + ins[1][...]
    else:
        out_ref[...] = (ins[0][...] + ins[1][...]) + (ins[2][...] + ins[3][...])


def sum_small(x, axes):
    for axis in axes:
        n = lax.axis_size(axis)
        if n == 4:
            x = run(k_add_small, "add_small", [(x.shape, f32, "a")], x, *[flip(x, axis, k) for k in (1, 2, 3)])[0]
        elif n & (n - 1):
            x = lax.psum(x, axis)
        else:
            bit = 1
            while bit < n:
                x = run(k_add_small, "add_small", [(x.shape, f32, "a")], x, flip(x, axis, bit))[0]
                bit *= 2
    return x


def sum_small_dp(x):
    n = lax.axis_size("dp")
    if n & (n - 1):
        return lax.psum(x, "dp"), x
    half_way, bit = x, 1
    while bit < n:
        x = run(k_add_small, "add_small", [(x.shape, f32, "a")], x, flip(x, "dp", bit))[0]
        half_way = x if bit == 1 else half_way
        bit *= 2
    return x, half_way


def after(x, *others):
    return lax.optimization_barrier((x, *others))[0]


AHEAD = ["xdt", "cum", "bc", "c"], ["act", "xb", "slope", "dt"], ["wz", "wx"]
AHEAD_WEIGHT, AHEAD_NORM = ["y", "yw"], ["wo", "z", "act"]


def on_device(hidden_in, cotangent, norm_gain, in_weight, conv_weight, conv_bias, dt_bias, a_log, skip, gate_gain, out_weight):
    core = lax.axis_index("section")
    first = core == 0
    odd = lax.axis_index("seq") % 2
    even = odd == 0
    length = hidden_in.shape[1]
    t = 2 * length
    n = lax.axis_size("seq")
    shard = in_weight.shape[1]
    half = WIDTH // 2
    packed = XD + 2 * OWN

    def given(x):
        return lax.dynamic_index_in_dim(x, 1 - odd, 0, keepdims=False)

    def both_sequences(mine, give):
        got = flip(give, "seq", 1)
        return jnp.stack([jnp.where(even, mine, got), jnp.where(even, got, mine)])

    hid_half, cot_half, mine_x, give_x, mine_zo, give_zo, mine_p, give_p = run(
        k_prep, "prep",
        [((length // 2, WIDTH), bf16, "a"), ((length // 2, WIDTH), bf16, "a"), ((shard, XD), bf16, "v"),
         ((shard, XD), bf16, "a"), ((shard, 2 * OWN), bf16, "v"), ((shard, 2 * OWN), bf16, "a"),
         ((PARAMS, XC), f32, "v"), ((PARAMS, XC), f32, "a")],
        *[
            far_away(a)
            for a in (hidden_in, cotangent, in_weight[0], out_weight[0], norm_gain, conv_weight[0], conv_bias, dt_bias, a_log, skip, gate_gain)
        ],
    )
    x0, x1, par0, par1 = run(
        k_pick, "pick",
        [((shard, XD), bf16, "a"), ((shard, XD), bf16, "a"), ((PARAMS, XC), f32), ((PARAMS, XC), f32)],
        mine_x, across(give_x), mine_p, across(give_p),
    )
    zo0, zo1 = run(
        k_pick_rest, "pick_rest", [((shard, 2 * OWN), bf16, "a"), ((shard, 2 * OWN), bf16, "a")], mine_zo, across(give_zo)
    )
    params = [par0, par1]

    def half_given(x):
        return lax.dynamic_slice_in_dim(given(x), core * (length // 2), length // 2, 0)

    def both_halves(mine):
        got = flip(mine, "seq", 1)
        return got, across(got)

    ga, gb = both_halves(hid_half)
    give_cot = cot_half
    parts_x0 = gather_rows(after(x0, ga, give_cot))
    near_zo0 = gather_near(after(zo0, *parts_x0))

    saved = [{}, {}]

    def keeping(layer, soon):
        return "vh" if soon else "h"

    def named(layer, names, results, modes, stayed=()):
        soon, at_result = {}, 0
        for name, mode in zip(names, modes):
            for m in mode:
                value = results[at_result]
                at_result += 1
                if m != "h":
                    soon[name] = value
                if m == mode[-1]:
                    saved[layer][name] = value
        for name in stayed:
            saved[layer][name] = results[len(results) - len(stayed) + stayed.index(name)]
        return soon

    def scan_part(layer, x, tail, near_zo, before_front):
        par = params[layer]
        last = keeping(layer, False)
        before = chain_step(tail, 1, False)
        saved[layer]["before"] = before
        modes = ["v"] * 8 + ["a"]
        shapes = [((t, XC), f32), ((t, XC), bf16), ((t, 2 * STATE), bf16), ((t, OWN), bf16), ((t, 128), f32), ((t, 128), f32),
                  ((2 * STATE, OWN), f32), ((16, OWN), f32), ((STATE, OWN), bf16)]
        x |= named(
            layer, ["act", "slope", "bc", "xdt", "dt", "cum", "s", "dec", "tot"],
            run(
                k_front, "front", [(*shape, m) for shape, m in zip(shapes, modes)],
                x["xb"], after(before, *before_front), par, scratch=[((t, OWN), f32), ((16, XC), f32)],
            ),
            modes,
        )
        dec = saved[layer]["dec"]
        saved[layer]["decay"] = dec[:8] * dec[8:] if n > 4 else None
        entered = chain(x["tot"], saved[layer]["decay"], False)
        x |= named(
            layer, ["yw"],
            run(
                k_within, "within", [((t, OWN), f32, "v")], x["cum"], x["bc"], x["xdt"],
                scratch=[((t, HEADS * 128), f32), ((t // 128, HEADS * 8, 128), f32), ((t, BLOCK), f32)],
                stay=[x[k] for k in ("xb", "slope", "dt", "cum")],
            ),
            ["v"],
            ["xb", "slope", "dt", "cum"],
        )
        parts_zo = gather_across(near_zo, before)
        x["parts_zo"] = parts_zo
        modes = ["v", "h", "v", "p"]
        x |= named(
            layer, ["z", "wz", "keep", "give"],
            run(
                k_z, "gate_in",
                [((t, OWN), f32, modes[0]), ((WIDTH, OWN), bf16, modes[1]), ((WIDTH // 2, OWN), bf16, "v"),
                 ((WIDTH // 2, OWN), bf16, "p")],
                near(after(x["normed"], x["yw"], entered)), *parts_zo, scratch=[((WIDTH, OWN), bf16)],
                stay=[x[k] for k in ("normed", "xdt", "bc", "dec")],
            ),
            modes,
            ["normed", "xdt", "bc", "dec"],
        )
        ogot = across(x["give"])
        x["entered"] = entered
        cot_halves = [ca, cb] if layer else []
        ins = [x["yw"], x["act"], x["bc"], x["cum"], entered, x["s"], x["dec"], x["z"], par, x["keep"], ogot]
        kept = "v" if layer else "h"
        stayed = ["act"] if layer else ["act", "yw", "z"]
        modes = [kept, "h" if layer else "v", "p", "vh" if layer else "v", last, kept] + ["vh"] * layer
        shapes = [((t, OWN), f32), ((t, WIDTH), f32), ((t, half + 128 if layer else WIDTH + 128), bf16),
                  ((t, 256 if layer else 128), f32), ((2 * STATE, OWN), f32), ((OWN, WIDTH), bf16)]
        shapes += [((t, WIDTH), bf16)] * layer
        results = run(
            functools.partial(k_out, layer == 0), "out", [(*shape, m) for shape, m in zip(shapes, modes)],
            *ins, *([cotangent, *cot_halves] if layer else []), scratch=[((t, OWN), f32), ((t, OWN), bf16)],
            ahead=[] if layer else [saved[0]["h"]], stay=[x[k] for k in stayed],
        )
        x |= named(layer, ["y", "p", "msg", "st", "c", "wo", "g"][: len(modes)], results, modes, stayed)
        if layer == 0:
            x["h"] = results[-1 - len(stayed)]
        return x

    outs_in = [((t, WIDTH), bf16), ((t + 8, XD), f32), ((WIDTH, XD), bf16), ((8, XC), f32)]
    names_in = ["normed", "xb", "wx", "tail"]
    modes = ["h", "v", "v", "h", "a"]
    shapes = [((t, WIDTH), bf16), *outs_in]
    x = named(
        0, ["h", *names_in],
        run(k_in, "project", [(*shape, m) for shape, m in zip(shapes, modes)], hidden_in, ga, gb, par0, *parts_x0),
        modes,
    )
    tail0 = x["tail"]
    x = scan_part(0, x, tail0, near_zo0, [])
    parts_x1 = gather_across(gather_near(after(x1, x["entered"], x["yw"], *x["parts_zo"][3:])), x["msg"])
    msg = across(x["msg"])
    near_zo1 = gather_near(after(zo1, *parts_x1, *msg))
    modes = ["h", "h", "h", "v", "v", "h", "a"]
    shapes = [((t, WIDTH), bf16), ((t, WIDTH), f32), ((t, 128), f32), *outs_in]
    x = named(
        1, ["h", "pt", "rs", *names_in],
        run(
            k_mid, "middle", [(*shape, m) for shape, m in zip(shapes, modes)],
            x["h"], x["p"], x["st"], msg, par1, *parts_x1,
        ),
        modes,
    )
    h1_far, pt, rs0 = saved[1]["h"], saved[1]["pt"], saved[1]["rs"]
    tail1 = x["tail"]
    ca, cb = both_halves(after(give_cot, tail1))
    x = scan_part(1, x, x["tail"], near_zo1, near_zo1[1:])
    p1, st1, st1_far = saved[1]["p"], x["st"], saved[1]["st"]
    msg = across(x["msg"])
    count = 4 if n == 4 else 1

    ahead_zw, ahead_within, ahead_front = AHEAD

    def backward(layer, v, g, rs, rd, close=None, before_zw=(), before_zo=()):
        par = params[layer]
        v = dict(v)
        far = dict(v)

        def fetched(names, results):
            if names:
                v.update(zip(names, results[-len(names) :]))

        qz, dy, df, dca, okeep, ogive, d, e, small_a = run(
            kb_gate, "back_gate",
            [((t, OWN), bf16, "v"), ((t, OWN), f32, "v"), ((t, OWN), bf16, "v"), ((t, 128), f32, "v"),
             ((OWN, half), bf16, "v"), ((OWN, half), bf16, "p"), ((2 * STATE, OWN), f32, "v"),
             ((STATE, OWN), bf16, "a"), ((16, OWN), f32)],
            g, *[(close or v)[k] for k in ("wo", "y", "yw", "z", "act", "bc", "cum")], rs, rd, par, (close or v)["dec"],
            scratch=[((t, OWN), f32), ((t, OWN), f32), ((t, OWN), bf16)],
        )
        entered = chain(e, v["decay"], True)
        ogot = across(ogive)
        results = run(
            kb_z_weight, "back_zw", [((WIDTH // count, 2 * OWN), bf16, "a")] * count, v["normed"], qz, okeep,
            after(ogot, *before_zw),
            scratch=[((WIDTH, 2 * OWN), bf16)], ahead=[v[k] for k in ahead_zw],
        )
        zo = list(results[:count])
        beside_zw = [*zo]
        if layer:
            zo = [after(b, entered) for b in zo]
        fetched(ahead_zw, results)
        v["act"] = far["act"]
        dy = near(after(dy, *beside_zw))
        results = run(
            kb_within, "back_within", [((t, OWN), f32, "v"), ((t, 2 * STATE), f32, "v")],
            dy, v["xdt"], v["cum"], v["bc"], df, v["c"],
            scratch=[((t, HEADS * 128), f32), ((t // 128, HEADS * 8, 128), f32), ((t, BLOCK), f32), ((t, BLOCK), f32)],
            ahead=[v[k] for k in ahead_within],
        )
        dxw, dbc = results[:2]
        if layer == 0:
            dxw, dbc = near(*lax.optimization_barrier((dxw, dbc)))
            zo = [after(b, entered, dxw, *before_zo) for b in zo]
        fetched(ahead_within, results)
        results = run(
            kb_front, "back_front",
            [((t + 8, XC), f32, "v"), ((8, XC), f32, "a"), ((t, 128), bf16, "v"), ((40, XC), f32), ((16, 128), f32)],
            entered, d, v["c"], far["dec"], v["bc"], v["xdt"], v["act"], v["xb"], v["slope"], v["before"], v["dt"], v["cum"],
            dxw, dbc, dy, dca, par,
            scratch=[((2 * STATE, OWN), f32), ((t, OWN), f32), ((t, OWN), f32), ((t, OWN), f32), ((t, XC), f32),
                     ((t, 128), f32), ((t, 128), f32), ((16, OWN), f32), ((t + 16, 128), f32)],
            ahead=[v[k] for k in ahead_front],
        )
        dxb, halo, qdt, small_b, small_c = results[:5]
        fetched(ahead_front, results)
        ret = chain_step(halo, 1, True)
        dnz = run(kb_z_normed, "back_z", [((t, WIDTH), f32, "v")], near(after(qz, halo)), v["wz"])[0]
        return dxb, ret, qdt, dnz, zo, (small_a, small_b, small_c), v, (e, dbc, halo)

    shape_q, shape_n = ((t, XD), bf16, "v"), [((t, WIDTH), f32, "v"), ((t, WIDTH), bf16, "p")]
    x_blocks = [((WIDTH // count, XD), bf16, "a")] * count
    x_scratch = [((WIDTH, XD), bf16)]
    dxb, ret, qdt, dnz, zo1, small1, v1, _ = backward(1, saved[1], x["g"], st1, msg, x)
    got_zo1 = send_blocks(zo1)
    v0 = saved[0]
    early = []
    q, dn, dnb1, *fetched = run(
        kb_x_normed, "back_x", [shape_q, shape_n[0], ((t, WIDTH), bf16, "a")], dxb, ret, qdt, dnz, v1["wx"], ahead=[v0[k] for k in early]
    )
    v0.update(zip(early, fetched))
    dr = across(dnb1)
    shapes_x = [((2 * shard, CUT), bf16, "a"), ((2 * shard, XD - CUT), bf16, "a")] * 2
    x1 = run(
        kb_x_weight, "back_xw", shapes_x if count > 1 else [((WIDTH, XD), bf16, "a")], v1["normed"],
        near(after(q, dnb1, *got_zo1)), scratch=x_scratch, ahead=[*[v0[k] for k in AHEAD_WEIGHT], h1_far, pt],
    )
    *x1, h1_near, pt_near = x1
    v0.update(zip(AHEAD_WEIGHT, x1[-len(AHEAD_WEIGHT) :]))
    x1 = x1[: -len(AHEAD_WEIGHT)]
    got_x1 = [flip(x1[0], "seq", 1), flip(x1[1], "seq", 2)] if count > 1 else []

    def second_phase(*pins):
        if count == 1:
            return [[lax.psum_scatter(x1[0], "seq", scatter_dimension=0, tiled=True)]]
        own_a, own_b, give_a, give_b = run(
            k_phase, "phase", [((shard, CUT), bf16, "a"), ((shard, XD - CUT), bf16, "a")] * 2,
            after(x1[2], *pins), x1[3], *got_x1,
        )
        return [[own_a, flip(give_a, "seq", 2)], [own_b, flip(give_b, "seq", 1)]]

    phase = second_phase()
    early = AHEAD_NORM
    g0, g0_far, small_d1, rd0, *fetched = run(
        kb_norm, "back_norm", [((t, WIDTH), bf16, "vh"), ((8, WIDTH), f32), ((t, 128), f32, "v")],
        h1_near, dn, after(dr, *x1), saved[1]["g"], par1, pt_near, ahead=[v0[k] for k in early],
    )
    v0.update(zip(early, fetched))
    dxb, ret, qdt, dnz, zo0, small0, v0, (e0, dbc0, halo0) = backward(
        0, v0, g0, rs0, rd0, before_zw=phase[0][:1], before_zo=[p[-1] for p in phase]
    )
    got_zo0 = send_blocks(zo0)
    simple = simple_dp(shard)
    halves1 = [] if simple else halved([*phase, got_zo1], dbc0)
    over1 = [] if simple else [paired(halves1[0], flip(halves1[1], "dp", 1))]
    q, *x0 = run(kb_x_weight_first, "back_xw", [shape_q] + x_blocks, v0["normed"], dxb, after(ret, *over1, *got_zo0), qdt, scratch=x_scratch)
    got_x0 = send_blocks(x0)
    dn, dnb0 = run(kb_x_normed_last, "back_x", [shape_n[0], ((t, WIDTH), bf16, "a")], near(after(q, *x0)), dnz, v0["wx"])
    dr = across(dnb0)
    sum1 = whole_sum([*phase, got_zo1]) if simple else further(over1, x0[0])
    sum_zo0 = summed_dp([got_zo0], before=[x0[0]])
    final = run(
        k_final, "final", [((length, half), bf16, "a"), ((length, half), bf16, "a")],
        h1_far, p1, st1_far, after(msg, dnb0),
    )
    hidden_out = both_sequences(*final)
    keep, give, small_d0 = run(
        kb_norm_last, "back_norm", [((length, half), bf16, "a"), ((length, half), bf16, "a"), ((8, WIDTH), f32)],
        saved[0]["h"], dn, dr, g0_far, par0, scratch=[((t, WIDTH), bf16)],
    )
    grad_in = both_sequences(keep, give)
    small = run(k_small, "small", [((2 * SMALL, XC), f32, "a")], *small0, small_d0, *small1, small_d1)[0]
    halves0 = [] if simple else halved([got_x0], final[0], keep, small)
    small = sum_small(small, ["seq"])
    first_small = small
    small, half_way = sum_small_dp(small)
    if simple:
        sum_x0 = whole_sum([got_x0])
    else:
        sum_x0 = over_dp(halves0[0], flip(halves0[1], "dp", 1), first_small, later=[half_way])
    sums = [*sum1, *sum_zo0, after(sum_x0[0], small), *sum_x0[1:]]
    heads = 2 * HEADS
    smalls = run(
        k_small_out, "small_out",
        [((1, WIDTH), f32, "a"), ((4, CONV), f32, "a"), ((1, CONV), f32, "a"), ((1, heads), f32, "a"), ((1, heads), f32, "a"), ((1, heads), f32, "a"),
         ((1, INNER), f32, "a")],
        small, across(small),
    )
    give = run(k_home, "home", [((shard, packed), bf16, "p")], *sums, scratch=[((shard, 2 * OWN), bf16), ((shard, XD), bf16)])[0]
    grad_w, grad_o = run(
        k_grads, "grads", [((shard, INNER + CONV + heads), f32, "a"), ((2 * shard, WIDTH), f32, "a")],
        *sums, across(give),
        scratch=[((shard, packed), bf16), ((shard, 2 * OWN), bf16), ((shard, XD), bf16)],
    )
    norm, taps, bias, dtb, rates, skips, gates = smalls
    return (hidden_out, grad_in, norm, grad_w[None], taps[None], bias, dtb, rates, skips, gates, grad_o[None])


def solution(mesh):
    by_section = P("section", None)
    rows = P("section", "seq", None)
    tokens = P("dp", "seq", None)
    taps = P("section", None, None)
    out = P("dp", "seq", "section")
    small = (by_section,) * 4
    return jax.shard_map(
        on_device,
        mesh=mesh,
        in_specs=(tokens, tokens, by_section, rows, taps, by_section, *small, rows),
        out_specs=(out, out, by_section, rows, taps, by_section, *small, rows),
        check_vma=False,
    )
```
